32 devices in a mesh: row: 8 (over z, y), col: 4 (over x, core).
Axes of the slice: x: 2, y: 2, z: 4, core: 2. Of those that a mesh axis runs over, the one named last changes fastest.
Arguments:
- a_send: bfloat16 [2, 32, 32, 128, 128], P(None, ('row', 'col')), may hold values from -6 to 6
- a_where: int32 [2, 32, 32], P(None, ('row', 'col')), may hold values from -1 to 255, as said below
- b_strips: bfloat16 [8, 4, 16, 8, 128, 128], P('row', 'col'), may hold values from -0.25 to 0.25
- b_cols: int32 [8, 4, 16, 8], P('row', 'col'), may hold values from -1 to 7, as said below
Outputs:
- c_panel: bfloat16 [16384, 4096], P('row', 'col')
The draws below stay inside these ranges and needn't reach their ends.
Inputs may be any that keep to these rules, and one draw needn't show every extreme that they name: `a_where`: positions named within one panel half of one grid device are distinct. Each panel half of each grid device has at least 12 and at most 24 named slots, and in every draw some have exactly 24. `b_cols`: block columns named within one block row of one panel are distinct. Each block row has at least 4 named slots, and in every draw some have exactly 8; the named slots lie anywhere in the row.
All inputs are finite; a program needn't handle non-finite values.
Results may differ from the reference program's by a relative error of at most 0.001.
Values may be sent and summed in bfloat16 or wider, within the bound.
No kernel may reach another device: no remote copies, remote signals or barrier semaphores. Data moves between devices by JAX's collectives and lax.ppermute only.
A program may use at most 128 MiB of HBM per device.

```python
import jax
import jax.numpy as jnp
from jax import lax

BS = 128
RB = 16
KB = 16
NJ = 8
RCAP = 8
STEPS = 2
CAPA = 24
N_ROW = 8
N_COL = 4


def draw_a_where(key, part):
    key = jax.random.fold_in(key, 11)
    devices = N_ROW * N_COL
    total_slots = 2 * devices
    key_list = jax.random.split(key, total_slots + 1)
    offset = jax.random.randint(key_list[total_slots], (), 0, 5)

    def one_panel(subkey, which_panel):
        key_rank, key_place, key_count = jax.random.split(subkey, 3)
        rank_of = jax.random.permutation(key_rank, devices)
        places = jax.random.permutation(key_place, RB * KB)
        filled = jax.random.randint(key_count, (), CAPA // 2, CAPA + 1)
        filled = jnp.where(which_panel % 5 == offset, CAPA, filled)
        chosen = jnp.take(places, jnp.minimum(rank_of, RB * KB - 1))
        return jnp.where(rank_of < filled, chosen, -1).astype(jnp.int32)
    panel_table = jax.vmap(one_panel)(key_list[:total_slots], jnp.arange(total_slots, dtype=jnp.int32))
    return panel_table.reshape(2, devices, devices).transpose(0, 2, 1)


def draw_b_cols(key, part):
    key = jax.random.fold_in(key, 23)
    row_count = N_ROW * N_COL * KB
    key_list = jax.random.split(key, row_count + 1)
    offset = jax.random.randint(key_list[row_count], (), 0, 7)

    def one_row(subkey, which_row):
        key_cols, key_slots, key_count = jax.random.split(subkey, 3)
        columns = jax.random.permutation(key_cols, NJ)[:RCAP]
        slot_rank = jax.random.permutation(key_slots, RCAP)
        filled = jax.random.randint(key_count, (), RCAP // 2, RCAP + 1)
        filled = jnp.where(which_row % 7 == offset, RCAP, filled)
        return jnp.where(slot_rank < filled, columns, -1).astype(jnp.int32)
    row_table = jax.vmap(one_row)(key_list[:row_count], jnp.arange(row_count, dtype=jnp.int32))
    return row_table.reshape(N_ROW, N_COL, KB, RCAP)


def block_scale(key, shape, shards, least, top_value):
    def one(axis_at, blocks):
        steps = jax.random.uniform(jax.random.fold_in(jax.random.fold_in(key, 6), axis_at), (blocks,), jnp.float32, least / len(shards), top_value / len(shards))
        return jnp.repeat(jnp.exp(steps), shape[axis_at] // blocks).reshape((-1,) + (1,) * (len(shape) - axis_at - 1))

    level = one(*shards[0])
    for cut in shards[1:]:
        level = level * one(*cut)
    return level


def noise(stream_key, shape, scale, limit, pieces=(), kind=jnp.bfloat16):
    result = scale * jax.random.normal(stream_key, shape, jnp.float32)
    if pieces:
        result = result * block_scale(stream_key, shape, pieces, -0.22, 0.18)
    return jnp.clip(result, -limit, limit).astype(kind)


def setup_inputs(seed: int = 0) -> dict:
    streams_of = jax.random.split(jax.random.key(seed), 5)
    return {
        "a_send": noise(streams_of[0], (2, N_ROW * N_COL, N_ROW * N_COL, BS, BS), 1.0, 6.0, ((1, 32),)),
        "a_where": draw_a_where(jax.random.fold_in(streams_of[4], 71), 0),
        "b_strips": noise(streams_of[2], (N_ROW, N_COL, KB, RCAP, BS, BS), (4 * BS) ** -0.5, 0.25, ((0, 8), (1, 4))),
        "b_cols": draw_b_cols(jax.random.fold_in(streams_of[4], 71), 0),
    }


def panel_product(totals, blocks, places, strips, columns):
    group = blocks.shape[0] // 4

    def one_turn(turn, totals):
        block_part = lax.dynamic_slice_in_dim(blocks, turn * group, group, 0)
        place_part = lax.dynamic_slice_in_dim(places, turn * group, group, 0)
        safe_place = jnp.maximum(place_part, 0)
        k_column = (safe_place % KB).astype(jnp.int32)
        block_row = (safe_place // KB).astype(jnp.int32)
        chosen = jnp.take(strips, k_column, axis=0)
        chosen_cols = jnp.take(columns, k_column, axis=0)
        product = jnp.einsum("gab,grbc->grac", block_part.astype(jnp.float32), chosen.astype(jnp.float32), precision=lax.Precision.HIGHEST)
        valid = (place_part[:, None] >= 0) & (chosen_cols >= 0)
        target = jnp.where(valid, block_row[:, None] * NJ + chosen_cols, RB * NJ).astype(jnp.int32)
        return totals.at[target].add(product, mode="drop")

    return lax.fori_loop(0, 4, one_turn, totals)


def reference(a_send, a_where, b_strips, b_cols):
    devices = N_ROW * N_COL

    def one_device(number):
        grid_row = number // N_COL
        grid_col = number % N_COL
        totals = jnp.zeros((RB * NJ, BS, BS), jnp.float32)
        for step_number in range(STEPS):
            holder_col = (grid_col + step_number) % N_COL
            which_half = ((grid_col + step_number) // N_COL) % 2
            holder = grid_row * N_COL + holder_col
            blocks = a_send[which_half, :, holder]
            places = a_where[which_half, :, holder]
            source_row = (grid_row + step_number) % N_ROW
            totals = panel_product(totals, blocks, places, b_strips[source_row, grid_col], b_cols[source_row, grid_col])
        shaped = totals.reshape(RB, NJ, BS, BS).transpose(0, 2, 1, 3)
        return shaped.reshape(RB * BS, NJ * BS).astype(jnp.bfloat16)

    panels = lax.map(one_device, jnp.arange(devices, dtype=jnp.int32))
    panels = panels.reshape(N_ROW, N_COL, RB * BS, NJ * BS).transpose(0, 2, 1, 3)
    return panels.reshape(N_ROW * RB * BS, N_COL * NJ * BS)
```

```python
import functools

import jax
import jax.numpy as jnp
from jax import lax
from jax.experimental import pallas as pl
from jax.experimental.pallas import tpu as pltpu
from jax.sharding import PartitionSpec as P

RB = 16
KB = 16
NJ = 8


def product_kernel(with_prev, pieces, places, cols, blocks, *refs):
    strips = refs[:pieces]
    refs = refs[pieces:]
    if with_prev:
        prev, refs = refs[0], refs[1:]
    out, left, right, total, order, first, sem_left, sem_right = refs
    slots = blocks.shape[0]
    size = blocks.shape[-1]
    per_piece = strips[0].shape[0]
    rcap = pieces * per_piece // KB
    row = pl.program_id(0)

    def right_copy(piece, index):
        slot = piece * per_piece + index
        return pltpu.make_async_copy(
            strips[piece].at[index],
            right.at[slot // rcap, :, pl.ds(pl.multiple_of(cols[slot] * size, size), size)],
            sem_right,
        )

    @pl.when(row == 0)
    def _():
        left_copy = pltpu.make_async_copy(blocks, left, sem_left)
        left_copy.start()

        def clear(j, carry):
            right[j] = jnp.zeros(right.shape[1:], right.dtype)
            return carry

        lax.fori_loop(0, KB, clear, 0)
        for piece in range(pieces):

            def begin(index, carry):
                @pl.when(cols[piece * per_piece + index] >= 0)
                def _():
                    right_copy(piece, index).start()

                return carry

            lax.fori_loop(0, per_piece, begin, 0)

        def reset(i, carry):
            first[i] = 0
            return carry

        lax.fori_loop(0, RB + 2, reset, 0)

        def count(s, carry):
            @pl.when(places[s] >= 0)
            def _():
                i = places[s] // KB + 2
                first[i] = first[i] + 1

            return carry

        lax.fori_loop(0, slots, count, 0)

        def scan(i, carry):
            first[i] = first[i] + first[i - 1]
            return carry

        lax.fori_loop(1, RB + 2, scan, 0)

        def sort(s, carry):
            @pl.when(places[s] >= 0)
            def _():
                i = places[s] // KB + 1
                order[first[i]] = s
                first[i] = first[i] + 1

            return carry

        lax.fori_loop(0, slots, sort, 0)
        left_copy.wait()
        for piece in range(pieces):

            def finish(index, carry):
                @pl.when(cols[piece * per_piece + index] >= 0)
                def _():
                    right_copy(piece, index).wait()

                return carry

            lax.fori_loop(0, per_piece, finish, 0)

    if with_prev:
        total[...] = prev[...]
    else:
        total[...] = jnp.zeros(total.shape, total.dtype)

    def add(entry, carry):
        slot = order[entry]
        total[...] += jnp.dot(
            left[slot], right[places[slot] % KB], preferred_element_type=jnp.float32
        )
        return carry

    lax.fori_loop(first[row], first[row + 1], add, 0)
    out[...] = total[...].astype(out.dtype)


def product(places, cols, blocks, strips, prev, kind):
    slots, size, _ = blocks.shape
    wide = NJ * size
    strip = pl.BlockSpec((size, wide), lambda i, *_: (i, 0))
    anywhere = pl.BlockSpec(memory_space=pl.ANY)
    with_prev = prev is not None
    operands = (blocks, *strips) + ((prev,) if with_prev else ())
    return pl.pallas_call(
        functools.partial(product_kernel, with_prev, len(strips)),
        out_shape=jax.ShapeDtypeStruct((RB * size, wide), kind),
        grid_spec=pltpu.PrefetchScalarGridSpec(
            num_scalar_prefetch=2,
            grid=(RB,),
            in_specs=[anywhere] * (1 + len(strips)) + ([strip] if with_prev else []),
            out_specs=strip,
            scratch_shapes=[
                pltpu.VMEM((slots, size, size), jnp.bfloat16),
                pltpu.VMEM((KB, size, wide), jnp.bfloat16),
                pltpu.VMEM((size, wide), jnp.float32),
                pltpu.SMEM((slots,), jnp.int32),
                pltpu.SMEM((RB + 2,), jnp.int32),
                pltpu.SemaphoreType.DMA,
                pltpu.SemaphoreType.DMA,
            ],
        ),
        compiler_params=pltpu.CompilerParams(
            dimension_semantics=("arbitrary",), vmem_limit_bytes=32 * 1024 * 1024
        ),
        cost_estimate=pl.CostEstimate(
            flops=2 * 24 * size * size * wide,
            bytes_accessed=16 * 1024 * 1024,
            transcendentals=0,
        ),
    )(places, cols, *operands)


def local(a_send, a_where, b_strips, b_cols):
    size = a_send.shape[-1]
    rows_count = lax.axis_size("row")
    cols_count = lax.axis_size("col")
    devices = rows_count * cols_count
    both = ("row", "col")
    row_index = lax.axis_index("row")
    col_index = lax.axis_index("col")
    rcap = b_strips.shape[3]

    table = jnp.concatenate([a_where.reshape(-1), b_cols.reshape(-1)])
    tables = lax.all_gather(table, both, axis=0, tiled=False)
    where_all = tables[:, : 2 * devices].reshape(devices, 2, devices)
    cols_all = tables[:, 2 * devices :]
    me = row_index * cols_count + col_index
    after_col = (col_index + 1) % cols_count
    after_half = (col_index + 1) // cols_count
    after_owner = row_index * cols_count + after_col
    places = lax.dynamic_index_in_dim(where_all[:, 0], me, 1, keepdims=False)
    next_places = lax.dynamic_index_in_dim(
        lax.dynamic_index_in_dim(where_all, after_half, 1, keepdims=False),
        after_owner, 1, keepdims=False,
    )
    source = ((row_index + 1) % rows_count) * cols_count + col_index
    next_cols = lax.dynamic_index_in_dim(cols_all, source, 0, keepdims=False)
    columns = b_cols.reshape(-1)

    strips = b_strips.reshape(KB * rcap, size, size)
    half = KB * rcap // 2
    one, two = strips[:half], strips[half:]
    next_one = lax.ppermute(one, "row", [(i, (i - 1) % rows_count) for i in range(rows_count)])
    relayed = lax.ppermute(two, "row", [(i, (i - 2) % rows_count) for i in range(0, rows_count, 2)])
    two_even = lax.ppermute(two, "row", [(i, i - 1) for i in range(1, rows_count, 2)])

    blocks = lax.all_to_all(a_send[0, 0], both, split_axis=0, concat_axis=0, tiled=True)
    wrapped = a_send[1, 0].reshape(rows_count, cols_count, size, size)[:, 0]
    wrapped = wrapped.reshape(devices, size // cols_count, size)
    parts = lax.all_to_all(wrapped, both, split_axis=0, concat_axis=0, tiled=True)

    two_odd = lax.ppermute(relayed, "row", [(i, i + 1) for i in range(0, rows_count, 2)])
    next_two = jnp.where(row_index % 2 == 0, two_even, two_odd)

    shifted_blocks = lax.ppermute(
        blocks, "col", [(i + 1, i) for i in range(cols_count - 1)]
    )
    last = cols_count - 1
    gathered = [lax.ppermute(parts, "col", [(i, last)]) for i in range(last)] + [parts]
    joined = jnp.concatenate(gathered, axis=1)
    next_blocks = jnp.where(col_index == last, joined, shifted_blocks)

    begun = product(places, columns, blocks, (strips,), None, jnp.float32)
    return product(
        next_places, next_cols, next_blocks, (next_one, next_two), begun, jnp.bfloat16
    )


def solution(mesh):
    placed = (
        P(None, ("row", "col"), None, None, None),
        P(None, ("row", "col"), None),
        P("row", "col", None, None, None, None),
        P("row", "col", None, None),
    )
    return jax.shard_map(
        local, mesh=mesh, in_specs=placed, out_specs=P("row", "col"), check_vma=False
    )
```

```python
import functools

import jax
import jax.numpy as jnp
from jax import lax
from jax.experimental import pallas as pl
from jax.experimental.pallas import tpu as pltpu
from jax.sharding import PartitionSpec as P

RB = 16
KB = 16
NJ = 8
DIRECT = 72
RELAYED = 56
ANYWHERE = pl.BlockSpec(memory_space=pl.ANY)
LIMIT = 32 * 1024 * 1024


def mark_rows(places, slots, named):
    def reset(j, carry):
        named[j] = 0
        return carry

    def mark(s, carry):
        @pl.when(places[s] >= 0)
        def _():
            named[places[s] % KB] = 1

        return carry

    lax.fori_loop(0, KB, reset, 0)
    lax.fori_loop(0, slots, mark, 0)


def for_wanted(cols, named, rcap, action):
    def visit(slot, number):
        wanted = (cols[slot] >= 0) & (named[slot // rcap] > 0)

        @pl.when(wanted)
        def _():
            action(slot, number)

        return number + wanted.astype(jnp.int32)

    return lax.fori_loop(0, KB * rcap, visit, 0)


def pack_kernel(places, cols, strips, direct, relayed, named, sem):
    slots = places.shape[0]
    rcap = cols.shape[0] // KB
    split = direct.shape[0]
    mark_rows(places, slots, named)

    def send(slot, number):
        @pl.when(number < split)
        def _():
            pltpu.make_async_copy(strips.at[slot], direct.at[number], sem).start()

        @pl.when(number >= split)
        def _():
            pltpu.make_async_copy(strips.at[slot], relayed.at[number - split], sem).start()

    count = for_wanted(cols, named, rcap, send)

    def finish(number, carry):
        pltpu.make_async_copy(strips.at[0], direct.at[0], sem).wait()
        return carry

    lax.fori_loop(0, count, finish, 0)


def pack(places, cols, strips):
    size = strips.shape[-1]
    return pl.pallas_call(
        pack_kernel,
        out_shape=[
            jax.ShapeDtypeStruct((DIRECT, size, size), strips.dtype),
            jax.ShapeDtypeStruct((RELAYED, size, size), strips.dtype),
        ],
        grid_spec=pltpu.PrefetchScalarGridSpec(
            num_scalar_prefetch=2,
            grid=(1,),
            in_specs=[ANYWHERE],
            out_specs=[ANYWHERE, ANYWHERE],
            scratch_shapes=[pltpu.SMEM((KB,), jnp.int32), pltpu.SemaphoreType.DMA],
        ),
        compiler_params=pltpu.CompilerParams(vmem_limit_bytes=LIMIT),
        cost_estimate=pl.CostEstimate(
            flops=0, bytes_accessed=2 * strips.size * 2, transcendentals=0
        ),
    )(places, cols, strips)


def by_block_row(places, slots, order, first):
    def reset(i, carry):
        first[i] = 0
        return carry

    def count(s, carry):
        @pl.when(places[s] >= 0)
        def _():
            i = places[s] // KB + 2
            first[i] = first[i] + 1

        return carry

    def scan(i, carry):
        first[i] = first[i] + first[i - 1]
        return carry

    def sort(s, carry):
        @pl.when(places[s] >= 0)
        def _():
            i = places[s] // KB + 1
            order[first[i]] = s
            first[i] = first[i] + 1

        return carry

    lax.fori_loop(0, RB + 2, reset, 0)
    lax.fori_loop(0, slots, count, 0)
    lax.fori_loop(1, RB + 2, scan, 0)
    lax.fori_loop(0, slots, sort, 0)


def clear(right):
    def one(j, carry):
        right[j] = jnp.zeros(right.shape[1:], right.dtype)
        return carry

    lax.fori_loop(0, KB, one, 0)


def add_row(row, places, left, right, total, order, first):
    def add(entry, carry):
        slot = order[entry]
        total[...] += jnp.dot(
            left[slot], right[places[slot] % KB], preferred_element_type=jnp.float32
        )
        return carry

    lax.fori_loop(first[row], first[row + 1], add, 0)


def place_at(right, cols, slot, rcap):
    size = right.shape[1]
    start = pl.multiple_of(cols[slot] * size, size)
    return right.at[slot // rcap, :, pl.ds(start, size)]


def first_kernel(
    places, cols, received, strips, out, left, right, total, order, first, named, sem_left, sem_right
):
    slots, size, _ = left.shape
    rcap = cols.shape[0] // KB
    row = pl.program_id(0)

    @pl.when(row == 0)
    def _():
        left_copy = pltpu.make_async_copy(received.at[:, pl.ds(0, size)], left, sem_left)
        left_copy.start()
        clear(right)
        mark_rows(places, slots, named)

        def fetch(slot, number):
            pltpu.make_async_copy(
                strips.at[slot], place_at(right, cols, slot, rcap), sem_right
            ).start()

        count = for_wanted(cols, named, rcap, fetch)
        by_block_row(places, slots, order, first)
        left_copy.wait()

        def finish(number, carry):
            pltpu.make_async_copy(
                strips.at[0], right.at[0, :, pl.ds(0, size)], sem_right
            ).wait()
            return carry

        lax.fori_loop(0, count, finish, 0)

    total[...] = jnp.zeros(total.shape, total.dtype)
    add_row(row, places, left, right, total, order, first)
    out[...] = total[...]


def second_kernel(parts_count, places, cols, flags, *refs):
    shifted = refs[0]
    parts = refs[1 : 1 + parts_count]
    (
        direct, from_odd, from_even, prev, out,
        left, right, total, order, first, named, sem_left, sem_right,
    ) = refs[1 + parts_count :]
    slots, size, _ = left.shape
    rcap = cols.shape[0] // KB
    split = direct.shape[0]
    step = size // parts_count
    row = pl.program_id(0)
    on_last = flags[0] > 0
    on_even = flags[1] > 0

    def whole():
        return pltpu.make_async_copy(shifted.at[:, pl.ds(0, size)], left, sem_left)

    @pl.when(row == 0)
    def _():
        @pl.when(on_last)
        def _():
            for q in range(parts_count):
                pltpu.make_async_copy(
                    parts[q], left.at[:, pl.ds(q * step, step)], sem_left
                ).start()

        @pl.when(jnp.logical_not(on_last))
        def _():
            whole().start()

        clear(right)
        mark_rows(places, slots, named)

        def fetch(slot, number):
            target = place_at(right, cols, slot, rcap)

            @pl.when(number < split)
            def _():
                pltpu.make_async_copy(direct.at[number], target, sem_right).start()

            @pl.when((number >= split) & on_even)
            def _():
                pltpu.make_async_copy(from_odd.at[number - split], target, sem_right).start()

            @pl.when((number >= split) & jnp.logical_not(on_even))
            def _():
                pltpu.make_async_copy(from_even.at[number - split], target, sem_right).start()

        count = for_wanted(cols, named, rcap, fetch)
        by_block_row(places, slots, order, first)
        whole().wait()

        def finish(number, carry):
            pltpu.make_async_copy(
                direct.at[0], right.at[0, :, pl.ds(0, size)], sem_right
            ).wait()
            return carry

        lax.fori_loop(0, count, finish, 0)

    total[...] = prev[...]
    add_row(row, places, left, right, total, order, first)
    out[...] = total[...].astype(out.dtype)


def step_call(kernel, scalars, operands, streamed, slots, size, kind):
    wide = NJ * size
    strip = pl.BlockSpec((size, wide), lambda i, *_: (i, 0))
    return pl.pallas_call(
        kernel,
        out_shape=jax.ShapeDtypeStruct((RB * size, wide), kind),
        grid_spec=pltpu.PrefetchScalarGridSpec(
            num_scalar_prefetch=len(scalars),
            grid=(RB,),
            in_specs=[ANYWHERE] * len(operands) + [strip] * len(streamed),
            out_specs=strip,
            scratch_shapes=[
                pltpu.VMEM((slots, size, size), jnp.bfloat16),
                pltpu.VMEM((KB, size, wide), jnp.bfloat16),
                pltpu.VMEM((size, wide), jnp.float32),
                pltpu.SMEM((slots,), jnp.int32),
                pltpu.SMEM((RB + 2,), jnp.int32),
                pltpu.SMEM((KB,), jnp.int32),
                pltpu.SemaphoreType.DMA,
                pltpu.SemaphoreType.DMA,
            ],
        ),
        compiler_params=pltpu.CompilerParams(
            dimension_semantics=("arbitrary",), vmem_limit_bytes=LIMIT
        ),
        cost_estimate=pl.CostEstimate(
            flops=2 * 24 * size * size * wide,
            bytes_accessed=16 * 1024 * 1024,
            transcendentals=0,
        ),
    )(*scalars, *operands, *streamed)


def local(a_send, a_where, b_strips, b_cols):
    size = a_send.shape[-1]
    rows_count = lax.axis_size("row")
    cols_count = lax.axis_size("col")
    devices = rows_count * cols_count
    both = ("row", "col")
    row_index = lax.axis_index("row")
    col_index = lax.axis_index("col")
    rcap = b_strips.shape[3]
    last = cols_count - 1

    table = jnp.concatenate([a_where.reshape(-1), b_cols.reshape(-1)])
    rest = -table.shape[0] % 1024
    table = jnp.pad(table, (0, rest)).reshape(1, -1, 128)
    tables = lax.all_to_all(
        jnp.broadcast_to(table, (devices,) + table.shape[1:]),
        both, split_axis=0, concat_axis=0, tiled=True,
    ).reshape(devices, -1)

    def places_of(half, owner):
        return lax.dynamic_slice_in_dim(tables, half * devices + owner, 1, 1)[:, 0]

    def cols_of(owner):
        return lax.dynamic_slice(tables, (owner, 2 * devices), (1, KB * rcap))[0]

    after_col = (col_index + 1) % cols_count
    after_half = (col_index + 1) // cols_count
    row_before = (row_index + rows_count - 1) % rows_count
    row_after = (row_index + 1) % rows_count
    places = places_of(0, row_index * cols_count + col_index)
    next_places = places_of(after_half, row_index * cols_count + after_col)
    sent_places = places_of(after_half, row_before * cols_count + after_col)
    columns = b_cols.reshape(-1)
    next_columns = cols_of(row_after * cols_count + col_index)

    wrapped = a_send[1, 0].reshape(rows_count, cols_count, size, size)[:, 0]
    wrapped = wrapped.reshape(devices, size // cols_count, size)
    received = lax.all_to_all(
        jnp.concatenate([a_send[0, 0], wrapped], axis=1),
        both, split_axis=0, concat_axis=0, tiled=True,
    )

    strips = b_strips.reshape(KB * rcap, size, size)
    direct, relayed = pack(sent_places, columns, strips)
    next_direct = lax.ppermute(
        direct, "row", [(i, (i - 1) % rows_count) for i in range(rows_count)]
    )
    halfway = lax.ppermute(
        relayed, "row", [(i, (i - 2) % rows_count) for i in range(0, rows_count, 2)]
    )
    from_odd = lax.ppermute(relayed, "row", [(i, i - 1) for i in range(1, rows_count, 2)])

    shifted = lax.ppermute(received, "col", [(i + 1, i) for i in range(last)])
    part = received[:, size:]
    parts = [lax.ppermute(part, "col", [(i, last)]) for i in range(last)] + [part]
    begun = step_call(
        first_kernel, (places, columns), (received, strips), (), devices, size, jnp.float32
    )
    from_even = lax.ppermute(halfway, "row", [(i, i + 1) for i in range(0, rows_count, 2)])
    flags = jnp.stack([col_index == last, row_index % 2 == 0]).astype(jnp.int32)
    return step_call(
        functools.partial(second_kernel, cols_count),
        (next_places, next_columns, flags),
        (shifted, *parts, next_direct, from_odd, from_even),
        (begun,), devices, size, jnp.bfloat16,
    )


def solution(mesh):
    placed = (
        P(None, ("row", "col"), None, None, None),
        P(None, ("row", "col"), None),
        P("row", "col", None, None, None, None),
        P("row", "col", None, None),
    )
    return jax.shard_map(
        local, mesh=mesh, in_specs=placed, out_specs=P("row", "col"), check_vma=False
    )
```

```python
import functools

import jax
import jax.numpy as jnp
from jax import lax
from jax.experimental import pallas as pl
from jax.experimental.pallas import tpu as pltpu
from jax.sharding import PartitionSpec as P

RB = 16
KB = 16
NJ = 8
PARTS = (40, 56, 8, 24)
ALWAYS = PARTS[0] + PARTS[1]
GROUP = 4
IN_HBM = pl.BlockSpec(memory_space=pltpu.HBM)
ANYWHERE = pl.BlockSpec(memory_space=pl.ANY)
LIMIT = 40 * 1024 * 1024


def mark_rows(places, slots, named):
    def reset(j, carry):
        named[j] = 0
        return carry

    def mark(s, carry):
        @pl.when(places[s] >= 0)
        def _():
            named[places[s] % KB] = 1

        return carry

    lax.fori_loop(0, KB, reset, 0)
    lax.fori_loop(0, slots, mark, 0)


def for_wanted(cols, named, rcap, action):
    def visit(slot, number):
        wanted = (cols[slot] >= 0) & (named[slot // rcap] > 0)

        @pl.when(wanted)
        def _():
            action(slot, number)

        return number + wanted.astype(jnp.int32)

    return lax.fori_loop(0, KB * rcap, visit, 0)


def pack_kernel(begin, places, cols, strips, *refs):
    outs, named, sem = refs[:-2], refs[-2], refs[-1]
    mark_rows(places, places.shape[0], named)
    starts = [begin]
    for out in outs:
        starts.append(starts[-1] + out.shape[0])

    def send(slot, number):
        for out, low, high in zip(outs, starts, starts[1:]):

            @pl.when((number >= low) & (number < high))
            def _():
                pltpu.make_async_copy(strips.at[slot], out.at[number - low], sem).start()

    count = for_wanted(cols, named, cols.shape[0] // KB, send)

    def finish(number, carry):
        pltpu.make_async_copy(strips.at[0], outs[0].at[0], sem).wait()
        return carry

    lax.fori_loop(begin, jnp.minimum(count, starts[-1]), finish, 0)


def pack(begin, counts, places, cols, strips, after=None):
    size = strips.shape[-1]
    operands = (strips,) if after is None else (strips, after)

    def kernel(places, cols, strips, *refs):
        pack_kernel(begin, places, cols, strips, *refs[len(operands) - 1 :])

    return pl.pallas_call(
        kernel,
        out_shape=[jax.ShapeDtypeStruct((n, size, size), strips.dtype) for n in counts],
        grid_spec=pltpu.PrefetchScalarGridSpec(
            num_scalar_prefetch=2,
            grid=(1,),
            in_specs=[IN_HBM] + [ANYWHERE] * (len(operands) - 1),
            out_specs=[IN_HBM] * len(counts),
            scratch_shapes=[pltpu.SMEM((KB,), jnp.int32), pltpu.SemaphoreType.DMA],
        ),
        compiler_params=pltpu.CompilerParams(vmem_limit_bytes=LIMIT),
        cost_estimate=pl.CostEstimate(
            flops=0, bytes_accessed=4 * sum(counts) * size * size, transcendentals=0
        ),
    )(places, cols, *operands)


def by_block_row(places, slots, order, first):
    def reset(i, carry):
        first[i] = 0
        return carry

    def count(s, carry):
        @pl.when(places[s] >= 0)
        def _():
            i = places[s] // KB + 2
            first[i] = first[i] + 1

        return carry

    def scan(i, carry):
        first[i] = first[i] + first[i - 1]
        return carry

    def sort(s, carry):
        @pl.when(places[s] >= 0)
        def _():
            i = places[s] // KB + 1
            order[first[i]] = s
            first[i] = first[i] + 1

        return carry

    lax.fori_loop(0, RB + 2, reset, 0)
    lax.fori_loop(0, slots, count, 0)
    lax.fori_loop(1, RB + 2, scan, 0)
    lax.fori_loop(0, slots, sort, 0)


def clear(right):
    def one(j, carry):
        right[j] = jnp.zeros(right.shape[1:], right.dtype)
        return carry

    lax.fori_loop(0, KB, one, 0)


def add_rows(places, left, right, total, order, first):
    size = left.shape[1]

    def one_row(i, carry):
        row = pl.program_id(0) * GROUP + i
        here = pl.ds(pl.multiple_of(i * size, size), size)

        def add(entry, carry):
            slot = order[entry]
            total[here, :] += jnp.dot(
                left[slot], right[places[slot] % KB], preferred_element_type=jnp.float32
            )
            return carry

        return lax.fori_loop(first[row], first[row + 1], add, carry)

    lax.fori_loop(0, GROUP, one_row, 0)


def place_at(right, where):
    size = right.shape[1]
    start = pl.multiple_of((where % NJ) * size, size)
    return right.at[where // NJ, :, pl.ds(start, size)]


def finish_right(source, right, sem, count):
    def finish(number, carry):
        pltpu.make_async_copy(source, place_at(right, 0), sem).wait()
        return carry

    lax.fori_loop(0, count, finish, 0)


def first_kernel(
    places, cols, next_places, next_cols, received, strips,
    out, next_order, next_first, next_target,
    left, right, order, first, named, sem_left, sem_right,
):
    slots, size, _ = left.shape
    rcap = cols.shape[0] // KB

    @pl.when(pl.program_id(0) == 0)
    def _():
        left_copy = pltpu.make_async_copy(received.at[:, pl.ds(0, size)], left, sem_left)
        left_copy.start()
        clear(right)
        mark_rows(places, slots, named)

        def fetch(slot, number):
            where = slot // rcap * NJ + cols[slot]
            pltpu.make_async_copy(strips.at[slot], place_at(right, where), sem_right).start()

        count = for_wanted(cols, named, rcap, fetch)
        by_block_row(places, slots, order, first)

        by_block_row(next_places, slots, next_order, next_first)
        mark_rows(next_places, slots, named)

        def note(slot, number):
            next_target[number] = slot // rcap * NJ + next_cols[slot]

        next_first[RB + 2] = for_wanted(next_cols, named, rcap, note)
        left_copy.wait()
        finish_right(strips.at[0], right, sem_right, count)

    out[...] = jnp.zeros(out.shape, out.dtype)
    add_rows(places, left, right, out, order, first)


def second_kernel(parts_count, places, order, first, target, flags, *refs):
    shifted = refs[0]
    parts = refs[1 : 1 + parts_count]
    pieces = refs[1 + parts_count : 1 + parts_count + len(PARTS)]
    prev, out, left, right, total, sem_left, sem_right = refs[1 + parts_count + len(PARTS) :]
    size = left.shape[1]
    step = size // parts_count
    on_last = flags[0] > 0

    def whole():
        return pltpu.make_async_copy(shifted.at[:, pl.ds(0, size)], left, sem_left)

    @pl.when(pl.program_id(0) == 0)
    def _():
        @pl.when(on_last)
        def _():
            for q in range(parts_count):
                pltpu.make_async_copy(
                    parts[q], left.at[:, pl.ds(q * step, step)], sem_left
                ).start()

        @pl.when(jnp.logical_not(on_last))
        def _():
            whole().start()

        clear(right)
        count = first[RB + 2]
        begin = 0
        for piece in pieces:

            def fetch(number, carry):
                pltpu.make_async_copy(
                    piece.at[number - begin], place_at(right, target[number]), sem_right
                ).start()
                return carry

            end = begin + piece.shape[0]
            lax.fori_loop(begin, jnp.minimum(count, end), fetch, 0)
            begin = end
        whole().wait()
        finish_right(pieces[0].at[0], right, sem_right, count)

    total[...] = prev[...]
    add_rows(places, left, right, total, order, first)
    out[...] = total[...].astype(out.dtype)


def step_call(kernel, scalars, operands, specs, out_shape, out_specs, scratch, slots, size):
    return pl.pallas_call(
        kernel,
        out_shape=out_shape,
        grid_spec=pltpu.PrefetchScalarGridSpec(
            num_scalar_prefetch=len(scalars),
            grid=(RB // GROUP,),
            in_specs=specs,
            out_specs=out_specs,
            scratch_shapes=[
                pltpu.VMEM((slots, size, size), jnp.bfloat16),
                pltpu.VMEM((KB, size, NJ * size), jnp.bfloat16),
                *scratch,
                pltpu.SemaphoreType.DMA,
                pltpu.SemaphoreType.DMA,
            ],
        ),
        compiler_params=pltpu.CompilerParams(
            dimension_semantics=("arbitrary",), vmem_limit_bytes=LIMIT
        ),
        cost_estimate=pl.CostEstimate(
            flops=2 * 24 * NJ * size * size * size,
            bytes_accessed=16 * 1024 * 1024,
            transcendentals=0,
        ),
    )(*scalars, *operands)


def most_needed(where_all, cols_all, rows_count, cols_count):
    grid = where_all.reshape(-1, 2, rows_count, cols_count)
    after = jnp.concatenate([grid[:, 0, :, 1:], grid[:, 1, :, :1]], axis=-1)
    columns = jnp.arange(KB, dtype=jnp.int32)
    hit = (after[..., None] >= 0) & (after[..., None] % KB == columns)
    wanted = jnp.any(hit, axis=0).astype(jnp.int32)
    counts = jnp.sum((cols_all >= 0).astype(jnp.int32), axis=-1)
    counts = jnp.roll(counts.reshape(rows_count, cols_count, KB), -1, axis=0)
    return jnp.max(jnp.sum(wanted * counts, axis=-1))


def local(a_send, a_where, b_strips, b_cols):
    size = a_send.shape[-1]
    rows_count = lax.axis_size("row")
    cols_count = lax.axis_size("col")
    devices = rows_count * cols_count
    both = ("row", "col")
    row_index = lax.axis_index("row")
    col_index = lax.axis_index("col")
    rcap = b_strips.shape[3]
    last = cols_count - 1

    table = jnp.concatenate([a_where.reshape(-1), b_cols.reshape(-1)])
    rest = -table.shape[0] % 1024
    table = jnp.pad(table, (0, rest)).reshape(-1, 128)
    tables = lax.all_gather(table, both, axis=0, tiled=False).reshape(devices, -1)
    where_all = tables[:, : 2 * devices]
    cols_all = tables[:, 2 * devices : 2 * devices + KB * rcap]

    def places_of(half, owner):
        return lax.dynamic_slice_in_dim(where_all, half * devices + owner, 1, 1)[:, 0]

    after_col = (col_index + 1) % cols_count
    after_half = (col_index + 1) // cols_count
    row_before = (row_index + rows_count - 1) % rows_count
    row_after = (row_index + 1) % rows_count
    places = places_of(0, row_index * cols_count + col_index)
    next_places = places_of(after_half, row_index * cols_count + after_col)
    sent_places = places_of(after_half, row_before * cols_count + after_col)
    columns = b_cols.reshape(-1)
    next_columns = lax.dynamic_index_in_dim(
        cols_all, row_after * cols_count + col_index, 0, keepdims=False
    )
    most = most_needed(
        where_all, cols_all.reshape(devices, KB, rcap), rows_count, cols_count
    )

    wrapped = a_send[1, 0].reshape(rows_count, cols_count, size, size)[:, 0]
    wrapped = wrapped.reshape(devices, size // cols_count, size)
    received = lax.all_to_all(
        jnp.concatenate([a_send[0, 0], wrapped], axis=1),
        both, split_axis=0, concat_axis=0, tiled=True,
    )

    def to_row_before(blocks):
        return lax.ppermute(
            blocks, "row", [(i, (i - 1) % rows_count) for i in range(rows_count)]
        )

    strips = b_strips.reshape(KB * rcap, size, size)
    (early,) = pack(0, PARTS[:1], sent_places, columns, strips)
    pieces = [to_row_before(early)]

    shifted = lax.ppermute(received, "col", [(i + 1, i) for i in range(last)])
    part = received[:, size:]
    parts = [lax.ppermute(part, "col", [(i, last)]) for i in range(last)] + [part]

    late, *over = pack(PARTS[0], PARTS[1:], sent_places, columns, strips, after=received)
    pieces.append(to_row_before(late))

    wide = NJ * size
    strip = pl.BlockSpec((GROUP * size, wide), lambda i, *_: (i, 0))
    in_smem = pl.BlockSpec(memory_space=pltpu.SMEM)
    begun, order, first, target = step_call(
        first_kernel,
        (places, columns, next_places, next_columns),
        (received, strips), [ANYWHERE, IN_HBM],
        [
            jax.ShapeDtypeStruct((RB * size, wide), jnp.float32),
            jax.ShapeDtypeStruct((devices,), jnp.int32),
            jax.ShapeDtypeStruct((RB + 3,), jnp.int32),
            jax.ShapeDtypeStruct((KB * rcap,), jnp.int32),
        ],
        [strip, in_smem, in_smem, in_smem],
        [
            pltpu.SMEM((devices,), jnp.int32),
            pltpu.SMEM((RB + 2,), jnp.int32),
            pltpu.SMEM((KB,), jnp.int32),
        ],
        devices, size,
    )

    begin = ALWAYS
    for blocks in over:
        pieces.append(lax.cond(most > begin, to_row_before, lambda same: same, blocks))
        begin += blocks.shape[0]

    flags = (col_index == last).astype(jnp.int32).reshape(1)
    return step_call(
        functools.partial(second_kernel, cols_count),
        (next_places, order, first, target, flags),
        (shifted, *parts, *pieces, begun),
        [ANYWHERE] * (1 + len(parts) + len(pieces)) + [strip],
        jax.ShapeDtypeStruct((RB * size, wide), jnp.bfloat16),
        strip,
        [pltpu.VMEM((GROUP * size, wide), jnp.float32)],
        devices, size,
    )


def solution(mesh):
    placed = (
        P(None, ("row", "col"), None, None, None),
        P(None, ("row", "col"), None),
        P("row", "col", None, None, None, None),
        P("row", "col", None, None),
    )
    return jax.shard_map(
        local, mesh=mesh, in_specs=placed, out_specs=P("row", "col"), check_vma=False
    )
```

```python
import functools

import jax
import jax.numpy as jnp
from jax import lax
from jax.experimental import pallas as pl
from jax.experimental.pallas import tpu as pltpu
from jax.sharding import PartitionSpec as P

RB = 16
KB = 16
NJ = 8
PARTS = (48, 48, 8, 24)
ALWAYS = PARTS[0] + PARTS[1]
GROUP = 4
IN_HBM = pl.BlockSpec(memory_space=pltpu.HBM)
ANYWHERE = pl.BlockSpec(memory_space=pl.ANY)
LIMIT = 60 * 1024 * 1024


def mark_rows(places, slots, named):
    def reset(j, carry):
        named[j] = 0
        return carry

    def mark(s, carry):
        @pl.when(places[s] >= 0)
        def _():
            named[places[s] % KB] = 1

        return carry

    lax.fori_loop(0, KB, reset, 0)
    lax.fori_loop(0, slots, mark, 0)


def column_of(cols, slot, rcap):
    return cols[slot % rcap * KB + slot // rcap]


def for_wanted(cols, named, rcap, action):
    def visit(slot, number):
        wanted = (column_of(cols, slot, rcap) >= 0) & (named[slot // rcap] > 0)

        @pl.when(wanted)
        def _():
            action(slot, number)

        return number + wanted.astype(jnp.int32)

    return lax.fori_loop(0, KB * rcap, visit, 0)


def pack_kernel(begin, places, cols, strips, *refs):
    outs, named, sem = refs[:-2], refs[-2], refs[-1]
    mark_rows(places, places.shape[0], named)
    starts = [begin]
    for out in outs:
        starts.append(starts[-1] + out.shape[0])

    def send(slot, number):
        for out, low, high in zip(outs, starts, starts[1:]):

            @pl.when((number >= low) & (number < high))
            def _():
                pltpu.make_async_copy(strips.at[slot], out.at[number - low], sem).start()

    count = for_wanted(cols, named, cols.shape[0] // KB, send)

    def finish(number, carry):
        pltpu.make_async_copy(strips.at[0], outs[0].at[0], sem).wait()
        return carry

    lax.fori_loop(begin, jnp.minimum(count, starts[-1]), finish, 0)


def pack(begin, counts, places, cols, strips, after=None):
    size = strips.shape[-1]
    operands = (strips,) if after is None else (strips, after)

    def kernel(places, cols, strips, *refs):
        pack_kernel(begin, places, cols, strips, *refs[len(operands) - 1 :])

    return pl.pallas_call(
        kernel,
        out_shape=[jax.ShapeDtypeStruct((n, size, size), strips.dtype) for n in counts],
        grid_spec=pltpu.PrefetchScalarGridSpec(
            num_scalar_prefetch=2,
            grid=(1,),
            in_specs=[IN_HBM] + [ANYWHERE] * (len(operands) - 1),
            out_specs=[IN_HBM] * len(counts),
            scratch_shapes=[pltpu.SMEM((KB,), jnp.int32), pltpu.SemaphoreType.DMA],
        ),
        compiler_params=pltpu.CompilerParams(vmem_limit_bytes=LIMIT),
        cost_estimate=pl.CostEstimate(
            flops=0, bytes_accessed=4 * sum(counts) * size * size, transcendentals=0
        ),
    )(places, cols, *operands)


def by_block_row(places, slots, order, first):
    def reset(i, carry):
        first[i] = 0
        return carry

    def count(s, carry):
        @pl.when(places[s] >= 0)
        def _():
            i = places[s] // KB + 2
            first[i] = first[i] + 1

        return carry

    def scan(i, carry):
        first[i] = first[i] + first[i - 1]
        return carry

    def sort(s, carry):
        @pl.when(places[s] >= 0)
        def _():
            i = places[s] // KB + 1
            order[first[i]] = s
            first[i] = first[i] + 1

        return carry

    lax.fori_loop(0, RB + 2, reset, 0)
    lax.fori_loop(0, slots, count, 0)
    lax.fori_loop(1, RB + 2, scan, 0)
    lax.fori_loop(0, slots, sort, 0)


def clear(right):
    def one(j, carry):
        right[j] = jnp.zeros(right.shape[1:], right.dtype)
        return carry

    lax.fori_loop(0, KB, one, 0)


def add_rows(places, left, right, total, order, first, touched):
    size = left.shape[1]

    def one_row(i, carry):
        row = pl.program_id(0) * GROUP + i
        here = pl.ds(pl.multiple_of(i * size, size), size)

        def add(entry, carry):
            slot = order[entry]
            column = places[slot] % KB

            @pl.when(touched[column] > 0)
            def _():
                total[here, :] += jnp.dot(
                    left[slot], right[column], preferred_element_type=jnp.float32
                )

            return carry

        return lax.fori_loop(first[row], first[row + 1], add, carry)

    lax.fori_loop(0, GROUP, one_row, 0)


def place_at(right, where):
    size = right.shape[1]
    start = pl.multiple_of((where % NJ) * size, size)
    return right.at[where // NJ, :, pl.ds(start, size)]


def finish_right(source, right, sem, count):
    def finish(number, carry):
        pltpu.make_async_copy(source, place_at(right, 0), sem).wait()
        return carry

    lax.fori_loop(0, count, finish, 0)


def first_kernel(
    places, cols, next_places, next_cols, received, strips,
    out, next_order, next_first, next_target,
    left, right, order, first, named, other, sem_left, sem_right,
):
    slots, size, _ = left.shape
    rcap = cols.shape[0] // KB

    @pl.when(pl.program_id(0) == 0)
    def _():
        left_copy = pltpu.make_async_copy(received.at[:, pl.ds(0, size)], left, sem_left)
        left_copy.start()
        clear(right)
        mark_rows(places, slots, named)

        def fetch(slot, number):
            where = slot // rcap * NJ + column_of(cols, slot, rcap)
            pltpu.make_async_copy(strips.at[slot], place_at(right, where), sem_right).start()

        count = for_wanted(cols, named, rcap, fetch)
        by_block_row(places, slots, order, first)

        by_block_row(next_places, slots, next_order, next_first)
        mark_rows(next_places, slots, other)

        def note(slot, number):
            next_target[number] = slot // rcap * NJ + column_of(next_cols, slot, rcap)

        next_first[RB + 2] = for_wanted(next_cols, other, rcap, note)
        left_copy.wait()
        finish_right(strips.at[0], right, sem_right, count)

    out[...] = jnp.zeros(out.shape, out.dtype)
    add_rows(places, left, right, out, order, first, named)


def second_kernel(parts_count, begin, counts, places, order, first, target, flags, *refs):
    shifted = refs[0]
    parts = refs[1 : 1 + parts_count]
    pieces = refs[1 + parts_count : 1 + parts_count + len(counts)]
    prev, out, *level, left, right, total, touched, sem_left, sem_right = refs[
        1 + parts_count + len(counts) :
    ]
    size = left.shape[1]
    step = size // parts_count
    on_last = flags[0] > 0

    def whole():
        return pltpu.make_async_copy(shifted.at[:, pl.ds(0, size)], left, sem_left)

    @pl.when(pl.program_id(0) == 0)
    def _():
        @pl.when(on_last)
        def _():
            for q in range(parts_count):
                pltpu.make_async_copy(
                    parts[q], left.at[:, pl.ds(q * step, step)], sem_left
                ).start()

        @pl.when(jnp.logical_not(on_last))
        def _():
            whole().start()

        def reset(j, carry):
            touched[j] = 0
            return carry

        lax.fori_loop(0, KB, reset, 0)
        clear(right)
        count = first[RB + 2]
        low = begin
        for piece in pieces:

            def fetch(number, carry):
                touched[target[number] // NJ] = 1
                pltpu.make_async_copy(
                    piece.at[number - low], place_at(right, target[number]), sem_right
                ).start()
                return carry

            high = low + piece.shape[0]
            lax.fori_loop(low, jnp.minimum(count, high), fetch, 0)
            low = high
        for ref in level:
            ref[0] = flags[1]
        whole().wait()
        finish_right(pieces[0].at[0], right, sem_right, jnp.minimum(count, low) - begin)

    total[...] = prev[...]
    add_rows(places, left, right, total, order, first, touched)
    out[...] = total[...].astype(out.dtype)


def step_call(kernel, scalars, operands, specs, out_shape, out_specs, scratch, slots, size):
    return pl.pallas_call(
        kernel,
        out_shape=out_shape,
        grid_spec=pltpu.PrefetchScalarGridSpec(
            num_scalar_prefetch=len(scalars),
            grid=(RB // GROUP,),
            in_specs=specs,
            out_specs=out_specs,
            scratch_shapes=[
                pltpu.VMEM((slots, size, size), jnp.bfloat16),
                pltpu.VMEM((KB, size, NJ * size), jnp.bfloat16),
                *scratch,
                pltpu.SemaphoreType.DMA,
                pltpu.SemaphoreType.DMA,
            ],
        ),
        compiler_params=pltpu.CompilerParams(
            dimension_semantics=("arbitrary",), vmem_limit_bytes=LIMIT
        ),
        cost_estimate=pl.CostEstimate(
            flops=2 * 24 * NJ * size * size * size,
            bytes_accessed=16 * 1024 * 1024,
            transcendentals=0,
        ),
    )(*scalars, *operands)


def table_kernel(where, cols, out, tile):
    rcap, across = cols.shape
    tile[...] = jnp.zeros(tile.shape, tile.dtype)
    tile[pl.ds(0, rcap), pl.ds(0, across)] = cols[...]
    for half in range(2):
        tile[pl.ds(rcap + half, 1), pl.ds(0, where.shape[-1])] = where[half]

    def fill(device, carry):
        out[device] = tile[...]
        return carry

    lax.fori_loop(0, out.shape[0], fill, 0)


def table_for_all(where, cols):
    devices = where.shape[-1]
    rows = -(-(cols.shape[0] + 2) // 8) * 8
    return pl.pallas_call(
        table_kernel,
        out_shape=jax.ShapeDtypeStruct((devices, rows, 128), jnp.int32),
        scratch_shapes=[pltpu.VMEM((rows, 128), jnp.int32)],
        compiler_params=pltpu.CompilerParams(vmem_limit_bytes=LIMIT),
    )(where, cols)


def most_needed(where_all, cols_all, rows_count, cols_count):
    grid = where_all.reshape(-1, 2, rows_count, cols_count)
    after = jnp.concatenate([grid[:, 0, :, 1:], grid[:, 1, :, :1]], axis=-1)
    columns = jnp.arange(KB, dtype=jnp.int32)
    hit = (after[..., None] >= 0) & (after[..., None] % KB == columns)
    wanted = jnp.any(hit, axis=0).astype(jnp.int32)
    counts = jnp.sum((cols_all >= 0).astype(jnp.int32), axis=1)
    counts = jnp.roll(counts.reshape(rows_count, cols_count, KB), -1, axis=0)
    return jnp.max(jnp.sum(wanted * counts, axis=-1))


def local(a_send, a_where, b_strips, b_cols):
    size = a_send.shape[-1]
    rows_count = lax.axis_size("row")
    cols_count = lax.axis_size("col")
    devices = rows_count * cols_count
    both = ("row", "col")
    row_index = lax.axis_index("row")
    col_index = lax.axis_index("col")
    rcap = b_strips.shape[3]
    last = cols_count - 1

    by_slot = jnp.swapaxes(b_cols, 2, 3).reshape(rcap, KB)
    tables = lax.all_to_all(
        table_for_all(a_where, by_slot), both, split_axis=0, concat_axis=0, tiled=True
    )
    cols_all = tables[:, :rcap, :KB]
    where_all = tables[:, rcap : rcap + 2, :devices]

    def places_of(half, owner):
        one_half = lax.dynamic_index_in_dim(where_all, half, 1, keepdims=False)
        return lax.dynamic_index_in_dim(one_half, owner, 1, keepdims=False)

    after_col = (col_index + 1) % cols_count
    after_half = (col_index + 1) // cols_count
    row_before = (row_index + rows_count - 1) % rows_count
    row_after = (row_index + 1) % rows_count
    places = places_of(0, row_index * cols_count + col_index)
    next_places = places_of(after_half, row_index * cols_count + after_col)
    sent_places = places_of(after_half, row_before * cols_count + after_col)
    columns = by_slot.reshape(-1)
    next_columns = lax.dynamic_index_in_dim(
        cols_all, row_after * cols_count + col_index, 0, keepdims=False
    ).reshape(-1)
    most = most_needed(where_all, cols_all, rows_count, cols_count)

    wrapped = a_send[1, 0].reshape(rows_count, cols_count, size, size)[:, 0]
    wrapped = wrapped.reshape(devices, size // cols_count, size)
    received = lax.all_to_all(
        jnp.concatenate([a_send[0, 0], wrapped], axis=1),
        both, split_axis=0, concat_axis=0, tiled=True,
    )

    def to_row_before(blocks):
        return lax.ppermute(
            blocks, "row", [(i, (i - 1) % rows_count) for i in range(rows_count)]
        )

    strips = b_strips.reshape(KB * rcap, size, size)
    (early,) = pack(0, PARTS[:1], sent_places, columns, strips)
    pieces = [to_row_before(early)]

    shifted = lax.ppermute(received, "col", [(i + 1, i) for i in range(last)])
    part = received[:, size:]
    parts = [lax.ppermute(part, "col", [(i, last)]) for i in range(last)] + [part]

    wide = NJ * size
    strip = pl.BlockSpec((GROUP * size, wide), lambda i, *_: (i, 0))
    in_smem = pl.BlockSpec(memory_space=pltpu.SMEM)
    begun, order, first, target = step_call(
        first_kernel,
        (places, columns, next_places, next_columns),
        (received, strips), [IN_HBM, IN_HBM],
        [
            jax.ShapeDtypeStruct((RB * size, wide), jnp.float32),
            jax.ShapeDtypeStruct((devices,), jnp.int32),
            jax.ShapeDtypeStruct((RB + 3,), jnp.int32),
            jax.ShapeDtypeStruct((KB * rcap,), jnp.int32),
        ],
        [strip, in_smem, in_smem, in_smem],
        [
            pltpu.SMEM((devices,), jnp.int32),
            pltpu.SMEM((RB + 2,), jnp.int32),
            pltpu.SMEM((KB,), jnp.int32),
            pltpu.SMEM((KB,), jnp.int32),
        ],
        devices, size,
    )

    late, *over = pack(PARTS[0], PARTS[1:], sent_places, columns, strips, after=order)
    pieces.append(to_row_before(late))

    on_last = (col_index == last).astype(jnp.int32)
    scalars = (next_places, order, first, target, jnp.stack([on_last, most]))
    lefts = (shifted, *parts)
    scratch = [
        pltpu.VMEM((GROUP * size, wide), jnp.float32),
        pltpu.SMEM((KB,), jnp.int32),
    ]
    begun, level = step_call(
        functools.partial(second_kernel, cols_count, 0, PARTS[:1]),
        scalars, (*lefts, pieces[0], begun),
        [IN_HBM] * (len(lefts) + 1) + [strip],
        [
            jax.ShapeDtypeStruct((RB * size, wide), jnp.float32),
            jax.ShapeDtypeStruct((1,), jnp.int32),
        ],
        [strip, in_smem], scratch, devices, size,
    )

    begin = ALWAYS
    for blocks in over:
        pieces.append(lax.cond(level[0] > begin, to_row_before, lambda same: same, blocks))
        begin += blocks.shape[0]

    return step_call(
        functools.partial(second_kernel, cols_count, PARTS[0], PARTS[1:]),
        scalars, (*lefts, *pieces[1:], begun),
        [IN_HBM] * (len(lefts) + len(PARTS) - 1) + [strip],
        jax.ShapeDtypeStruct((RB * size, wide), jnp.bfloat16),
        strip, scratch, devices, size,
    )


def solution(mesh):
    placed = (
        P(None, ("row", "col"), None, None, None),
        P(None, ("row", "col"), None),
        P("row", "col", None, None, None, None),
        P("row", "col", None, None),
    )
    return jax.shard_map(
        local, mesh=mesh, in_specs=placed, out_specs=P("row", "col"), check_vma=False
    )
```

```python
import functools

import jax
import jax.numpy as jnp
from jax import lax
from jax.experimental import pallas as pl
from jax.experimental.pallas import tpu as pltpu
from jax.sharding import PartitionSpec as P

RB = 16
KB = 16
NJ = 8
PARTS = (48, 48, 8, 24)
ALWAYS = PARTS[0] + PARTS[1]
GROUP = 4
IN_SMEM = pl.BlockSpec(memory_space=pltpu.SMEM)
ANYWHERE = pl.BlockSpec(memory_space=pl.ANY)
LIMIT = 24 * 1024 * 1024


def in_hbm(value):
    return pltpu.with_memory_space_constraint(value, pltpu.HBM)


def places_in(where, half, owner):
    return lambda source: where[source, half, owner]


def columns_in(cols):
    rcap = cols.shape[0]
    return lambda slot: cols[slot % rcap, slot // rcap]


def fetch_tables(tables, where, sem_where, wanted):
    rcap = tables.shape[1] - where.shape[1]
    copies = [
        pltpu.make_async_copy(tables.at[:, pl.ds(rcap, where.shape[1])], where, sem_where)
    ]
    for device, cols, sem in wanted:
        copies.append(
            pltpu.make_async_copy(tables.at[device, pl.ds(0, rcap)], cols, sem)
        )
    for copy in copies:
        copy.start()
    for copy in copies:
        copy.wait()


def table_scratch(tables, rcap, count):
    devices, rows, width = tables.shape
    return [
        pltpu.SMEM((devices, rows - rcap, width), jnp.int32),
        *[pltpu.SMEM((rcap, width), jnp.int32)] * count,
        *[pltpu.SemaphoreType.DMA] * (1 + count),
    ]


def mark_rows(place, slots, named):
    def reset(j, carry):
        named[j] = 0
        return carry

    def mark(s, carry):
        here = place(s)

        @pl.when(here >= 0)
        def _():
            named[here % KB] = 1

        return carry

    lax.fori_loop(0, KB, reset, 0)
    lax.fori_loop(0, slots, mark, 0)


def for_wanted(column, named, rcap, action):
    def visit(slot, number):
        wanted = (column(slot) >= 0) & (named[slot // rcap] > 0)

        @pl.when(wanted)
        def _():
            action(slot, number)

        return number + wanted.astype(jnp.int32)

    return lax.fori_loop(0, KB * rcap, visit, 0)


def pack_kernel(begin, end, through, spot, tables, strips, *refs):
    where, cols, sem_where, sem_cols, named, sem, sem_out = refs[-7:]
    outs = refs[:-8] if through else refs[:-7]
    stage = refs[-8] if through else outs[0]
    rcap = cols.shape[0]
    fetch_tables(tables, where, sem_where, [(spot[1], cols, sem_cols)])
    mark_rows(places_in(where, spot[0], spot[3]), where.shape[0], named)

    def fetch(slot, number):
        @pl.when((number >= begin) & (number < end))
        def _():
            pltpu.make_async_copy(strips.at[slot], stage.at[number - begin], sem).start()

    count = for_wanted(columns_in(cols), named, rcap, fetch)

    def finish(number, carry):
        pltpu.make_async_copy(strips.at[0], stage.at[0], sem).wait()
        return carry

    lax.fori_loop(begin, jnp.minimum(count, end), finish, 0)
    if through:
        copies, low = [], 0
        for i, out in enumerate(outs):
            size = out.shape[0]
            copies.append(
                pltpu.make_async_copy(stage.at[pl.ds(low, size)], out, sem_out.at[i])
            )
            copies[-1].start()
            low += size
        for copy in copies:
            copy.wait()


def pack(begin, counts, through, rcap, spot, tables, strips):
    size = strips.shape[-1]
    room = pltpu.HBM if through else pltpu.VMEM
    stage = [pltpu.VMEM((sum(counts), size, size), strips.dtype)] if through else []
    return pl.pallas_call(
        functools.partial(pack_kernel, begin, begin + sum(counts), through),
        out_shape=[room((n, size, size), strips.dtype) for n in counts],
        grid_spec=pltpu.PrefetchScalarGridSpec(
            num_scalar_prefetch=1,
            grid=(1,),
            in_specs=[ANYWHERE, ANYWHERE],
            out_specs=[ANYWHERE] * len(counts),
            scratch_shapes=[
                *stage,
                *table_scratch(tables, rcap, 1),
                pltpu.SMEM((KB,), jnp.int32),
                pltpu.SemaphoreType.DMA,
                pltpu.SemaphoreType.DMA((len(counts),)),
            ],
        ),
        compiler_params=pltpu.CompilerParams(vmem_limit_bytes=LIMIT),
        cost_estimate=pl.CostEstimate(
            flops=0, bytes_accessed=4 * sum(counts) * size * size, transcendentals=0
        ),
    )(spot, tables, in_hbm(strips))


def by_block_row(place, slots, order, first):
    def reset(i, carry):
        first[i] = 0
        return carry

    def count(s, carry):
        here = place(s)

        @pl.when(here >= 0)
        def _():
            i = here // KB + 2
            first[i] = first[i] + 1

        return carry

    def scan(i, carry):
        first[i] = first[i] + first[i - 1]
        return carry

    def sort(s, carry):
        here = place(s)

        @pl.when(here >= 0)
        def _():
            i = here // KB + 1
            order[first[i]] = s * KB + here % KB
            first[i] = first[i] + 1

        return carry

    lax.fori_loop(0, RB + 2, reset, 0)
    lax.fori_loop(0, slots, count, 0)
    lax.fori_loop(1, RB + 2, scan, 0)
    lax.fori_loop(0, slots, sort, 0)


def clear(right):
    def one(j, carry):
        right[j] = jnp.zeros(right.shape[1:], right.dtype)
        return carry

    lax.fori_loop(0, KB, one, 0)


def add_rows(left, right, total, order, first, touched):
    size = left.shape[1]

    def one_row(i, carry):
        row = pl.program_id(0) * GROUP + i
        here = pl.ds(pl.multiple_of(i * size, size), size)

        def add(entry, carry):
            slot = order[entry] // KB
            column = order[entry] % KB

            @pl.when(touched[column] > 0)
            def _():
                total[here, :] += jnp.dot(
                    left[slot], right[column], preferred_element_type=jnp.float32
                )

            return carry

        return lax.fori_loop(first[row], first[row + 1], add, carry)

    lax.fori_loop(0, GROUP, one_row, 0)


def place_at(right, where):
    size = right.shape[1]
    start = pl.multiple_of((where % NJ) * size, size)
    return right.at[where // NJ, :, pl.ds(start, size)]


def finish_right(source, right, sem, count):
    def finish(number, carry):
        pltpu.make_async_copy(source, place_at(right, 0), sem).wait()
        return carry

    lax.fori_loop(0, count, finish, 0)


def first_kernel(
    spot, tables, received, strips,
    out, next_order, next_first, next_target,
    left, right, where, cols, next_cols, sem_where, sem_cols, sem_next,
    order, first, named, other, sem_left, sem_right,
):
    slots, size, _ = left.shape
    rcap = cols.shape[0]

    @pl.when(pl.program_id(0) == 0)
    def _():
        left_copy = pltpu.make_async_copy(received.at[:, pl.ds(0, size)], left, sem_left)
        left_copy.start()
        fetch_tables(
            tables, where, sem_where,
            [(spot[1], cols, sem_cols), (spot[4], next_cols, sem_next)],
        )
        clear(right)
        place = places_in(where, 0, spot[1])
        column = columns_in(cols)
        mark_rows(place, slots, named)

        def fetch(slot, number):
            target = place_at(right, slot // rcap * NJ + column(slot))
            pltpu.make_async_copy(strips.at[slot], target, sem_right).start()

        count = for_wanted(column, named, rcap, fetch)
        by_block_row(place, slots, order, first)

        next_place = places_in(where, spot[0], spot[2])
        next_column = columns_in(next_cols)
        by_block_row(next_place, slots, next_order, next_first)
        mark_rows(next_place, slots, other)

        def note(slot, number):
            next_target[number] = slot // rcap * NJ + next_column(slot)

        next_first[RB + 2] = for_wanted(next_column, other, rcap, note)
        left_copy.wait()
        finish_right(strips.at[0], right, sem_right, count)

    out[...] = jnp.zeros(out.shape, out.dtype)
    add_rows(left, right, out, order, first, named)


def second_kernel(parts_count, begin, counts, order, first, target, flags, *refs):
    shifted = refs[0]
    parts = refs[1 : 1 + parts_count]
    pieces = refs[1 + parts_count : 1 + parts_count + len(counts)]
    prev, out, *level, left, right, total, touched, sem_left, sem_right = refs[
        1 + parts_count + len(counts) :
    ]
    size = left.shape[1]
    step = size // parts_count
    on_last = flags[0] > 0

    def whole():
        return pltpu.make_async_copy(shifted.at[:, pl.ds(0, size)], left, sem_left)

    @pl.when(pl.program_id(0) == 0)
    def _():
        @pl.when(on_last)
        def _():
            for q in range(parts_count):
                pltpu.make_async_copy(
                    parts[q], left.at[:, pl.ds(q * step, step)], sem_left
                ).start()

        @pl.when(jnp.logical_not(on_last))
        def _():
            whole().start()

        def reset(j, carry):
            touched[j] = 0
            return carry

        lax.fori_loop(0, KB, reset, 0)
        clear(right)
        count = first[RB + 2]
        low = begin
        for piece in pieces:

            def fetch(number, carry):
                touched[target[number] // NJ] = 1
                pltpu.make_async_copy(
                    piece.at[number - low], place_at(right, target[number]), sem_right
                ).start()
                return carry

            high = low + piece.shape[0]
            lax.fori_loop(low, jnp.minimum(count, high), fetch, 0)
            low = high
        for ref in level:
            ref[0] = flags[1]
        whole().wait()
        finish_right(pieces[0].at[0], right, sem_right, jnp.minimum(count, low) - begin)

    total[...] = prev[...]
    add_rows(left, right, total, order, first, touched)
    out[...] = total[...].astype(out.dtype)


def step_call(kernel, scalars, operands, specs, out_shape, out_specs, scratch, slots, size):
    return pl.pallas_call(
        kernel,
        out_shape=out_shape,
        grid_spec=pltpu.PrefetchScalarGridSpec(
            num_scalar_prefetch=len(scalars),
            grid=(RB // GROUP,),
            in_specs=specs,
            out_specs=out_specs,
            scratch_shapes=[
                pltpu.VMEM((slots, size, size), jnp.bfloat16),
                pltpu.VMEM((KB, size, NJ * size), jnp.bfloat16),
                *scratch,
                pltpu.SemaphoreType.DMA,
                pltpu.SemaphoreType.DMA,
            ],
        ),
        compiler_params=pltpu.CompilerParams(
            dimension_semantics=("arbitrary",), vmem_limit_bytes=LIMIT
        ),
        cost_estimate=pl.CostEstimate(
            flops=2 * 24 * NJ * size * size * size,
            bytes_accessed=16 * 1024 * 1024,
            transcendentals=0,
        ),
    )(*scalars, *operands)


def table_kernel(where, cols, out, tile):
    rcap, across = cols.shape
    tile[...] = jnp.zeros(tile.shape, tile.dtype)
    tile[pl.ds(0, rcap), pl.ds(0, across)] = cols[...]
    for half in range(2):
        tile[pl.ds(rcap + half, 1), pl.ds(0, where.shape[-1])] = where[half]

    def fill(device, carry):
        out[device] = tile[...]
        return carry

    lax.fori_loop(0, out.shape[0], fill, 0)


def table_for_all(where, cols):
    devices = where.shape[-1]
    rows = -(-(cols.shape[0] + 2) // 8) * 8
    return pl.pallas_call(
        table_kernel,
        out_shape=jax.ShapeDtypeStruct((devices, rows, 128), jnp.int32),
        scratch_shapes=[pltpu.VMEM((rows, 128), jnp.int32)],
        compiler_params=pltpu.CompilerParams(vmem_limit_bytes=LIMIT),
    )(where, cols)


def most_needed(where_all, cols_all, rows_count, cols_count):
    grid = where_all.reshape(-1, 2, rows_count, cols_count)
    after = jnp.concatenate([grid[:, 0, :, 1:], grid[:, 1, :, :1]], axis=-1)
    columns = jnp.arange(KB, dtype=jnp.int32)
    hit = (after[..., None] >= 0) & (after[..., None] % KB == columns)
    wanted = jnp.any(hit, axis=0).astype(jnp.int32)
    counts = jnp.sum((cols_all >= 0).astype(jnp.int32), axis=1)
    counts = jnp.roll(counts.reshape(rows_count, cols_count, KB), -1, axis=0)
    return jnp.max(jnp.sum(wanted * counts, axis=-1))


def local(a_send, a_where, b_strips, b_cols):
    size = a_send.shape[-1]
    rows_count = lax.axis_size("row")
    cols_count = lax.axis_size("col")
    devices = rows_count * cols_count
    both = ("row", "col")
    row_index = lax.axis_index("row")
    col_index = lax.axis_index("col")
    rcap = b_strips.shape[3]
    last = cols_count - 1

    by_slot = jnp.swapaxes(b_cols, 2, 3).reshape(rcap, KB)
    tables = lax.all_to_all(
        table_for_all(a_where, by_slot), both, split_axis=0, concat_axis=0, tiled=True
    )
    after_col = (col_index + 1) % cols_count
    after_half = (col_index + 1) // cols_count
    row_before = (row_index + rows_count - 1) % rows_count
    row_after = (row_index + 1) % rows_count
    spot = jnp.stack([
        after_half,
        row_index * cols_count + col_index,
        row_index * cols_count + after_col,
        row_before * cols_count + after_col,
        row_after * cols_count + col_index,
    ]).astype(jnp.int32)
    most = most_needed(
        tables[:, rcap : rcap + 2, :devices], tables[:, :rcap, :KB], rows_count, cols_count
    )

    wrapped = a_send[1, 0].reshape(rows_count, cols_count, size, size)[:, 0]
    wrapped = wrapped.reshape(devices, size // cols_count, size)
    received = lax.all_to_all(
        jnp.concatenate([a_send[0, 0], wrapped], axis=1),
        both, split_axis=0, concat_axis=0, tiled=True,
    )

    def to_row_before(blocks):
        return lax.ppermute(
            blocks, "row", [(i, (i - 1) % rows_count) for i in range(rows_count)]
        )

    strips = b_strips.reshape(KB * rcap, size, size)
    (early,) = pack(0, PARTS[:1], False, rcap, spot, tables, strips)
    late, *over = pack(PARTS[0], PARTS[1:], True, rcap, spot, tables, strips)
    pieces = [to_row_before(early), to_row_before(late)]

    shifted = lax.ppermute(received, "col", [(i + 1, i) for i in range(last)])
    part = received[:, size:]
    parts = [lax.ppermute(part, "col", [(i, last)]) for i in range(last)] + [part]

    wide = NJ * size
    strip = pl.BlockSpec((GROUP * size, wide), lambda i, *_: (i, 0))
    begun, order, first, target = step_call(
        first_kernel,
        (spot,), (tables, received, in_hbm(strips)), [ANYWHERE, ANYWHERE, ANYWHERE],
        [
            pltpu.HBM((RB * size, wide), jnp.float32),
            jax.ShapeDtypeStruct((devices,), jnp.int32),
            jax.ShapeDtypeStruct((RB + 3,), jnp.int32),
            jax.ShapeDtypeStruct((KB * rcap,), jnp.int32),
        ],
        [strip, IN_SMEM, IN_SMEM, IN_SMEM],
        [
            *table_scratch(tables, rcap, 2),
            pltpu.SMEM((devices,), jnp.int32),
            pltpu.SMEM((RB + 2,), jnp.int32),
            pltpu.SMEM((KB,), jnp.int32),
            pltpu.SMEM((KB,), jnp.int32),
        ],
        devices, size,
    )

    on_last = (col_index == last).astype(jnp.int32)
    scalars = (order, first, target, jnp.stack([on_last, most]))
    lefts = (shifted, *parts)
    scratch = [
        pltpu.VMEM((GROUP * size, wide), jnp.float32),
        pltpu.SMEM((KB,), jnp.int32),
    ]
    begun, level = step_call(
        functools.partial(second_kernel, cols_count, 0, PARTS[:1]),
        scalars, (*lefts, pieces[0], in_hbm(begun)),
        [ANYWHERE] * (len(lefts) + 1) + [strip],
        [
            pltpu.HBM((RB * size, wide), jnp.float32),
            jax.ShapeDtypeStruct((1,), jnp.int32),
        ],
        [strip, IN_SMEM], scratch, devices, size,
    )

    begin = ALWAYS
    for blocks in over:
        pieces.append(lax.cond(level[0] > begin, to_row_before, lambda same: same, blocks))
        begin += blocks.shape[0]

    return step_call(
        functools.partial(second_kernel, cols_count, PARTS[0], PARTS[1:]),
        scalars, (*lefts, *pieces[1:], in_hbm(begun)),
        [ANYWHERE] * (len(lefts) + len(PARTS) - 1) + [strip],
        jax.ShapeDtypeStruct((RB * size, wide), jnp.bfloat16),
        strip, scratch, devices, size,
    )


def solution(mesh):
    placed = (
        P(None, ("row", "col"), None, None, None),
        P(None, ("row", "col"), None),
        P("row", "col", None, None, None, None),
        P("row", "col", None, None),
    )
    return jax.shard_map(
        local, mesh=mesh, in_specs=placed, out_specs=P("row", "col"), check_vma=False
    )
```

```python
import functools

import jax
import jax.numpy as jnp
from jax import lax
from jax.experimental import pallas as pl
from jax.experimental.pallas import tpu as pltpu
from jax.sharding import PartitionSpec as P

RB = 16
KB = 16
NJ = 8
PARTS = (48, 48, 8, 24)
ALWAYS = PARTS[0] + PARTS[1]
GROUP = 4
IN_SMEM = pl.BlockSpec(memory_space=pltpu.SMEM)
ANYWHERE = pl.BlockSpec(memory_space=pl.ANY)
LIMIT = 24 * 1024 * 1024


def in_hbm(value):
    return pltpu.with_memory_space_constraint(value, pltpu.HBM)


def places_in(where, half, owner):
    return lambda source: where[source, half, owner]


def columns_in(cols):
    rcap = cols.shape[0]
    return lambda slot: cols[slot % rcap, slot // rcap]


def fetch_tables(tables, where, sem_where, wanted):
    rcap = tables.shape[1] - where.shape[1]
    copies = [
        pltpu.make_async_copy(tables.at[:, pl.ds(rcap, where.shape[1])], where, sem_where)
    ]
    for device, cols, sem in wanted:
        copies.append(
            pltpu.make_async_copy(tables.at[device, pl.ds(0, rcap)], cols, sem)
        )
    for copy in copies:
        copy.start(priority=1)
    for copy in copies:
        copy.wait()


def table_scratch(tables, rcap, count):
    devices, rows, width = tables.shape
    return [
        pltpu.SMEM((devices, rows - rcap, width), jnp.int32),
        *[pltpu.SMEM((rcap, width), jnp.int32)] * count,
        *[pltpu.SemaphoreType.DMA] * (1 + count),
    ]


def mark_rows(place, slots, named):
    def reset(j, carry):
        named[j] = 0
        return carry

    def mark(s, carry):
        here = place(s)

        @pl.when(here >= 0)
        def _():
            named[here % KB] = 1

        return carry

    lax.fori_loop(0, KB, reset, 0)
    lax.fori_loop(0, slots, mark, 0)


def for_wanted(column, named, rcap, action):
    def visit(slot, number):
        wanted = (column(slot) >= 0) & (named[slot // rcap] > 0)

        @pl.when(wanted)
        def _():
            action(slot, number)

        return number + wanted.astype(jnp.int32)

    return lax.fori_loop(0, KB * rcap, visit, 0)


def pack_kernel(begin, end, through, spot, tables, strips, *refs):
    where, cols, sem_where, sem_cols, named, sem, sem_out = refs[-7:]
    outs = refs[:-8] if through else refs[:-7]
    stage = refs[-8] if through else outs[0]
    rcap = cols.shape[0]
    fetch_tables(tables, where, sem_where, [(spot[1], cols, sem_cols)])
    mark_rows(places_in(where, spot[0], spot[3]), where.shape[0], named)

    def fetch(slot, number):
        @pl.when((number >= begin) & (number < end))
        def _():
            pltpu.make_async_copy(strips.at[slot], stage.at[number - begin], sem).start(priority=1)

    count = for_wanted(columns_in(cols), named, rcap, fetch)

    def finish(number, carry):
        pltpu.make_async_copy(strips.at[0], stage.at[0], sem).wait()
        return carry

    lax.fori_loop(begin, jnp.minimum(count, end), finish, 0)
    if through:
        copies, low = [], 0
        for i, out in enumerate(outs):
            size = out.shape[0]
            copies.append(
                pltpu.make_async_copy(stage.at[pl.ds(low, size)], out, sem_out.at[i])
            )
            copies[-1].start(priority=1)
            low += size
        for copy in copies:
            copy.wait()


def pack(begin, counts, through, rcap, spot, tables, strips):
    size = strips.shape[-1]
    room = pltpu.HBM if through else pltpu.VMEM
    stage = [pltpu.VMEM((sum(counts), size, size), strips.dtype)] if through else []
    return pl.pallas_call(
        functools.partial(pack_kernel, begin, begin + sum(counts), through),
        out_shape=[room((n, size, size), strips.dtype) for n in counts],
        grid_spec=pltpu.PrefetchScalarGridSpec(
            num_scalar_prefetch=1,
            grid=(1,),
            in_specs=[ANYWHERE, ANYWHERE],
            out_specs=[ANYWHERE] * len(counts),
            scratch_shapes=[
                *stage,
                *table_scratch(tables, rcap, 1),
                pltpu.SMEM((KB,), jnp.int32),
                pltpu.SemaphoreType.DMA,
                pltpu.SemaphoreType.DMA((len(counts),)),
            ],
        ),
        compiler_params=pltpu.CompilerParams(vmem_limit_bytes=LIMIT),
        cost_estimate=pl.CostEstimate(
            flops=0, bytes_accessed=4 * sum(counts) * size * size, transcendentals=0
        ),
    )(spot, tables, in_hbm(strips))


def by_block_row(place, slots, order, first):
    def reset(i, carry):
        first[i] = 0
        return carry

    def count(s, carry):
        here = place(s)

        @pl.when(here >= 0)
        def _():
            i = here // KB + 2
            first[i] = first[i] + 1

        return carry

    def scan(i, carry):
        first[i] = first[i] + first[i - 1]
        return carry

    def sort(s, carry):
        here = place(s)

        @pl.when(here >= 0)
        def _():
            i = here // KB + 1
            order[first[i]] = s * KB + here % KB
            first[i] = first[i] + 1

        return carry

    lax.fori_loop(0, RB + 2, reset, 0)
    lax.fori_loop(0, slots, count, 0)
    lax.fori_loop(1, RB + 2, scan, 0)
    lax.fori_loop(0, slots, sort, 0)


def clear(right):
    def one(j, carry):
        right[j] = jnp.zeros(right.shape[1:], right.dtype)
        return carry

    lax.fori_loop(0, KB, one, 0)


def add_rows(left, right, total, order, first, touched):
    size = left.shape[1]

    def one_row(i, carry):
        row = pl.program_id(0) * GROUP + i
        here = pl.ds(pl.multiple_of(i * size, size), size)

        def add(entry, carry):
            slot = order[entry] // KB
            column = order[entry] % KB

            @pl.when(touched[column] > 0)
            def _():
                total[here, :] += jnp.dot(
                    left[slot], right[column], preferred_element_type=jnp.float32
                )

            return carry

        return lax.fori_loop(first[row], first[row + 1], add, carry)

    lax.fori_loop(0, GROUP, one_row, 0)


def place_at(right, where):
    size = right.shape[1]
    start = pl.multiple_of((where % NJ) * size, size)
    return right.at[where // NJ, :, pl.ds(start, size)]


def finish_right(source, right, sem, count):
    def finish(number, carry):
        pltpu.make_async_copy(source, place_at(right, 0), sem).wait()
        return carry

    lax.fori_loop(0, count, finish, 0)


def first_kernel(
    spot, tables, received, strips,
    out, next_order, next_first, next_target,
    left, right, where, cols, next_cols, sem_where, sem_cols, sem_next,
    order, first, named, other, sem_left, sem_right,
):
    slots, size, _ = left.shape
    rcap = cols.shape[0]

    @pl.when(pl.program_id(0) == 0)
    def _():
        left_copy = pltpu.make_async_copy(received.at[:, pl.ds(0, size)], left, sem_left)
        left_copy.start(priority=1)
        fetch_tables(
            tables, where, sem_where,
            [(spot[1], cols, sem_cols), (spot[4], next_cols, sem_next)],
        )
        clear(right)
        place = places_in(where, 0, spot[1])
        column = columns_in(cols)
        mark_rows(place, slots, named)

        def fetch(slot, number):
            target = place_at(right, slot // rcap * NJ + column(slot))
            pltpu.make_async_copy(strips.at[slot], target, sem_right).start(priority=1)

        count = for_wanted(column, named, rcap, fetch)
        by_block_row(place, slots, order, first)

        next_place = places_in(where, spot[0], spot[2])
        next_column = columns_in(next_cols)
        by_block_row(next_place, slots, next_order, next_first)
        mark_rows(next_place, slots, other)

        def note(slot, number):
            next_target[number] = slot // rcap * NJ + next_column(slot)

        next_first[RB + 2] = for_wanted(next_column, other, rcap, note)
        left_copy.wait()
        finish_right(strips.at[0], right, sem_right, count)

    out[...] = jnp.zeros(out.shape, out.dtype)
    add_rows(left, right, out, order, first, named)


def second_kernel(parts_count, begin, counts, order, first, target, flags, *refs):
    shifted = refs[0]
    parts = refs[1 : 1 + parts_count]
    pieces = refs[1 + parts_count : 1 + parts_count + len(counts)]
    prev, out, *level, left, right, total, touched, sem_left, sem_right = refs[
        1 + parts_count + len(counts) :
    ]
    size = left.shape[1]
    step = size // parts_count
    on_last = flags[0] > 0

    def whole():
        return pltpu.make_async_copy(shifted.at[:, pl.ds(0, size)], left, sem_left)

    @pl.when(pl.program_id(0) == 0)
    def _():
        @pl.when(on_last)
        def _():
            for q in range(parts_count):
                pltpu.make_async_copy(
                    parts[q], left.at[:, pl.ds(q * step, step)], sem_left
                ).start(priority=1)

        @pl.when(jnp.logical_not(on_last))
        def _():
            whole().start(priority=1)

        def reset(j, carry):
            touched[j] = 0
            return carry

        lax.fori_loop(0, KB, reset, 0)
        clear(right)
        count = first[RB + 2]
        low = begin
        for piece in pieces:

            def fetch(number, carry):
                touched[target[number] // NJ] = 1
                pltpu.make_async_copy(
                    piece.at[number - low], place_at(right, target[number]), sem_right
                ).start(priority=1)
                return carry

            high = low + piece.shape[0]
            lax.fori_loop(low, jnp.minimum(count, high), fetch, 0)
            low = high
        for ref in level:
            ref[0] = flags[1]
        whole().wait()
        finish_right(pieces[0].at[0], right, sem_right, jnp.minimum(count, low) - begin)

    total[...] = prev[...]
    add_rows(left, right, total, order, first, touched)
    out[...] = total[...].astype(out.dtype)


def step_call(kernel, scalars, operands, specs, out_shape, out_specs, scratch, slots, size):
    return pl.pallas_call(
        kernel,
        out_shape=out_shape,
        grid_spec=pltpu.PrefetchScalarGridSpec(
            num_scalar_prefetch=len(scalars),
            grid=(RB // GROUP,),
            in_specs=specs,
            out_specs=out_specs,
            scratch_shapes=[
                pltpu.VMEM((slots, size, size), jnp.bfloat16),
                pltpu.VMEM((KB, size, NJ * size), jnp.bfloat16),
                *scratch,
                pltpu.SemaphoreType.DMA,
                pltpu.SemaphoreType.DMA,
            ],
        ),
        compiler_params=pltpu.CompilerParams(
            dimension_semantics=("arbitrary",), vmem_limit_bytes=LIMIT
        ),
        cost_estimate=pl.CostEstimate(
            flops=2 * 24 * NJ * size * size * size,
            bytes_accessed=16 * 1024 * 1024,
            transcendentals=0,
        ),
    )(*scalars, *operands)


def table_kernel(where, cols, out, tile):
    rcap, across = cols.shape
    tile[...] = jnp.zeros(tile.shape, tile.dtype)
    tile[pl.ds(0, rcap), pl.ds(0, across)] = cols[...]
    for half in range(2):
        tile[pl.ds(rcap + half, 1), pl.ds(0, where.shape[-1])] = where[half]

    def fill(device, carry):
        out[device] = tile[...]
        return carry

    lax.fori_loop(0, out.shape[0], fill, 0)


def table_for_all(where, cols):
    devices = where.shape[-1]
    rows = -(-(cols.shape[0] + 2) // 8) * 8
    return pl.pallas_call(
        table_kernel,
        out_shape=jax.ShapeDtypeStruct((devices, rows, 128), jnp.int32),
        scratch_shapes=[pltpu.VMEM((rows, 128), jnp.int32)],
        compiler_params=pltpu.CompilerParams(vmem_limit_bytes=LIMIT),
    )(where, cols)


def most_needed(where_all, cols_all, rows_count, cols_count):
    grid = where_all.reshape(-1, 2, rows_count, cols_count)
    after = jnp.concatenate([grid[:, 0, :, 1:], grid[:, 1, :, :1]], axis=-1)
    columns = jnp.arange(KB, dtype=jnp.int32)
    hit = (after[..., None] >= 0) & (after[..., None] % KB == columns)
    wanted = jnp.any(hit, axis=0).astype(jnp.int32)
    counts = jnp.sum((cols_all >= 0).astype(jnp.int32), axis=1)
    counts = jnp.roll(counts.reshape(rows_count, cols_count, KB), -1, axis=0)
    return jnp.max(jnp.sum(wanted * counts, axis=-1))


def local(a_send, a_where, b_strips, b_cols):
    size = a_send.shape[-1]
    rows_count = lax.axis_size("row")
    cols_count = lax.axis_size("col")
    devices = rows_count * cols_count
    both = ("row", "col")
    row_index = lax.axis_index("row")
    col_index = lax.axis_index("col")
    rcap = b_strips.shape[3]
    last = cols_count - 1

    by_slot = jnp.swapaxes(b_cols, 2, 3).reshape(rcap, KB)
    tables = lax.all_to_all(
        table_for_all(a_where, by_slot), both, split_axis=0, concat_axis=0, tiled=True
    )
    after_col = (col_index + 1) % cols_count
    after_half = (col_index + 1) // cols_count
    row_before = (row_index + rows_count - 1) % rows_count
    row_after = (row_index + 1) % rows_count
    spot = jnp.stack([
        after_half,
        row_index * cols_count + col_index,
        row_index * cols_count + after_col,
        row_before * cols_count + after_col,
        row_after * cols_count + col_index,
    ]).astype(jnp.int32)
    most = most_needed(
        tables[:, rcap : rcap + 2, :devices], tables[:, :rcap, :KB], rows_count, cols_count
    )

    wrapped = a_send[1, 0].reshape(rows_count, cols_count, size, size)[:, 0]
    wrapped = wrapped.reshape(devices, size // cols_count, size)
    received = lax.all_to_all(
        jnp.concatenate([a_send[0, 0], wrapped], axis=1),
        both, split_axis=0, concat_axis=0, tiled=True,
    )

    def to_row_before(blocks):
        return lax.ppermute(
            blocks, "row", [(i, (i - 1) % rows_count) for i in range(rows_count)]
        )

    strips = b_strips.reshape(KB * rcap, size, size)
    (early,) = pack(0, PARTS[:1], False, rcap, spot, tables, strips)
    late, *over = pack(PARTS[0], PARTS[1:], True, rcap, spot, tables, strips)
    pieces = [to_row_before(early), to_row_before(late)]

    shifted = lax.ppermute(received, "col", [(i + 1, i) for i in range(last)])
    part = received[:, size:]
    parts = [lax.ppermute(part, "col", [(i, last)]) for i in range(last)] + [part]

    wide = NJ * size
    strip = pl.BlockSpec((GROUP * size, wide), lambda i, *_: (i, 0))
    begun, order, first, target = step_call(
        first_kernel,
        (spot,), (tables, received, in_hbm(strips)), [ANYWHERE, ANYWHERE, ANYWHERE],
        [
            pltpu.HBM((RB * size, wide), jnp.float32),
            jax.ShapeDtypeStruct((devices,), jnp.int32),
            jax.ShapeDtypeStruct((RB + 3,), jnp.int32),
            jax.ShapeDtypeStruct((KB * rcap,), jnp.int32),
        ],
        [strip, IN_SMEM, IN_SMEM, IN_SMEM],
        [
            *table_scratch(tables, rcap, 2),
            pltpu.SMEM((devices,), jnp.int32),
            pltpu.SMEM((RB + 2,), jnp.int32),
            pltpu.SMEM((KB,), jnp.int32),
            pltpu.SMEM((KB,), jnp.int32),
        ],
        devices, size,
    )

    on_last = (col_index == last).astype(jnp.int32)
    scalars = (order, first, target, jnp.stack([on_last, most]))
    lefts = (shifted, *parts)
    scratch = [
        pltpu.VMEM((GROUP * size, wide), jnp.float32),
        pltpu.SMEM((KB,), jnp.int32),
    ]
    begun, level = step_call(
        functools.partial(second_kernel, cols_count, 0, PARTS[:1]),
        scalars, (*lefts, pieces[0], in_hbm(begun)),
        [ANYWHERE] * (len(lefts) + 1) + [strip],
        [
            pltpu.HBM((RB * size, wide), jnp.float32),
            jax.ShapeDtypeStruct((1,), jnp.int32),
        ],
        [strip, IN_SMEM], scratch, devices, size,
    )

    begin = ALWAYS
    for blocks in over:
        pieces.append(lax.cond(level[0] > begin, to_row_before, lambda same: same, blocks))
        begin += blocks.shape[0]

    return step_call(
        functools.partial(second_kernel, cols_count, PARTS[0], PARTS[1:]),
        scalars, (*lefts, *pieces[1:], in_hbm(begun)),
        [ANYWHERE] * (len(lefts) + len(PARTS) - 1) + [strip],
        jax.ShapeDtypeStruct((RB * size, wide), jnp.bfloat16),
        strip, scratch, devices, size,
    )


def solution(mesh):
    placed = (
        P(None, ("row", "col"), None, None, None),
        P(None, ("row", "col"), None),
        P("row", "col", None, None, None, None),
        P("row", "col", None, None),
    )
    return jax.shard_map(
        local, mesh=mesh, in_specs=placed, out_specs=P("row", "col"), check_vma=False
    )
```

```python
import functools

import jax
import jax.numpy as jnp
from jax import lax
from jax.experimental import pallas as pl
from jax.experimental.pallas import tpu as pltpu
from jax.sharding import PartitionSpec as P

RB = 16
KB = 16
NJ = 8
PARTS = (48, 48, 8, 24)
ALWAYS = PARTS[0] + PARTS[1]
GROUP = 4
IN_SMEM = pl.BlockSpec(memory_space=pltpu.SMEM)
ANYWHERE = pl.BlockSpec(memory_space=pl.ANY)
LIMIT = 24 * 1024 * 1024


def in_hbm(value):
    return pltpu.with_memory_space_constraint(value, pltpu.HBM)


def places_in(where, half, owner):
    return lambda source: where[source, half, owner]


def columns_in(cols):
    rcap = cols.shape[0]
    return lambda slot: cols[slot % rcap, slot // rcap]


def fetch_tables(tables, where, sem_where, wanted):
    rcap = tables.shape[1] - where.shape[1]
    copies = [
        pltpu.make_async_copy(tables.at[:, pl.ds(rcap, where.shape[1])], where, sem_where)
    ]
    for device, cols, sem in wanted:
        copies.append(
            pltpu.make_async_copy(tables.at[device, pl.ds(0, rcap)], cols, sem)
        )
    for copy in copies:
        copy.start()
    for copy in copies:
        copy.wait()


def table_scratch(tables, rcap, count):
    devices, rows, width = tables.shape
    return [
        pltpu.SMEM((devices, rows - rcap, width), jnp.int32),
        *[pltpu.SMEM((rcap, width), jnp.int32)] * count,
        *[pltpu.SemaphoreType.DMA] * (1 + count),
    ]


def mark_rows(place, slots, named):
    def reset(j, carry):
        named[j] = 0
        return carry

    def mark(s, carry):
        here = place(s)

        @pl.when(here >= 0)
        def _():
            named[here % KB] = 1

        return carry

    lax.fori_loop(0, KB, reset, 0)
    lax.fori_loop(0, slots, mark, 0)


def for_wanted(column, named, rcap, action):
    def visit(slot, number):
        wanted = (column(slot) >= 0) & (named[slot // rcap] > 0)

        @pl.when(wanted)
        def _():
            action(slot, number)

        return number + wanted.astype(jnp.int32)

    return lax.fori_loop(0, KB * rcap, visit, 0)


def pack_kernel(begin, end, spot, tables, strips, *refs):
    outs = refs[:-8]
    stage, where, cols, sem_where, sem_cols, named, sem, sem_out = refs[-8:]
    rcap = cols.shape[0]
    fetch_tables(tables, where, sem_where, [(spot[1], cols, sem_cols)])
    mark_rows(places_in(where, spot[0], spot[3]), where.shape[0], named)

    def fetch(slot, number):
        @pl.when((number >= begin) & (number < end))
        def _():
            pltpu.make_async_copy(strips.at[slot], stage.at[number - begin], sem).start()

    count = for_wanted(columns_in(cols), named, rcap, fetch)

    def finish(number, carry):
        pltpu.make_async_copy(strips.at[0], stage.at[0], sem).wait()
        return carry

    lax.fori_loop(begin, jnp.minimum(count, end), finish, 0)
    copies, low = [], 0
    for i, out in enumerate(outs):
        size = out.shape[0]
        copies.append(pltpu.make_async_copy(stage.at[pl.ds(low, size)], out, sem_out.at[i]))
        copies[-1].start()
        low += size
    for copy in copies:
        copy.wait()


def pack(begin, counts, room, rcap, spot, tables, strips):
    size = strips.shape[-1]
    return pl.pallas_call(
        functools.partial(pack_kernel, begin, begin + sum(counts)),
        out_shape=[room((n, size, size), strips.dtype) for n in counts],
        grid_spec=pltpu.PrefetchScalarGridSpec(
            num_scalar_prefetch=1,
            grid=(1,),
            in_specs=[ANYWHERE, ANYWHERE],
            out_specs=[ANYWHERE] * len(counts),
            scratch_shapes=[
                pltpu.VMEM((sum(counts), size, size), strips.dtype),
                *table_scratch(tables, rcap, 1),
                pltpu.SMEM((KB,), jnp.int32),
                pltpu.SemaphoreType.DMA,
                pltpu.SemaphoreType.DMA((len(counts),)),
            ],
        ),
        compiler_params=pltpu.CompilerParams(vmem_limit_bytes=LIMIT),
        cost_estimate=pl.CostEstimate(
            flops=0, bytes_accessed=4 * sum(counts) * size * size, transcendentals=0
        ),
    )(spot, tables, in_hbm(strips))


def by_block_row(place, slots, order, first):
    def reset(i, carry):
        first[i] = 0
        return carry

    def count(s, carry):
        here = place(s)

        @pl.when(here >= 0)
        def _():
            i = here // KB + 2
            first[i] = first[i] + 1

        return carry

    def scan(i, carry):
        first[i] = first[i] + first[i - 1]
        return carry

    def sort(s, carry):
        here = place(s)

        @pl.when(here >= 0)
        def _():
            i = here // KB + 1
            order[first[i]] = s * KB + here % KB
            first[i] = first[i] + 1

        return carry

    lax.fori_loop(0, RB + 2, reset, 0)
    lax.fori_loop(0, slots, count, 0)
    lax.fori_loop(1, RB + 2, scan, 0)
    lax.fori_loop(0, slots, sort, 0)


def clear(right):
    def one(j, carry):
        right[j] = jnp.zeros(right.shape[1:], right.dtype)
        return carry

    lax.fori_loop(0, KB, one, 0)


def add_rows(left, right, total, order, first, touched):
    size = left.shape[1]

    def one_row(i, carry):
        row = pl.program_id(0) * GROUP + i
        here = pl.ds(pl.multiple_of(i * size, size), size)

        def add(entry, carry):
            slot = order[entry] // KB
            column = order[entry] % KB

            @pl.when(touched[column] > 0)
            def _():
                total[here, :] += jnp.dot(
                    left[slot], right[column], preferred_element_type=jnp.float32
                )

            return carry

        return lax.fori_loop(first[row], first[row + 1], add, carry)

    lax.fori_loop(0, GROUP, one_row, 0)


def place_at(right, where):
    size = right.shape[1]
    start = pl.multiple_of((where % NJ) * size, size)
    return right.at[where // NJ, :, pl.ds(start, size)]


def finish_right(source, right, sem, count):
    def finish(number, carry):
        pltpu.make_async_copy(source, place_at(right, 0), sem).wait()
        return carry

    lax.fori_loop(0, count, finish, 0)


def first_kernel(
    spot, tables, received, strips,
    out, next_order, next_first, next_target,
    left, right, where, cols, next_cols, sem_where, sem_cols, sem_next,
    order, first, named, other, sem_left, sem_right,
):
    slots, size, _ = left.shape
    rcap = cols.shape[0]

    @pl.when(pl.program_id(0) == 0)
    def _():
        left_copy = pltpu.make_async_copy(received.at[:, pl.ds(0, size)], left, sem_left)
        left_copy.start()
        fetch_tables(
            tables, where, sem_where,
            [(spot[1], cols, sem_cols), (spot[4], next_cols, sem_next)],
        )
        clear(right)
        place = places_in(where, 0, spot[1])
        column = columns_in(cols)
        mark_rows(place, slots, named)

        def fetch(slot, number):
            target = place_at(right, slot // rcap * NJ + column(slot))
            pltpu.make_async_copy(strips.at[slot], target, sem_right).start()

        count = for_wanted(column, named, rcap, fetch)
        by_block_row(place, slots, order, first)

        next_place = places_in(where, spot[0], spot[2])
        next_column = columns_in(next_cols)
        by_block_row(next_place, slots, next_order, next_first)
        mark_rows(next_place, slots, other)

        def note(slot, number):
            next_target[number] = slot // rcap * NJ + next_column(slot)

        next_first[RB + 2] = for_wanted(next_column, other, rcap, note)
        left_copy.wait()
        finish_right(strips.at[0], right, sem_right, count)

    out[...] = jnp.zeros(out.shape, out.dtype)
    add_rows(left, right, out, order, first, named)


def second_kernel(parts_count, begin, counts, order, first, target, flags, *refs):
    shifted = refs[0]
    parts = refs[1 : 1 + parts_count]
    pieces = refs[1 + parts_count : 1 + parts_count + len(counts)]
    prev, out, *level, left, right, total, touched, sem_left, sem_right = refs[
        1 + parts_count + len(counts) :
    ]
    size = left.shape[1]
    step = size // parts_count
    on_last = flags[0] > 0

    def whole():
        return pltpu.make_async_copy(shifted.at[:, pl.ds(0, size)], left, sem_left)

    @pl.when(pl.program_id(0) == 0)
    def _():
        @pl.when(on_last)
        def _():
            for q in range(parts_count):
                pltpu.make_async_copy(
                    parts[q], left.at[:, pl.ds(q * step, step)], sem_left
                ).start()

        @pl.when(jnp.logical_not(on_last))
        def _():
            whole().start()

        def reset(j, carry):
            touched[j] = 0
            return carry

        lax.fori_loop(0, KB, reset, 0)
        clear(right)
        count = first[RB + 2]
        low = begin
        for piece in pieces:

            def fetch(number, carry):
                touched[target[number] // NJ] = 1
                pltpu.make_async_copy(
                    piece.at[number - low], place_at(right, target[number]), sem_right
                ).start()
                return carry

            high = low + piece.shape[0]
            lax.fori_loop(low, jnp.minimum(count, high), fetch, 0)
            low = high
        for ref in level:
            ref[0] = flags[1]
        whole().wait()
        finish_right(pieces[0].at[0], right, sem_right, jnp.minimum(count, low) - begin)

    total[...] = prev[...]
    add_rows(left, right, total, order, first, touched)
    out[...] = total[...].astype(out.dtype)


def step_call(kernel, scalars, operands, specs, out_shape, out_specs, scratch, slots, size):
    return pl.pallas_call(
        kernel,
        out_shape=out_shape,
        grid_spec=pltpu.PrefetchScalarGridSpec(
            num_scalar_prefetch=len(scalars),
            grid=(RB // GROUP,),
            in_specs=specs,
            out_specs=out_specs,
            scratch_shapes=[
                pltpu.VMEM((slots, size, size), jnp.bfloat16),
                pltpu.VMEM((KB, size, NJ * size), jnp.bfloat16),
                *scratch,
                pltpu.SemaphoreType.DMA,
                pltpu.SemaphoreType.DMA,
            ],
        ),
        compiler_params=pltpu.CompilerParams(
            dimension_semantics=("arbitrary",), vmem_limit_bytes=LIMIT
        ),
        cost_estimate=pl.CostEstimate(
            flops=2 * 24 * NJ * size * size * size,
            bytes_accessed=16 * 1024 * 1024,
            transcendentals=0,
        ),
    )(*scalars, *operands)


def table_kernel(where, cols, out, tile):
    rcap, across = cols.shape
    tile[...] = jnp.zeros(tile.shape, tile.dtype)
    tile[pl.ds(0, rcap), pl.ds(0, across)] = cols[...]
    for half in range(2):
        tile[pl.ds(rcap + half, 1), pl.ds(0, where.shape[-1])] = where[half]

    def fill(device, carry):
        out[device] = tile[...]
        return carry

    lax.fori_loop(0, out.shape[0], fill, 0)


def table_for_all(where, cols):
    devices = where.shape[-1]
    rows = -(-(cols.shape[0] + 2) // 8) * 8
    return pl.pallas_call(
        table_kernel,
        out_shape=jax.ShapeDtypeStruct((devices, rows, 128), jnp.int32),
        scratch_shapes=[pltpu.VMEM((rows, 128), jnp.int32)],
        compiler_params=pltpu.CompilerParams(vmem_limit_bytes=LIMIT),
    )(where, cols)


def most_needed(where_all, cols_all, rows_count, cols_count):
    grid = where_all.reshape(-1, 2, rows_count, cols_count)
    after = jnp.concatenate([grid[:, 0, :, 1:], grid[:, 1, :, :1]], axis=-1)
    columns = jnp.arange(KB, dtype=jnp.int32)
    hit = (after[..., None] >= 0) & (after[..., None] % KB == columns)
    wanted = jnp.any(hit, axis=0).astype(jnp.int32)
    counts = jnp.sum((cols_all >= 0).astype(jnp.int32), axis=1)
    counts = jnp.roll(counts.reshape(rows_count, cols_count, KB), -1, axis=0)
    return jnp.max(jnp.sum(wanted * counts, axis=-1))


def local(a_send, a_where, b_strips, b_cols):
    size = a_send.shape[-1]
    rows_count = lax.axis_size("row")
    cols_count = lax.axis_size("col")
    devices = rows_count * cols_count
    both = ("row", "col")
    row_index = lax.axis_index("row")
    col_index = lax.axis_index("col")
    rcap = b_strips.shape[3]
    last = cols_count - 1

    by_slot = jnp.swapaxes(b_cols, 2, 3).reshape(rcap, KB)
    tables = lax.all_to_all(
        table_for_all(a_where, by_slot), both, split_axis=0, concat_axis=0, tiled=True
    )
    after_col = (col_index + 1) % cols_count
    after_half = (col_index + 1) // cols_count
    row_before = (row_index + rows_count - 1) % rows_count
    row_after = (row_index + 1) % rows_count
    spot = jnp.stack([
        after_half,
        row_index * cols_count + col_index,
        row_index * cols_count + after_col,
        row_before * cols_count + after_col,
        row_after * cols_count + col_index,
    ]).astype(jnp.int32)
    most = most_needed(
        tables[:, rcap : rcap + 2, :devices], tables[:, :rcap, :KB], rows_count, cols_count
    )

    wrapped = a_send[1, 0].reshape(rows_count, cols_count, size, size)[:, 0]
    wrapped = wrapped.reshape(devices, size // cols_count, size)
    received = lax.all_to_all(
        jnp.concatenate([a_send[0, 0], wrapped], axis=1),
        both, split_axis=0, concat_axis=0, tiled=True,
    )

    def to_row_before(blocks):
        return lax.ppermute(
            blocks, "row", [(i, (i - 1) % rows_count) for i in range(rows_count)]
        )

    strips = b_strips.reshape(KB * rcap, size, size)
    (early,) = pack(0, PARTS[:1], pltpu.VMEM, rcap, spot, tables, strips)
    late, *over = pack(PARTS[0], PARTS[1:], pltpu.HBM, rcap, spot, tables, strips)
    pieces = [to_row_before(early), to_row_before(late)]

    shifted = lax.ppermute(received, "col", [(i + 1, i) for i in range(last)])
    part = received[:, size:]
    parts = [lax.ppermute(part, "col", [(i, last)]) for i in range(last)] + [part]

    wide = NJ * size
    strip = pl.BlockSpec((GROUP * size, wide), lambda i, *_: (i, 0))
    begun, order, first, target = step_call(
        first_kernel,
        (spot,), (tables, received, in_hbm(strips)), [ANYWHERE, ANYWHERE, ANYWHERE],
        [
            pltpu.HBM((RB * size, wide), jnp.float32),
            jax.ShapeDtypeStruct((devices,), jnp.int32),
            jax.ShapeDtypeStruct((RB + 3,), jnp.int32),
            jax.ShapeDtypeStruct((KB * rcap,), jnp.int32),
        ],
        [strip, IN_SMEM, IN_SMEM, IN_SMEM],
        [
            *table_scratch(tables, rcap, 2),
            pltpu.SMEM((devices,), jnp.int32),
            pltpu.SMEM((RB + 2,), jnp.int32),
            pltpu.SMEM((KB,), jnp.int32),
            pltpu.SMEM((KB,), jnp.int32),
        ],
        devices, size,
    )

    on_last = (col_index == last).astype(jnp.int32)
    scalars = (order, first, target, jnp.stack([on_last, most]))
    lefts = (shifted, *parts)
    scratch = [
        pltpu.VMEM((GROUP * size, wide), jnp.float32),
        pltpu.SMEM((KB,), jnp.int32),
    ]
    begun, level = step_call(
        functools.partial(second_kernel, cols_count, 0, PARTS[:1]),
        scalars, (*lefts, pieces[0], in_hbm(begun)),
        [ANYWHERE] * (len(lefts) + 1) + [strip],
        [
            pltpu.HBM((RB * size, wide), jnp.float32),
            jax.ShapeDtypeStruct((1,), jnp.int32),
        ],
        [strip, IN_SMEM], scratch, devices, size,
    )

    begin = ALWAYS
    for blocks in over:
        pieces.append(lax.cond(level[0] > begin, to_row_before, lambda same: same, blocks))
        begin += blocks.shape[0]

    return step_call(
        functools.partial(second_kernel, cols_count, PARTS[0], PARTS[1:]),
        scalars, (*lefts, *pieces[1:], in_hbm(begun)),
        [ANYWHERE] * (len(lefts) + len(PARTS) - 1) + [strip],
        jax.ShapeDtypeStruct((RB * size, wide), jnp.bfloat16),
        strip, scratch, devices, size,
    )


def solution(mesh):
    placed = (
        P(None, ("row", "col"), None, None, None),
        P(None, ("row", "col"), None),
        P("row", "col", None, None, None, None),
        P("row", "col", None, None),
    )
    return jax.shard_map(
        local, mesh=mesh, in_specs=placed, out_specs=P("row", "col"), check_vma=False
    )
```

```python
import functools

import jax
import jax.numpy as jnp
from jax import lax
from jax.experimental import pallas as pl
from jax.experimental.pallas import tpu as pltpu
from jax.sharding import PartitionSpec as P

RB = 16
KB = 16
NJ = 8
PARTS = (64, 32, 8, 24)
ALWAYS = PARTS[0] + PARTS[1]
GROUP = 4
IN_SMEM = pl.BlockSpec(memory_space=pltpu.SMEM)
ANYWHERE = pl.BlockSpec(memory_space=pl.ANY)
LIMIT = 24 * 1024 * 1024


def in_hbm(value):
    return pltpu.with_memory_space_constraint(value, pltpu.HBM)


def places_in(table, half, owner):
    rows = table.shape[1] // 2
    width = table.shape[0] // rows
    return lambda source: table[source, half * rows + owner // width, KB + owner % width]


def columns_in(table, device):
    rcap = table.shape[1]
    return lambda slot: table[device, slot % rcap, slot // rcap]


def mark_rows(place, slots, named):
    def reset(j, carry):
        named[j] = 0
        return carry

    def mark(s, carry):
        here = place(s)

        @pl.when(here >= 0)
        def _():
            named[here % KB] = 1

        return carry

    lax.fori_loop(0, KB, reset, 0)
    lax.fori_loop(0, slots, mark, 0)


def for_wanted(column, named, rcap, action):
    def visit(slot, number):
        wanted = (column(slot) >= 0) & (named[slot // rcap] > 0)

        @pl.when(wanted)
        def _():
            action(slot, number)

        return number + wanted.astype(jnp.int32)

    return lax.fori_loop(0, KB * rcap, visit, 0)


def pack_kernel(begin, end, spot, tables, strips, *refs):
    outs = refs[:-6]
    stage, table, sem_table, named, sem, sem_out = refs[-6:]
    devices, rcap, _ = table.shape
    table_copy = pltpu.make_async_copy(tables, table, sem_table)
    table_copy.start()
    table_copy.wait()
    mark_rows(places_in(table, spot[0], spot[3]), devices, named)

    def fetch(slot, number):
        @pl.when((number >= begin) & (number < end))
        def _():
            pltpu.make_async_copy(strips.at[slot], stage.at[number - begin], sem).start()

    count = for_wanted(columns_in(table, spot[1]), named, rcap, fetch)

    def finish(number, carry):
        pltpu.make_async_copy(strips.at[0], stage.at[0], sem).wait()
        return carry

    lax.fori_loop(begin, jnp.minimum(count, end), finish, 0)
    copies, low = [], 0
    for i, out in enumerate(outs):
        size = out.shape[0]
        copies.append(pltpu.make_async_copy(stage.at[pl.ds(low, size)], out, sem_out.at[i]))
        copies[-1].start()
        low += size
    for copy in copies:
        copy.wait()


def pack(begin, counts, spot, tables, strips):
    size = strips.shape[-1]
    return pl.pallas_call(
        functools.partial(pack_kernel, begin, begin + sum(counts)),
        out_shape=[pltpu.HBM((n, size, size), strips.dtype) for n in counts],
        grid_spec=pltpu.PrefetchScalarGridSpec(
            num_scalar_prefetch=1,
            grid=(1,),
            in_specs=[ANYWHERE, ANYWHERE],
            out_specs=[ANYWHERE] * len(counts),
            scratch_shapes=[
                pltpu.VMEM((sum(counts), size, size), strips.dtype),
                pltpu.SMEM(tables.shape, jnp.int32),
                pltpu.SemaphoreType.DMA,
                pltpu.SMEM((KB,), jnp.int32),
                pltpu.SemaphoreType.DMA,
                pltpu.SemaphoreType.DMA((len(counts),)),
            ],
        ),
        compiler_params=pltpu.CompilerParams(vmem_limit_bytes=LIMIT),
        cost_estimate=pl.CostEstimate(
            flops=0, bytes_accessed=4 * sum(counts) * size * size, transcendentals=0
        ),
    )(spot, tables, in_hbm(strips))


def after(value, blocks):
    count = len(blocks)
    return pl.pallas_call(
        lambda *refs: None,
        out_shape=[pltpu.HBM(each.shape, each.dtype) for each in blocks],
        in_specs=[ANYWHERE] * (count + 1),
        out_specs=[ANYWHERE] * count,
        input_output_aliases={i: i for i in range(count)},
    )(*blocks, value)


def by_block_row(place, slots, order, first):
    def reset(i, carry):
        first[i] = 0
        return carry

    def count(s, carry):
        here = place(s)

        @pl.when(here >= 0)
        def _():
            i = here // KB + 2
            first[i] = first[i] + 1

        return carry

    def scan(i, carry):
        first[i] = first[i] + first[i - 1]
        return carry

    def sort(s, carry):
        here = place(s)

        @pl.when(here >= 0)
        def _():
            i = here // KB + 1
            order[first[i]] = s * KB + here % KB
            first[i] = first[i] + 1

        return carry

    lax.fori_loop(0, RB + 2, reset, 0)
    lax.fori_loop(0, slots, count, 0)
    lax.fori_loop(1, RB + 2, scan, 0)
    lax.fori_loop(0, slots, sort, 0)


def clear(right, low):
    def one(j, carry):
        right[j] = jnp.zeros(right.shape[1:], right.dtype)
        return carry

    lax.fori_loop(low, KB, one, 0)


def add_rows(left, right, total, order, first):
    size = left.shape[1]

    def one_row(i, carry):
        row = pl.program_id(0) * GROUP + i
        here = pl.ds(pl.multiple_of(i * size, size), size)

        def add(entry, carry):
            total[here, :] += jnp.dot(
                left[order[entry] // KB], right[order[entry] % KB],
                preferred_element_type=jnp.float32,
            )
            return carry

        return lax.fori_loop(first[row], first[row + 1], add, carry)

    lax.fori_loop(0, GROUP, one_row, 0)


def place_at(right, where):
    size = right.shape[1]
    start = pl.multiple_of((where % NJ) * size, size)
    return right.at[where // NJ, :, pl.ds(start, size)]


def finish_right(source, right, sem, count):
    def finish(number, carry):
        pltpu.make_async_copy(source, place_at(right, 0), sem).wait()
        return carry

    lax.fori_loop(0, count, finish, 0)


def first_kernel(
    spot, tables, received, strips,
    out, next_order, next_first, next_target,
    left, right, table, sem_table, order, first, named, other, sem_left, sem_right,
):
    slots, size, _ = left.shape
    rcap = table.shape[1]

    @pl.when(pl.program_id(0) == 0)
    def _():
        left_copy = pltpu.make_async_copy(received.at[:, pl.ds(0, size)], left, sem_left)
        left_copy.start()
        table_copy = pltpu.make_async_copy(tables, table, sem_table)
        table_copy.start()
        clear(right, 0)
        table_copy.wait()
        place = places_in(table, 0, spot[1])
        column = columns_in(table, spot[1])
        mark_rows(place, slots, named)

        def fetch(slot, number):
            target = place_at(right, slot // rcap * NJ + column(slot))
            pltpu.make_async_copy(strips.at[slot], target, sem_right).start()

        count = for_wanted(column, named, rcap, fetch)
        by_block_row(place, slots, order, first)

        next_place = places_in(table, spot[0], spot[2])
        next_column = columns_in(table, spot[4])
        by_block_row(next_place, slots, next_order, next_first)
        mark_rows(next_place, slots, other)

        def note(slot, number):
            next_target[number] = slot // rcap * NJ + next_column(slot)

        next_first[RB + 2] = for_wanted(next_column, other, rcap, note)
        left_copy.wait()
        finish_right(strips.at[0], right, sem_right, count)

    out[...] = jnp.zeros(out.shape, out.dtype)
    add_rows(left, right, out, order, first)


def second_kernel(parts_count, begin, counts, order, first, target, flags, *refs):
    shifted = refs[0]
    parts = refs[1 : 1 + parts_count]
    pieces = refs[1 + parts_count : 1 + parts_count + len(counts)]
    prev, out, *level, left, right, total, touched, sem_left, sem_right = refs[
        1 + parts_count + len(counts) :
    ]
    size = left.shape[1]
    step = size // parts_count
    on_last = flags[0] > 0

    def whole():
        return pltpu.make_async_copy(shifted.at[:, pl.ds(0, size)], left, sem_left)

    @pl.when(pl.program_id(0) == 0)
    def _():
        @pl.when(on_last)
        def _():
            for q in range(parts_count):
                pltpu.make_async_copy(
                    parts[q], left.at[:, pl.ds(q * step, step)], sem_left
                ).start()

        @pl.when(jnp.logical_not(on_last))
        def _():
            whole().start()

        def reset(j, carry):
            touched[j] = 0
            return carry

        lax.fori_loop(0, KB, reset, 0)
        count = first[RB + 2]
        clear(right, jnp.where(count > begin, target[begin] // NJ, KB))
        low = begin
        for piece in pieces:

            def fetch(number, carry):
                touched[target[number] // NJ] = 1
                pltpu.make_async_copy(
                    piece.at[number - low], place_at(right, target[number]), sem_right
                ).start()
                return carry

            high = low + piece.shape[0]
            lax.fori_loop(low, jnp.minimum(count, high), fetch, 0)
            low = high
        for ref in level:
            ref[0] = flags[1]
        whole().wait()
        finish_right(pieces[0].at[0], right, sem_right, jnp.minimum(count, low) - begin)

    def one_row(i, carry):
        row = pl.program_id(0) * GROUP + i
        here = pl.ds(pl.multiple_of(i * size, size), size)

        def product(entry):
            return jnp.dot(
                left[order[entry] // KB], right[order[entry] % KB],
                preferred_element_type=jnp.float32,
            )

        def add(entry, fresh):
            wanted = touched[order[entry] % KB] > 0

            @pl.when(wanted & (fresh > 0))
            def _():
                total[...] = prev[here, :] + product(entry)

            @pl.when(wanted & (fresh == 0))
            def _():
                total[...] += product(entry)

            return jnp.where(wanted, 0, fresh)

        fresh = lax.fori_loop(first[row], first[row + 1], add, jnp.int32(1))

        @pl.when(fresh > 0)
        def _():
            out[here, :] = prev[here, :].astype(out.dtype)

        @pl.when(fresh == 0)
        def _():
            out[here, :] = total[...].astype(out.dtype)

        return carry

    lax.fori_loop(0, GROUP, one_row, 0)


def step_call(kernel, scalars, operands, specs, out_shape, out_specs, scratch, slots, size):
    return pl.pallas_call(
        kernel,
        out_shape=out_shape,
        grid_spec=pltpu.PrefetchScalarGridSpec(
            num_scalar_prefetch=len(scalars),
            grid=(RB // GROUP,),
            in_specs=specs,
            out_specs=out_specs,
            scratch_shapes=[
                pltpu.VMEM((slots, size, size), jnp.bfloat16),
                pltpu.VMEM((KB, size, NJ * size), jnp.bfloat16),
                *scratch,
                pltpu.SemaphoreType.DMA,
                pltpu.SemaphoreType.DMA,
            ],
        ),
        compiler_params=pltpu.CompilerParams(
            dimension_semantics=("arbitrary",), vmem_limit_bytes=LIMIT
        ),
        cost_estimate=pl.CostEstimate(
            flops=2 * 24 * NJ * size * size * size,
            bytes_accessed=16 * 1024 * 1024,
            transcendentals=0,
        ),
    )(*scalars, *operands)


def table_kernel(where, cols, out, tile):
    rcap, across = cols.shape
    width = 2 * where.shape[-1] // rcap
    tile[...] = jnp.zeros(tile.shape, tile.dtype)
    tile[:, pl.ds(0, across)] = cols[...]
    for row in range(rcap):
        half, low = divmod(row * width, where.shape[-1])
        tile[pl.ds(row, 1), pl.ds(across, width)] = where[half, :, pl.ds(low, width)]

    def fill(device, carry):
        out[device] = tile[...]
        return carry

    lax.fori_loop(0, out.shape[0], fill, 0)


def table_for_all(where, cols):
    shape = (cols.shape[0], 128)
    return pl.pallas_call(
        table_kernel,
        out_shape=jax.ShapeDtypeStruct((where.shape[-1], *shape), jnp.int32),
        scratch_shapes=[pltpu.VMEM(shape, jnp.int32)],
        compiler_params=pltpu.CompilerParams(vmem_limit_bytes=LIMIT),
    )(where, cols)


def most_needed(where_all, cols_all, rows_count, cols_count):
    grid = where_all.reshape(-1, 2, rows_count, cols_count)
    after = jnp.concatenate([grid[:, 0, :, 1:], grid[:, 1, :, :1]], axis=-1)
    columns = jnp.arange(KB, dtype=jnp.int32)
    hit = (after[..., None] >= 0) & (after[..., None] % KB == columns)
    wanted = jnp.any(hit, axis=0).astype(jnp.int32)
    counts = jnp.sum((cols_all >= 0).astype(jnp.int32), axis=1)
    counts = jnp.roll(counts.reshape(rows_count, cols_count, KB), -1, axis=0)
    return jnp.max(jnp.sum(wanted * counts, axis=-1))


def local(a_send, a_where, b_strips, b_cols):
    size = a_send.shape[-1]
    rows_count = lax.axis_size("row")
    cols_count = lax.axis_size("col")
    devices = rows_count * cols_count
    both = ("row", "col")
    row_index = lax.axis_index("row")
    col_index = lax.axis_index("col")
    rcap = b_strips.shape[3]
    last = cols_count - 1

    by_slot = jnp.swapaxes(b_cols, 2, 3).reshape(rcap, KB)
    tables = lax.all_to_all(
        table_for_all(a_where, by_slot), both, split_axis=0, concat_axis=0, tiled=True
    )
    after_col = (col_index + 1) % cols_count
    after_half = (col_index + 1) // cols_count
    row_before = (row_index + rows_count - 1) % rows_count
    row_after = (row_index + 1) % rows_count
    spot = jnp.stack([
        after_half,
        row_index * cols_count + col_index,
        row_index * cols_count + after_col,
        row_before * cols_count + after_col,
        row_after * cols_count + col_index,
    ]).astype(jnp.int32)
    most = most_needed(
        tables[:, :, KB : KB + 2 * devices // rcap], tables[:, :, :KB], rows_count, cols_count
    )

    wrapped = a_send[1, 0].reshape(rows_count, cols_count, size, size)[:, 0]
    wrapped = wrapped.reshape(devices, size // cols_count, size)
    received = lax.all_to_all(
        jnp.concatenate([a_send[0, 0], wrapped], axis=1),
        both, split_axis=0, concat_axis=0, tiled=True,
    )

    def to_row_before(blocks):
        return lax.ppermute(
            blocks, "row", [(i, (i - 1) % rows_count) for i in range(rows_count)]
        )

    strips = b_strips.reshape(KB * rcap, size, size)
    (early,) = pack(0, PARTS[:1], spot, tables, strips)
    late, *over = pack(PARTS[0], PARTS[1:], spot, tables, strips)
    early, late, *over = after(received, [early, late, *over])
    pieces = [to_row_before(early), to_row_before(late)]

    shifted = lax.ppermute(received, "col", [(i + 1, i) for i in range(last)])
    part = received[:, size:]
    parts = [lax.ppermute(part, "col", [(i, last)]) for i in range(last)] + [part]

    wide = NJ * size
    strip = pl.BlockSpec((GROUP * size, wide), lambda i, *_: (i, 0))
    begun, order, first, target = step_call(
        first_kernel,
        (spot,), (tables, received, in_hbm(strips)), [ANYWHERE, ANYWHERE, ANYWHERE],
        [
            pltpu.HBM((RB * size, wide), jnp.float32),
            jax.ShapeDtypeStruct((devices,), jnp.int32),
            jax.ShapeDtypeStruct((RB + 3,), jnp.int32),
            jax.ShapeDtypeStruct((KB * rcap,), jnp.int32),
        ],
        [strip, IN_SMEM, IN_SMEM, IN_SMEM],
        [
            pltpu.SMEM(tables.shape, jnp.int32),
            pltpu.SemaphoreType.DMA,
            pltpu.SMEM((devices,), jnp.int32),
            pltpu.SMEM((RB + 2,), jnp.int32),
            pltpu.SMEM((KB,), jnp.int32),
            pltpu.SMEM((KB,), jnp.int32),
        ],
        devices, size,
    )

    on_last = (col_index == last).astype(jnp.int32)
    scalars = (order, first, target, jnp.stack([on_last, most]))
    lefts = (shifted, *parts)
    scratch = [
        pltpu.VMEM((size, wide), jnp.float32),
        pltpu.SMEM((KB,), jnp.int32),
    ]
    begun, level = step_call(
        functools.partial(second_kernel, cols_count, 0, PARTS[:1]),
        scalars, (*lefts, pieces[0], in_hbm(begun)),
        [ANYWHERE] * (len(lefts) + 1) + [strip],
        [
            pltpu.HBM((RB * size, wide), jnp.float32),
            jax.ShapeDtypeStruct((1,), jnp.int32),
        ],
        [strip, IN_SMEM], scratch, devices, size,
    )

    begin = ALWAYS
    for blocks in over:
        pieces.append(lax.cond(level[0] > begin, to_row_before, lambda same: same, blocks))
        begin += blocks.shape[0]

    return step_call(
        functools.partial(second_kernel, cols_count, PARTS[0], PARTS[1:]),
        scalars, (*lefts, *pieces[1:], in_hbm(begun)),
        [ANYWHERE] * (len(lefts) + len(PARTS) - 1) + [strip],
        jax.ShapeDtypeStruct((RB * size, wide), jnp.bfloat16),
        strip, scratch, devices, size,
    )


def solution(mesh):
    placed = (
        P(None, ("row", "col"), None, None, None),
        P(None, ("row", "col"), None),
        P("row", "col", None, None, None, None),
        P("row", "col", None, None),
    )
    return jax.shard_map(
        local, mesh=mesh, in_specs=placed, out_specs=P("row", "col"), check_vma=False
    )
```

```python
import functools

import jax
import jax.numpy as jnp
from jax import lax
from jax.experimental import pallas as pl
from jax.experimental.pallas import tpu as pltpu
from jax.sharding import PartitionSpec as P

RB = 16
KB = 16
NJ = 8
PARTS = (64, 32, 8, 24)
ALWAYS = PARTS[0] + PARTS[1]
GROUP = 4
IN_SMEM = pl.BlockSpec(memory_space=pltpu.SMEM)
ANYWHERE = pl.BlockSpec(memory_space=pl.ANY)
LIMIT = 24 * 1024 * 1024


def in_hbm(value):
    return pltpu.with_memory_space_constraint(value, pltpu.HBM)


def places_in(table, half, owner):
    at = half * table.shape[0] + owner
    return lambda source: table[source, 1 + at // 128, at % 128]


def columns_in(table, rcap, device):
    return lambda slot: table[device, 0, slot % rcap * KB + slot // rcap]


def mark_rows(place, slots, named):
    def reset(j, carry):
        named[j] = 0
        return carry

    def mark(s, carry):
        here = place(s)

        @pl.when(here >= 0)
        def _():
            named[here % KB] = 1

        return carry

    lax.fori_loop(0, KB, reset, 0)
    lax.fori_loop(0, slots, mark, 0)


def for_wanted(column, named, rcap, action):
    def visit(slot, number):
        wanted = (column(slot) >= 0) & (named[slot // rcap] > 0)

        @pl.when(wanted)
        def _():
            action(slot, number)

        return number + wanted.astype(jnp.int32)

    return lax.fori_loop(0, KB * rcap, visit, 0)


def pack_kernel(begin, end, rcap, spot, tables, strips, *refs):
    outs = refs[:-6]
    stage, table, sem_table, named, sem, sem_out = refs[-6:]
    table_copy = pltpu.make_async_copy(tables, table, sem_table)
    table_copy.start()
    table_copy.wait()
    mark_rows(places_in(table, spot[0], spot[3]), table.shape[0], named)

    def fetch(slot, number):
        @pl.when((number >= begin) & (number < end))
        def _():
            pltpu.make_async_copy(strips.at[slot], stage.at[number - begin], sem).start()

    count = for_wanted(columns_in(table, rcap, spot[1]), named, rcap, fetch)

    def finish(number, carry):
        pltpu.make_async_copy(strips.at[0], stage.at[0], sem).wait()
        return carry

    lax.fori_loop(begin, jnp.minimum(count, end), finish, 0)
    copies, low = [], 0
    for i, out in enumerate(outs):
        size = out.shape[0]
        copies.append(pltpu.make_async_copy(stage.at[pl.ds(low, size)], out, sem_out.at[i]))
        copies[-1].start()
        low += size
    for copy in copies:
        copy.wait()


def pack(begin, counts, spot, tables, strips):
    size = strips.shape[-1]
    return pl.pallas_call(
        functools.partial(pack_kernel, begin, begin + sum(counts), strips.shape[0] // KB),
        out_shape=[pltpu.HBM((n, size, size), strips.dtype) for n in counts],
        grid_spec=pltpu.PrefetchScalarGridSpec(
            num_scalar_prefetch=1,
            grid=(1,),
            in_specs=[ANYWHERE, ANYWHERE],
            out_specs=[ANYWHERE] * len(counts),
            scratch_shapes=[
                pltpu.VMEM((sum(counts), size, size), strips.dtype),
                pltpu.SMEM(tables.shape, jnp.int32),
                pltpu.SemaphoreType.DMA,
                pltpu.SMEM((KB,), jnp.int32),
                pltpu.SemaphoreType.DMA,
                pltpu.SemaphoreType.DMA((len(counts),)),
            ],
        ),
        compiler_params=pltpu.CompilerParams(vmem_limit_bytes=LIMIT),
        cost_estimate=pl.CostEstimate(
            flops=0, bytes_accessed=4 * sum(counts) * size * size, transcendentals=0
        ),
    )(spot, tables, in_hbm(strips))


def after(value, blocks):
    count = len(blocks)
    return pl.pallas_call(
        lambda *refs: None,
        out_shape=[pltpu.HBM(each.shape, each.dtype) for each in blocks],
        in_specs=[ANYWHERE] * (count + 1),
        out_specs=[ANYWHERE] * count,
        input_output_aliases={i: i for i in range(count)},
    )(*blocks, value)


def by_block_row(place, slots, order, first):
    def reset(i, carry):
        first[i] = 0
        return carry

    def count(s, carry):
        here = place(s)

        @pl.when(here >= 0)
        def _():
            i = here // KB + 2
            first[i] = first[i] + 1

        return carry

    def scan(i, carry):
        first[i] = first[i] + first[i - 1]
        return carry

    def sort(s, carry):
        here = place(s)

        @pl.when(here >= 0)
        def _():
            i = here // KB + 1
            order[first[i]] = s * KB + here % KB
            first[i] = first[i] + 1

        return carry

    lax.fori_loop(0, RB + 2, reset, 0)
    lax.fori_loop(0, slots, count, 0)
    lax.fori_loop(1, RB + 2, scan, 0)
    lax.fori_loop(0, slots, sort, 0)


def clear(right, low):
    def one(j, carry):
        right[j] = jnp.zeros(right.shape[1:], right.dtype)
        return carry

    lax.fori_loop(low, KB, one, 0)


def add_rows(left, right, total, order, first):
    size = left.shape[1]

    def one_row(i, carry):
        row = pl.program_id(0) * GROUP + i
        here = pl.ds(pl.multiple_of(i * size, size), size)

        def add(entry, carry):
            total[here, :] += jnp.dot(
                left[order[entry] // KB], right[order[entry] % KB],
                preferred_element_type=jnp.float32,
            )
            return carry

        return lax.fori_loop(first[row], first[row + 1], add, carry)

    lax.fori_loop(0, GROUP, one_row, 0)


def place_at(right, where):
    size = right.shape[1]
    start = pl.multiple_of((where % NJ) * size, size)
    return right.at[where // NJ, :, pl.ds(start, size)]


def finish_right(source, right, sem, count):
    def finish(number, carry):
        pltpu.make_async_copy(source, place_at(right, 0), sem).wait()
        return carry

    lax.fori_loop(0, count, finish, 0)


def first_kernel(
    rcap, spot, tables, received, strips,
    out, next_order, next_first, next_target,
    left, right, table, sem_table, order, first, named, other, sem_left, sem_right,
):
    slots, size, _ = left.shape

    @pl.when(pl.program_id(0) == 0)
    def _():
        left_copy = pltpu.make_async_copy(received.at[:, pl.ds(0, size)], left, sem_left)
        left_copy.start()
        table_copy = pltpu.make_async_copy(tables, table, sem_table)
        table_copy.start()
        clear(right, 0)
        table_copy.wait()
        place = places_in(table, 0, spot[1])
        column = columns_in(table, rcap, spot[1])
        mark_rows(place, slots, named)

        def fetch(slot, number):
            target = place_at(right, slot // rcap * NJ + column(slot))
            pltpu.make_async_copy(strips.at[slot], target, sem_right).start()

        count = for_wanted(column, named, rcap, fetch)
        by_block_row(place, slots, order, first)

        next_place = places_in(table, spot[0], spot[2])
        next_column = columns_in(table, rcap, spot[4])
        by_block_row(next_place, slots, next_order, next_first)
        mark_rows(next_place, slots, other)

        def note(slot, number):
            next_target[number] = slot // rcap * NJ + next_column(slot)

        next_first[RB + 2] = for_wanted(next_column, other, rcap, note)
        left_copy.wait()
        finish_right(strips.at[0], right, sem_right, count)

    out[...] = jnp.zeros(out.shape, out.dtype)
    add_rows(left, right, out, order, first)


def start_left(shifted, parts, left, on_last, sem):
    size = left.shape[1]
    step = size // len(parts)
    whole = pltpu.make_async_copy(shifted.at[:, pl.ds(0, size)], left, sem)

    @pl.when(on_last)
    def _():
        for q, part in enumerate(parts):
            pltpu.make_async_copy(part, left.at[:, pl.ds(q * step, step)], sem).start()

    @pl.when(jnp.logical_not(on_last))
    def _():
        whole.start()

    return whole


def start_right(pieces, begin, count, target, right, touched, sem):
    def reset(j, carry):
        touched[j] = 0
        return carry

    lax.fori_loop(0, KB, reset, 0)
    clear(right, jnp.where(count > begin, target[begin] // NJ, KB))
    low = begin
    for piece in pieces:

        def fetch(number, carry):
            touched[target[number] // NJ] = 1
            pltpu.make_async_copy(
                piece.at[number - low], place_at(right, target[number]), sem
            ).start()
            return carry

        high = low + piece.shape[0]
        lax.fori_loop(low, jnp.minimum(count, high), fetch, 0)
        low = high
    return jnp.minimum(count, low) - begin


def middle_kernel(parts_count, order, first, target, flags, *refs):
    shifted, *parts = refs[: 1 + parts_count]
    (
        piece, prev, out, rounded, level,
        left, right, total, touched, sem_left, sem_right,
    ) = refs[1 + parts_count :]
    size = left.shape[1]

    @pl.when(pl.program_id(0) == 0)
    def _():
        whole = start_left(shifted, parts, left, flags[0] > 0, sem_left)
        count = start_right([piece], 0, first[RB + 2], target, right, touched, sem_right)
        level[0] = flags[1]
        whole.wait()
        finish_right(piece.at[0], right, sem_right, count)

    def one_row(i, carry):
        row = pl.program_id(0) * GROUP + i
        here = pl.ds(pl.multiple_of(i * size, size), size)
        total[...] = prev[here, :]

        def add(entry, carry):
            @pl.when(touched[order[entry] % KB] > 0)
            def _():
                total[...] += jnp.dot(
                    left[order[entry] // KB], right[order[entry] % KB],
                    preferred_element_type=jnp.float32,
                )

            return carry

        lax.fori_loop(first[row], first[row + 1], add, 0)
        out[here, :] = total[...]
        rounded[here, :] = total[...].astype(rounded.dtype)
        return carry

    lax.fori_loop(0, GROUP, one_row, 0)


def last_kernel(parts_count, begin, order, first, target, flags, *refs):
    shifted, *parts = refs[: 1 + parts_count]
    pieces = refs[1 + parts_count : len(PARTS) + parts_count]
    (
        prev, _, out,
        left, right, total, rounded, touched, open_row,
        sem_left, sem_right, sem_prev, sem_out,
    ) = refs[len(PARTS) + parts_count :]
    size = left.shape[1]
    whole = start_left(shifted, parts, left, flags[0] > 0, sem_left)
    count = start_right(pieces, begin, first[RB + 2], target, right, touched, sem_right)

    def rows_at(row):
        return pl.ds(pl.multiple_of(row * size, size), size)

    def prev_copy(row):
        return pltpu.make_async_copy(prev.at[rows_at(row)], total.at[row], sem_prev.at[row])

    def out_copy(row):
        return pltpu.make_async_copy(rounded.at[row], out.at[rows_at(row)], sem_out.at[row])

    def open_one(row, carry):
        def look(entry, found):
            return jnp.maximum(found, touched[order[entry] % KB])

        open_row[row] = lax.fori_loop(first[row], first[row + 1], look, jnp.int32(0))

        @pl.when(open_row[row] > 0)
        def _():
            prev_copy(row).start()

        return carry

    lax.fori_loop(0, RB, open_one, 0)
    whole.wait()
    finish_right(pieces[0].at[0], right, sem_right, count)

    def add_row(row, carry):
        def add(entry, carry):
            @pl.when(touched[order[entry] % KB] > 0)
            def _():
                total[row] += jnp.dot(
                    left[order[entry] // KB], right[order[entry] % KB],
                    preferred_element_type=jnp.float32,
                )

            return carry

        @pl.when(open_row[row] > 0)
        def _():
            prev_copy(row).wait()
            lax.fori_loop(first[row], first[row + 1], add, 0)
            rounded[row] = total[row].astype(rounded.dtype)
            out_copy(row).start()

        return carry

    def close_row(row, carry):
        @pl.when(open_row[row] > 0)
        def _():
            out_copy(row).wait()

        return carry

    lax.fori_loop(0, RB, add_row, 0)
    lax.fori_loop(0, RB, close_row, 0)


def step_call(kernel, scalars, operands, specs, out_shape, out_specs, scratch, slots, size):
    return pl.pallas_call(
        kernel,
        out_shape=out_shape,
        grid_spec=pltpu.PrefetchScalarGridSpec(
            num_scalar_prefetch=len(scalars),
            grid=(RB // GROUP,),
            in_specs=specs,
            out_specs=out_specs,
            scratch_shapes=[
                pltpu.VMEM((slots, size, size), jnp.bfloat16),
                pltpu.VMEM((KB, size, NJ * size), jnp.bfloat16),
                *scratch,
                pltpu.SemaphoreType.DMA,
                pltpu.SemaphoreType.DMA,
            ],
        ),
        compiler_params=pltpu.CompilerParams(
            dimension_semantics=("arbitrary",), vmem_limit_bytes=LIMIT
        ),
        cost_estimate=pl.CostEstimate(
            flops=2 * 24 * NJ * size * size * size,
            bytes_accessed=16 * 1024 * 1024,
            transcendentals=0,
        ),
    )(*scalars, *operands)


def table_kernel(where, cols, out, tile):
    rcap, across = cols.shape
    devices = where.shape[-1]
    tile[...] = jnp.zeros(tile.shape, tile.dtype)
    for slot in range(rcap):
        tile[pl.ds(0, 1), pl.ds(slot * across, across)] = cols[pl.ds(slot, 1), :]
    for half in range(2):
        row, lane = divmod(half * devices, 128)
        tile[pl.ds(1 + row, 1), pl.ds(lane, devices)] = where[half]

    def fill(device, carry):
        out[device] = tile[...]
        return carry

    lax.fori_loop(0, out.shape[0], fill, 0)


def table_for_all(where, cols):
    devices = where.shape[-1]
    shape = (1 + -(-2 * devices // 128), 128)
    return pl.pallas_call(
        table_kernel,
        out_shape=jax.ShapeDtypeStruct((devices, *shape), jnp.int32),
        scratch_shapes=[pltpu.VMEM(shape, jnp.int32)],
        compiler_params=pltpu.CompilerParams(vmem_limit_bytes=LIMIT),
    )(where, cols)


def most_needed(where_all, cols_all, rows_count, cols_count):
    grid = where_all.reshape(-1, 2, rows_count, cols_count)
    after = jnp.concatenate([grid[:, 0, :, 1:], grid[:, 1, :, :1]], axis=-1)
    columns = jnp.arange(KB, dtype=jnp.int32)
    hit = (after[..., None] >= 0) & (after[..., None] % KB == columns)
    wanted = jnp.any(hit, axis=0).astype(jnp.int32)
    counts = jnp.sum((cols_all >= 0).astype(jnp.int32), axis=1)
    counts = jnp.roll(counts.reshape(rows_count, cols_count, KB), -1, axis=0)
    return jnp.max(jnp.sum(wanted * counts, axis=-1))


def local(a_send, a_where, b_strips, b_cols):
    size = a_send.shape[-1]
    rows_count = lax.axis_size("row")
    cols_count = lax.axis_size("col")
    devices = rows_count * cols_count
    both = ("row", "col")
    row_index = lax.axis_index("row")
    col_index = lax.axis_index("col")
    rcap = b_strips.shape[3]
    last = cols_count - 1

    by_slot = jnp.swapaxes(b_cols, 2, 3).reshape(rcap, KB)
    tables = lax.all_to_all(
        table_for_all(a_where, by_slot), both, split_axis=0, concat_axis=0, tiled=True
    )
    after_col = (col_index + 1) % cols_count
    after_half = (col_index + 1) // cols_count
    row_before = (row_index + rows_count - 1) % rows_count
    row_after = (row_index + 1) % rows_count
    spot = jnp.stack([
        after_half,
        row_index * cols_count + col_index,
        row_index * cols_count + after_col,
        row_before * cols_count + after_col,
        row_after * cols_count + col_index,
    ]).astype(jnp.int32)
    most = most_needed(
        tables[:, 1:].reshape(devices, -1)[:, : 2 * devices],
        tables[:, 0].reshape(devices, rcap, KB), rows_count, cols_count,
    )

    wrapped = a_send[1, 0].reshape(rows_count, cols_count, size, size)[:, 0]
    wrapped = wrapped.reshape(devices, size // cols_count, size)
    received = lax.all_to_all(
        jnp.concatenate([a_send[0, 0], wrapped], axis=1),
        both, split_axis=0, concat_axis=0, tiled=True,
    )

    def to_row_before(blocks):
        return lax.ppermute(
            blocks, "row", [(i, (i - 1) % rows_count) for i in range(rows_count)]
        )

    strips = b_strips.reshape(KB * rcap, size, size)
    (early,) = pack(0, PARTS[:1], spot, tables, strips)
    late, *over = pack(PARTS[0], PARTS[1:], spot, tables, strips)
    early, late, *over = after(received[0, :16], [early, late, *over])
    pieces = [to_row_before(early), to_row_before(late)]

    shifted = lax.ppermute(received, "col", [(i + 1, i) for i in range(last)])
    part = received[:, size:]
    parts = [lax.ppermute(part, "col", [(i, last)]) for i in range(last)] + [part]

    wide = NJ * size
    strip = pl.BlockSpec((GROUP * size, wide), lambda i, *_: (i, 0))
    begun, order, first, target = step_call(
        functools.partial(first_kernel, rcap),
        (spot,), (tables, received, in_hbm(strips)), [ANYWHERE, ANYWHERE, ANYWHERE],
        [
            pltpu.HBM((RB * size, wide), jnp.float32),
            jax.ShapeDtypeStruct((devices,), jnp.int32),
            jax.ShapeDtypeStruct((RB + 3,), jnp.int32),
            jax.ShapeDtypeStruct((KB * rcap,), jnp.int32),
        ],
        [strip, IN_SMEM, IN_SMEM, IN_SMEM],
        [
            pltpu.SMEM(tables.shape, jnp.int32),
            pltpu.SemaphoreType.DMA,
            pltpu.SMEM((devices,), jnp.int32),
            pltpu.SMEM((RB + 2,), jnp.int32),
            pltpu.SMEM((KB,), jnp.int32),
            pltpu.SMEM((KB,), jnp.int32),
        ],
        devices, size,
    )

    on_last = (col_index == last).astype(jnp.int32)
    scalars = (order, first, target, jnp.stack([on_last, most]))
    lefts = (shifted, *parts)
    begun, rounded, level = step_call(
        functools.partial(middle_kernel, cols_count),
        scalars, (*lefts, pieces[0], in_hbm(begun)),
        [ANYWHERE] * (len(lefts) + 1) + [strip],
        [
            pltpu.HBM((RB * size, wide), jnp.float32),
            pltpu.HBM((RB * size, wide), jnp.bfloat16),
            jax.ShapeDtypeStruct((1,), jnp.int32),
        ],
        [strip, strip, IN_SMEM],
        [pltpu.VMEM((size, wide), jnp.float32), pltpu.SMEM((KB,), jnp.int32)],
        devices, size,
    )

    begin = ALWAYS
    for blocks in over:
        pieces.append(lax.cond(level[0] > begin, to_row_before, lambda same: same, blocks))
        begin += blocks.shape[0]

    operands = (*lefts, *pieces[1:], in_hbm(begun), rounded)
    return pl.pallas_call(
        functools.partial(last_kernel, cols_count, PARTS[0]),
        out_shape=jax.ShapeDtypeStruct((RB * size, wide), jnp.bfloat16),
        grid_spec=pltpu.PrefetchScalarGridSpec(
            num_scalar_prefetch=len(scalars),
            grid=(1,),
            in_specs=[ANYWHERE] * len(operands),
            out_specs=ANYWHERE,
            scratch_shapes=[
                pltpu.VMEM((devices, size, size), jnp.bfloat16),
                pltpu.VMEM((KB, size, wide), jnp.bfloat16),
                pltpu.VMEM((RB, size, wide), jnp.float32),
                pltpu.VMEM((RB, size, wide), jnp.bfloat16),
                pltpu.SMEM((KB,), jnp.int32),
                pltpu.SMEM((RB,), jnp.int32),
                pltpu.SemaphoreType.DMA,
                pltpu.SemaphoreType.DMA,
                pltpu.SemaphoreType.DMA((RB,)),
                pltpu.SemaphoreType.DMA((RB,)),
            ],
        ),
        input_output_aliases={len(scalars) + len(operands) - 1: 0},
        compiler_params=pltpu.CompilerParams(vmem_limit_bytes=LIMIT),
        cost_estimate=pl.CostEstimate(
            flops=2 * 8 * NJ * size * size * size,
            bytes_accessed=8 * 1024 * 1024,
            transcendentals=0,
        ),
    )(*scalars, *operands)


def solution(mesh):
    placed = (
        P(None, ("row", "col"), None, None, None),
        P(None, ("row", "col"), None),
        P("row", "col", None, None, None, None),
        P("row", "col", None, None),
    )
    return jax.shard_map(
        local, mesh=mesh, in_specs=placed, out_specs=P("row", "col"), check_vma=False
    )
```

```python
import functools

import jax
import jax.numpy as jnp
from jax import lax
from jax.experimental import pallas as pl
from jax.experimental.pallas import tpu as pltpu
from jax.sharding import PartitionSpec as P

RB = 16
KB = 16
NJ = 8
PARTS = (64, 32, 8, 24)
ALWAYS = PARTS[0] + PARTS[1]
GROUP = 4
IN_SMEM = pl.BlockSpec(memory_space=pltpu.SMEM)
ANYWHERE = pl.BlockSpec(memory_space=pl.ANY)
LIMIT = 24 * 1024 * 1024


def in_hbm(value):
    return pltpu.with_memory_space_constraint(value, pltpu.HBM)


def places_in(table, half, owner):
    at = half * table.shape[0] + owner
    return lambda source: table[source, 1 + at // 128, at % 128]


def columns_in(table, rcap, device):
    return lambda slot: table[device, 0, slot % rcap * KB + slot // rcap]


def mark_rows(place, slots, named):
    def reset(j, carry):
        named[j] = 0
        return carry

    def mark(s, carry):
        here = place(s)

        @pl.when(here >= 0)
        def _():
            named[here % KB] = 1

        return carry

    lax.fori_loop(0, KB, reset, 0)
    lax.fori_loop(0, slots, mark, 0)


def for_wanted(column, named, rcap, action):
    def visit(slot, number):
        wanted = (column(slot) >= 0) & (named[slot // rcap] > 0)

        @pl.when(wanted)
        def _():
            action(slot, number)

        return number + wanted.astype(jnp.int32)

    return lax.fori_loop(0, KB * rcap, visit, 0)


def pack_kernel(begin, end, lows, rcap, spot, tables, strips, *refs):
    outs = refs[-6 - len(lows) : -6]
    stage, table, sem_table, named, sem, sem_out = refs[-6:]
    table_copy = pltpu.make_async_copy(tables, table, sem_table)
    table_copy.start()
    table_copy.wait()
    mark_rows(places_in(table, spot[0], spot[3]), table.shape[0], named)

    def fetch(slot, number):
        @pl.when((number >= begin) & (number < end))
        def _():
            pltpu.make_async_copy(strips.at[slot], stage.at[number - begin], sem).start()

    count = for_wanted(columns_in(table, rcap, spot[1]), named, rcap, fetch)

    def finish(number, carry):
        pltpu.make_async_copy(strips.at[0], stage.at[0], sem).wait()
        return carry

    lax.fori_loop(begin, jnp.minimum(count, end), finish, 0)
    copies = []
    for i, (out, low) in enumerate(zip(outs, lows)):
        here = stage.at[pl.ds(low, out.shape[0])]
        copies.append(pltpu.make_async_copy(here, out, sem_out.at[i]))
        copies[-1].start()
    for copy in copies:
        copy.wait()


def pack(begin, end, ranges, spot, tables, strips, *before):
    size = strips.shape[-1]
    counts = [high - low for low, high in ranges]
    lows = [low - begin for low, _ in ranges]
    return pl.pallas_call(
        functools.partial(pack_kernel, begin, end, lows, strips.shape[0] // KB),
        out_shape=[pltpu.HBM((n, size, size), strips.dtype) for n in counts],
        grid_spec=pltpu.PrefetchScalarGridSpec(
            num_scalar_prefetch=1,
            grid=(1,),
            in_specs=[ANYWHERE] * (2 + len(before)),
            out_specs=[ANYWHERE] * len(counts),
            scratch_shapes=[
                pltpu.VMEM((end - begin, size, size), strips.dtype),
                pltpu.SMEM(tables.shape, jnp.int32),
                pltpu.SemaphoreType.DMA,
                pltpu.SMEM((KB,), jnp.int32),
                pltpu.SemaphoreType.DMA,
                pltpu.SemaphoreType.DMA((len(counts),)),
            ],
        ),
        compiler_params=pltpu.CompilerParams(vmem_limit_bytes=LIMIT),
        cost_estimate=pl.CostEstimate(
            flops=0, bytes_accessed=4 * sum(counts) * size * size, transcendentals=0
        ),
    )(spot, tables, in_hbm(strips), *before)


def after(value, blocks):
    count = len(blocks)
    return pl.pallas_call(
        lambda *refs: None,
        out_shape=[pltpu.HBM(each.shape, each.dtype) for each in blocks],
        in_specs=[ANYWHERE] * (count + 1),
        out_specs=[ANYWHERE] * count,
        input_output_aliases={i: i for i in range(count)},
    )(*blocks, value)


def by_block_row(place, slots, order, first):
    def reset(i, carry):
        first[i] = 0
        return carry

    def count(s, carry):
        here = place(s)

        @pl.when(here >= 0)
        def _():
            i = here // KB + 2
            first[i] = first[i] + 1

        return carry

    def scan(i, carry):
        first[i] = first[i] + first[i - 1]
        return carry

    def sort(s, carry):
        here = place(s)

        @pl.when(here >= 0)
        def _():
            i = here // KB + 1
            order[first[i]] = s * KB + here % KB
            first[i] = first[i] + 1

        return carry

    lax.fori_loop(0, RB + 2, reset, 0)
    lax.fori_loop(0, slots, count, 0)
    lax.fori_loop(1, RB + 2, scan, 0)
    lax.fori_loop(0, slots, sort, 0)


def clear(right, low):
    def one(j, carry):
        right[j] = jnp.zeros(right.shape[1:], right.dtype)
        return carry

    lax.fori_loop(low, KB, one, 0)


def add_rows(left, right, total, order, first):
    size = left.shape[1]

    def one_row(i, carry):
        row = pl.program_id(0) * GROUP + i
        here = pl.ds(pl.multiple_of(i * size, size), size)

        def add(entry, carry):
            total[here, :] += jnp.dot(
                left[order[entry] // KB], right[order[entry] % KB],
                preferred_element_type=jnp.float32,
            )
            return carry

        return lax.fori_loop(first[row], first[row + 1], add, carry)

    lax.fori_loop(0, GROUP, one_row, 0)


def place_at(right, where):
    size = right.shape[1]
    start = pl.multiple_of((where % NJ) * size, size)
    return right.at[where // NJ, :, pl.ds(start, size)]


def finish_right(source, right, sem, count):
    def finish(number, carry):
        pltpu.make_async_copy(source, place_at(right, 0), sem).wait()
        return carry

    lax.fori_loop(0, count, finish, 0)


def first_kernel(
    rcap, spot, tables, received, strips,
    out, next_order, next_first, next_target,
    left, right, table, sem_table, order, first, named, other, sem_left, sem_right,
):
    slots, size, _ = left.shape

    @pl.when(pl.program_id(0) == 0)
    def _():
        left_copy = pltpu.make_async_copy(received.at[:, pl.ds(0, size)], left, sem_left)
        left_copy.start()
        table_copy = pltpu.make_async_copy(tables, table, sem_table)
        table_copy.start()
        clear(right, 0)
        table_copy.wait()
        place = places_in(table, 0, spot[1])
        column = columns_in(table, rcap, spot[1])
        mark_rows(place, slots, named)

        def fetch(slot, number):
            target = place_at(right, slot // rcap * NJ + column(slot))
            pltpu.make_async_copy(strips.at[slot], target, sem_right).start()

        count = for_wanted(column, named, rcap, fetch)
        by_block_row(place, slots, order, first)

        next_place = places_in(table, spot[0], spot[2])
        next_column = columns_in(table, rcap, spot[4])
        by_block_row(next_place, slots, next_order, next_first)
        mark_rows(next_place, slots, other)

        def note(slot, number):
            next_target[number] = slot // rcap * NJ + next_column(slot)

        next_first[RB + 2] = for_wanted(next_column, other, rcap, note)
        left_copy.wait()
        finish_right(strips.at[0], right, sem_right, count)

    out[...] = jnp.zeros(out.shape, out.dtype)
    add_rows(left, right, out, order, first)


def start_left(shifted, parts, left, on_last, sem):
    size = left.shape[1]
    step = size // len(parts)
    whole = pltpu.make_async_copy(shifted.at[:, pl.ds(0, size)], left, sem)

    @pl.when(on_last)
    def _():
        for q, part in enumerate(parts):
            pltpu.make_async_copy(part, left.at[:, pl.ds(q * step, step)], sem).start()

    @pl.when(jnp.logical_not(on_last))
    def _():
        whole.start()

    return whole


def start_right(pieces, begin, count, on_round, target, right, touched, sem):
    def reset(j, carry):
        touched[j] = 0
        return carry

    lax.fori_loop(0, KB, reset, 0)
    clear(right, jnp.where(count > begin, target[begin] // NJ, KB))
    low = begin
    for piece in pieces:

        def fetch(number, carry):
            touched[target[number] // NJ] = 1
            where = place_at(right, target[number])
            if len(piece) == 1:
                pltpu.make_async_copy(piece[0].at[number - low], where, sem).start()
            else:

                @pl.when(on_round)
                def _():
                    pltpu.make_async_copy(piece[1].at[number - low], where, sem).start()

                @pl.when(jnp.logical_not(on_round))
                def _():
                    pltpu.make_async_copy(piece[0].at[number - low], where, sem).start()

            return carry

        high = low + piece[0].shape[0]
        lax.fori_loop(low, jnp.minimum(count, high), fetch, 0)
        low = high
    return jnp.minimum(count, low) - begin


def middle_kernel(parts_count, order, first, target, flags, *refs):
    shifted, *parts = refs[: 1 + parts_count]
    (
        piece, piece_round, prev, out, rounded, level,
        left, right, total, touched, sem_left, sem_right,
    ) = refs[1 + parts_count :]
    size = left.shape[1]

    @pl.when(pl.program_id(0) == 0)
    def _():
        whole = start_left(shifted, parts, left, flags[0] > 0, sem_left)
        count = start_right(
            [(piece, piece_round)], 0, first[RB + 2], flags[2] > 0,
            target, right, touched, sem_right,
        )
        level[0] = flags[1]
        whole.wait()
        finish_right(piece.at[0], right, sem_right, count)

    def one_row(i, carry):
        row = pl.program_id(0) * GROUP + i
        here = pl.ds(pl.multiple_of(i * size, size), size)
        total[...] = prev[here, :]

        def add(entry, carry):
            @pl.when(touched[order[entry] % KB] > 0)
            def _():
                total[...] += jnp.dot(
                    left[order[entry] // KB], right[order[entry] % KB],
                    preferred_element_type=jnp.float32,
                )

            return carry

        lax.fori_loop(first[row], first[row + 1], add, 0)
        out[here, :] = total[...]
        rounded[here, :] = total[...].astype(rounded.dtype)
        return carry

    lax.fori_loop(0, GROUP, one_row, 0)


def last_kernel(parts_count, begin, order, first, target, flags, *refs):
    shifted, *parts = refs[: 1 + parts_count]
    piece, piece_round, *over = refs[1 + parts_count : 1 + len(PARTS) + parts_count]
    pieces = [(piece, piece_round), *((each,) for each in over)]
    (
        prev, _, out,
        left, right, total, rounded, touched, open_row,
        sem_left, sem_right, sem_prev, sem_out,
    ) = refs[1 + len(PARTS) + parts_count :]
    size = left.shape[1]
    whole = start_left(shifted, parts, left, flags[0] > 0, sem_left)
    count = start_right(
        pieces, begin, first[RB + 2], flags[2] > 0, target, right, touched, sem_right
    )

    def rows_at(row):
        return pl.ds(pl.multiple_of(row * size, size), size)

    def prev_copy(row):
        return pltpu.make_async_copy(prev.at[rows_at(row)], total.at[row], sem_prev.at[row])

    def out_copy(row):
        return pltpu.make_async_copy(rounded.at[row], out.at[rows_at(row)], sem_out.at[row])

    def open_one(row, carry):
        def look(entry, found):
            return jnp.maximum(found, touched[order[entry] % KB])

        open_row[row] = lax.fori_loop(first[row], first[row + 1], look, jnp.int32(0))

        @pl.when(open_row[row] > 0)
        def _():
            prev_copy(row).start()

        return carry

    lax.fori_loop(0, RB, open_one, 0)
    whole.wait()
    finish_right(piece.at[0], right, sem_right, count)

    def add_row(row, carry):
        def add(entry, carry):
            @pl.when(touched[order[entry] % KB] > 0)
            def _():
                total[row] += jnp.dot(
                    left[order[entry] // KB], right[order[entry] % KB],
                    preferred_element_type=jnp.float32,
                )

            return carry

        @pl.when(open_row[row] > 0)
        def _():
            prev_copy(row).wait()
            lax.fori_loop(first[row], first[row + 1], add, 0)
            rounded[row] = total[row].astype(rounded.dtype)
            out_copy(row).start()

        return carry

    def close_row(row, carry):
        @pl.when(open_row[row] > 0)
        def _():
            out_copy(row).wait()

        return carry

    lax.fori_loop(0, RB, add_row, 0)
    lax.fori_loop(0, RB, close_row, 0)


def step_call(kernel, scalars, operands, specs, out_shape, out_specs, scratch, slots, size):
    return pl.pallas_call(
        kernel,
        out_shape=out_shape,
        grid_spec=pltpu.PrefetchScalarGridSpec(
            num_scalar_prefetch=len(scalars),
            grid=(RB // GROUP,),
            in_specs=specs,
            out_specs=out_specs,
            scratch_shapes=[
                pltpu.VMEM((slots, size, size), jnp.bfloat16),
                pltpu.VMEM((KB, size, NJ * size), jnp.bfloat16),
                *scratch,
                pltpu.SemaphoreType.DMA,
                pltpu.SemaphoreType.DMA,
            ],
        ),
        compiler_params=pltpu.CompilerParams(
            dimension_semantics=("arbitrary",), vmem_limit_bytes=LIMIT
        ),
        cost_estimate=pl.CostEstimate(
            flops=2 * 24 * NJ * size * size * size,
            bytes_accessed=16 * 1024 * 1024,
            transcendentals=0,
        ),
    )(*scalars, *operands)


def table_kernel(where, cols, out, tile):
    rcap, across = cols.shape
    devices = where.shape[-1]
    tile[...] = jnp.zeros(tile.shape, tile.dtype)
    for slot in range(rcap):
        tile[pl.ds(0, 1), pl.ds(slot * across, across)] = cols[pl.ds(slot, 1), :]
    for half in range(2):
        row, lane = divmod(half * devices, 128)
        tile[pl.ds(1 + row, 1), pl.ds(lane, devices)] = where[half]

    def fill(device, carry):
        out[device] = tile[...]
        return carry

    lax.fori_loop(0, out.shape[0], fill, 0)


def table_for_all(where, cols):
    devices = where.shape[-1]
    shape = (1 + -(-2 * devices // 128), 128)
    return pl.pallas_call(
        table_kernel,
        out_shape=jax.ShapeDtypeStruct((devices, *shape), jnp.int32),
        scratch_shapes=[pltpu.VMEM(shape, jnp.int32)],
        compiler_params=pltpu.CompilerParams(vmem_limit_bytes=LIMIT),
    )(where, cols)


def most_needed(where_all, cols_all, rows_count, cols_count):
    grid = where_all.reshape(-1, 2, rows_count, cols_count)
    after = jnp.concatenate([grid[:, 0, :, 1:], grid[:, 1, :, :1]], axis=-1)
    columns = jnp.arange(KB, dtype=jnp.int32)
    hit = (after[..., None] >= 0) & (after[..., None] % KB == columns)
    wanted = jnp.any(hit, axis=0).astype(jnp.int32)
    counts = jnp.sum((cols_all >= 0).astype(jnp.int32), axis=1)
    counts = jnp.roll(counts.reshape(rows_count, cols_count, KB), -1, axis=0)
    return jnp.max(jnp.sum(wanted * counts, axis=-1))


def local(a_send, a_where, b_strips, b_cols):
    size = a_send.shape[-1]
    rows_count = lax.axis_size("row")
    cols_count = lax.axis_size("col")
    devices = rows_count * cols_count
    both = ("row", "col")
    row_index = lax.axis_index("row")
    col_index = lax.axis_index("col")
    rcap = b_strips.shape[3]
    last = cols_count - 1

    by_slot = jnp.swapaxes(b_cols, 2, 3).reshape(rcap, KB)
    tables = lax.all_to_all(
        table_for_all(a_where, by_slot), both, split_axis=0, concat_axis=0, tiled=True
    )
    after_col = (col_index + 1) % cols_count
    after_half = (col_index + 1) // cols_count
    row_before = (row_index + rows_count - 1) % rows_count
    row_after = (row_index + 1) % rows_count
    spot = jnp.stack([
        after_half,
        row_index * cols_count + col_index,
        row_index * cols_count + after_col,
        row_before * cols_count + after_col,
        row_after * cols_count + col_index,
    ]).astype(jnp.int32)
    most = most_needed(
        tables[:, 1:].reshape(devices, -1)[:, : 2 * devices],
        tables[:, 0].reshape(devices, rcap, KB), rows_count, cols_count,
    )

    wrapped = a_send[1, 0].reshape(rows_count, cols_count, size, size)[:, 0]
    wrapped = wrapped.reshape(devices, size // cols_count, size)
    received = lax.all_to_all(
        jnp.concatenate([a_send[0, 0], wrapped], axis=1),
        both, split_axis=0, concat_axis=0, tiled=True,
    )

    def to_row_before(blocks):
        return lax.ppermute(
            blocks, "row", [(i, (i - 1) % rows_count) for i in range(rows_count)]
        )

    def down(blocks):
        return lax.ppermute(blocks, "row", [(i, i - 1) for i in range(1, rows_count)])

    def around(blocks):
        return lax.ppermute(blocks, "row", [(0, rows_count - 1)])

    strips = b_strips.reshape(KB * rcap, size, size)
    split, full = PARTS[0], KB * rcap
    early, early_round = pack(0, split, [(0, split)] * 2, spot, tables, strips)
    ends = [ALWAYS, ALWAYS + PARTS[2], full]
    late, late_round, *over = pack(
        split, full,
        [(split, ALWAYS), (split, ALWAYS), (ends[0], ends[1]), (ends[1], ends[2])],
        spot, tables, strips, early,
    )
    early_round, late_round = after(received[0, :16], [early_round, late_round])
    pieces = [(down(early), around(early_round)), (down(late), around(late_round))]

    shifted = lax.ppermute(received, "col", [(i + 1, i) for i in range(last)])
    part = received[:, size:]
    parts = [lax.ppermute(part, "col", [(i, last)]) for i in range(last)] + [part]

    wide = NJ * size
    strip = pl.BlockSpec((GROUP * size, wide), lambda i, *_: (i, 0))
    begun, order, first, target = step_call(
        functools.partial(first_kernel, rcap),
        (spot,), (tables, received, in_hbm(strips)), [ANYWHERE, ANYWHERE, ANYWHERE],
        [
            pltpu.HBM((RB * size, wide), jnp.float32),
            jax.ShapeDtypeStruct((devices,), jnp.int32),
            jax.ShapeDtypeStruct((RB + 3,), jnp.int32),
            jax.ShapeDtypeStruct((KB * rcap,), jnp.int32),
        ],
        [strip, IN_SMEM, IN_SMEM, IN_SMEM],
        [
            pltpu.SMEM(tables.shape, jnp.int32),
            pltpu.SemaphoreType.DMA,
            pltpu.SMEM((devices,), jnp.int32),
            pltpu.SMEM((RB + 2,), jnp.int32),
            pltpu.SMEM((KB,), jnp.int32),
            pltpu.SMEM((KB,), jnp.int32),
        ],
        devices, size,
    )

    on_last = (col_index == last).astype(jnp.int32)
    on_round = (row_index == rows_count - 1).astype(jnp.int32)
    scalars = (order, first, target, jnp.stack([on_last, most, on_round]))
    lefts = (shifted, *parts)
    begun, rounded, level = step_call(
        functools.partial(middle_kernel, cols_count),
        scalars, (*lefts, *pieces[0], in_hbm(begun)),
        [ANYWHERE] * (len(lefts) + 2) + [strip],
        [
            pltpu.HBM((RB * size, wide), jnp.float32),
            pltpu.HBM((RB * size, wide), jnp.bfloat16),
            jax.ShapeDtypeStruct((1,), jnp.int32),
        ],
        [strip, strip, IN_SMEM],
        [pltpu.VMEM((size, wide), jnp.float32), pltpu.SMEM((KB,), jnp.int32)],
        devices, size,
    )

    begin = ALWAYS
    extra = []
    for blocks in over:
        extra.append(lax.cond(level[0] > begin, to_row_before, lambda same: same, blocks))
        begin += blocks.shape[0]

    operands = (*lefts, *pieces[1], *extra, in_hbm(begun), rounded)
    return pl.pallas_call(
        functools.partial(last_kernel, cols_count, PARTS[0]),
        out_shape=jax.ShapeDtypeStruct((RB * size, wide), jnp.bfloat16),
        grid_spec=pltpu.PrefetchScalarGridSpec(
            num_scalar_prefetch=len(scalars),
            grid=(1,),
            in_specs=[ANYWHERE] * len(operands),
            out_specs=ANYWHERE,
            scratch_shapes=[
                pltpu.VMEM((devices, size, size), jnp.bfloat16),
                pltpu.VMEM((KB, size, wide), jnp.bfloat16),
                pltpu.VMEM((RB, size, wide), jnp.float32),
                pltpu.VMEM((RB, size, wide), jnp.bfloat16),
                pltpu.SMEM((KB,), jnp.int32),
                pltpu.SMEM((RB,), jnp.int32),
                pltpu.SemaphoreType.DMA,
                pltpu.SemaphoreType.DMA,
                pltpu.SemaphoreType.DMA((RB,)),
                pltpu.SemaphoreType.DMA((RB,)),
            ],
        ),
        input_output_aliases={len(scalars) + len(operands) - 1: 0},
        compiler_params=pltpu.CompilerParams(vmem_limit_bytes=LIMIT),
        cost_estimate=pl.CostEstimate(
            flops=2 * 8 * NJ * size * size * size,
            bytes_accessed=8 * 1024 * 1024,
            transcendentals=0,
        ),
    )(*scalars, *operands)


def solution(mesh):
    placed = (
        P(None, ("row", "col"), None, None, None),
        P(None, ("row", "col"), None),
        P("row", "col", None, None, None, None),
        P("row", "col", None, None),
    )
    return jax.shard_map(
        local, mesh=mesh, in_specs=placed, out_specs=P("row", "col"), check_vma=False
    )
```

```python
import functools

import jax
import jax.numpy as jnp
from jax import lax
from jax.experimental import pallas as pl
from jax.experimental.pallas import tpu as pltpu
from jax.sharding import PartitionSpec as P

RB = 16
KB = 16
NJ = 8
PARTS = (64, 32, 8, 24)
ALWAYS = PARTS[0] + PARTS[1]
GROUP = 4
IN_SMEM = pl.BlockSpec(memory_space=pltpu.SMEM)
ANYWHERE = pl.BlockSpec(memory_space=pl.ANY)
LIMIT = 24 * 1024 * 1024


def in_hbm(value):
    return pltpu.with_memory_space_constraint(value, pltpu.HBM)


def places_in(table, half, owner):
    at = half * table.shape[0] + owner
    return lambda source: table[source, 1 + at // 128, at % 128]


def columns_in(table, rcap, device):
    return lambda slot: table[device, 0, slot % rcap * KB + slot // rcap]


def mark_rows(place, slots, named):
    def reset(j, carry):
        named[j] = 0
        return carry

    def mark(s, carry):
        here = place(s)

        @pl.when(here >= 0)
        def _():
            named[here % KB] = 1

        return carry

    lax.fori_loop(0, KB, reset, 0)
    lax.fori_loop(0, slots, mark, 0)


def for_wanted(column, named, rcap, action):
    def visit(slot, number):
        wanted = (column(slot) >= 0) & (named[slot // rcap] > 0)

        @pl.when(wanted)
        def _():
            action(slot, number)

        return number + wanted.astype(jnp.int32)

    return lax.fori_loop(0, KB * rcap, visit, 0)


def pack_kernel(begin, end, lows, rcap, spot, tables, strips, *refs):
    outs = refs[-6 - len(lows) : -6]
    stage, table, sem_table, named, sem, sem_out = refs[-6:]
    table_copy = pltpu.make_async_copy(tables, table, sem_table)
    table_copy.start()
    table_copy.wait()
    mark_rows(places_in(table, spot[0], spot[3]), table.shape[0], named)

    def fetch(slot, number):
        @pl.when((number >= begin) & (number < end))
        def _():
            pltpu.make_async_copy(strips.at[slot], stage.at[number - begin], sem).start()

    count = for_wanted(columns_in(table, rcap, spot[1]), named, rcap, fetch)

    def finish(number, carry):
        pltpu.make_async_copy(strips.at[0], stage.at[0], sem).wait()
        return carry

    lax.fori_loop(begin, jnp.minimum(count, end), finish, 0)
    copies = []
    for i, (out, low) in enumerate(zip(outs, lows)):
        here = stage.at[pl.ds(low, out.shape[0])]
        copies.append(pltpu.make_async_copy(here, out, sem_out.at[i]))
        copies[-1].start()
    for copy in copies:
        copy.wait()


def pack(begin, end, ranges, spot, tables, strips, *before):
    size = strips.shape[-1]
    counts = [high - low for low, high in ranges]
    lows = [low - begin for low, _ in ranges]
    return pl.pallas_call(
        functools.partial(pack_kernel, begin, end, lows, strips.shape[0] // KB),
        out_shape=[pltpu.HBM((n, size, size), strips.dtype) for n in counts],
        grid_spec=pltpu.PrefetchScalarGridSpec(
            num_scalar_prefetch=1,
            grid=(1,),
            in_specs=[ANYWHERE] * (2 + len(before)),
            out_specs=[ANYWHERE] * len(counts),
            scratch_shapes=[
                pltpu.VMEM((end - begin, size, size), strips.dtype),
                pltpu.SMEM(tables.shape, jnp.int32),
                pltpu.SemaphoreType.DMA,
                pltpu.SMEM((KB,), jnp.int32),
                pltpu.SemaphoreType.DMA,
                pltpu.SemaphoreType.DMA((len(counts),)),
            ],
        ),
        compiler_params=pltpu.CompilerParams(vmem_limit_bytes=LIMIT),
        cost_estimate=pl.CostEstimate(
            flops=0, bytes_accessed=4 * sum(counts) * size * size, transcendentals=0
        ),
    )(spot, tables, in_hbm(strips), *before)


def after(value, blocks):
    count = len(blocks)
    return pl.pallas_call(
        lambda *refs: None,
        out_shape=[pltpu.HBM(each.shape, each.dtype) for each in blocks],
        in_specs=[ANYWHERE] * (count + 1),
        out_specs=[ANYWHERE] * count,
        input_output_aliases={i: i for i in range(count)},
    )(*blocks, value)


def by_block_row(place, slots, order, first):
    def reset(i, carry):
        first[i] = 0
        return carry

    def count(s, carry):
        here = place(s)

        @pl.when(here >= 0)
        def _():
            i = here // KB + 2
            first[i] = first[i] + 1

        return carry

    def scan(i, carry):
        first[i] = first[i] + first[i - 1]
        return carry

    def sort(s, carry):
        here = place(s)

        @pl.when(here >= 0)
        def _():
            i = here // KB + 1
            order[first[i]] = s * KB + here % KB
            first[i] = first[i] + 1

        return carry

    lax.fori_loop(0, RB + 2, reset, 0)
    lax.fori_loop(0, slots, count, 0)
    lax.fori_loop(1, RB + 2, scan, 0)
    lax.fori_loop(0, slots, sort, 0)


def clear(right, low):
    def one(j, carry):
        right[j] = jnp.zeros(right.shape[1:], right.dtype)
        return carry

    lax.fori_loop(low, KB, one, 0)


def add_rows(left, right, total, order, first):
    size = left.shape[1]

    def one_row(i, carry):
        row = pl.program_id(0) * GROUP + i
        here = pl.ds(pl.multiple_of(i * size, size), size)

        def add(entry, carry):
            total[here, :] += jnp.dot(
                left[order[entry] // KB], right[order[entry] % KB],
                preferred_element_type=jnp.float32,
            )
            return carry

        return lax.fori_loop(first[row], first[row + 1], add, carry)

    lax.fori_loop(0, GROUP, one_row, 0)


def place_at(right, where):
    size = right.shape[1]
    start = pl.multiple_of((where % NJ) * size, size)
    return right.at[where // NJ, :, pl.ds(start, size)]


def finish_right(source, right, sem, count):
    def finish(number, carry):
        pltpu.make_async_copy(source, place_at(right, 0), sem).wait()
        return carry

    lax.fori_loop(0, count, finish, 0)


def first_kernel(
    rcap, spot, tables, received, strips,
    out, next_order, next_first, next_target,
    left, right, table, sem_table, order, first, named, other, sem_left, sem_right,
):
    slots, size, _ = left.shape

    @pl.when(pl.program_id(0) == 0)
    def _():
        left_copy = pltpu.make_async_copy(received.at[:, pl.ds(0, size)], left, sem_left)
        left_copy.start()
        table_copy = pltpu.make_async_copy(tables, table, sem_table)
        table_copy.start()
        clear(right, 0)
        table_copy.wait()
        place = places_in(table, 0, spot[1])
        column = columns_in(table, rcap, spot[1])
        mark_rows(place, slots, named)

        def fetch(slot, number):
            target = place_at(right, slot // rcap * NJ + column(slot))
            pltpu.make_async_copy(strips.at[slot], target, sem_right).start()

        count = for_wanted(column, named, rcap, fetch)
        by_block_row(place, slots, order, first)

        next_place = places_in(table, spot[0], spot[2])
        next_column = columns_in(table, rcap, spot[4])
        by_block_row(next_place, slots, next_order, next_first)
        mark_rows(next_place, slots, other)

        def note(slot, number):
            next_target[number] = slot // rcap * NJ + next_column(slot)

        next_first[RB + 2] = for_wanted(next_column, other, rcap, note)
        left_copy.wait()
        finish_right(strips.at[0], right, sem_right, count)

    out[...] = jnp.zeros(out.shape, out.dtype)
    add_rows(left, right, out, order, first)


def start_left(shifted, parts, left, on_last, sem):
    size = left.shape[1]
    step = shifted.shape[1] - size
    whole = pltpu.make_async_copy(shifted.at[:, pl.ds(0, size)], left, sem)

    @pl.when(on_last)
    def _():
        for q, part in enumerate([shifted.at[:, pl.ds(size, step)], *parts]):
            pltpu.make_async_copy(part, left.at[:, pl.ds(q * step, step)], sem).start()

    @pl.when(jnp.logical_not(on_last))
    def _():
        whole.start()

    return whole


def start_right(sources, begin, end, count, target, right, touched, sem):
    def reset(j, carry):
        touched[j] = 0
        return carry

    lax.fori_loop(0, KB, reset, 0)
    clear(right, jnp.where(count > begin, target[begin] // NJ, KB))
    for blocks, low, wanted in sources:

        def fetch(number, carry):
            touched[target[number] // NJ] = 1
            pltpu.make_async_copy(
                blocks.at[number - low], place_at(right, target[number]), sem
            ).start()
            return carry

        high = jnp.minimum(jnp.minimum(count, end), low + blocks.shape[0])
        start = max(low, begin)
        lax.fori_loop(start, jnp.where(wanted, high, start), fetch, 0)
    return jnp.minimum(count, end) - begin


def add_products(row, order, first, left, right, touched, total):
    def add(entry, carry):
        @pl.when(touched[order[entry] % KB] > 0)
        def _():
            total[row] += jnp.dot(
                left[order[entry] // KB], right[order[entry] % KB],
                preferred_element_type=jnp.float32,
            )

        return carry

    lax.fori_loop(first[row], first[row + 1], add, 0)


def mark_open(order, first, touched, open_row):
    def one(row, carry):
        def look(entry, found):
            return jnp.maximum(found, touched[order[entry] % KB])

        open_row[row] = lax.fori_loop(first[row], first[row + 1], look, jnp.int32(0))
        return carry

    lax.fori_loop(0, RB, one, 0)


def strip_of(ref, row, size):
    return ref.at[pl.ds(pl.multiple_of(row * size, size), size)]


def middle_kernel(parts_count, order, first, target, flags, *refs):
    shifted, *parts = refs[: 1 + parts_count]
    (
        direct, around, prev, out, rounded, level,
        left, right, total, short, touched, later, open_row,
        sem_left, sem_right, sem_prev, sem_out,
    ) = refs[1 + parts_count :]
    size = left.shape[1]
    count = first[RB + 2]
    on_round = flags[2] > 0
    end = around.shape[0]

    def prev_copy(row):
        return pltpu.make_async_copy(strip_of(prev, row, size), total.at[row], sem_prev.at[row])

    def start_prev(row, carry):
        prev_copy(row).start()
        return carry

    lax.fori_loop(0, RB, start_prev, 0)
    whole = start_left(shifted, parts, left, flags[0] > 0, sem_left)
    fetched = start_right(
        [(direct, 0, jnp.logical_not(on_round)), (around, 0, on_round)],
        0, end, count, target, right, touched, sem_right,
    )
    level[0] = flags[1]

    def reset(j, carry):
        later[j] = 0
        return carry

    def mark(number, carry):
        later[target[number] // NJ] = 1
        return carry

    lax.fori_loop(0, KB, reset, 0)
    lax.fori_loop(end, count, mark, 0)
    mark_open(order, first, later, open_row)
    whole.wait()
    finish_right(direct.at[0], right, sem_right, fetched)

    def out_copies(row):
        return (
            pltpu.make_async_copy(total.at[row], strip_of(out, row, size), sem_out.at[row]),
            pltpu.make_async_copy(short.at[row], strip_of(rounded, row, size), sem_out.at[row]),
        )

    def one_row(row, carry):
        open_copy, closed_copy = out_copies(row)
        prev_copy(row).wait()
        add_products(row, order, first, left, right, touched, total)

        @pl.when(open_row[row] > 0)
        def _():
            open_copy.start()

        @pl.when(open_row[row] == 0)
        def _():
            short[row] = total[row].astype(short.dtype)
            closed_copy.start()

        return carry

    def close_row(row, carry):
        open_copy, closed_copy = out_copies(row)

        @pl.when(open_row[row] > 0)
        def _():
            open_copy.wait()

        @pl.when(open_row[row] == 0)
        def _():
            closed_copy.wait()

        return carry

    lax.fori_loop(0, RB, one_row, 0)
    lax.fori_loop(0, RB, close_row, 0)


def last_kernel(parts_count, begin, order, first, target, flags, *refs):
    shifted, *parts = refs[: 1 + parts_count]
    (
        direct, around, *over, prev, _, out,
        left, right, total, short, touched, open_row,
        sem_left, sem_right, sem_prev, sem_out,
    ) = refs[1 + parts_count :]
    size = left.shape[1]
    on_round = flags[2] > 0
    whole = start_left(shifted, parts, left, flags[0] > 0, sem_left)
    sources = [(direct, 0, jnp.logical_not(on_round)), (around, begin, on_round)]
    low = direct.shape[0]
    for blocks in over:
        sources.append((blocks, low, jnp.bool_(True)))
        low += blocks.shape[0]
    count = start_right(
        sources, begin, low, first[RB + 2], target, right, touched, sem_right
    )
    mark_open(order, first, touched, open_row)

    def prev_copy(row):
        return pltpu.make_async_copy(strip_of(prev, row, size), total.at[row], sem_prev.at[row])

    def out_copy(row):
        return pltpu.make_async_copy(short.at[row], strip_of(out, row, size), sem_out.at[row])

    def start_prev(row, carry):
        @pl.when(open_row[row] > 0)
        def _():
            prev_copy(row).start()

        return carry

    lax.fori_loop(0, RB, start_prev, 0)
    whole.wait()
    finish_right(direct.at[0], right, sem_right, count)

    def one_row(row, carry):
        @pl.when(open_row[row] > 0)
        def _():
            prev_copy(row).wait()
            add_products(row, order, first, left, right, touched, total)
            short[row] = total[row].astype(short.dtype)
            out_copy(row).start()

        return carry

    def close_row(row, carry):
        @pl.when(open_row[row] > 0)
        def _():
            out_copy(row).wait()

        return carry

    lax.fori_loop(0, RB, one_row, 0)
    lax.fori_loop(0, RB, close_row, 0)


def step_call(kernel, scalars, operands, specs, out_shape, out_specs, scratch, slots, size):
    return pl.pallas_call(
        kernel,
        out_shape=out_shape,
        grid_spec=pltpu.PrefetchScalarGridSpec(
            num_scalar_prefetch=len(scalars),
            grid=(RB // GROUP,),
            in_specs=specs,
            out_specs=out_specs,
            scratch_shapes=[
                pltpu.VMEM((slots, size, size), jnp.bfloat16),
                pltpu.VMEM((KB, size, NJ * size), jnp.bfloat16),
                *scratch,
                pltpu.SemaphoreType.DMA,
                pltpu.SemaphoreType.DMA,
            ],
        ),
        compiler_params=pltpu.CompilerParams(
            dimension_semantics=("arbitrary",), vmem_limit_bytes=LIMIT
        ),
        cost_estimate=pl.CostEstimate(
            flops=2 * 24 * NJ * size * size * size,
            bytes_accessed=16 * 1024 * 1024,
            transcendentals=0,
        ),
    )(*scalars, *operands)


def table_kernel(where, cols, out, tile):
    rcap, across = cols.shape
    devices = where.shape[-1]
    tile[...] = jnp.zeros(tile.shape, tile.dtype)
    for slot in range(rcap):
        tile[pl.ds(0, 1), pl.ds(slot * across, across)] = cols[pl.ds(slot, 1), :]
    for half in range(2):
        row, lane = divmod(half * devices, 128)
        tile[pl.ds(1 + row, 1), pl.ds(lane, devices)] = where[half]

    def fill(device, carry):
        out[device] = tile[...]
        return carry

    lax.fori_loop(0, out.shape[0], fill, 0)


def table_for_all(where, cols):
    devices = where.shape[-1]
    shape = (1 + -(-2 * devices // 128), 128)
    return pl.pallas_call(
        table_kernel,
        out_shape=jax.ShapeDtypeStruct((devices, *shape), jnp.int32),
        scratch_shapes=[pltpu.VMEM(shape, jnp.int32)],
        compiler_params=pltpu.CompilerParams(vmem_limit_bytes=LIMIT),
    )(where, cols)


def most_needed(where_all, cols_all, rows_count, cols_count):
    grid = where_all.reshape(-1, 2, rows_count, cols_count)
    after = jnp.concatenate([grid[:, 0, :, 1:], grid[:, 1, :, :1]], axis=-1)
    columns = jnp.arange(KB, dtype=jnp.int32)
    hit = (after[..., None] >= 0) & (after[..., None] % KB == columns)
    wanted = jnp.any(hit, axis=0).astype(jnp.int32)
    counts = jnp.sum((cols_all >= 0).astype(jnp.int32), axis=1)
    counts = jnp.roll(counts.reshape(rows_count, cols_count, KB), -1, axis=0)
    return jnp.max(jnp.sum(wanted * counts, axis=-1))


def local(a_send, a_where, b_strips, b_cols):
    size = a_send.shape[-1]
    rows_count = lax.axis_size("row")
    cols_count = lax.axis_size("col")
    devices = rows_count * cols_count
    both = ("row", "col")
    row_index = lax.axis_index("row")
    col_index = lax.axis_index("col")
    rcap = b_strips.shape[3]
    last = cols_count - 1

    by_slot = jnp.swapaxes(b_cols, 2, 3).reshape(rcap, KB)
    tables = lax.all_to_all(
        table_for_all(a_where, by_slot), both, split_axis=0, concat_axis=0, tiled=True
    )
    after_col = (col_index + 1) % cols_count
    after_half = (col_index + 1) // cols_count
    row_before = (row_index + rows_count - 1) % rows_count
    row_after = (row_index + 1) % rows_count
    spot = jnp.stack([
        after_half,
        row_index * cols_count + col_index,
        row_index * cols_count + after_col,
        row_before * cols_count + after_col,
        row_after * cols_count + col_index,
    ]).astype(jnp.int32)
    most = most_needed(
        tables[:, 1:].reshape(devices, -1)[:, : 2 * devices],
        tables[:, 0].reshape(devices, rcap, KB), rows_count, cols_count,
    )

    wrapped = a_send[1, 0].reshape(rows_count, cols_count, size, size)[:, 0]
    wrapped = wrapped.reshape(devices, size // cols_count, size)
    received = lax.all_to_all(
        jnp.concatenate([a_send[0, 0], wrapped], axis=1),
        both, split_axis=0, concat_axis=0, tiled=True,
    )

    def to_row_before(blocks):
        return lax.ppermute(
            blocks, "row", [(i, (i - 1) % rows_count) for i in range(rows_count)]
        )

    def down(blocks):
        return lax.ppermute(blocks, "row", [(i, i - 1) for i in range(1, rows_count)])

    def around(blocks):
        return lax.ppermute(blocks, "row", [(0, rows_count - 1)])

    strips = b_strips.reshape(KB * rcap, size, size)
    split, full = PARTS[0], KB * rcap
    (direct,) = pack(0, ALWAYS, [(0, ALWAYS)], spot, tables, strips)
    ends = [0, split, ALWAYS, ALWAYS + PARTS[2], full]
    early_round, late_round, *over = pack(
        0, full, list(zip(ends, ends[1:])), spot, tables, strips, direct[0, :16]
    )
    direct = down(direct)
    early_round, late_round = map(around, after(received[0, :16], [early_round, late_round]))

    shifted = lax.ppermute(
        received, "col", [(i, (i - 1) % cols_count) for i in range(cols_count)]
    )
    part = received[:, size:]
    parts = [lax.ppermute(part, "col", [(i, last)]) for i in range(1, last)] + [part]

    wide = NJ * size
    strip = pl.BlockSpec((GROUP * size, wide), lambda i, *_: (i, 0))
    begun, order, first, target = step_call(
        functools.partial(first_kernel, rcap),
        (spot,), (tables, received, in_hbm(strips)), [ANYWHERE, ANYWHERE, ANYWHERE],
        [
            pltpu.HBM((RB * size, wide), jnp.float32),
            jax.ShapeDtypeStruct((devices,), jnp.int32),
            jax.ShapeDtypeStruct((RB + 3,), jnp.int32),
            jax.ShapeDtypeStruct((KB * rcap,), jnp.int32),
        ],
        [strip, IN_SMEM, IN_SMEM, IN_SMEM],
        [
            pltpu.SMEM(tables.shape, jnp.int32),
            pltpu.SemaphoreType.DMA,
            pltpu.SMEM((devices,), jnp.int32),
            pltpu.SMEM((RB + 2,), jnp.int32),
            pltpu.SMEM((KB,), jnp.int32),
            pltpu.SMEM((KB,), jnp.int32),
        ],
        devices, size,
    )

    on_last = (col_index == last).astype(jnp.int32)
    on_round = (row_index == rows_count - 1).astype(jnp.int32)
    scalars = (order, first, target, jnp.stack([on_last, most, on_round]))
    lefts = (shifted, *parts)
    def finish_call(kernel, operands, out_shape, out_specs, marks, aliases, flops):
        return pl.pallas_call(
            kernel,
            out_shape=out_shape,
            grid_spec=pltpu.PrefetchScalarGridSpec(
                num_scalar_prefetch=len(scalars),
                grid=(1,),
                in_specs=[ANYWHERE] * len(operands),
                out_specs=out_specs,
                scratch_shapes=[
                    pltpu.VMEM((devices, size, size), jnp.bfloat16),
                    pltpu.VMEM((KB, size, wide), jnp.bfloat16),
                    pltpu.VMEM((RB, size, wide), jnp.float32),
                    pltpu.VMEM((RB, size, wide), jnp.bfloat16),
                    *[pltpu.SMEM((KB,), jnp.int32)] * marks,
                    pltpu.SMEM((RB,), jnp.int32),
                    pltpu.SemaphoreType.DMA,
                    pltpu.SemaphoreType.DMA,
                    pltpu.SemaphoreType.DMA((RB,)),
                    pltpu.SemaphoreType.DMA((RB,)),
                ],
            ),
            input_output_aliases=aliases,
            compiler_params=pltpu.CompilerParams(vmem_limit_bytes=LIMIT),
            cost_estimate=pl.CostEstimate(
                flops=flops, bytes_accessed=12 * 1024 * 1024, transcendentals=0
            ),
        )(*scalars, *operands)

    flops = 2 * 16 * NJ * size * size * size
    begun, rounded, level = finish_call(
        functools.partial(middle_kernel, len(parts)),
        (*lefts, direct, early_round, in_hbm(begun)),
        [
            pltpu.HBM((RB * size, wide), jnp.float32),
            pltpu.HBM((RB * size, wide), jnp.bfloat16),
            jax.ShapeDtypeStruct((1,), jnp.int32),
        ],
        [ANYWHERE, ANYWHERE, IN_SMEM], 2, {}, flops,
    )

    begin = ALWAYS
    extra = []
    for blocks in over:
        extra.append(lax.cond(level[0] > begin, to_row_before, lambda same: same, blocks))
        begin += blocks.shape[0]

    operands = (*lefts, direct, late_round, *extra, in_hbm(begun), rounded)
    return finish_call(
        functools.partial(last_kernel, len(parts), split),
        operands,
        jax.ShapeDtypeStruct((RB * size, wide), jnp.bfloat16),
        ANYWHERE, 1, {len(scalars) + len(operands) - 1: 0}, flops,
    )


def solution(mesh):
    placed = (
        P(None, ("row", "col"), None, None, None),
        P(None, ("row", "col"), None),
        P("row", "col", None, None, None, None),
        P("row", "col", None, None),
    )
    return jax.shard_map(
        local, mesh=mesh, in_specs=placed, out_specs=P("row", "col"), check_vma=False
    )
```

```python
import functools

import jax
import jax.numpy as jnp
from jax import lax
from jax.experimental import pallas as pl
from jax.experimental.pallas import tpu as pltpu
from jax.sharding import PartitionSpec as P

RB = 16
KB = 16
NJ = 8
PARTS = (64, 24, 8, 32)
ALWAYS = PARTS[0] + PARTS[1]
LENT = 16
GROUP = 4
IN_SMEM = pl.BlockSpec(memory_space=pltpu.SMEM)
ANYWHERE = pl.BlockSpec(memory_space=pl.ANY)
LIMIT = 24 * 1024 * 1024


def in_hbm(value):
    return pltpu.with_memory_space_constraint(value, pltpu.HBM)


def places_in(table, half, owner):
    at = half * table.shape[0] + owner
    return lambda source: table[source, 1 + at // 128, at % 128]


def columns_in(table, rcap, device):
    return lambda slot: table[device, 0, slot % rcap * KB + slot // rcap]


def mark_rows(place, slots, named):
    def reset(j, carry):
        named[j] = 0
        return carry

    def mark(s, carry):
        here = place(s)

        @pl.when(here >= 0)
        def _():
            named[here % KB] = 1

        return carry

    lax.fori_loop(0, KB, reset, 0)
    lax.fori_loop(0, slots, mark, 0)


def for_wanted(column, named, rcap, action):
    def visit(slot, number):
        wanted = (column(slot) >= 0) & (named[slot // rcap] > 0)

        @pl.when(wanted)
        def _():
            action(slot, number)

        return number + wanted.astype(jnp.int32)

    return lax.fori_loop(0, KB * rcap, visit, 0)


def pack_kernel(begin, end, lows, rcap, spot, tables, strips, *refs):
    guests = refs[: -6 - len(lows)]
    outs = refs[-6 - len(lows) : -6]
    stage, table, sem_table, named, sem, sem_out = refs[-6:]
    table_copy = pltpu.make_async_copy(tables, table, sem_table)
    table_copy.start()
    shift = spot[5] if guests else 0
    for guest in guests:

        def greet(number, carry):
            pltpu.make_async_copy(guest.at[number], stage.at[number], sem).start()
            return carry

        lax.fori_loop(0, shift, greet, 0)
    table_copy.wait()
    mark_rows(places_in(table, spot[0], spot[3]), table.shape[0], named)
    stop = end - shift

    def fetch(slot, number):
        @pl.when((number >= begin) & (number < stop))
        def _():
            at = number + shift - begin
            pltpu.make_async_copy(strips.at[slot], stage.at[at], sem).start()

    count = for_wanted(columns_in(table, rcap, spot[1]), named, rcap, fetch)

    def finish(number, carry):
        pltpu.make_async_copy(strips.at[0], stage.at[0], sem).wait()
        return carry

    lax.fori_loop(begin, jnp.minimum(count, stop) + shift, finish, 0)
    copies = []
    for i, (out, low) in enumerate(zip(outs, lows)):
        here = stage.at[pl.ds(low, out.shape[0])]
        copies.append(pltpu.make_async_copy(here, out, sem_out.at[i]))
        copies[-1].start()
    for copy in copies:
        copy.wait()


def pack(begin, end, ranges, spot, tables, strips, *guests):
    size = strips.shape[-1]
    counts = [high - low for low, high in ranges]
    lows = [low - begin for low, _ in ranges]
    return pl.pallas_call(
        functools.partial(pack_kernel, begin, end, lows, strips.shape[0] // KB),
        out_shape=[pltpu.HBM((n, size, size), strips.dtype) for n in counts],
        grid_spec=pltpu.PrefetchScalarGridSpec(
            num_scalar_prefetch=1,
            grid=(1,),
            in_specs=[ANYWHERE] * (2 + len(guests)),
            out_specs=[ANYWHERE] * len(counts),
            scratch_shapes=[
                pltpu.VMEM((end - begin, size, size), strips.dtype),
                pltpu.SMEM(tables.shape, jnp.int32),
                pltpu.SemaphoreType.DMA,
                pltpu.SMEM((KB,), jnp.int32),
                pltpu.SemaphoreType.DMA,
                pltpu.SemaphoreType.DMA((len(counts),)),
            ],
        ),
        compiler_params=pltpu.CompilerParams(vmem_limit_bytes=LIMIT),
        cost_estimate=pl.CostEstimate(
            flops=0, bytes_accessed=4 * sum(counts) * size * size, transcendentals=0
        ),
    )(spot, tables, in_hbm(strips), *guests)


def after(value, blocks):
    count = len(blocks)
    return pl.pallas_call(
        lambda *refs: None,
        out_shape=[pltpu.HBM(each.shape, each.dtype) for each in blocks],
        in_specs=[ANYWHERE] * (count + 1),
        out_specs=[ANYWHERE] * count,
        input_output_aliases={i: i for i in range(count)},
    )(*blocks, value)


def by_block_row(place, slots, order, first):
    def reset(i, carry):
        first[i] = 0
        return carry

    def count(s, carry):
        here = place(s)

        @pl.when(here >= 0)
        def _():
            i = here // KB + 2
            first[i] = first[i] + 1

        return carry

    def scan(i, carry):
        first[i] = first[i] + first[i - 1]
        return carry

    def sort(s, carry):
        here = place(s)

        @pl.when(here >= 0)
        def _():
            i = here // KB + 1
            order[first[i]] = s * KB + here % KB
            first[i] = first[i] + 1

        return carry

    lax.fori_loop(0, RB + 2, reset, 0)
    lax.fori_loop(0, slots, count, 0)
    lax.fori_loop(1, RB + 2, scan, 0)
    lax.fori_loop(0, slots, sort, 0)


def clear(right, low):
    def one(j, carry):
        right[j] = jnp.zeros(right.shape[1:], right.dtype)
        return carry

    lax.fori_loop(low, KB, one, 0)


def add_rows(left, right, total, order, first):
    size = left.shape[1]

    def one_row(i, carry):
        row = pl.program_id(0) * GROUP + i
        here = pl.ds(pl.multiple_of(i * size, size), size)

        def add(entry, carry):
            total[here, :] += jnp.dot(
                left[order[entry] // KB], right[order[entry] % KB],
                preferred_element_type=jnp.float32,
            )
            return carry

        return lax.fori_loop(first[row], first[row + 1], add, carry)

    lax.fori_loop(0, GROUP, one_row, 0)


def place_at(right, where):
    size = right.shape[1]
    start = pl.multiple_of((where % NJ) * size, size)
    return right.at[where // NJ, :, pl.ds(start, size)]


def finish_right(source, right, sem, count):
    def finish(number, carry):
        pltpu.make_async_copy(source, place_at(right, 0), sem).wait()
        return carry

    lax.fori_loop(0, count, finish, 0)


def first_kernel(
    rcap, spot, tables, received, strips,
    out, next_order, next_first, next_target,
    left, right, table, sem_table, order, first, named, other, sem_left, sem_right,
):
    slots, size, _ = left.shape

    @pl.when(pl.program_id(0) == 0)
    def _():
        left_copy = pltpu.make_async_copy(received.at[:, pl.ds(0, size)], left, sem_left)
        left_copy.start()
        table_copy = pltpu.make_async_copy(tables, table, sem_table)
        table_copy.start()
        clear(right, 0)
        table_copy.wait()
        place = places_in(table, 0, spot[1])
        column = columns_in(table, rcap, spot[1])
        mark_rows(place, slots, named)

        def fetch(slot, number):
            target = place_at(right, slot // rcap * NJ + column(slot))
            pltpu.make_async_copy(strips.at[slot], target, sem_right).start()

        count = for_wanted(column, named, rcap, fetch)
        by_block_row(place, slots, order, first)

        next_place = places_in(table, spot[0], spot[2])
        next_column = columns_in(table, rcap, spot[4])
        by_block_row(next_place, slots, next_order, next_first)
        mark_rows(next_place, slots, other)

        def note(slot, number):
            next_target[number] = slot // rcap * NJ + next_column(slot)

        next_first[RB + 2] = for_wanted(next_column, other, rcap, note)
        left_copy.wait()
        finish_right(strips.at[0], right, sem_right, count)

    out[...] = jnp.zeros(out.shape, out.dtype)
    add_rows(left, right, out, order, first)


def start_left(shifted, parts, left, on_last, sem):
    size = left.shape[1]
    step = shifted.shape[1] - size
    whole = pltpu.make_async_copy(shifted.at[:, pl.ds(0, size)], left, sem)

    @pl.when(on_last)
    def _():
        for q, part in enumerate([shifted.at[:, pl.ds(size, step)], *parts]):
            pltpu.make_async_copy(part, left.at[:, pl.ds(q * step, step)], sem).start()

    @pl.when(jnp.logical_not(on_last))
    def _():
        whole.start()

    return whole


def start_right(sources, begin, count, target, right, touched, sem):
    def reset(j, carry):
        touched[j] = 0
        return carry

    lax.fori_loop(0, KB, reset, 0)
    clear(right, jnp.where(count > begin, target[begin] // NJ, KB))
    for blocks, low, start, stop in sources:

        def fetch(number, carry):
            touched[target[number] // NJ] = 1
            pltpu.make_async_copy(
                blocks.at[number - low], place_at(right, target[number]), sem
            ).start()
            return carry

        lax.fori_loop(start, jnp.minimum(count, stop), fetch, 0)


def add_products(row, order, first, left, right, touched, total):
    def add(entry, carry):
        @pl.when(touched[order[entry] % KB] > 0)
        def _():
            total[row] += jnp.dot(
                left[order[entry] // KB], right[order[entry] % KB],
                preferred_element_type=jnp.float32,
            )

        return carry

    lax.fori_loop(first[row], first[row + 1], add, 0)


def mark_open(order, first, touched, open_row):
    def one(row, carry):
        def look(entry, found):
            return jnp.maximum(found, touched[order[entry] % KB])

        open_row[row] = lax.fori_loop(first[row], first[row + 1], look, jnp.int32(0))
        return carry

    lax.fori_loop(0, RB, one, 0)


def strip_of(ref, row, size):
    return ref.at[pl.ds(pl.multiple_of(row * size, size), size)]


def middle_kernel(parts_count, order, first, target, flags, *refs):
    shifted, *parts = refs[: 1 + parts_count]
    (
        piece, prev, out, rounded, level,
        left, right, total, short, touched, later, open_row,
        sem_left, sem_right, sem_prev, sem_out,
    ) = refs[1 + parts_count :]
    size = left.shape[1]
    count = first[RB + 2]
    shift = flags[2]
    end = piece.shape[0] - shift

    def prev_copy(row):
        return pltpu.make_async_copy(strip_of(prev, row, size), total.at[row], sem_prev.at[row])

    def start_prev(row, carry):
        prev_copy(row).start()
        return carry

    lax.fori_loop(0, RB, start_prev, 0)
    whole = start_left(shifted, parts, left, flags[0] > 0, sem_left)
    fetched = jnp.minimum(count, end)
    start_right([(piece, -shift, 0, end)], 0, fetched, target, right, touched, sem_right)
    level[0] = flags[1]

    def reset(j, carry):
        later[j] = 0
        return carry

    def mark(number, carry):
        later[target[number] // NJ] = 1
        return carry

    lax.fori_loop(0, KB, reset, 0)
    lax.fori_loop(end, count, mark, 0)
    mark_open(order, first, later, open_row)
    whole.wait()
    finish_right(piece.at[0], right, sem_right, fetched)

    def out_copies(row):
        return (
            pltpu.make_async_copy(total.at[row], strip_of(out, row, size), sem_out.at[row]),
            pltpu.make_async_copy(short.at[row], strip_of(rounded, row, size), sem_out.at[row]),
        )

    def one_row(row, carry):
        open_copy, closed_copy = out_copies(row)
        prev_copy(row).wait()
        add_products(row, order, first, left, right, touched, total)

        @pl.when(open_row[row] > 0)
        def _():
            open_copy.start()

        @pl.when(open_row[row] == 0)
        def _():
            short[row] = total[row].astype(short.dtype)
            closed_copy.start()

        return carry

    def close_row(row, carry):
        open_copy, closed_copy = out_copies(row)

        @pl.when(open_row[row] > 0)
        def _():
            open_copy.wait()

        @pl.when(open_row[row] == 0)
        def _():
            closed_copy.wait()

        return carry

    lax.fori_loop(0, RB, one_row, 0)
    lax.fori_loop(0, RB, close_row, 0)


def last_kernel(parts_count, order, first, target, flags, *refs):
    shifted, *parts = refs[: 1 + parts_count]
    (
        piece, back, *over, prev, _, out,
        left, right, total, short, touched, open_row,
        sem_left, sem_right, sem_prev, sem_out,
    ) = refs[1 + parts_count :]
    size = left.shape[1]
    count = first[RB + 2]
    shift, lent = flags[2], flags[3]
    begin = PARTS[0] - shift
    whole = start_left(shifted, parts, left, flags[0] > 0, sem_left)
    low = ALWAYS
    sources = [(piece, begin, begin, low - shift), (back, low, low, low + lent)]
    for blocks in over:
        high = low + blocks.shape[0]
        sources.append((blocks, low, low, jnp.where(lent > 0, low, high)))
        low = high
    start_right(sources, begin, count, target, right, touched, sem_right)
    mark_open(order, first, touched, open_row)

    def prev_copy(row):
        return pltpu.make_async_copy(strip_of(prev, row, size), total.at[row], sem_prev.at[row])

    def out_copy(row):
        return pltpu.make_async_copy(short.at[row], strip_of(out, row, size), sem_out.at[row])

    def start_prev(row, carry):
        @pl.when(open_row[row] > 0)
        def _():
            prev_copy(row).start()

        return carry

    lax.fori_loop(0, RB, start_prev, 0)
    whole.wait()
    finish_right(piece.at[0], right, sem_right, count - begin)

    def one_row(row, carry):
        @pl.when(open_row[row] > 0)
        def _():
            prev_copy(row).wait()
            add_products(row, order, first, left, right, touched, total)
            short[row] = total[row].astype(short.dtype)
            out_copy(row).start()

        return carry

    def close_row(row, carry):
        @pl.when(open_row[row] > 0)
        def _():
            out_copy(row).wait()

        return carry

    lax.fori_loop(0, RB, one_row, 0)
    lax.fori_loop(0, RB, close_row, 0)


def step_call(kernel, scalars, operands, specs, out_shape, out_specs, scratch, slots, size):
    return pl.pallas_call(
        kernel,
        out_shape=out_shape,
        grid_spec=pltpu.PrefetchScalarGridSpec(
            num_scalar_prefetch=len(scalars),
            grid=(RB // GROUP,),
            in_specs=specs,
            out_specs=out_specs,
            scratch_shapes=[
                pltpu.VMEM((slots, size, size), jnp.bfloat16),
                pltpu.VMEM((KB, size, NJ * size), jnp.bfloat16),
                *scratch,
                pltpu.SemaphoreType.DMA,
                pltpu.SemaphoreType.DMA,
            ],
        ),
        compiler_params=pltpu.CompilerParams(
            dimension_semantics=("arbitrary",), vmem_limit_bytes=LIMIT
        ),
        cost_estimate=pl.CostEstimate(
            flops=2 * 24 * NJ * size * size * size,
            bytes_accessed=16 * 1024 * 1024,
            transcendentals=0,
        ),
    )(*scalars, *operands)


def table_kernel(where, cols, out, tile):
    rcap, across = cols.shape
    devices = where.shape[-1]
    tile[...] = jnp.zeros(tile.shape, tile.dtype)
    for slot in range(rcap):
        tile[pl.ds(0, 1), pl.ds(slot * across, across)] = cols[pl.ds(slot, 1), :]
    for half in range(2):
        row, lane = divmod(half * devices, 128)
        tile[pl.ds(1 + row, 1), pl.ds(lane, devices)] = where[half]

    def fill(device, carry):
        out[device] = tile[...]
        return carry

    lax.fori_loop(0, out.shape[0], fill, 0)


def table_for_all(where, cols):
    devices = where.shape[-1]
    shape = (1 + -(-2 * devices // 128), 128)
    return pl.pallas_call(
        table_kernel,
        out_shape=jax.ShapeDtypeStruct((devices, *shape), jnp.int32),
        scratch_shapes=[pltpu.VMEM(shape, jnp.int32)],
        compiler_params=pltpu.CompilerParams(vmem_limit_bytes=LIMIT),
    )(where, cols)


def needed(where_all, cols_all, rows_count, cols_count):
    grid = where_all.reshape(-1, 2, rows_count, cols_count)
    after = jnp.concatenate([grid[:, 0, :, 1:], grid[:, 1, :, :1]], axis=-1)
    columns = jnp.arange(KB, dtype=jnp.int32)
    hit = (after[..., None] >= 0) & (after[..., None] % KB == columns)
    wanted = jnp.any(hit, axis=0).astype(jnp.int32)
    counts = jnp.sum((cols_all >= 0).astype(jnp.int32), axis=1)
    counts = jnp.roll(counts.reshape(rows_count, cols_count, KB), -1, axis=0)
    return jnp.sum(wanted * counts, axis=-1)


def swapped(value):
    return lax.ppermute(value, "col", [(i, i ^ 1) for i in range(lax.axis_size("col"))])


def local(a_send, a_where, b_strips, b_cols):
    size = a_send.shape[-1]
    rows_count = lax.axis_size("row")
    cols_count = lax.axis_size("col")
    devices = rows_count * cols_count
    both = ("row", "col")
    row_index = lax.axis_index("row")
    col_index = lax.axis_index("col")
    rcap = b_strips.shape[3]
    last = cols_count - 1

    by_slot = jnp.swapaxes(b_cols, 2, 3).reshape(rcap, KB)
    tables = lax.all_to_all(
        table_for_all(a_where, by_slot), both, split_axis=0, concat_axis=0, tiled=True
    )
    after_col = (col_index + 1) % cols_count
    after_half = (col_index + 1) // cols_count
    row_before = (row_index + rows_count - 1) % rows_count
    row_after = (row_index + 1) % rows_count
    needs = needed(
        tables[:, 1:].reshape(devices, -1)[:, : 2 * devices],
        tables[:, 0].reshape(devices, rcap, KB), rows_count, cols_count,
    )
    room = ALWAYS - jnp.flip(needs.reshape(rows_count, -1, 2), -1).reshape(needs.shape)
    fits = (needs > ALWAYS) & (needs - ALWAYS <= jnp.minimum(room, LENT))
    lent = jnp.where(fits, needs - ALWAYS, 0)
    most = jnp.max(jnp.where(fits, ALWAYS, needs))

    def lent_to(row, col):
        return lax.dynamic_slice(lent, (row, col), (1, 1))[0, 0]

    spot = jnp.stack([
        after_half,
        row_index * cols_count + col_index,
        row_index * cols_count + after_col,
        row_before * cols_count + after_col,
        row_after * cols_count + col_index,
        lent_to(row_before, col_index ^ 1),
    ]).astype(jnp.int32)

    wrapped = a_send[1, 0].reshape(rows_count, cols_count, size, size)[:, 0]
    wrapped = wrapped.reshape(devices, size // cols_count, size)
    received = lax.all_to_all(
        jnp.concatenate([a_send[0, 0], wrapped], axis=1),
        both, split_axis=0, concat_axis=0, tiled=True,
    )

    def to_row_before(blocks):
        return lax.ppermute(
            blocks, "row", [(i, (i - 1) % rows_count) for i in range(rows_count)]
        )

    strips = b_strips.reshape(KB * rcap, size, size)
    split, full = PARTS[0], KB * rcap
    over_at = ALWAYS + PARTS[2]
    guests, *over = pack(
        ALWAYS, full, [(ALWAYS, ALWAYS + LENT), (ALWAYS, over_at), (over_at, full)],
        spot, tables, strips,
    )
    early, late = pack(
        0, ALWAYS, [(0, split), (split, ALWAYS)], spot, tables, strips, swapped(guests)
    )
    early, late = map(to_row_before, after(received[0, :16], [early, late]))
    back = swapped(early[:LENT])

    shifted = lax.ppermute(
        received, "col", [(i, (i - 1) % cols_count) for i in range(cols_count)]
    )
    part = received[:, size:]
    parts = [lax.ppermute(part, "col", [(i, last)]) for i in range(1, last)] + [part]

    wide = NJ * size
    strip = pl.BlockSpec((GROUP * size, wide), lambda i, *_: (i, 0))
    begun, order, first, target = step_call(
        functools.partial(first_kernel, rcap),
        (spot,), (tables, received, in_hbm(strips)), [ANYWHERE, ANYWHERE, ANYWHERE],
        [
            pltpu.HBM((RB * size, wide), jnp.float32),
            jax.ShapeDtypeStruct((devices,), jnp.int32),
            jax.ShapeDtypeStruct((RB + 3,), jnp.int32),
            jax.ShapeDtypeStruct((KB * rcap,), jnp.int32),
        ],
        [strip, IN_SMEM, IN_SMEM, IN_SMEM],
        [
            pltpu.SMEM(tables.shape, jnp.int32),
            pltpu.SemaphoreType.DMA,
            pltpu.SMEM((devices,), jnp.int32),
            pltpu.SMEM((RB + 2,), jnp.int32),
            pltpu.SMEM((KB,), jnp.int32),
            pltpu.SMEM((KB,), jnp.int32),
        ],
        devices, size,
    )

    on_last = (col_index == last).astype(jnp.int32)
    lent_here = [lent_to(row_index, col_index ^ 1), lent_to(row_index, col_index)]
    scalars = (order, first, target, jnp.stack([on_last, most, *lent_here]))
    lefts = (shifted, *parts)

    def finish_call(kernel, operands, out_shape, out_specs, marks, aliases, flops):
        return pl.pallas_call(
            kernel,
            out_shape=out_shape,
            grid_spec=pltpu.PrefetchScalarGridSpec(
                num_scalar_prefetch=len(scalars),
                grid=(1,),
                in_specs=[ANYWHERE] * len(operands),
                out_specs=out_specs,
                scratch_shapes=[
                    pltpu.VMEM((devices, size, size), jnp.bfloat16),
                    pltpu.VMEM((KB, size, wide), jnp.bfloat16),
                    pltpu.VMEM((RB, size, wide), jnp.float32),
                    pltpu.VMEM((RB, size, wide), jnp.bfloat16),
                    *[pltpu.SMEM((KB,), jnp.int32)] * marks,
                    pltpu.SMEM((RB,), jnp.int32),
                    pltpu.SemaphoreType.DMA,
                    pltpu.SemaphoreType.DMA,
                    pltpu.SemaphoreType.DMA((RB,)),
                    pltpu.SemaphoreType.DMA((RB,)),
                ],
            ),
            input_output_aliases=aliases,
            compiler_params=pltpu.CompilerParams(vmem_limit_bytes=LIMIT),
            cost_estimate=pl.CostEstimate(
                flops=flops, bytes_accessed=12 * 1024 * 1024, transcendentals=0
            ),
        )(*scalars, *operands)

    flops = 2 * 16 * NJ * size * size * size
    begun, rounded, level = finish_call(
        functools.partial(middle_kernel, len(parts)),
        (*lefts, early, in_hbm(begun)),
        [
            pltpu.HBM((RB * size, wide), jnp.float32),
            pltpu.HBM((RB * size, wide), jnp.bfloat16),
            jax.ShapeDtypeStruct((1,), jnp.int32),
        ],
        [ANYWHERE, ANYWHERE, IN_SMEM], 2, {}, flops,
    )

    begin = ALWAYS
    extra = []
    for blocks in over:
        extra.append(lax.cond(level[0] > begin, to_row_before, lambda same: same, blocks))
        begin += blocks.shape[0]

    operands = (*lefts, late, back, *extra, in_hbm(begun), rounded)
    return finish_call(
        functools.partial(last_kernel, len(parts)),
        operands,
        jax.ShapeDtypeStruct((RB * size, wide), jnp.bfloat16),
        ANYWHERE, 1, {len(scalars) + len(operands) - 1: 0}, flops,
    )


def solution(mesh):
    placed = (
        P(None, ("row", "col"), None, None, None),
        P(None, ("row", "col"), None),
        P("row", "col", None, None, None, None),
        P("row", "col", None, None),
    )
    return jax.shard_map(
        local, mesh=mesh, in_specs=placed, out_specs=P("row", "col"), check_vma=False
    )
```

```python
import functools

import jax
import jax.numpy as jnp
from jax import lax
from jax.experimental import pallas as pl
from jax.experimental.pallas import tpu as pltpu
from jax.sharding import PartitionSpec as P

RB = 16
KB = 16
NJ = 8
PARTS = (64, 24, 8, 8, 24)
ALWAYS = PARTS[0] + PARTS[1]
LENT = 16
GROUP = 4
IN_SMEM = pl.BlockSpec(memory_space=pltpu.SMEM)
ANYWHERE = pl.BlockSpec(memory_space=pl.ANY)
LIMIT = 24 * 1024 * 1024


def in_hbm(value):
    return pltpu.with_memory_space_constraint(value, pltpu.HBM)


def places_in(table, half, owner):
    at = half * table.shape[0] + owner
    return lambda source: table[source, 1 + at // 128, at % 128]


def columns_in(table, rcap, device):
    return lambda slot: table[device, 0, slot % rcap * KB + slot // rcap]


def mark_rows(place, slots, named):
    def reset(j, carry):
        named[j] = 0
        return carry

    def mark(s, carry):
        here = place(s)

        @pl.when(here >= 0)
        def _():
            named[here % KB] = 1

        return carry

    lax.fori_loop(0, KB, reset, 0)
    lax.fori_loop(0, slots, mark, 0)


def for_wanted(column, named, rcap, action):
    def visit(slot, number):
        wanted = (column(slot) >= 0) & (named[slot // rcap] > 0)

        @pl.when(wanted)
        def _():
            action(slot, number)

        return number + wanted.astype(jnp.int32)

    return lax.fori_loop(0, KB * rcap, visit, 0)


def pack_main(spot, tables, strips, guests, early, late, *scratch):
    stage, table, sem_table, named, sem, sem_out = scratch
    shift = spot[5]
    stop = stage.shape[0] - shift

    def greet(number, carry):
        pltpu.make_async_copy(guests.at[number], stage.at[number], sem).start()
        return carry

    lax.fori_loop(0, shift, greet, 0)

    def fetch(slot, number):
        @pl.when(number < stop)
        def _():
            pltpu.make_async_copy(strips.at[slot], stage.at[number + shift], sem).start()

    count = find_wanted(spot, tables, strips, table, sem_table, named, fetch)
    finish_blocks(strips, stage, sem, jnp.minimum(count, stop) + shift)
    hand_over(stage, [early, late], sem_out)


def pack_spare(spot, tables, strips, guests, *refs):
    *over, stage, table, sem_table, named, sem, sem_out = refs
    lent = spot[6]

    def fetch(slot, number):
        beyond = number - ALWAYS

        @pl.when((beyond >= 0) & (beyond < LENT))
        def _():
            pltpu.make_async_copy(strips.at[slot], stage.at[beyond], sem).start()

        @pl.when(beyond >= lent)
        def _():
            at = LENT + beyond - lent
            pltpu.make_async_copy(strips.at[slot], stage.at[at], sem).start()

    count = find_wanted(spot, tables, strips, table, sem_table, named, fetch)
    beyond = jnp.maximum(count - ALWAYS, 0)
    copied = jnp.minimum(beyond, LENT) + jnp.maximum(beyond - lent, 0)
    finish_blocks(strips, stage, sem, copied)
    hand_over(stage, [guests, *over], sem_out)


def find_wanted(spot, tables, strips, table, sem_table, named, action):
    rcap = strips.shape[0] // KB
    table_copy = pltpu.make_async_copy(tables, table, sem_table)
    table_copy.start()
    table_copy.wait()
    mark_rows(places_in(table, spot[0], spot[3]), table.shape[0], named)
    return for_wanted(columns_in(table, rcap, spot[1]), named, rcap, action)


def finish_blocks(source, target, sem, count):
    def finish(number, carry):
        pltpu.make_async_copy(source.at[0], target.at[0], sem).wait()
        return carry

    lax.fori_loop(0, count, finish, 0)


def hand_over(stage, outs, sem_out):
    copies, low = [], 0
    for i, out in enumerate(outs):
        here = stage.at[pl.ds(low, out.shape[0])]
        copies.append(pltpu.make_async_copy(here, out, sem_out.at[i]))
        copies[-1].start()
        low += out.shape[0]
    for copy in copies:
        copy.wait()


def pack(kernel, counts, spot, tables, strips, *more):
    size = strips.shape[-1]
    return pl.pallas_call(
        kernel,
        out_shape=[pltpu.HBM((n, size, size), strips.dtype) for n in counts],
        grid_spec=pltpu.PrefetchScalarGridSpec(
            num_scalar_prefetch=1,
            grid=(1,),
            in_specs=[ANYWHERE] * (2 + len(more)),
            out_specs=[ANYWHERE] * len(counts),
            scratch_shapes=[
                pltpu.VMEM((sum(counts), size, size), strips.dtype),
                pltpu.SMEM(tables.shape, jnp.int32),
                pltpu.SemaphoreType.DMA,
                pltpu.SMEM((KB,), jnp.int32),
                pltpu.SemaphoreType.DMA,
                pltpu.SemaphoreType.DMA((len(counts),)),
            ],
        ),
        compiler_params=pltpu.CompilerParams(vmem_limit_bytes=LIMIT),
        cost_estimate=pl.CostEstimate(
            flops=0, bytes_accessed=4 * sum(counts) * size * size, transcendentals=0
        ),
    )(spot, tables, in_hbm(strips), *more)


def after(value, blocks):
    count = len(blocks)
    return pl.pallas_call(
        lambda *refs: None,
        out_shape=[pltpu.HBM(each.shape, each.dtype) for each in blocks],
        in_specs=[ANYWHERE] * (count + 1),
        out_specs=[ANYWHERE] * count,
        input_output_aliases={i: i for i in range(count)},
    )(*blocks, value)


def by_block_row(place, slots, order, first):
    def reset(i, carry):
        first[i] = 0
        return carry

    def count(s, carry):
        here = place(s)

        @pl.when(here >= 0)
        def _():
            i = here // KB + 2
            first[i] = first[i] + 1

        return carry

    def scan(i, carry):
        first[i] = first[i] + first[i - 1]
        return carry

    def sort(s, carry):
        here = place(s)

        @pl.when(here >= 0)
        def _():
            i = here // KB + 1
            order[first[i]] = s * KB + here % KB
            first[i] = first[i] + 1

        return carry

    lax.fori_loop(0, RB + 2, reset, 0)
    lax.fori_loop(0, slots, count, 0)
    lax.fori_loop(1, RB + 2, scan, 0)
    lax.fori_loop(0, slots, sort, 0)


def clear(right, low):
    def one(j, carry):
        right[j] = jnp.zeros(right.shape[1:], right.dtype)
        return carry

    lax.fori_loop(low, KB, one, 0)


def add_rows(left, right, total, order, first):
    size = left.shape[1]

    def one_row(i, carry):
        row = pl.program_id(0) * GROUP + i
        here = pl.ds(pl.multiple_of(i * size, size), size)

        def add(entry, carry):
            total[here, :] += jnp.dot(
                left[order[entry] // KB], right[order[entry] % KB],
                preferred_element_type=jnp.float32,
            )
            return carry

        return lax.fori_loop(first[row], first[row + 1], add, carry)

    lax.fori_loop(0, GROUP, one_row, 0)


def place_at(right, where):
    size = right.shape[1]
    start = pl.multiple_of((where % NJ) * size, size)
    return right.at[where // NJ, :, pl.ds(start, size)]


def finish_right(source, right, sem, count):
    def finish(number, carry):
        pltpu.make_async_copy(source, place_at(right, 0), sem).wait()
        return carry

    lax.fori_loop(0, count, finish, 0)


def first_kernel(
    rcap, spot, tables, received, strips,
    out, next_order, next_first, next_target,
    left, right, table, sem_table, order, first, named, other, sem_left, sem_right,
):
    slots, size, _ = left.shape

    @pl.when(pl.program_id(0) == 0)
    def _():
        left_copy = pltpu.make_async_copy(received.at[:, pl.ds(0, size)], left, sem_left)
        left_copy.start()
        table_copy = pltpu.make_async_copy(tables, table, sem_table)
        table_copy.start()
        clear(right, 0)
        table_copy.wait()
        place = places_in(table, 0, spot[1])
        column = columns_in(table, rcap, spot[1])
        mark_rows(place, slots, named)

        def fetch(slot, number):
            target = place_at(right, slot // rcap * NJ + column(slot))
            pltpu.make_async_copy(strips.at[slot], target, sem_right).start()

        count = for_wanted(column, named, rcap, fetch)
        by_block_row(place, slots, order, first)

        next_place = places_in(table, spot[0], spot[2])
        next_column = columns_in(table, rcap, spot[4])
        by_block_row(next_place, slots, next_order, next_first)
        mark_rows(next_place, slots, other)

        def note(slot, number):
            next_target[number] = slot // rcap * NJ + next_column(slot)

        next_first[RB + 2] = for_wanted(next_column, other, rcap, note)
        left_copy.wait()
        finish_right(strips.at[0], right, sem_right, count)

    out[...] = jnp.zeros(out.shape, out.dtype)
    add_rows(left, right, out, order, first)


def start_left(shifted, parts, left, on_last, sem):
    size = left.shape[1]
    step = shifted.shape[1] - size
    whole = pltpu.make_async_copy(shifted.at[:, pl.ds(0, size)], left, sem)

    @pl.when(on_last)
    def _():
        for q, part in enumerate([shifted.at[:, pl.ds(size, step)], *parts]):
            pltpu.make_async_copy(part, left.at[:, pl.ds(q * step, step)], sem).start()

    @pl.when(jnp.logical_not(on_last))
    def _():
        whole.start()

    return whole


def start_right(sources, begin, count, target, right, touched, sem):
    def reset(j, carry):
        touched[j] = 0
        return carry

    lax.fori_loop(0, KB, reset, 0)
    clear(right, jnp.where(count > begin, target[begin] // NJ, KB))
    for blocks, low, start, stop in sources:

        def fetch(number, carry):
            touched[target[number] // NJ] = 1
            pltpu.make_async_copy(
                blocks.at[number - low], place_at(right, target[number]), sem
            ).start()
            return carry

        lax.fori_loop(start, jnp.minimum(count, stop), fetch, 0)


def add_products(row, order, first, left, right, touched, total):
    def add(entry, carry):
        @pl.when(touched[order[entry] % KB] > 0)
        def _():
            total[row] += jnp.dot(
                left[order[entry] // KB], right[order[entry] % KB],
                preferred_element_type=jnp.float32,
            )

        return carry

    lax.fori_loop(first[row], first[row + 1], add, 0)


def mark_open(order, first, touched, open_row):
    def one(row, carry):
        def look(entry, found):
            return jnp.maximum(found, touched[order[entry] % KB])

        open_row[row] = lax.fori_loop(first[row], first[row + 1], look, jnp.int32(0))
        return carry

    lax.fori_loop(0, RB, one, 0)


def strip_of(ref, row, size):
    return ref.at[pl.ds(pl.multiple_of(row * size, size), size)]


def middle_kernel(parts_count, order, first, target, flags, *refs):
    shifted, *parts = refs[: 1 + parts_count]
    (
        piece, prev, out, rounded, guests, level,
        hall, sem_in, sem_home,
        left, right, total, short, touched, later, open_row,
        sem_left, sem_right, sem_prev, sem_out,
    ) = refs[1 + parts_count :]
    arrive = pltpu.make_async_copy(piece.at[pl.ds(0, LENT)], hall, sem_in)
    leave = pltpu.make_async_copy(hall, guests, sem_home)
    arrive.start()
    size = left.shape[1]
    count = first[RB + 2]
    shift = flags[2]
    end = piece.shape[0] - shift

    def prev_copy(row):
        return pltpu.make_async_copy(strip_of(prev, row, size), total.at[row], sem_prev.at[row])

    def start_prev(row, carry):
        prev_copy(row).start()
        return carry

    lax.fori_loop(0, RB, start_prev, 0)
    whole = start_left(shifted, parts, left, flags[0] > 0, sem_left)
    fetched = jnp.minimum(count, end)
    start_right([(piece, -shift, 0, end)], 0, fetched, target, right, touched, sem_right)
    level[0] = flags[1]
    arrive.wait()
    leave.start()

    def reset(j, carry):
        later[j] = 0
        return carry

    def mark(number, carry):
        later[target[number] // NJ] = 1
        return carry

    lax.fori_loop(0, KB, reset, 0)
    lax.fori_loop(end, count, mark, 0)
    mark_open(order, first, later, open_row)
    whole.wait()
    finish_right(piece.at[0], right, sem_right, fetched)

    def out_copies(row):
        return (
            pltpu.make_async_copy(total.at[row], strip_of(out, row, size), sem_out.at[row]),
            pltpu.make_async_copy(short.at[row], strip_of(rounded, row, size), sem_out.at[row]),
        )

    def one_row(row, carry):
        open_copy, closed_copy = out_copies(row)
        prev_copy(row).wait()
        add_products(row, order, first, left, right, touched, total)

        @pl.when(open_row[row] > 0)
        def _():
            open_copy.start()

        @pl.when(open_row[row] == 0)
        def _():
            short[row] = total[row].astype(short.dtype)
            closed_copy.start()

        return carry

    def close_row(row, carry):
        open_copy, closed_copy = out_copies(row)

        @pl.when(open_row[row] > 0)
        def _():
            open_copy.wait()

        @pl.when(open_row[row] == 0)
        def _():
            closed_copy.wait()

        return carry

    lax.fori_loop(0, RB, one_row, 0)
    lax.fori_loop(0, RB, close_row, 0)
    leave.wait()


def last_kernel(parts_count, order, first, target, flags, *refs):
    shifted, *parts = refs[: 1 + parts_count]
    (
        piece, back, *over, prev, _, out,
        left, right, total, short, touched, open_row,
        sem_left, sem_right, sem_prev, sem_out,
    ) = refs[1 + parts_count :]
    size = left.shape[1]
    count = first[RB + 2]
    shift, lent = flags[2], flags[3]
    begin = PARTS[0] - shift
    whole = start_left(shifted, parts, left, flags[0] > 0, sem_left)
    low = ALWAYS
    sources = [(piece, begin, begin, low - shift), (back, low, low, low + lent)]
    low = low + lent
    for blocks in over:
        high = low + blocks.shape[0]
        sources.append((blocks, low, low, high))
        low = high
    start_right(sources, begin, count, target, right, touched, sem_right)
    mark_open(order, first, touched, open_row)

    def prev_copy(row):
        return pltpu.make_async_copy(strip_of(prev, row, size), total.at[row], sem_prev.at[row])

    def out_copy(row):
        return pltpu.make_async_copy(short.at[row], strip_of(out, row, size), sem_out.at[row])

    def start_prev(row, carry):
        @pl.when(open_row[row] > 0)
        def _():
            prev_copy(row).start()

        return carry

    lax.fori_loop(0, RB, start_prev, 0)
    whole.wait()
    finish_right(piece.at[0], right, sem_right, count - begin)

    def one_row(row, carry):
        @pl.when(open_row[row] > 0)
        def _():
            prev_copy(row).wait()
            add_products(row, order, first, left, right, touched, total)
            short[row] = total[row].astype(short.dtype)
            out_copy(row).start()

        return carry

    def close_row(row, carry):
        @pl.when(open_row[row] > 0)
        def _():
            out_copy(row).wait()

        return carry

    lax.fori_loop(0, RB, one_row, 0)
    lax.fori_loop(0, RB, close_row, 0)


def step_call(kernel, scalars, operands, specs, out_shape, out_specs, scratch, slots, size):
    return pl.pallas_call(
        kernel,
        out_shape=out_shape,
        grid_spec=pltpu.PrefetchScalarGridSpec(
            num_scalar_prefetch=len(scalars),
            grid=(RB // GROUP,),
            in_specs=specs,
            out_specs=out_specs,
            scratch_shapes=[
                pltpu.VMEM((slots, size, size), jnp.bfloat16),
                pltpu.VMEM((KB, size, NJ * size), jnp.bfloat16),
                *scratch,
                pltpu.SemaphoreType.DMA,
                pltpu.SemaphoreType.DMA,
            ],
        ),
        compiler_params=pltpu.CompilerParams(
            dimension_semantics=("arbitrary",), vmem_limit_bytes=LIMIT
        ),
        cost_estimate=pl.CostEstimate(
            flops=2 * 24 * NJ * size * size * size,
            bytes_accessed=16 * 1024 * 1024,
            transcendentals=0,
        ),
    )(*scalars, *operands)


def table_kernel(where, cols, out, tile):
    rcap, across = cols.shape
    devices = where.shape[-1]
    tile[...] = jnp.zeros(tile.shape, tile.dtype)
    for slot in range(rcap):
        tile[pl.ds(0, 1), pl.ds(slot * across, across)] = cols[pl.ds(slot, 1), :]
    for half in range(2):
        row, lane = divmod(half * devices, 128)
        tile[pl.ds(1 + row, 1), pl.ds(lane, devices)] = where[half]

    def fill(device, carry):
        out[device] = tile[...]
        return carry

    lax.fori_loop(0, out.shape[0], fill, 0)


def table_for_all(where, cols):
    devices = where.shape[-1]
    shape = (1 + -(-2 * devices // 128), 128)
    return pl.pallas_call(
        table_kernel,
        out_shape=jax.ShapeDtypeStruct((devices, *shape), jnp.int32),
        scratch_shapes=[pltpu.VMEM(shape, jnp.int32)],
        compiler_params=pltpu.CompilerParams(vmem_limit_bytes=LIMIT),
    )(where, cols)


def needed(where_all, cols_all, rows_count, cols_count):
    grid = where_all.reshape(-1, 2, rows_count, cols_count)
    after = jnp.concatenate([grid[:, 0, :, 1:], grid[:, 1, :, :1]], axis=-1)
    columns = jnp.arange(KB, dtype=jnp.int32)
    hit = (after[..., None] >= 0) & (after[..., None] % KB == columns)
    wanted = jnp.any(hit, axis=0).astype(jnp.int32)
    counts = jnp.sum((cols_all >= 0).astype(jnp.int32), axis=1)
    counts = jnp.roll(counts.reshape(rows_count, cols_count, KB), -1, axis=0)
    return jnp.sum(wanted * counts, axis=-1)


def swapped(value):
    return lax.ppermute(value, "col", [(i, i ^ 1) for i in range(lax.axis_size("col"))])


def local(a_send, a_where, b_strips, b_cols):
    size = a_send.shape[-1]
    rows_count = lax.axis_size("row")
    cols_count = lax.axis_size("col")
    devices = rows_count * cols_count
    both = ("row", "col")
    row_index = lax.axis_index("row")
    col_index = lax.axis_index("col")
    rcap = b_strips.shape[3]
    last = cols_count - 1

    by_slot = jnp.swapaxes(b_cols, 2, 3).reshape(rcap, KB)
    tables = lax.all_to_all(
        table_for_all(a_where, by_slot), both, split_axis=0, concat_axis=0, tiled=True
    )
    after_col = (col_index + 1) % cols_count
    after_half = (col_index + 1) // cols_count
    row_before = (row_index + rows_count - 1) % rows_count
    row_after = (row_index + 1) % rows_count
    needs = needed(
        tables[:, 1:].reshape(devices, -1)[:, : 2 * devices],
        tables[:, 0].reshape(devices, rcap, KB), rows_count, cols_count,
    )
    room = ALWAYS - jnp.flip(needs.reshape(rows_count, -1, 2), -1).reshape(needs.shape)
    lent = jnp.maximum(jnp.minimum(jnp.minimum(needs - ALWAYS, room), LENT), 0)
    most = jnp.max(needs - lent)

    def lent_to(row, col):
        return lax.dynamic_slice(lent, (row, col), (1, 1))[0, 0]

    spot = jnp.stack([
        after_half,
        row_index * cols_count + col_index,
        row_index * cols_count + after_col,
        row_before * cols_count + after_col,
        row_after * cols_count + col_index,
        lent_to(row_before, col_index ^ 1),
        lent_to(row_before, col_index),
    ]).astype(jnp.int32)

    wrapped = a_send[1, 0].reshape(rows_count, cols_count, size, size)[:, 0]
    wrapped = wrapped.reshape(devices, size // cols_count, size)
    received = lax.all_to_all(
        jnp.concatenate([a_send[0, 0], wrapped], axis=1),
        both, split_axis=0, concat_axis=0, tiled=True,
    )

    def to_row_before(blocks):
        return lax.ppermute(
            blocks, "row", [(i, (i - 1) % rows_count) for i in range(rows_count)]
        )

    strips = b_strips.reshape(KB * rcap, size, size)
    guests, *over = pack(pack_spare, (LENT, *PARTS[2:]), spot, tables, strips)
    early, late = pack(pack_main, PARTS[:2], spot, tables, strips, swapped(guests))
    early, late = map(to_row_before, after(received[0, :16], [early, late]))

    shifted = lax.ppermute(
        received, "col", [(i, (i - 1) % cols_count) for i in range(cols_count)]
    )
    part = received[:, size:]
    parts = [lax.ppermute(part, "col", [(i, last)]) for i in range(1, last)] + [part]

    wide = NJ * size
    strip = pl.BlockSpec((GROUP * size, wide), lambda i, *_: (i, 0))
    begun, order, first, target = step_call(
        functools.partial(first_kernel, rcap),
        (spot,), (tables, received, in_hbm(strips)), [ANYWHERE, ANYWHERE, ANYWHERE],
        [
            pltpu.HBM((RB * size, wide), jnp.float32),
            jax.ShapeDtypeStruct((devices,), jnp.int32),
            jax.ShapeDtypeStruct((RB + 3,), jnp.int32),
            jax.ShapeDtypeStruct((KB * rcap,), jnp.int32),
        ],
        [strip, IN_SMEM, IN_SMEM, IN_SMEM],
        [
            pltpu.SMEM(tables.shape, jnp.int32),
            pltpu.SemaphoreType.DMA,
            pltpu.SMEM((devices,), jnp.int32),
            pltpu.SMEM((RB + 2,), jnp.int32),
            pltpu.SMEM((KB,), jnp.int32),
            pltpu.SMEM((KB,), jnp.int32),
        ],
        devices, size,
    )

    on_last = (col_index == last).astype(jnp.int32)
    lent_here = [lent_to(row_index, col_index ^ 1), lent_to(row_index, col_index)]
    scalars = (order, first, target, jnp.stack([on_last, most, *lent_here]))
    lefts = (shifted, *parts)

    def finish_call(kernel, operands, out_shape, out_specs, scratch, marks, aliases, flops):
        return pl.pallas_call(
            kernel,
            out_shape=out_shape,
            grid_spec=pltpu.PrefetchScalarGridSpec(
                num_scalar_prefetch=len(scalars),
                grid=(1,),
                in_specs=[ANYWHERE] * len(operands),
                out_specs=out_specs,
                scratch_shapes=[
                    *scratch,
                    pltpu.VMEM((devices, size, size), jnp.bfloat16),
                    pltpu.VMEM((KB, size, wide), jnp.bfloat16),
                    pltpu.VMEM((RB, size, wide), jnp.float32),
                    pltpu.VMEM((RB, size, wide), jnp.bfloat16),
                    *[pltpu.SMEM((KB,), jnp.int32)] * marks,
                    pltpu.SMEM((RB,), jnp.int32),
                    pltpu.SemaphoreType.DMA,
                    pltpu.SemaphoreType.DMA,
                    pltpu.SemaphoreType.DMA((RB,)),
                    pltpu.SemaphoreType.DMA((RB,)),
                ],
            ),
            input_output_aliases=aliases,
            compiler_params=pltpu.CompilerParams(vmem_limit_bytes=LIMIT),
            cost_estimate=pl.CostEstimate(
                flops=flops, bytes_accessed=12 * 1024 * 1024, transcendentals=0
            ),
        )(*scalars, *operands)

    flops = 2 * 16 * NJ * size * size * size
    begun, rounded, guests, level = finish_call(
        functools.partial(middle_kernel, len(parts)),
        (*lefts, early, in_hbm(begun)),
        [
            pltpu.HBM((RB * size, wide), jnp.float32),
            pltpu.HBM((RB * size, wide), jnp.bfloat16),
            pltpu.HBM((LENT, size, size), jnp.bfloat16),
            jax.ShapeDtypeStruct((1,), jnp.int32),
        ],
        [ANYWHERE, ANYWHERE, ANYWHERE, IN_SMEM],
        [
            pltpu.VMEM((LENT, size, size), jnp.bfloat16),
            pltpu.SemaphoreType.DMA,
            pltpu.SemaphoreType.DMA,
        ],
        2, {}, flops,
    )
    back = swapped(guests)

    begin = ALWAYS
    extra = []
    for blocks in over:
        extra.append(lax.cond(level[0] > begin, to_row_before, lambda same: same, blocks))
        begin += blocks.shape[0]

    operands = (*lefts, late, back, *extra, in_hbm(begun), rounded)
    return finish_call(
        functools.partial(last_kernel, len(parts)),
        operands,
        jax.ShapeDtypeStruct((RB * size, wide), jnp.bfloat16),
        ANYWHERE, [], 1, {len(scalars) + len(operands) - 1: 0}, flops,
    )


def solution(mesh):
    placed = (
        P(None, ("row", "col"), None, None, None),
        P(None, ("row", "col"), None),
        P("row", "col", None, None, None, None),
        P("row", "col", None, None),
    )
    return jax.shard_map(
        local, mesh=mesh, in_specs=placed, out_specs=P("row", "col"), check_vma=False
    )
```

```python
import functools

import jax
import jax.numpy as jnp
from jax import lax
from jax.experimental import pallas as pl
from jax.experimental.pallas import tpu as pltpu
from jax.sharding import PartitionSpec as P

RB = 16
KB = 16
NJ = 8
PARTS = (64, 24, 8, 8, 24)
ALWAYS = PARTS[0] + PARTS[1]
LENT = 16
GROUP = 4
IN_SMEM = pl.BlockSpec(memory_space=pltpu.SMEM)
ANYWHERE = pl.BlockSpec(memory_space=pl.ANY)
LIMIT = 24 * 1024 * 1024


def in_hbm(value):
    return pltpu.with_memory_space_constraint(value, pltpu.HBM)


def places_in(table, half, owner):
    at = half * table.shape[0] + owner
    return lambda source: table[source, 1 + at // 128, at % 128]


def columns_in(table, rcap, device):
    return lambda slot: table[device, 0, slot % rcap * KB + slot // rcap]


def mark_rows(place, slots, named):
    def reset(j, carry):
        named[j] = 0
        return carry

    def mark(s, carry):
        here = place(s)

        @pl.when(here >= 0)
        def _():
            named[here % KB] = 1

        return carry

    lax.fori_loop(0, KB, reset, 0)
    lax.fori_loop(0, slots, mark, 0)


def for_wanted(column, named, rcap, action):
    def visit(slot, number):
        wanted = (column(slot) >= 0) & (named[slot // rcap] > 0)

        @pl.when(wanted)
        def _():
            action(slot, number)

        return number + wanted.astype(jnp.int32)

    return lax.fori_loop(0, KB * rcap, visit, 0)


def pack_main(spot, tables, strips, guests, *refs):
    early, late, stage, table, sem_table, named, sem, sem_out = refs[-8:]
    shift = spot[5]
    stop = stage.shape[0] - shift

    def greet(number, carry):
        pltpu.make_async_copy(guests.at[number], stage.at[number], sem).start()
        return carry

    lax.fori_loop(0, shift, greet, 0)

    def fetch(slot, number):
        @pl.when(number < stop)
        def _():
            pltpu.make_async_copy(strips.at[slot], stage.at[number + shift], sem).start()

    count = find_wanted(spot, tables, strips, table, sem_table, named, fetch)
    finish_blocks(strips, stage, sem, jnp.minimum(count, stop) + shift)
    hand_over(stage, [early, late], sem_out)


def pack_spare(spot, tables, strips, guests, *refs):
    *over, stage, table, sem_table, named, sem, sem_out = refs
    lent = spot[6]

    def fetch(slot, number):
        beyond = number - ALWAYS

        @pl.when((beyond >= 0) & (beyond < LENT))
        def _():
            pltpu.make_async_copy(strips.at[slot], stage.at[beyond], sem).start()

        @pl.when(beyond >= lent)
        def _():
            at = LENT + beyond - lent
            pltpu.make_async_copy(strips.at[slot], stage.at[at], sem).start()

    count = find_wanted(spot, tables, strips, table, sem_table, named, fetch)
    beyond = jnp.maximum(count - ALWAYS, 0)
    copied = jnp.minimum(beyond, LENT) + jnp.maximum(beyond - lent, 0)
    finish_blocks(strips, stage, sem, copied)
    hand_over(stage, [guests, *over], sem_out)


def find_wanted(spot, tables, strips, table, sem_table, named, action):
    rcap = strips.shape[0] // KB
    table_copy = pltpu.make_async_copy(tables, table, sem_table)
    table_copy.start()
    table_copy.wait()
    mark_rows(places_in(table, spot[0], spot[3]), table.shape[0], named)
    return for_wanted(columns_in(table, rcap, spot[1]), named, rcap, action)


def finish_blocks(source, target, sem, count):
    def finish(number, carry):
        pltpu.make_async_copy(source.at[0], target.at[0], sem).wait()
        return carry

    lax.fori_loop(0, count, finish, 0)


def hand_over(stage, outs, sem_out):
    copies, low = [], 0
    for i, out in enumerate(outs):
        here = stage.at[pl.ds(low, out.shape[0])]
        copies.append(pltpu.make_async_copy(here, out, sem_out.at[i]))
        copies[-1].start()
        low += out.shape[0]
    for copy in copies:
        copy.wait()


def pack(kernel, counts, spot, tables, strips, *more):
    size = strips.shape[-1]
    return pl.pallas_call(
        kernel,
        out_shape=[pltpu.HBM((n, size, size), strips.dtype) for n in counts],
        grid_spec=pltpu.PrefetchScalarGridSpec(
            num_scalar_prefetch=1,
            grid=(1,),
            in_specs=[ANYWHERE] * (2 + len(more)),
            out_specs=[ANYWHERE] * len(counts),
            scratch_shapes=[
                pltpu.VMEM((sum(counts), size, size), strips.dtype),
                pltpu.SMEM(tables.shape, jnp.int32),
                pltpu.SemaphoreType.DMA,
                pltpu.SMEM((KB,), jnp.int32),
                pltpu.SemaphoreType.DMA,
                pltpu.SemaphoreType.DMA((len(counts),)),
            ],
        ),
        compiler_params=pltpu.CompilerParams(vmem_limit_bytes=LIMIT),
        cost_estimate=pl.CostEstimate(
            flops=0, bytes_accessed=4 * sum(counts) * size * size, transcendentals=0
        ),
    )(spot, tables, in_hbm(strips), *more)


def after(value, blocks):
    count = len(blocks)
    return pl.pallas_call(
        lambda *refs: None,
        out_shape=[pltpu.HBM(each.shape, each.dtype) for each in blocks],
        in_specs=[ANYWHERE] * (count + 1),
        out_specs=[ANYWHERE] * count,
        input_output_aliases={i: i for i in range(count)},
    )(*blocks, value)


def by_block_row(place, slots, order, first):
    def reset(i, carry):
        first[i] = 0
        return carry

    def count(s, carry):
        here = place(s)

        @pl.when(here >= 0)
        def _():
            i = here // KB + 2
            first[i] = first[i] + 1

        return carry

    def scan(i, carry):
        first[i] = first[i] + first[i - 1]
        return carry

    def sort(s, carry):
        here = place(s)

        @pl.when(here >= 0)
        def _():
            i = here // KB + 1
            order[first[i]] = s * KB + here % KB
            first[i] = first[i] + 1

        return carry

    lax.fori_loop(0, RB + 2, reset, 0)
    lax.fori_loop(0, slots, count, 0)
    lax.fori_loop(1, RB + 2, scan, 0)
    lax.fori_loop(0, slots, sort, 0)


def clear(right, low):
    def one(j, carry):
        right[j] = jnp.zeros(right.shape[1:], right.dtype)
        return carry

    lax.fori_loop(low, KB, one, 0)


def add_rows(left, right, total, order, first):
    size = left.shape[1]

    def one_row(i, carry):
        row = pl.program_id(0) * GROUP + i
        here = pl.ds(pl.multiple_of(i * size, size), size)

        def add(entry, carry):
            total[here, :] += jnp.dot(
                left[order[entry] // KB], right[order[entry] % KB],
                preferred_element_type=jnp.float32,
            )
            return carry

        return lax.fori_loop(first[row], first[row + 1], add, carry)

    lax.fori_loop(0, GROUP, one_row, 0)


def place_at(right, where):
    size = right.shape[1]
    start = pl.multiple_of((where % NJ) * size, size)
    return right.at[where // NJ, :, pl.ds(start, size)]


def finish_right(source, right, sem, count):
    def finish(number, carry):
        pltpu.make_async_copy(source, place_at(right, 0), sem).wait()
        return carry

    lax.fori_loop(0, count, finish, 0)


def first_kernel(
    rcap, spot, tables, received, strips,
    out, next_order, next_first, next_target,
    left, right, table, sem_table, order, first, named, other, sem_left, sem_right,
):
    slots, size, _ = left.shape

    @pl.when(pl.program_id(0) == 0)
    def _():
        left_copy = pltpu.make_async_copy(received.at[:, pl.ds(0, size)], left, sem_left)
        left_copy.start()
        table_copy = pltpu.make_async_copy(tables, table, sem_table)
        table_copy.start()
        clear(right, 0)
        table_copy.wait()
        place = places_in(table, 0, spot[1])
        column = columns_in(table, rcap, spot[1])
        mark_rows(place, slots, named)

        def fetch(slot, number):
            target = place_at(right, slot // rcap * NJ + column(slot))
            pltpu.make_async_copy(strips.at[slot], target, sem_right).start()

        count = for_wanted(column, named, rcap, fetch)
        by_block_row(place, slots, order, first)

        next_place = places_in(table, spot[0], spot[2])
        next_column = columns_in(table, rcap, spot[4])
        by_block_row(next_place, slots, next_order, next_first)
        mark_rows(next_place, slots, other)

        def note(slot, number):
            next_target[number] = slot // rcap * NJ + next_column(slot)

        next_first[RB + 2] = for_wanted(next_column, other, rcap, note)
        left_copy.wait()
        finish_right(strips.at[0], right, sem_right, count)

    out[...] = jnp.zeros(out.shape, out.dtype)
    add_rows(left, right, out, order, first)


def start_left(shifted, parts, left, on_last, sem):
    size = left.shape[1]
    step = shifted.shape[1] - size
    whole = pltpu.make_async_copy(shifted.at[:, pl.ds(0, size)], left, sem)

    @pl.when(on_last)
    def _():
        for q, part in enumerate([shifted.at[:, pl.ds(size, step)], *parts]):
            pltpu.make_async_copy(part, left.at[:, pl.ds(q * step, step)], sem).start()

    @pl.when(jnp.logical_not(on_last))
    def _():
        whole.start()

    return whole


def start_right(sources, begin, count, target, right, sem):
    clear(right, jnp.where(count > begin, target[begin] // NJ, KB))
    for blocks, low, start, stop in sources:

        def fetch(number, carry):
            pltpu.make_async_copy(
                blocks.at[number - low], place_at(right, target[number]), sem
            ).start()
            return carry

        lax.fori_loop(start, jnp.minimum(count, stop), fetch, 0)


def add_products(row, order, first, left, right, touched, total):
    def add(entry, carry):
        @pl.when(touched[order[entry] % KB] > 0)
        def _():
            total[row] += jnp.dot(
                left[order[entry] // KB], right[order[entry] % KB],
                preferred_element_type=jnp.float32,
            )

        return carry

    lax.fori_loop(first[row], first[row + 1], add, 0)


def mark_targets(target, begin, end, marks):
    def reset(j, carry):
        marks[j] = 0
        return carry

    def mark(number, carry):
        marks[target[number] // NJ] = 1
        return carry

    lax.fori_loop(0, KB, reset, 0)
    lax.fori_loop(begin, end, mark, 0)


def mark_open(order, first, touched, open_row):
    def one(row, carry):
        def look(entry, found):
            return jnp.maximum(found, touched[order[entry] % KB])

        open_row[row] = lax.fori_loop(first[row], first[row + 1], look, jnp.int32(0))
        return carry

    lax.fori_loop(0, RB, one, 0)


def strip_of(ref, row, size):
    return ref.at[pl.ds(pl.multiple_of(row * size, size), size)]


def middle_kernel(parts_count, order, first, target, flags, *refs):
    shifted, *parts = refs[: 1 + parts_count]
    (
        piece, prev, out, rounded, guests, later, open_row,
        hall, sem_in, sem_home,
        left, right, total, short, touched,
        sem_left, sem_right, sem_prev, sem_out,
    ) = refs[1 + parts_count :]
    arrive = pltpu.make_async_copy(piece.at[pl.ds(0, LENT)], hall, sem_in)
    leave = pltpu.make_async_copy(hall, guests, sem_home)
    arrive.start()
    size = left.shape[1]
    count = first[RB + 2]
    shift = flags[1]
    end = piece.shape[0] - shift

    def prev_copy(row):
        return pltpu.make_async_copy(strip_of(prev, row, size), total.at[row], sem_prev.at[row])

    def start_prev(row, carry):
        prev_copy(row).start()
        return carry

    lax.fori_loop(0, RB, start_prev, 0)
    whole = start_left(shifted, parts, left, flags[0] > 0, sem_left)
    fetched = jnp.minimum(count, end)
    start_right([(piece, -shift, 0, end)], 0, fetched, target, right, sem_right)
    arrive.wait()
    leave.start()

    mark_targets(target, 0, fetched, touched)
    mark_targets(target, end, count, later)
    mark_open(order, first, later, open_row)
    whole.wait()
    finish_right(piece.at[0], right, sem_right, fetched)

    def out_copies(row):
        return (
            pltpu.make_async_copy(total.at[row], strip_of(out, row, size), sem_out.at[row]),
            pltpu.make_async_copy(short.at[row], strip_of(rounded, row, size), sem_out.at[row]),
        )

    def one_row(row, carry):
        open_copy, closed_copy = out_copies(row)
        prev_copy(row).wait()
        add_products(row, order, first, left, right, touched, total)

        @pl.when(open_row[row] > 0)
        def _():
            open_copy.start()

        @pl.when(open_row[row] == 0)
        def _():
            short[row] = total[row].astype(short.dtype)
            closed_copy.start()

        return carry

    def close_row(row, carry):
        open_copy, closed_copy = out_copies(row)

        @pl.when(open_row[row] > 0)
        def _():
            open_copy.wait()

        @pl.when(open_row[row] == 0)
        def _():
            closed_copy.wait()

        return carry

    lax.fori_loop(0, RB, one_row, 0)
    lax.fori_loop(0, RB, close_row, 0)
    leave.wait()


def last_kernel(parts_count, order, first, target, flags, touched, open_row, *refs):
    shifted, *parts = refs[: 1 + parts_count]
    (
        piece, back, *over, prev, _, out,
        left, right, total, short,
        sem_left, sem_right, sem_prev, sem_out,
    ) = refs[1 + parts_count :]
    size = left.shape[1]
    count = first[RB + 2]
    shift, lent = flags[1], flags[2]
    begin = PARTS[0] - shift

    def prev_copy(row):
        return pltpu.make_async_copy(strip_of(prev, row, size), total.at[row], sem_prev.at[row])

    def start_prev(row, carry):
        @pl.when(open_row[row] > 0)
        def _():
            prev_copy(row).start()

        return carry

    lax.fori_loop(0, RB, start_prev, 0)
    whole = start_left(shifted, parts, left, flags[0] > 0, sem_left)
    low = ALWAYS
    sources = [(piece, begin, begin, low - shift), (back, low, low, low + lent)]
    low = low + lent
    for blocks in over:
        high = low + blocks.shape[0]
        sources.append((blocks, low, low, high))
        low = high
    start_right(sources, begin, count, target, right, sem_right)

    def out_copy(row):
        return pltpu.make_async_copy(short.at[row], strip_of(out, row, size), sem_out.at[row])

    whole.wait()
    finish_right(piece.at[0], right, sem_right, count - begin)

    def one_row(row, carry):
        @pl.when(open_row[row] > 0)
        def _():
            prev_copy(row).wait()
            add_products(row, order, first, left, right, touched, total)
            short[row] = total[row].astype(short.dtype)
            out_copy(row).start()

        return carry

    def close_row(row, carry):
        @pl.when(open_row[row] > 0)
        def _():
            out_copy(row).wait()

        return carry

    lax.fori_loop(0, RB, one_row, 0)
    lax.fori_loop(0, RB, close_row, 0)


def step_call(kernel, scalars, operands, specs, out_shape, out_specs, scratch, slots, size):
    return pl.pallas_call(
        kernel,
        out_shape=out_shape,
        grid_spec=pltpu.PrefetchScalarGridSpec(
            num_scalar_prefetch=len(scalars),
            grid=(RB // GROUP,),
            in_specs=specs,
            out_specs=out_specs,
            scratch_shapes=[
                pltpu.VMEM((slots, size, size), jnp.bfloat16),
                pltpu.VMEM((KB, size, NJ * size), jnp.bfloat16),
                *scratch,
                pltpu.SemaphoreType.DMA,
                pltpu.SemaphoreType.DMA,
            ],
        ),
        compiler_params=pltpu.CompilerParams(
            dimension_semantics=("arbitrary",), vmem_limit_bytes=LIMIT
        ),
        cost_estimate=pl.CostEstimate(
            flops=2 * 24 * NJ * size * size * size,
            bytes_accessed=16 * 1024 * 1024,
            transcendentals=0,
        ),
    )(*scalars, *operands)


def table_kernel(where_ref, cols_ref, out, where, cols, tile, sems):
    copies = [
        pltpu.make_async_copy(where_ref, where, sems.at[0]),
        pltpu.make_async_copy(cols_ref, cols, sems.at[1]),
    ]
    for copy in copies:
        copy.start()
    rcap, across = cols.shape
    devices = where.shape[-1]
    tile[...] = jnp.zeros(tile.shape, tile.dtype)
    for copy in copies:
        copy.wait()
    for slot in range(rcap):
        tile[pl.ds(0, 1), pl.ds(slot * across, across)] = cols[pl.ds(slot, 1), :]
    for half in range(2):
        row, lane = divmod(half * devices, 128)
        tile[pl.ds(1 + row, 1), pl.ds(lane, devices)] = where[half]

    def fill(device, carry):
        out[device] = tile[...]
        return carry

    lax.fori_loop(0, out.shape[0], fill, 0)


def table_for_all(where, cols):
    devices = where.shape[-1]
    shape = (1 + -(-2 * devices // 128), 128)
    return pl.pallas_call(
        table_kernel,
        out_shape=jax.ShapeDtypeStruct((devices, *shape), jnp.int32),
        in_specs=[ANYWHERE, ANYWHERE],
        scratch_shapes=[
            pltpu.VMEM(where.shape, jnp.int32),
            pltpu.VMEM(cols.shape, jnp.int32),
            pltpu.VMEM(shape, jnp.int32),
            pltpu.SemaphoreType.DMA((2,)),
        ],
        compiler_params=pltpu.CompilerParams(vmem_limit_bytes=LIMIT),
    )(in_hbm(where), in_hbm(cols))


def needed(where_all, cols_all, rows_count, cols_count):
    grid = where_all.reshape(-1, 2, rows_count, cols_count)
    after = jnp.concatenate([grid[:, 0, :, 1:], grid[:, 1, :, :1]], axis=-1)
    columns = jnp.arange(KB, dtype=jnp.int32)
    hit = (after[..., None] >= 0) & (after[..., None] % KB == columns)
    wanted = jnp.any(hit, axis=0).astype(jnp.int32)
    counts = jnp.sum((cols_all >= 0).astype(jnp.int32), axis=1)
    counts = jnp.roll(counts.reshape(rows_count, cols_count, KB), -1, axis=0)
    return jnp.sum(wanted * counts, axis=-1)


def swapped(value):
    return lax.ppermute(value, "col", [(i, i ^ 1) for i in range(lax.axis_size("col"))])


def local(a_send, a_where, b_strips, b_cols):
    size = a_send.shape[-1]
    rows_count = lax.axis_size("row")
    cols_count = lax.axis_size("col")
    devices = rows_count * cols_count
    both = ("row", "col")
    row_index = lax.axis_index("row")
    col_index = lax.axis_index("col")
    rcap = b_strips.shape[3]
    last = cols_count - 1

    by_slot = jnp.swapaxes(b_cols, 2, 3).reshape(rcap, KB)
    tables = lax.all_to_all(
        table_for_all(a_where, by_slot), both, split_axis=0, concat_axis=0, tiled=True
    )
    after_col = (col_index + 1) % cols_count
    after_half = (col_index + 1) // cols_count
    row_before = (row_index + rows_count - 1) % rows_count
    row_after = (row_index + 1) % rows_count
    needs = needed(
        tables[:, 1:].reshape(devices, -1)[:, : 2 * devices],
        tables[:, 0].reshape(devices, rcap, KB), rows_count, cols_count,
    )
    room = ALWAYS - jnp.flip(needs.reshape(rows_count, -1, 2), -1).reshape(needs.shape)
    lent = jnp.maximum(jnp.minimum(jnp.minimum(needs - ALWAYS, room), LENT), 0)
    most = jnp.max(needs - lent)

    def lent_to(row, col):
        return lax.dynamic_slice(lent, (row, col), (1, 1))[0, 0]

    spot = jnp.stack([
        after_half,
        row_index * cols_count + col_index,
        row_index * cols_count + after_col,
        row_before * cols_count + after_col,
        row_after * cols_count + col_index,
        lent_to(row_before, col_index ^ 1),
        lent_to(row_before, col_index),
    ]).astype(jnp.int32)

    wrapped = a_send[1, 0].reshape(rows_count, cols_count, size, size)[:, 0]
    wrapped = wrapped.reshape(devices, size // cols_count, size)
    received = lax.all_to_all(
        jnp.concatenate([a_send[0, 0], wrapped], axis=1),
        both, split_axis=0, concat_axis=0, tiled=True,
    )

    def to_row_before(blocks):
        return lax.ppermute(
            blocks, "row", [(i, (i - 1) % rows_count) for i in range(rows_count)]
        )

    strips = b_strips.reshape(KB * rcap, size, size)
    guests, *over = pack(pack_spare, (LENT, *PARTS[2:]), spot, tables, strips)
    begin, extra = ALWAYS, []
    for blocks in over:
        extra.append(lax.cond(most > begin, to_row_before, lambda same: same, blocks))
        begin += blocks.shape[0]
    early, late = pack(
        pack_main, PARTS[:2], spot, tables, strips, swapped(guests),
        *(blocks[0, :16] for blocks in extra),
    )
    early, late = map(to_row_before, after(received[0, :16], [early, late]))

    shifted = lax.ppermute(
        received, "col", [(i, (i - 1) % cols_count) for i in range(cols_count)]
    )
    part = received[:, size:]
    parts = [lax.ppermute(part, "col", [(i, last)]) for i in range(1, last)] + [part]

    wide = NJ * size
    strip = pl.BlockSpec((GROUP * size, wide), lambda i, *_: (i, 0))
    begun, order, first, target = step_call(
        functools.partial(first_kernel, rcap),
        (spot,), (tables, received, in_hbm(strips)), [ANYWHERE, ANYWHERE, ANYWHERE],
        [
            pltpu.HBM((RB * size, wide), jnp.float32),
            jax.ShapeDtypeStruct((devices,), jnp.int32),
            jax.ShapeDtypeStruct((RB + 3,), jnp.int32),
            jax.ShapeDtypeStruct((KB * rcap,), jnp.int32),
        ],
        [strip, IN_SMEM, IN_SMEM, IN_SMEM],
        [
            pltpu.SMEM(tables.shape, jnp.int32),
            pltpu.SemaphoreType.DMA,
            pltpu.SMEM((devices,), jnp.int32),
            pltpu.SMEM((RB + 2,), jnp.int32),
            pltpu.SMEM((KB,), jnp.int32),
            pltpu.SMEM((KB,), jnp.int32),
        ],
        devices, size,
    )

    on_last = (col_index == last).astype(jnp.int32)
    lent_here = [lent_to(row_index, col_index ^ 1), lent_to(row_index, col_index)]
    scalars = (order, first, target, jnp.stack([on_last, *lent_here]))
    lefts = (shifted, *parts)

    def finish_call(kernel, scalars, operands, out_shape, out_specs, scratch, marks, aliases):
        return pl.pallas_call(
            kernel,
            out_shape=out_shape,
            grid_spec=pltpu.PrefetchScalarGridSpec(
                num_scalar_prefetch=len(scalars),
                grid=(1,),
                in_specs=[ANYWHERE] * len(operands),
                out_specs=out_specs,
                scratch_shapes=[
                    *scratch,
                    pltpu.VMEM((devices, size, size), jnp.bfloat16),
                    pltpu.VMEM((KB, size, wide), jnp.bfloat16),
                    pltpu.VMEM((RB, size, wide), jnp.float32),
                    pltpu.VMEM((RB, size, wide), jnp.bfloat16),
                    *marks,
                    pltpu.SemaphoreType.DMA,
                    pltpu.SemaphoreType.DMA,
                    pltpu.SemaphoreType.DMA((RB,)),
                    pltpu.SemaphoreType.DMA((RB,)),
                ],
            ),
            input_output_aliases=aliases,
            compiler_params=pltpu.CompilerParams(vmem_limit_bytes=LIMIT),
            cost_estimate=pl.CostEstimate(
                flops=2 * 16 * NJ * size * size * size,
                bytes_accessed=12 * 1024 * 1024,
                transcendentals=0,
            ),
        )(*scalars, *operands)

    begun, rounded, guests, later, open_row = finish_call(
        functools.partial(middle_kernel, len(parts)), scalars,
        (*lefts, early, in_hbm(begun)),
        [
            pltpu.HBM((RB * size, wide), jnp.float32),
            pltpu.HBM((RB * size, wide), jnp.bfloat16),
            pltpu.HBM((LENT, size, size), jnp.bfloat16),
            jax.ShapeDtypeStruct((KB,), jnp.int32),
            jax.ShapeDtypeStruct((RB,), jnp.int32),
        ],
        [ANYWHERE, ANYWHERE, ANYWHERE, IN_SMEM, IN_SMEM],
        [
            pltpu.VMEM((LENT, size, size), jnp.bfloat16),
            pltpu.SemaphoreType.DMA,
            pltpu.SemaphoreType.DMA,
        ],
        [pltpu.SMEM((KB,), jnp.int32)], {},
    )
    back = swapped(guests)

    operands = (*lefts, late, back, *extra, in_hbm(begun), rounded)
    scalars = (*scalars, later, open_row)
    return finish_call(
        functools.partial(last_kernel, len(parts)), scalars, operands,
        jax.ShapeDtypeStruct((RB * size, wide), jnp.bfloat16),
        ANYWHERE, [], [], {len(scalars) + len(operands) - 1: 0},
    )


def solution(mesh):
    placed = (
        P(None, ("row", "col"), None, None, None),
        P(None, ("row", "col"), None),
        P("row", "col", None, None, None, None),
        P("row", "col", None, None),
    )
    return jax.shard_map(
        local, mesh=mesh, in_specs=placed, out_specs=P("row", "col"), check_vma=False
    )
```

```python
import functools

import jax
import jax.numpy as jnp
from jax import lax
from jax.experimental import pallas as pl
from jax.experimental.pallas import tpu as pltpu
from jax.sharding import PartitionSpec as P

RB = 16
KB = 16
NJ = 8
AHEAD = 16
PARTS = (48, 24)
OVER = (8, 8, 24)
ALWAYS = AHEAD + sum(PARTS)
LENT = 16
GROUP = 4
IN_SMEM = pl.BlockSpec(memory_space=pltpu.SMEM)
ANYWHERE = pl.BlockSpec(memory_space=pl.ANY)
LIMIT = 24 * 1024 * 1024


def in_hbm(value):
    return pltpu.with_memory_space_constraint(value, pltpu.HBM)


def places_in(table, half, owner):
    at = half * table.shape[0] + owner
    return lambda source: table[source, 1 + at // 128, at % 128]


def columns_in(table, rcap, device):
    return lambda slot: table[device, 0, slot % rcap * KB + slot // rcap]


def mark_rows(place, slots, named):
    def reset(j, carry):
        named[j] = 0
        return carry

    def mark(s, carry):
        here = place(s)

        @pl.when(here >= 0)
        def _():
            named[here % KB] = 1

        return carry

    lax.fori_loop(0, KB, reset, 0)
    lax.fori_loop(0, slots, mark, 0)


def for_wanted(column, named, rcap, action):
    def visit(slot, number):
        wanted = (column(slot) >= 0) & (named[slot // rcap] > 0)

        @pl.when(wanted)
        def _():
            action(slot, number)

        return number + wanted.astype(jnp.int32)

    return lax.fori_loop(0, KB * rcap, visit, 0)


def pack_main(spot, tables, strips, guests, *refs):
    early, late, stage, table, sem_table, named, sem, sem_out = refs[-8:]
    shift = spot[5]
    stop = ALWAYS - shift

    def greet(number, carry):
        pltpu.make_async_copy(guests.at[number], stage.at[number], sem).start()
        return carry

    lax.fori_loop(0, shift, greet, 0)

    def fetch(slot, number):
        @pl.when((number >= AHEAD) & (number < stop))
        def _():
            at = number - AHEAD + shift
            pltpu.make_async_copy(strips.at[slot], stage.at[at], sem).start()

    count = find_wanted(spot, tables, strips, table, sem_table, named, fetch)
    finish_blocks(strips, stage, sem, jnp.maximum(jnp.minimum(count, stop) - AHEAD, 0) + shift)
    hand_over(stage, [early, late], sem_out)


def pack_ahead(spot, tables, strips, ahead, guests, *refs):
    *over, stage, table, sem_table, named, sem, sem_out = refs
    lent = spot[6]

    def fetch(slot, number):
        beyond = number - ALWAYS

        @pl.when(number < AHEAD)
        def _():
            pltpu.make_async_copy(strips.at[slot], stage.at[number], sem).start()

        @pl.when((beyond >= 0) & (beyond < LENT))
        def _():
            at = AHEAD + beyond
            pltpu.make_async_copy(strips.at[slot], stage.at[at], sem).start()

        @pl.when(beyond >= lent)
        def _():
            at = AHEAD + LENT + beyond - lent
            pltpu.make_async_copy(strips.at[slot], stage.at[at], sem).start()

    count = find_wanted(spot, tables, strips, table, sem_table, named, fetch)
    beyond = jnp.maximum(count - ALWAYS, 0)
    copied = jnp.minimum(count, AHEAD) + jnp.minimum(beyond, LENT)
    finish_blocks(strips, stage, sem, copied + jnp.maximum(beyond - lent, 0))
    hand_over(stage, [ahead, guests, *over], sem_out)


def find_wanted(spot, tables, strips, table, sem_table, named, action):
    rcap = strips.shape[0] // KB
    table_copy = pltpu.make_async_copy(tables, table, sem_table)
    table_copy.start()
    table_copy.wait()
    mark_rows(places_in(table, spot[0], spot[3]), table.shape[0], named)
    return for_wanted(columns_in(table, rcap, spot[1]), named, rcap, action)


def finish_blocks(source, target, sem, count):
    def finish(number, carry):
        pltpu.make_async_copy(source.at[0], target.at[0], sem).wait()
        return carry

    lax.fori_loop(0, count, finish, 0)


def hand_over(stage, outs, sem_out):
    copies, low = [], 0
    for i, out in enumerate(outs):
        here = stage.at[pl.ds(low, out.shape[0])]
        copies.append(pltpu.make_async_copy(here, out, sem_out.at[i]))
        copies[-1].start()
        low += out.shape[0]
    for copy in copies:
        copy.wait()


def pack(kernel, counts, spot, tables, strips, *more):
    size = strips.shape[-1]
    return pl.pallas_call(
        kernel,
        out_shape=[pltpu.HBM((n, size, size), strips.dtype) for n in counts],
        grid_spec=pltpu.PrefetchScalarGridSpec(
            num_scalar_prefetch=1,
            grid=(1,),
            in_specs=[ANYWHERE] * (2 + len(more)),
            out_specs=[ANYWHERE] * len(counts),
            scratch_shapes=[
                pltpu.VMEM((sum(counts), size, size), strips.dtype),
                pltpu.SMEM(tables.shape, jnp.int32),
                pltpu.SemaphoreType.DMA,
                pltpu.SMEM((KB,), jnp.int32),
                pltpu.SemaphoreType.DMA,
                pltpu.SemaphoreType.DMA((len(counts),)),
            ],
        ),
        compiler_params=pltpu.CompilerParams(vmem_limit_bytes=LIMIT),
        cost_estimate=pl.CostEstimate(
            flops=0, bytes_accessed=4 * sum(counts) * size * size, transcendentals=0
        ),
    )(spot, tables, in_hbm(strips), *more)


def after(value, blocks):
    count = len(blocks)
    return pl.pallas_call(
        lambda *refs: None,
        out_shape=[pltpu.HBM(each.shape, each.dtype) for each in blocks],
        in_specs=[ANYWHERE] * (count + 1),
        out_specs=[ANYWHERE] * count,
        input_output_aliases={i: i for i in range(count)},
    )(*blocks, value)


def by_block_row(place, slots, order, first):
    def reset(i, carry):
        first[i] = 0
        return carry

    def count(s, carry):
        here = place(s)

        @pl.when(here >= 0)
        def _():
            i = here // KB + 2
            first[i] = first[i] + 1

        return carry

    def scan(i, carry):
        first[i] = first[i] + first[i - 1]
        return carry

    def sort(s, carry):
        here = place(s)

        @pl.when(here >= 0)
        def _():
            i = here // KB + 1
            order[first[i]] = s * KB + here % KB
            first[i] = first[i] + 1

        return carry

    lax.fori_loop(0, RB + 2, reset, 0)
    lax.fori_loop(0, slots, count, 0)
    lax.fori_loop(1, RB + 2, scan, 0)
    lax.fori_loop(0, slots, sort, 0)


def clear(right, low):
    def one(j, carry):
        right[j] = jnp.zeros(right.shape[1:], right.dtype)
        return carry

    lax.fori_loop(low, KB, one, 0)


def add_rows(left, right, total, order, first):
    size = left.shape[1]

    def one_row(i, carry):
        row = pl.program_id(0) * GROUP + i
        here = pl.ds(pl.multiple_of(i * size, size), size)

        def add(entry, carry):
            total[here, :] += jnp.dot(
                left[order[entry] // KB], right[order[entry] % KB],
                preferred_element_type=jnp.float32,
            )
            return carry

        return lax.fori_loop(first[row], first[row + 1], add, carry)

    lax.fori_loop(0, GROUP, one_row, 0)


def place_at(right, where):
    size = right.shape[1]
    start = pl.multiple_of((where % NJ) * size, size)
    return right.at[where // NJ, :, pl.ds(start, size)]


def finish_right(source, right, sem, count):
    def finish(number, carry):
        pltpu.make_async_copy(source, place_at(right, 0), sem).wait()
        return carry

    lax.fori_loop(0, count, finish, 0)


def first_kernel(
    rcap, spot, tables, received, strips,
    out, next_order, next_first, next_target,
    left, right, table, sem_table, order, first, named, other, sem_left, sem_right,
):
    slots, size, _ = left.shape

    @pl.when(pl.program_id(0) == 0)
    def _():
        left_copy = pltpu.make_async_copy(received.at[:, pl.ds(0, size)], left, sem_left)
        left_copy.start()
        table_copy = pltpu.make_async_copy(tables, table, sem_table)
        table_copy.start()
        clear(right, 0)
        table_copy.wait()
        place = places_in(table, 0, spot[1])
        column = columns_in(table, rcap, spot[1])
        mark_rows(place, slots, named)

        def fetch(slot, number):
            target = place_at(right, slot // rcap * NJ + column(slot))
            pltpu.make_async_copy(strips.at[slot], target, sem_right).start()

        count = for_wanted(column, named, rcap, fetch)
        by_block_row(place, slots, order, first)

        next_place = places_in(table, spot[0], spot[2])
        next_column = columns_in(table, rcap, spot[4])
        by_block_row(next_place, slots, next_order, next_first)
        mark_rows(next_place, slots, other)

        def note(slot, number):
            next_target[number] = slot // rcap * NJ + next_column(slot)

        next_first[RB + 2] = for_wanted(next_column, other, rcap, note)
        left_copy.wait()
        finish_right(strips.at[0], right, sem_right, count)

    out[...] = jnp.zeros(out.shape, out.dtype)
    add_rows(left, right, out, order, first)


def start_left(shifted, parts, left, on_last, sem):
    size = left.shape[1]
    step = shifted.shape[1] - size
    whole = pltpu.make_async_copy(shifted.at[:, pl.ds(0, size)], left, sem)

    @pl.when(on_last)
    def _():
        for q, part in enumerate([shifted.at[:, pl.ds(size, step)], *parts]):
            pltpu.make_async_copy(part, left.at[:, pl.ds(q * step, step)], sem).start()

    @pl.when(jnp.logical_not(on_last))
    def _():
        whole.start()

    return whole


def start_right(sources, begin, count, target, right, sem):
    clear(right, jnp.where(count > begin, target[begin] // NJ, KB))
    for blocks, low, start, stop in sources:

        def fetch(number, carry):
            pltpu.make_async_copy(
                blocks.at[number - low], place_at(right, target[number]), sem
            ).start()
            return carry

        lax.fori_loop(start, jnp.minimum(count, stop), fetch, 0)


def add_products(row, order, first, left, right, touched, total):
    def add(entry, carry):
        @pl.when(touched[order[entry] % KB] > 0)
        def _():
            total[row] += jnp.dot(
                left[order[entry] // KB], right[order[entry] % KB],
                preferred_element_type=jnp.float32,
            )

        return carry

    lax.fori_loop(first[row], first[row + 1], add, 0)


def mark_targets(target, begin, end, marks):
    def reset(j, carry):
        marks[j] = 0
        return carry

    def mark(number, carry):
        marks[target[number] // NJ] = 1
        return carry

    lax.fori_loop(0, KB, reset, 0)
    lax.fori_loop(begin, end, mark, 0)


def mark_open(order, first, touched, open_row):
    def one(row, carry):
        def look(entry, found):
            return jnp.maximum(found, touched[order[entry] % KB])

        open_row[row] = lax.fori_loop(first[row], first[row + 1], look, jnp.int32(0))
        return carry

    lax.fori_loop(0, RB, one, 0)


def strip_of(ref, row, size):
    return ref.at[pl.ds(pl.multiple_of(row * size, size), size)]


def middle_kernel(parts_count, order, first, target, flags, *refs):
    shifted, *parts = refs[: 1 + parts_count]
    (
        ahead, piece, prev, out, rounded, guests, later, open_row,
        hall, sem_in, sem_home,
        left, right, total, short, touched,
        sem_left, sem_right, sem_prev, sem_out,
    ) = refs[1 + parts_count :]
    arrive = pltpu.make_async_copy(piece.at[pl.ds(0, LENT)], hall, sem_in)
    leave = pltpu.make_async_copy(hall, guests, sem_home)
    arrive.start()
    size = left.shape[1]
    count = first[RB + 2]
    shift = flags[1]
    end = AHEAD + PARTS[0] - shift

    def prev_copy(row):
        return pltpu.make_async_copy(strip_of(prev, row, size), total.at[row], sem_prev.at[row])

    def start_prev(row, carry):
        prev_copy(row).start()
        return carry

    lax.fori_loop(0, RB, start_prev, 0)
    whole = start_left(shifted, parts, left, flags[0] > 0, sem_left)
    fetched = jnp.minimum(count, end)
    sources = [(ahead, 0, 0, AHEAD), (piece, AHEAD - shift, AHEAD, end)]
    start_right(sources, 0, fetched, target, right, sem_right)
    arrive.wait()
    leave.start()

    mark_targets(target, 0, fetched, touched)
    mark_targets(target, end, count, later)
    mark_open(order, first, later, open_row)
    whole.wait()
    finish_right(piece.at[0], right, sem_right, fetched)

    def out_copies(row):
        return (
            pltpu.make_async_copy(total.at[row], strip_of(out, row, size), sem_out.at[row]),
            pltpu.make_async_copy(short.at[row], strip_of(rounded, row, size), sem_out.at[row]),
        )

    def one_row(row, carry):
        open_copy, closed_copy = out_copies(row)
        prev_copy(row).wait()
        add_products(row, order, first, left, right, touched, total)

        @pl.when(open_row[row] > 0)
        def _():
            open_copy.start()

        @pl.when(open_row[row] == 0)
        def _():
            short[row] = total[row].astype(short.dtype)
            closed_copy.start()

        return carry

    def close_row(row, carry):
        open_copy, closed_copy = out_copies(row)

        @pl.when(open_row[row] > 0)
        def _():
            open_copy.wait()

        @pl.when(open_row[row] == 0)
        def _():
            closed_copy.wait()

        return carry

    lax.fori_loop(0, RB, one_row, 0)
    lax.fori_loop(0, RB, close_row, 0)
    leave.wait()


def last_kernel(parts_count, order, first, target, flags, touched, open_row, *refs):
    shifted, *parts = refs[: 1 + parts_count]
    (
        piece, back, *over, prev, _, out,
        left, right, total, short,
        sem_left, sem_right, sem_prev, sem_out,
    ) = refs[1 + parts_count :]
    size = left.shape[1]
    count = first[RB + 2]
    shift, lent = flags[1], flags[2]
    begin = AHEAD + PARTS[0] - shift

    def prev_copy(row):
        return pltpu.make_async_copy(strip_of(prev, row, size), total.at[row], sem_prev.at[row])

    def start_prev(row, carry):
        @pl.when(open_row[row] > 0)
        def _():
            prev_copy(row).start()

        return carry

    lax.fori_loop(0, RB, start_prev, 0)
    whole = start_left(shifted, parts, left, flags[0] > 0, sem_left)
    low = ALWAYS
    sources = [(piece, begin, begin, low - shift), (back, low, low, low + lent)]
    low = low + lent
    for blocks in over:
        high = low + blocks.shape[0]
        sources.append((blocks, low, low, high))
        low = high
    start_right(sources, begin, count, target, right, sem_right)

    def out_copy(row):
        return pltpu.make_async_copy(short.at[row], strip_of(out, row, size), sem_out.at[row])

    whole.wait()
    finish_right(piece.at[0], right, sem_right, count - begin)

    def one_row(row, carry):
        @pl.when(open_row[row] > 0)
        def _():
            prev_copy(row).wait()
            add_products(row, order, first, left, right, touched, total)
            short[row] = total[row].astype(short.dtype)
            out_copy(row).start()

        return carry

    def close_row(row, carry):
        @pl.when(open_row[row] > 0)
        def _():
            out_copy(row).wait()

        return carry

    lax.fori_loop(0, RB, one_row, 0)
    lax.fori_loop(0, RB, close_row, 0)


def step_call(kernel, scalars, operands, specs, out_shape, out_specs, scratch, slots, size):
    return pl.pallas_call(
        kernel,
        out_shape=out_shape,
        grid_spec=pltpu.PrefetchScalarGridSpec(
            num_scalar_prefetch=len(scalars),
            grid=(RB // GROUP,),
            in_specs=specs,
            out_specs=out_specs,
            scratch_shapes=[
                pltpu.VMEM((slots, size, size), jnp.bfloat16),
                pltpu.VMEM((KB, size, NJ * size), jnp.bfloat16),
                *scratch,
                pltpu.SemaphoreType.DMA,
                pltpu.SemaphoreType.DMA,
            ],
        ),
        compiler_params=pltpu.CompilerParams(
            dimension_semantics=("arbitrary",), vmem_limit_bytes=LIMIT
        ),
        cost_estimate=pl.CostEstimate(
            flops=2 * 24 * NJ * size * size * size,
            bytes_accessed=16 * 1024 * 1024,
            transcendentals=0,
        ),
    )(*scalars, *operands)


def table_kernel(where_ref, cols_ref, out, where, cols, tile, sems):
    copies = [
        pltpu.make_async_copy(where_ref, where, sems.at[0]),
        pltpu.make_async_copy(cols_ref, cols, sems.at[1]),
    ]
    for copy in copies:
        copy.start()
    rcap, across = cols.shape
    devices = where.shape[-1]
    tile[...] = jnp.zeros(tile.shape, tile.dtype)
    for copy in copies:
        copy.wait()
    for slot in range(rcap):
        tile[pl.ds(0, 1), pl.ds(slot * across, across)] = cols[pl.ds(slot, 1), :]
    for half in range(2):
        row, lane = divmod(half * devices, 128)
        tile[pl.ds(1 + row, 1), pl.ds(lane, devices)] = where[half]

    def fill(device, carry):
        out[device] = tile[...]
        return carry

    lax.fori_loop(0, out.shape[0], fill, 0)


def table_for_all(where, cols):
    devices = where.shape[-1]
    shape = (1 + -(-2 * devices // 128), 128)
    return pl.pallas_call(
        table_kernel,
        out_shape=jax.ShapeDtypeStruct((devices, *shape), jnp.int32),
        in_specs=[ANYWHERE, ANYWHERE],
        scratch_shapes=[
            pltpu.VMEM(where.shape, jnp.int32),
            pltpu.VMEM(cols.shape, jnp.int32),
            pltpu.VMEM(shape, jnp.int32),
            pltpu.SemaphoreType.DMA((2,)),
        ],
        compiler_params=pltpu.CompilerParams(vmem_limit_bytes=LIMIT),
    )(in_hbm(where), in_hbm(cols))


def needed(where_all, cols_all, rows_count, cols_count):
    grid = where_all.reshape(-1, 2, rows_count, cols_count)
    after = jnp.concatenate([grid[:, 0, :, 1:], grid[:, 1, :, :1]], axis=-1)
    columns = jnp.arange(KB, dtype=jnp.int32)
    hit = (after[..., None] >= 0) & (after[..., None] % KB == columns)
    wanted = jnp.any(hit, axis=0).astype(jnp.int32)
    counts = jnp.sum((cols_all >= 0).astype(jnp.int32), axis=1)
    counts = jnp.roll(counts.reshape(rows_count, cols_count, KB), -1, axis=0)
    return jnp.sum(wanted * counts, axis=-1)


def swapped(value):
    return lax.ppermute(value, "col", [(i, i ^ 1) for i in range(lax.axis_size("col"))])


def local(a_send, a_where, b_strips, b_cols):
    size = a_send.shape[-1]
    rows_count = lax.axis_size("row")
    cols_count = lax.axis_size("col")
    devices = rows_count * cols_count
    both = ("row", "col")
    row_index = lax.axis_index("row")
    col_index = lax.axis_index("col")
    rcap = b_strips.shape[3]
    last = cols_count - 1

    by_slot = jnp.swapaxes(b_cols, 2, 3).reshape(rcap, KB)
    tables = lax.all_to_all(
        table_for_all(a_where, by_slot), both, split_axis=0, concat_axis=0, tiled=True
    )
    after_col = (col_index + 1) % cols_count
    after_half = (col_index + 1) // cols_count
    row_before = (row_index + rows_count - 1) % rows_count
    row_after = (row_index + 1) % rows_count
    needs = needed(
        tables[:, 1:].reshape(devices, -1)[:, : 2 * devices],
        tables[:, 0].reshape(devices, rcap, KB), rows_count, cols_count,
    )
    room = ALWAYS - jnp.flip(needs.reshape(rows_count, -1, 2), -1).reshape(needs.shape)
    lent = jnp.maximum(jnp.minimum(jnp.minimum(needs - ALWAYS, room), LENT), 0)
    most = jnp.max(needs - lent)

    def lent_to(row, col):
        return lax.dynamic_slice(lent, (row, col), (1, 1))[0, 0]

    spot = jnp.stack([
        after_half,
        row_index * cols_count + col_index,
        row_index * cols_count + after_col,
        row_before * cols_count + after_col,
        row_after * cols_count + col_index,
        lent_to(row_before, col_index ^ 1),
        lent_to(row_before, col_index),
    ]).astype(jnp.int32)

    wrapped = a_send[1, 0].reshape(rows_count, cols_count, size, size)[:, 0]
    wrapped = wrapped.reshape(devices, size // cols_count, size)
    received = lax.all_to_all(
        jnp.concatenate([a_send[0, 0], wrapped], axis=1),
        both, split_axis=0, concat_axis=0, tiled=True,
    )

    def to_row_before(blocks):
        return lax.ppermute(
            blocks, "row", [(i, (i - 1) % rows_count) for i in range(rows_count)]
        )

    strips = b_strips.reshape(KB * rcap, size, size)
    ahead, guests, *over = pack(pack_ahead, (AHEAD, LENT, *OVER), spot, tables, strips)
    ahead = to_row_before(ahead)
    begin, extra = ALWAYS, []
    for blocks in over:
        extra.append(lax.cond(most > begin, to_row_before, lambda same: same, blocks))
        begin += blocks.shape[0]
    early, late = pack(
        pack_main, PARTS, spot, tables, strips, swapped(guests),
        *(blocks[0, :16] for blocks in extra),
    )
    early, late = map(to_row_before, after(received[0, :16], [early, late]))

    shifted = lax.ppermute(
        received, "col", [(i, (i - 1) % cols_count) for i in range(cols_count)]
    )
    part = received[:, size:]
    parts = [lax.ppermute(part, "col", [(i, last)]) for i in range(1, last)] + [part]

    wide = NJ * size
    strip = pl.BlockSpec((GROUP * size, wide), lambda i, *_: (i, 0))
    begun, order, first, target = step_call(
        functools.partial(first_kernel, rcap),
        (spot,), (tables, received, in_hbm(strips)), [ANYWHERE, ANYWHERE, ANYWHERE],
        [
            pltpu.HBM((RB * size, wide), jnp.float32),
            jax.ShapeDtypeStruct((devices,), jnp.int32),
            jax.ShapeDtypeStruct((RB + 3,), jnp.int32),
            jax.ShapeDtypeStruct((KB * rcap,), jnp.int32),
        ],
        [strip, IN_SMEM, IN_SMEM, IN_SMEM],
        [
            pltpu.SMEM(tables.shape, jnp.int32),
            pltpu.SemaphoreType.DMA,
            pltpu.SMEM((devices,), jnp.int32),
            pltpu.SMEM((RB + 2,), jnp.int32),
            pltpu.SMEM((KB,), jnp.int32),
            pltpu.SMEM((KB,), jnp.int32),
        ],
        devices, size,
    )

    on_last = (col_index == last).astype(jnp.int32)
    lent_here = [lent_to(row_index, col_index ^ 1), lent_to(row_index, col_index)]
    scalars = (order, first, target, jnp.stack([on_last, *lent_here]))
    lefts = (shifted, *parts)

    def finish_call(kernel, scalars, operands, out_shape, out_specs, scratch, marks, aliases):
        return pl.pallas_call(
            kernel,
            out_shape=out_shape,
            grid_spec=pltpu.PrefetchScalarGridSpec(
                num_scalar_prefetch=len(scalars),
                grid=(1,),
                in_specs=[ANYWHERE] * len(operands),
                out_specs=out_specs,
                scratch_shapes=[
                    *scratch,
                    pltpu.VMEM((devices, size, size), jnp.bfloat16),
                    pltpu.VMEM((KB, size, wide), jnp.bfloat16),
                    pltpu.VMEM((RB, size, wide), jnp.float32),
                    pltpu.VMEM((RB, size, wide), jnp.bfloat16),
                    *marks,
                    pltpu.SemaphoreType.DMA,
                    pltpu.SemaphoreType.DMA,
                    pltpu.SemaphoreType.DMA((RB,)),
                    pltpu.SemaphoreType.DMA((RB,)),
                ],
            ),
            input_output_aliases=aliases,
            compiler_params=pltpu.CompilerParams(vmem_limit_bytes=LIMIT),
            cost_estimate=pl.CostEstimate(
                flops=2 * 16 * NJ * size * size * size,
                bytes_accessed=12 * 1024 * 1024,
                transcendentals=0,
            ),
        )(*scalars, *operands)

    begun, rounded, guests, later, open_row = finish_call(
        functools.partial(middle_kernel, len(parts)), scalars,
        (*lefts, ahead, early, in_hbm(begun)),
        [
            pltpu.HBM((RB * size, wide), jnp.float32),
            pltpu.HBM((RB * size, wide), jnp.bfloat16),
            pltpu.HBM((LENT, size, size), jnp.bfloat16),
            jax.ShapeDtypeStruct((KB,), jnp.int32),
            jax.ShapeDtypeStruct((RB,), jnp.int32),
        ],
        [ANYWHERE, ANYWHERE, ANYWHERE, IN_SMEM, IN_SMEM],
        [
            pltpu.VMEM((LENT, size, size), jnp.bfloat16),
            pltpu.SemaphoreType.DMA,
            pltpu.SemaphoreType.DMA,
        ],
        [pltpu.SMEM((KB,), jnp.int32)], {},
    )
    back = swapped(guests)

    operands = (*lefts, late, back, *extra, in_hbm(begun), rounded)
    scalars = (*scalars, later, open_row)
    return finish_call(
        functools.partial(last_kernel, len(parts)), scalars, operands,
        jax.ShapeDtypeStruct((RB * size, wide), jnp.bfloat16),
        ANYWHERE, [], [], {len(scalars) + len(operands) - 1: 0},
    )


def solution(mesh):
    placed = (
        P(None, ("row", "col"), None, None, None),
        P(None, ("row", "col"), None),
        P("row", "col", None, None, None, None),
        P("row", "col", None, None),
    )
    return jax.shard_map(
        local, mesh=mesh, in_specs=placed, out_specs=P("row", "col"), check_vma=False
    )
```

```python
import functools

import jax
import jax.numpy as jnp
from jax import lax
from jax.experimental import pallas as pl
from jax.experimental.pallas import tpu as pltpu
from jax.sharding import PartitionSpec as P

RB = 16
KB = 16
NJ = 8
AHEAD = 24
PARTS = (40, 24)
OVER = (8, 8, 24)
ALWAYS = AHEAD + sum(PARTS)
LENT = 16
GROUP = 4
IN_SMEM = pl.BlockSpec(memory_space=pltpu.SMEM)
ANYWHERE = pl.BlockSpec(memory_space=pl.ANY)
LIMIT = 24 * 1024 * 1024


def in_hbm(value):
    return pltpu.with_memory_space_constraint(value, pltpu.HBM)


def places_in(table, half, owner):
    at = half * table.shape[0] + owner
    return lambda source: table[source, 1 + at // 128, at % 128]


def columns_in(table, rcap, device):
    return lambda slot: table[device, 0, slot % rcap * KB + slot // rcap]


def mark_rows(place, slots, named):
    def reset(j, carry):
        named[j] = 0
        return carry

    def mark(s, carry):
        here = place(s)

        @pl.when(here >= 0)
        def _():
            named[here % KB] = 1

        return carry

    lax.fori_loop(0, KB, reset, 0)
    lax.fori_loop(0, slots, mark, 0)


def for_wanted(column, named, rcap, action):
    def visit(slot, number):
        wanted = (column(slot) >= 0) & (named[slot // rcap] > 0)

        @pl.when(wanted)
        def _():
            action(slot, number)

        return number + wanted.astype(jnp.int32)

    return lax.fori_loop(0, KB * rcap, visit, 0)


def pack_main(spot, tables, strips, guests, *refs):
    early, late, stage, table, sem_table, named, sem, sem_out = refs[-8:]
    shift = spot[5]
    stop = ALWAYS - shift

    def greet(number, carry):
        pltpu.make_async_copy(guests.at[number], stage.at[number], sem).start()
        return carry

    lax.fori_loop(0, shift, greet, 0)

    def fetch(slot, number):
        @pl.when((number >= AHEAD) & (number < stop))
        def _():
            at = number - AHEAD + shift
            pltpu.make_async_copy(strips.at[slot], stage.at[at], sem).start()

    count = find_wanted(spot, tables, strips, table, sem_table, named, fetch)
    finish_blocks(strips, stage, sem, jnp.maximum(jnp.minimum(count, stop) - AHEAD, 0) + shift)
    hand_over(stage, [early, late], sem_out)


def pack_ahead(spot, tables, strips, ahead, guests, *refs):
    *over, stage, table, sem_table, named, sem, sem_out = refs
    lent = spot[6]

    def fetch(slot, number):
        beyond = number - ALWAYS

        @pl.when(number < AHEAD)
        def _():
            pltpu.make_async_copy(strips.at[slot], stage.at[number], sem).start()

        @pl.when((beyond >= 0) & (beyond < LENT))
        def _():
            at = AHEAD + beyond
            pltpu.make_async_copy(strips.at[slot], stage.at[at], sem).start()

        @pl.when(beyond >= lent)
        def _():
            at = AHEAD + LENT + beyond - lent
            pltpu.make_async_copy(strips.at[slot], stage.at[at], sem).start()

    count = find_wanted(spot, tables, strips, table, sem_table, named, fetch)
    beyond = jnp.maximum(count - ALWAYS, 0)
    copied = jnp.minimum(count, AHEAD) + jnp.minimum(beyond, LENT)
    finish_blocks(strips, stage, sem, copied + jnp.maximum(beyond - lent, 0))
    hand_over(stage, [ahead, guests, *over], sem_out)


def find_wanted(spot, tables, strips, table, sem_table, named, action):
    rcap = strips.shape[0] // KB
    table_copy = pltpu.make_async_copy(tables, table, sem_table)
    table_copy.start()
    table_copy.wait()
    mark_rows(places_in(table, spot[0], spot[3]), table.shape[0], named)
    return for_wanted(columns_in(table, rcap, spot[1]), named, rcap, action)


def finish_blocks(source, target, sem, count):
    def finish(number, carry):
        pltpu.make_async_copy(source.at[0], target.at[0], sem).wait()
        return carry

    lax.fori_loop(0, count, finish, 0)


def hand_over(stage, outs, sem_out):
    copies, low = [], 0
    for i, out in enumerate(outs):
        here = stage.at[pl.ds(low, out.shape[0])]
        copies.append(pltpu.make_async_copy(here, out, sem_out.at[i]))
        copies[-1].start()
        low += out.shape[0]
    for copy in copies:
        copy.wait()


def pack(kernel, counts, spot, tables, strips, *more):
    size = strips.shape[-1]
    return pl.pallas_call(
        kernel,
        out_shape=[pltpu.HBM((n, size, size), strips.dtype) for n in counts],
        grid_spec=pltpu.PrefetchScalarGridSpec(
            num_scalar_prefetch=1,
            grid=(1,),
            in_specs=[ANYWHERE] * (2 + len(more)),
            out_specs=[ANYWHERE] * len(counts),
            scratch_shapes=[
                pltpu.VMEM((sum(counts), size, size), strips.dtype),
                pltpu.SMEM(tables.shape, jnp.int32),
                pltpu.SemaphoreType.DMA,
                pltpu.SMEM((KB,), jnp.int32),
                pltpu.SemaphoreType.DMA,
                pltpu.SemaphoreType.DMA((len(counts),)),
            ],
        ),
        compiler_params=pltpu.CompilerParams(vmem_limit_bytes=LIMIT),
        cost_estimate=pl.CostEstimate(
            flops=0, bytes_accessed=4 * sum(counts) * size * size, transcendentals=0
        ),
    )(spot, tables, in_hbm(strips), *more)


def after(values, blocks):
    count = len(blocks)
    return pl.pallas_call(
        lambda *refs: None,
        out_shape=[pltpu.HBM(each.shape, each.dtype) for each in blocks],
        in_specs=[ANYWHERE] * (count + len(values)),
        out_specs=[ANYWHERE] * count,
        input_output_aliases={i: i for i in range(count)},
    )(*blocks, *values)


def by_block_row(place, slots, order, first):
    def reset(i, carry):
        first[i] = 0
        return carry

    def count(s, carry):
        here = place(s)

        @pl.when(here >= 0)
        def _():
            i = here // KB + 2
            first[i] = first[i] + 1

        return carry

    def scan(i, carry):
        first[i] = first[i] + first[i - 1]
        return carry

    def sort(s, carry):
        here = place(s)

        @pl.when(here >= 0)
        def _():
            i = here // KB + 1
            order[first[i]] = s * KB + here % KB
            first[i] = first[i] + 1

        return carry

    lax.fori_loop(0, RB + 2, reset, 0)
    lax.fori_loop(0, slots, count, 0)
    lax.fori_loop(1, RB + 2, scan, 0)
    lax.fori_loop(0, slots, sort, 0)


def clear(right, low):
    def one(j, carry):
        right[j] = jnp.zeros(right.shape[1:], right.dtype)
        return carry

    lax.fori_loop(low, KB, one, 0)


def add_rows(left, right, total, order, first):
    size = left.shape[1]

    def one_row(i, carry):
        row = pl.program_id(0) * GROUP + i
        here = pl.ds(pl.multiple_of(i * size, size), size)

        def add(entry, carry):
            total[here, :] += jnp.dot(
                left[order[entry] // KB], right[order[entry] % KB],
                preferred_element_type=jnp.float32,
            )
            return carry

        return lax.fori_loop(first[row], first[row + 1], add, carry)

    lax.fori_loop(0, GROUP, one_row, 0)


def place_at(right, where):
    size = right.shape[1]
    start = pl.multiple_of((where % NJ) * size, size)
    return right.at[where // NJ, :, pl.ds(start, size)]


def finish_right(source, right, sem, count):
    def finish(number, carry):
        pltpu.make_async_copy(source, place_at(right, 0), sem).wait()
        return carry

    lax.fori_loop(0, count, finish, 0)


def first_kernel(
    rcap, spot, tables, received, strips,
    out, next_order, next_first, next_target,
    left, right, table, sem_table, order, first, named, other, sem_left, sem_right,
):
    slots, size, _ = left.shape

    @pl.when(pl.program_id(0) == 0)
    def _():
        left_copy = pltpu.make_async_copy(received.at[:, pl.ds(0, size)], left, sem_left)
        left_copy.start()
        table_copy = pltpu.make_async_copy(tables, table, sem_table)
        table_copy.start()
        clear(right, 0)
        table_copy.wait()
        place = places_in(table, 0, spot[1])
        column = columns_in(table, rcap, spot[1])
        mark_rows(place, slots, named)

        def fetch(slot, number):
            target = place_at(right, slot // rcap * NJ + column(slot))
            pltpu.make_async_copy(strips.at[slot], target, sem_right).start()

        count = for_wanted(column, named, rcap, fetch)
        by_block_row(place, slots, order, first)

        next_place = places_in(table, spot[0], spot[2])
        next_column = columns_in(table, rcap, spot[4])
        by_block_row(next_place, slots, next_order, next_first)
        mark_rows(next_place, slots, other)

        def note(slot, number):
            next_target[number] = slot // rcap * NJ + next_column(slot)

        next_first[RB + 2] = for_wanted(next_column, other, rcap, note)
        left_copy.wait()
        finish_right(strips.at[0], right, sem_right, count)

    out[...] = jnp.zeros(out.shape, out.dtype)
    add_rows(left, right, out, order, first)


def start_left(shifted, parts, left, on_last, sem):
    size = left.shape[1]
    step = shifted.shape[1] - size
    whole = pltpu.make_async_copy(shifted.at[:, pl.ds(0, size)], left, sem)

    @pl.when(on_last)
    def _():
        for q, part in enumerate([shifted.at[:, pl.ds(size, step)], *parts]):
            pltpu.make_async_copy(part, left.at[:, pl.ds(q * step, step)], sem).start()

    @pl.when(jnp.logical_not(on_last))
    def _():
        whole.start()

    return whole


def start_right(sources, begin, count, target, right, sem):
    clear(right, jnp.where(count > begin, target[begin] // NJ, KB))
    for blocks, low, start, stop in sources:

        def fetch(number, carry):
            pltpu.make_async_copy(
                blocks.at[number - low], place_at(right, target[number]), sem
            ).start()
            return carry

        lax.fori_loop(start, jnp.minimum(count, stop), fetch, 0)


def add_products(row, order, first, left, right, touched, total):
    def add(entry, carry):
        @pl.when(touched[order[entry] % KB] > 0)
        def _():
            total[row] += jnp.dot(
                left[order[entry] // KB], right[order[entry] % KB],
                preferred_element_type=jnp.float32,
            )

        return carry

    lax.fori_loop(first[row], first[row + 1], add, 0)


def mark_targets(target, begin, end, marks):
    def reset(j, carry):
        marks[j] = 0
        return carry

    def mark(number, carry):
        marks[target[number] // NJ] = 1
        return carry

    lax.fori_loop(0, KB, reset, 0)
    lax.fori_loop(begin, end, mark, 0)


def mark_open(order, first, touched, open_row):
    def one(row, carry):
        def look(entry, found):
            return jnp.maximum(found, touched[order[entry] % KB])

        open_row[row] = lax.fori_loop(first[row], first[row + 1], look, jnp.int32(0))
        return carry

    lax.fori_loop(0, RB, one, 0)


def strip_of(ref, row, size):
    return ref.at[pl.ds(pl.multiple_of(row * size, size), size)]


def middle_kernel(parts_count, order, first, target, flags, *refs):
    shifted, *parts = refs[: 1 + parts_count]
    (
        ahead, piece, prev, out, rounded, guests, later, open_row,
        hall, sem_in, sem_home,
        left, right, total, short, touched,
        sem_left, sem_right, sem_prev, sem_out,
    ) = refs[1 + parts_count :]
    arrive = pltpu.make_async_copy(piece.at[pl.ds(0, LENT)], hall, sem_in)
    leave = pltpu.make_async_copy(hall, guests, sem_home)
    arrive.start()
    size = left.shape[1]
    count = first[RB + 2]
    shift = flags[1]
    end = AHEAD + PARTS[0] - shift

    def prev_copy(row):
        return pltpu.make_async_copy(strip_of(prev, row, size), total.at[row], sem_prev.at[row])

    def start_prev(row, carry):
        prev_copy(row).start()
        return carry

    lax.fori_loop(0, RB, start_prev, 0)
    whole = start_left(shifted, parts, left, flags[0] > 0, sem_left)
    fetched = jnp.minimum(count, end)
    sources = [(ahead, 0, 0, AHEAD), (piece, AHEAD - shift, AHEAD, end)]
    start_right(sources, 0, fetched, target, right, sem_right)
    arrive.wait()
    leave.start()

    mark_targets(target, 0, fetched, touched)
    mark_targets(target, end, count, later)
    mark_open(order, first, later, open_row)
    whole.wait()
    finish_right(piece.at[0], right, sem_right, fetched)

    def out_copies(row):
        return (
            pltpu.make_async_copy(total.at[row], strip_of(out, row, size), sem_out.at[row]),
            pltpu.make_async_copy(short.at[row], strip_of(rounded, row, size), sem_out.at[row]),
        )

    def one_row(row, carry):
        open_copy, closed_copy = out_copies(row)
        prev_copy(row).wait()
        add_products(row, order, first, left, right, touched, total)

        @pl.when(open_row[row] > 0)
        def _():
            open_copy.start()

        @pl.when(open_row[row] == 0)
        def _():
            short[row] = total[row].astype(short.dtype)
            closed_copy.start()

        return carry

    def close_row(row, carry):
        open_copy, closed_copy = out_copies(row)

        @pl.when(open_row[row] > 0)
        def _():
            open_copy.wait()

        @pl.when(open_row[row] == 0)
        def _():
            closed_copy.wait()

        return carry

    lax.fori_loop(0, RB, one_row, 0)
    lax.fori_loop(0, RB, close_row, 0)
    leave.wait()


def last_kernel(parts_count, order, first, target, flags, touched, open_row, *refs):
    shifted, *parts = refs[: 1 + parts_count]
    (
        piece, back, *over, prev, _, out,
        left, right, total, short,
        sem_left, sem_right, sem_prev, sem_out,
    ) = refs[1 + parts_count :]
    size = left.shape[1]
    count = first[RB + 2]
    shift, lent = flags[1], flags[2]
    begin = AHEAD + PARTS[0] - shift

    def prev_copy(row):
        return pltpu.make_async_copy(strip_of(prev, row, size), total.at[row], sem_prev.at[row])

    def start_prev(row, carry):
        @pl.when(open_row[row] > 0)
        def _():
            prev_copy(row).start()

        return carry

    lax.fori_loop(0, RB, start_prev, 0)
    whole = start_left(shifted, parts, left, flags[0] > 0, sem_left)
    low = ALWAYS
    sources = [(piece, begin, begin, low - shift), (back, low, low, low + lent)]
    low = low + lent
    for blocks in over:
        high = low + blocks.shape[0]
        sources.append((blocks, low, low, high))
        low = high
    start_right(sources, begin, count, target, right, sem_right)

    def out_copy(row):
        return pltpu.make_async_copy(short.at[row], strip_of(out, row, size), sem_out.at[row])

    whole.wait()
    finish_right(piece.at[0], right, sem_right, count - begin)

    def one_row(row, carry):
        @pl.when(open_row[row] > 0)
        def _():
            prev_copy(row).wait()
            add_products(row, order, first, left, right, touched, total)
            short[row] = total[row].astype(short.dtype)
            out_copy(row).start()

        return carry

    def close_row(row, carry):
        @pl.when(open_row[row] > 0)
        def _():
            out_copy(row).wait()

        return carry

    lax.fori_loop(0, RB, one_row, 0)
    lax.fori_loop(0, RB, close_row, 0)


def step_call(kernel, scalars, operands, specs, out_shape, out_specs, scratch, slots, size):
    return pl.pallas_call(
        kernel,
        out_shape=out_shape,
        grid_spec=pltpu.PrefetchScalarGridSpec(
            num_scalar_prefetch=len(scalars),
            grid=(RB // GROUP,),
            in_specs=specs,
            out_specs=out_specs,
            scratch_shapes=[
                pltpu.VMEM((slots, size, size), jnp.bfloat16),
                pltpu.VMEM((KB, size, NJ * size), jnp.bfloat16),
                *scratch,
                pltpu.SemaphoreType.DMA,
                pltpu.SemaphoreType.DMA,
            ],
        ),
        compiler_params=pltpu.CompilerParams(
            dimension_semantics=("arbitrary",), vmem_limit_bytes=LIMIT
        ),
        cost_estimate=pl.CostEstimate(
            flops=2 * 24 * NJ * size * size * size,
            bytes_accessed=16 * 1024 * 1024,
            transcendentals=0,
        ),
    )(*scalars, *operands)


def table_kernel(where_ref, cols_ref, out, where, cols, tile, sems):
    copies = [
        pltpu.make_async_copy(where_ref, where, sems.at[0]),
        pltpu.make_async_copy(cols_ref, cols, sems.at[1]),
    ]
    for copy in copies:
        copy.start()
    rcap, across = cols.shape
    devices = where.shape[-1]
    tile[...] = jnp.zeros(tile.shape, tile.dtype)
    for copy in copies:
        copy.wait()
    for slot in range(rcap):
        tile[pl.ds(0, 1), pl.ds(slot * across, across)] = cols[pl.ds(slot, 1), :]
    for half in range(2):
        row, lane = divmod(half * devices, 128)
        tile[pl.ds(1 + row, 1), pl.ds(lane, devices)] = where[half]

    def fill(device, carry):
        out[device] = tile[...]
        return carry

    lax.fori_loop(0, out.shape[0], fill, 0)


def table_for_all(where, cols):
    devices = where.shape[-1]
    shape = (1 + -(-2 * devices // 128), 128)
    return pl.pallas_call(
        table_kernel,
        out_shape=jax.ShapeDtypeStruct((devices, *shape), jnp.int32),
        in_specs=[ANYWHERE, ANYWHERE],
        scratch_shapes=[
            pltpu.VMEM(where.shape, jnp.int32),
            pltpu.VMEM(cols.shape, jnp.int32),
            pltpu.VMEM(shape, jnp.int32),
            pltpu.SemaphoreType.DMA((2,)),
        ],
        compiler_params=pltpu.CompilerParams(vmem_limit_bytes=LIMIT),
    )(in_hbm(where), in_hbm(cols))


def needed(where_all, cols_all, rows_count, cols_count):
    grid = where_all.reshape(-1, 2, rows_count, cols_count)
    after = jnp.concatenate([grid[:, 0, :, 1:], grid[:, 1, :, :1]], axis=-1)
    columns = jnp.arange(KB, dtype=jnp.int32)
    hit = (after[..., None] >= 0) & (after[..., None] % KB == columns)
    wanted = jnp.any(hit, axis=0).astype(jnp.int32)
    counts = jnp.sum((cols_all >= 0).astype(jnp.int32), axis=1)
    counts = jnp.roll(counts.reshape(rows_count, cols_count, KB), -1, axis=0)
    return jnp.sum(wanted * counts, axis=-1)


def swapped(value):
    return lax.ppermute(value, "col", [(i, i ^ 1) for i in range(lax.axis_size("col"))])


def local(a_send, a_where, b_strips, b_cols):
    size = a_send.shape[-1]
    rows_count = lax.axis_size("row")
    cols_count = lax.axis_size("col")
    devices = rows_count * cols_count
    both = ("row", "col")
    row_index = lax.axis_index("row")
    col_index = lax.axis_index("col")
    rcap = b_strips.shape[3]
    last = cols_count - 1

    by_slot = jnp.swapaxes(b_cols, 2, 3).reshape(rcap, KB)
    tables = lax.all_to_all(
        table_for_all(a_where, by_slot), both, split_axis=0, concat_axis=0, tiled=True
    )
    after_col = (col_index + 1) % cols_count
    after_half = (col_index + 1) // cols_count
    row_before = (row_index + rows_count - 1) % rows_count
    row_after = (row_index + 1) % rows_count
    needs = needed(
        tables[:, 1:].reshape(devices, -1)[:, : 2 * devices],
        tables[:, 0].reshape(devices, rcap, KB), rows_count, cols_count,
    )
    room = ALWAYS - jnp.flip(needs.reshape(rows_count, -1, 2), -1).reshape(needs.shape)
    lent = jnp.maximum(jnp.minimum(jnp.minimum(needs - ALWAYS, room), LENT), 0)
    most = jnp.max(needs - lent)

    def lent_to(row, col):
        return lax.dynamic_slice(lent, (row, col), (1, 1))[0, 0]

    spot = jnp.stack([
        after_half,
        row_index * cols_count + col_index,
        row_index * cols_count + after_col,
        row_before * cols_count + after_col,
        row_after * cols_count + col_index,
        lent_to(row_before, col_index ^ 1),
        lent_to(row_before, col_index),
    ]).astype(jnp.int32)

    wrapped = a_send[1, 0].reshape(rows_count, cols_count, size, size)[:, 0]
    wrapped = wrapped.reshape(devices, size // cols_count, size)
    received = lax.all_to_all(
        jnp.concatenate([a_send[0, 0], wrapped], axis=1),
        both, split_axis=0, concat_axis=0, tiled=True,
    )

    def to_row_before(blocks):
        return lax.ppermute(
            blocks, "row", [(i, (i - 1) % rows_count) for i in range(rows_count)]
        )

    strips = b_strips.reshape(KB * rcap, size, size)
    ahead, guests, *over = pack(pack_ahead, (AHEAD, LENT, *OVER), spot, tables, strips)
    ahead = to_row_before(ahead)
    begin, extra = ALWAYS, []
    for blocks in over:
        extra.append(lax.cond(most > begin, to_row_before, lambda same: same, blocks))
        begin += blocks.shape[0]
    early, late = pack(
        pack_main, PARTS, spot, tables, strips, swapped(guests),
        *(blocks[0, :16] for blocks in extra),
    )
    early, late = map(to_row_before, after([received[0, :16], ahead[0, :16]], [early, late]))

    shifted = lax.ppermute(
        received, "col", [(i, (i - 1) % cols_count) for i in range(cols_count)]
    )
    part = received[:, size:]
    parts = [lax.ppermute(part, "col", [(i, last)]) for i in range(1, last)] + [part]

    wide = NJ * size
    strip = pl.BlockSpec((GROUP * size, wide), lambda i, *_: (i, 0))
    begun, order, first, target = step_call(
        functools.partial(first_kernel, rcap),
        (spot,), (tables, received, in_hbm(strips)), [ANYWHERE, ANYWHERE, ANYWHERE],
        [
            pltpu.HBM((RB * size, wide), jnp.float32),
            jax.ShapeDtypeStruct((devices,), jnp.int32),
            jax.ShapeDtypeStruct((RB + 3,), jnp.int32),
            jax.ShapeDtypeStruct((KB * rcap,), jnp.int32),
        ],
        [strip, IN_SMEM, IN_SMEM, IN_SMEM],
        [
            pltpu.SMEM(tables.shape, jnp.int32),
            pltpu.SemaphoreType.DMA,
            pltpu.SMEM((devices,), jnp.int32),
            pltpu.SMEM((RB + 2,), jnp.int32),
            pltpu.SMEM((KB,), jnp.int32),
            pltpu.SMEM((KB,), jnp.int32),
        ],
        devices, size,
    )

    on_last = (col_index == last).astype(jnp.int32)
    lent_here = [lent_to(row_index, col_index ^ 1), lent_to(row_index, col_index)]
    scalars = (order, first, target, jnp.stack([on_last, *lent_here]))
    lefts = (shifted, *parts)

    def finish_call(kernel, scalars, operands, out_shape, out_specs, scratch, marks, aliases):
        return pl.pallas_call(
            kernel,
            out_shape=out_shape,
            grid_spec=pltpu.PrefetchScalarGridSpec(
                num_scalar_prefetch=len(scalars),
                grid=(1,),
                in_specs=[ANYWHERE] * len(operands),
                out_specs=out_specs,
                scratch_shapes=[
                    *scratch,
                    pltpu.VMEM((devices, size, size), jnp.bfloat16),
                    pltpu.VMEM((KB, size, wide), jnp.bfloat16),
                    pltpu.VMEM((RB, size, wide), jnp.float32),
                    pltpu.VMEM((RB, size, wide), jnp.bfloat16),
                    *marks,
                    pltpu.SemaphoreType.DMA,
                    pltpu.SemaphoreType.DMA,
                    pltpu.SemaphoreType.DMA((RB,)),
                    pltpu.SemaphoreType.DMA((RB,)),
                ],
            ),
            input_output_aliases=aliases,
            compiler_params=pltpu.CompilerParams(vmem_limit_bytes=LIMIT),
            cost_estimate=pl.CostEstimate(
                flops=2 * 16 * NJ * size * size * size,
                bytes_accessed=12 * 1024 * 1024,
                transcendentals=0,
            ),
        )(*scalars, *operands)

    begun, rounded, guests, later, open_row = finish_call(
        functools.partial(middle_kernel, len(parts)), scalars,
        (*lefts, ahead, early, in_hbm(begun)),
        [
            pltpu.HBM((RB * size, wide), jnp.float32),
            pltpu.HBM((RB * size, wide), jnp.bfloat16),
            pltpu.HBM((LENT, size, size), jnp.bfloat16),
            jax.ShapeDtypeStruct((KB,), jnp.int32),
            jax.ShapeDtypeStruct((RB,), jnp.int32),
        ],
        [ANYWHERE, ANYWHERE, ANYWHERE, IN_SMEM, IN_SMEM],
        [
            pltpu.VMEM((LENT, size, size), jnp.bfloat16),
            pltpu.SemaphoreType.DMA,
            pltpu.SemaphoreType.DMA,
        ],
        [pltpu.SMEM((KB,), jnp.int32)], {},
    )
    back = swapped(guests)

    operands = (*lefts, late, back, *extra, in_hbm(begun), rounded)
    scalars = (*scalars, later, open_row)
    return finish_call(
        functools.partial(last_kernel, len(parts)), scalars, operands,
        jax.ShapeDtypeStruct((RB * size, wide), jnp.bfloat16),
        ANYWHERE, [], [], {len(scalars) + len(operands) - 1: 0},
    )


def solution(mesh):
    placed = (
        P(None, ("row", "col"), None, None, None),
        P(None, ("row", "col"), None),
        P("row", "col", None, None, None, None),
        P("row", "col", None, None),
    )
    return jax.shard_map(
        local, mesh=mesh, in_specs=placed, out_specs=P("row", "col"), check_vma=False
    )
```

```python
import functools

import jax
import jax.numpy as jnp
from jax import lax
from jax.experimental import pallas as pl
from jax.experimental.pallas import tpu as pltpu
from jax.sharding import PartitionSpec as P

RB = 16
KB = 16
NJ = 8
AHEAD = 24
PARTS = (40, 24)
OVER = (8, 8, 24)
ALWAYS = AHEAD + sum(PARTS)
LENT = 16
GROUP = 4
IN_SMEM = pl.BlockSpec(memory_space=pltpu.SMEM)
ANYWHERE = pl.BlockSpec(memory_space=pl.ANY)
LIMIT = 24 * 1024 * 1024


def in_hbm(value):
    return pltpu.with_memory_space_constraint(value, pltpu.HBM)


def places_in(table, half, owner):
    at = half * table.shape[0] + owner
    return lambda source: table[source, 1 + at // 128, at % 128]


def columns_in(table, rcap, device):
    return lambda slot: table[device, 0, slot % rcap * KB + slot // rcap]


def mark_rows(place, slots, named):
    def reset(j, carry):
        named[j] = 0
        return carry

    def mark(s, carry):
        here = place(s)

        @pl.when(here >= 0)
        def _():
            named[here % KB] = 1

        return carry

    lax.fori_loop(0, KB, reset, 0)
    lax.fori_loop(0, slots, mark, 0)


def for_wanted(column, named, rcap, action):
    def visit(slot, number):
        wanted = (column(slot) >= 0) & (named[slot // rcap] > 0)

        @pl.when(wanted)
        def _():
            action(slot, number)

        return number + wanted.astype(jnp.int32)

    return lax.fori_loop(0, KB * rcap, visit, 0)


def pack_main(spot, tables, strips, guests, *refs):
    early, late, stage, table, sem_table, named, sem, sem_out = refs[-8:]
    shift = spot[5]
    stop = ALWAYS - shift

    def greet(number, carry):
        pltpu.make_async_copy(guests.at[number], stage.at[number], sem).start()
        return carry

    lax.fori_loop(0, shift, greet, 0)

    def fetch(slot, number):
        @pl.when((number >= AHEAD) & (number < stop))
        def _():
            at = number - AHEAD + shift
            pltpu.make_async_copy(strips.at[slot], stage.at[at], sem).start()

    count = find_wanted(spot, tables, strips, table, sem_table, named, fetch)
    finish_blocks(strips, stage, sem, jnp.maximum(jnp.minimum(count, stop) - AHEAD, 0) + shift)
    hand_over(stage, [(early, 0), (late, early.shape[0])], sem_out)


def pack_ahead(spot, tables, strips, *refs):
    ahead, round_one, round_two, guests, *over = refs[:-6]
    stage, table, sem_table, named, sem, sem_out = refs[-6:]
    lent = spot[6]

    def fetch(slot, number):
        beyond = number - ALWAYS

        @pl.when(number < AHEAD)
        def _():
            pltpu.make_async_copy(strips.at[slot], stage.at[number], sem).start()

        @pl.when((beyond >= 0) & (beyond < LENT))
        def _():
            at = AHEAD + beyond
            pltpu.make_async_copy(strips.at[slot], stage.at[at], sem).start()

        @pl.when(beyond >= lent)
        def _():
            at = AHEAD + LENT + beyond - lent
            pltpu.make_async_copy(strips.at[slot], stage.at[at], sem).start()

    count = find_wanted(spot, tables, strips, table, sem_table, named, fetch)
    beyond = jnp.maximum(count - ALWAYS, 0)
    copied = jnp.minimum(count, AHEAD) + jnp.minimum(beyond, LENT)
    finish_blocks(strips, stage, sem, copied + jnp.maximum(beyond - lent, 0))
    half = round_one.shape[0]
    outs = [(ahead, 0), (round_one, 0), (round_two, half)]
    low = AHEAD
    for out in (guests, *over):
        outs.append((out, low))
        low += out.shape[0]
    hand_over(stage, outs, sem_out)


def find_wanted(spot, tables, strips, table, sem_table, named, action):
    rcap = strips.shape[0] // KB
    table_copy = pltpu.make_async_copy(tables, table, sem_table)
    table_copy.start()
    table_copy.wait()
    mark_rows(places_in(table, spot[0], spot[3]), table.shape[0], named)
    return for_wanted(columns_in(table, rcap, spot[1]), named, rcap, action)


def finish_blocks(source, target, sem, count):
    def finish(number, carry):
        pltpu.make_async_copy(source.at[0], target.at[0], sem).wait()
        return carry

    lax.fori_loop(0, count, finish, 0)


def hand_over(stage, outs, sem_out):
    copies = []
    for i, (out, low) in enumerate(outs):
        here = stage.at[pl.ds(low, out.shape[0])]
        copies.append(pltpu.make_async_copy(here, out, sem_out.at[i]))
        copies[-1].start()
    for copy in copies:
        copy.wait()


def pack(kernel, room, outs, spot, tables, strips, *more):
    size = strips.shape[-1]
    counts = [count for count, _ in outs]
    return pl.pallas_call(
        kernel,
        out_shape=[space((n, size, size), strips.dtype) for n, space in outs],
        grid_spec=pltpu.PrefetchScalarGridSpec(
            num_scalar_prefetch=1,
            grid=(1,),
            in_specs=[ANYWHERE] * (2 + len(more)),
            out_specs=[ANYWHERE] * len(counts),
            scratch_shapes=[
                pltpu.VMEM((room, size, size), strips.dtype),
                pltpu.SMEM(tables.shape, jnp.int32),
                pltpu.SemaphoreType.DMA,
                pltpu.SMEM((KB,), jnp.int32),
                pltpu.SemaphoreType.DMA,
                pltpu.SemaphoreType.DMA((len(counts),)),
            ],
        ),
        compiler_params=pltpu.CompilerParams(vmem_limit_bytes=LIMIT),
        cost_estimate=pl.CostEstimate(
            flops=0, bytes_accessed=4 * sum(counts) * size * size, transcendentals=0
        ),
    )(spot, tables, in_hbm(strips), *more)


def after(values, blocks):
    count = len(blocks)
    return pl.pallas_call(
        lambda *refs: None,
        out_shape=[pltpu.HBM(each.shape, each.dtype) for each in blocks],
        in_specs=[ANYWHERE] * (count + len(values)),
        out_specs=[ANYWHERE] * count,
        input_output_aliases={i: i for i in range(count)},
    )(*blocks, *values)


def by_block_row(place, slots, order, first):
    def reset(i, carry):
        first[i] = 0
        return carry

    def count(s, carry):
        here = place(s)

        @pl.when(here >= 0)
        def _():
            i = here // KB + 2
            first[i] = first[i] + 1

        return carry

    def scan(i, carry):
        first[i] = first[i] + first[i - 1]
        return carry

    def sort(s, carry):
        here = place(s)

        @pl.when(here >= 0)
        def _():
            i = here // KB + 1
            order[first[i]] = s * KB + here % KB
            first[i] = first[i] + 1

        return carry

    lax.fori_loop(0, RB + 2, reset, 0)
    lax.fori_loop(0, slots, count, 0)
    lax.fori_loop(1, RB + 2, scan, 0)
    lax.fori_loop(0, slots, sort, 0)


def clear(right, low):
    def one(j, carry):
        right[j] = jnp.zeros(right.shape[1:], right.dtype)
        return carry

    lax.fori_loop(low, KB, one, 0)


def add_rows(left, right, total, order, first):
    size = left.shape[1]

    def one_row(i, carry):
        row = pl.program_id(0) * GROUP + i
        here = pl.ds(pl.multiple_of(i * size, size), size)

        def add(entry, carry):
            total[here, :] += jnp.dot(
                left[order[entry] // KB], right[order[entry] % KB],
                preferred_element_type=jnp.float32,
            )
            return carry

        return lax.fori_loop(first[row], first[row + 1], add, carry)

    lax.fori_loop(0, GROUP, one_row, 0)


def place_at(right, where):
    size = right.shape[1]
    start = pl.multiple_of((where % NJ) * size, size)
    return right.at[where // NJ, :, pl.ds(start, size)]


def finish_right(source, right, sem, count):
    def finish(number, carry):
        pltpu.make_async_copy(source, place_at(right, 0), sem).wait()
        return carry

    lax.fori_loop(0, count, finish, 0)


def first_kernel(
    rcap, spot, tables, received, strips,
    out, next_order, next_first, next_target,
    left, right, table, sem_table, order, first, named, other, sem_left, sem_right,
):
    slots, size, _ = left.shape

    @pl.when(pl.program_id(0) == 0)
    def _():
        left_copy = pltpu.make_async_copy(received.at[:, pl.ds(0, size)], left, sem_left)
        left_copy.start()
        table_copy = pltpu.make_async_copy(tables, table, sem_table)
        table_copy.start()
        clear(right, 0)
        table_copy.wait()
        place = places_in(table, 0, spot[1])
        column = columns_in(table, rcap, spot[1])
        mark_rows(place, slots, named)

        def fetch(slot, number):
            target = place_at(right, slot // rcap * NJ + column(slot))
            pltpu.make_async_copy(strips.at[slot], target, sem_right).start()

        count = for_wanted(column, named, rcap, fetch)
        by_block_row(place, slots, order, first)

        next_place = places_in(table, spot[0], spot[2])
        next_column = columns_in(table, rcap, spot[4])
        by_block_row(next_place, slots, next_order, next_first)
        mark_rows(next_place, slots, other)

        def note(slot, number):
            next_target[number] = slot // rcap * NJ + next_column(slot)

        next_first[RB + 2] = for_wanted(next_column, other, rcap, note)
        left_copy.wait()
        finish_right(strips.at[0], right, sem_right, count)

    out[...] = jnp.zeros(out.shape, out.dtype)
    add_rows(left, right, out, order, first)


def start_left(shifted, parts, left, on_last, sem):
    size = left.shape[1]
    step = shifted.shape[1] - size
    whole = pltpu.make_async_copy(shifted.at[:, pl.ds(0, size)], left, sem)

    @pl.when(on_last)
    def _():
        for q, part in enumerate([shifted.at[:, pl.ds(size, step)], *parts]):
            pltpu.make_async_copy(part, left.at[:, pl.ds(q * step, step)], sem).start()

    @pl.when(jnp.logical_not(on_last))
    def _():
        whole.start()

    return whole


def start_right(sources, begin, count, target, right, sem):
    clear(right, jnp.where(count > begin, target[begin] // NJ, KB))
    for blocks, low, start, stop in sources:

        def fetch(number, carry):
            pltpu.make_async_copy(
                blocks.at[number - low], place_at(right, target[number]), sem
            ).start()
            return carry

        lax.fori_loop(start, jnp.minimum(count, stop), fetch, 0)


def add_products(row, order, first, left, right, touched, total):
    def add(entry, carry):
        @pl.when(touched[order[entry] % KB] > 0)
        def _():
            total[row] += jnp.dot(
                left[order[entry] // KB], right[order[entry] % KB],
                preferred_element_type=jnp.float32,
            )

        return carry

    lax.fori_loop(first[row], first[row + 1], add, 0)


def mark_targets(target, ranges, marks):
    def reset(j, carry):
        marks[j] = 0
        return carry

    def mark(number, carry):
        marks[target[number] // NJ] = 1
        return carry

    lax.fori_loop(0, KB, reset, 0)
    for begin, end in ranges:
        lax.fori_loop(begin, end, mark, 0)


def mark_open(order, first, touched, open_row):
    def one(row, carry):
        def look(entry, found):
            return jnp.maximum(found, touched[order[entry] % KB])

        open_row[row] = lax.fori_loop(first[row], first[row + 1], look, jnp.int32(0))
        return carry

    lax.fori_loop(0, RB, one, 0)


def strip_of(ref, row, size):
    return ref.at[pl.ds(pl.multiple_of(row * size, size), size)]


def middle_kernel(parts_count, order, first, target, flags, *refs):
    shifted, *parts = refs[: 1 + parts_count]
    (
        ahead, piece, prev, out, rounded, guests, later, open_row,
        hall, sem_in, sem_home,
        left, right, total, short, touched,
        sem_left, sem_right, sem_prev, sem_out,
    ) = refs[1 + parts_count :]
    arrive = pltpu.make_async_copy(piece.at[pl.ds(0, LENT)], hall, sem_in)
    leave = pltpu.make_async_copy(hall, guests, sem_home)
    arrive.start()
    size = left.shape[1]
    count = first[RB + 2]
    shift = flags[1]
    end = AHEAD + PARTS[0] - shift

    def prev_copy(row):
        return pltpu.make_async_copy(strip_of(prev, row, size), total.at[row], sem_prev.at[row])

    def start_prev(row, carry):
        prev_copy(row).start()
        return carry

    lax.fori_loop(0, RB, start_prev, 0)
    whole = start_left(shifted, parts, left, flags[0] > 0, sem_left)
    fetched = jnp.minimum(count, end)
    begin = jnp.where(flags[3] > 0, AHEAD, 0)
    sources = [(ahead, 0, begin, AHEAD), (piece, AHEAD - shift, AHEAD, end)]
    start_right(sources, begin, fetched, target, right, sem_right)
    arrive.wait()
    leave.start()

    mark_targets(target, [(begin, fetched)], touched)
    mark_targets(target, [(0, jnp.minimum(begin, count)), (end, count)], later)
    mark_open(order, first, later, open_row)
    whole.wait()
    finish_right(piece.at[0], right, sem_right, fetched - begin)

    def out_copies(row):
        return (
            pltpu.make_async_copy(total.at[row], strip_of(out, row, size), sem_out.at[row]),
            pltpu.make_async_copy(short.at[row], strip_of(rounded, row, size), sem_out.at[row]),
        )

    def one_row(row, carry):
        open_copy, closed_copy = out_copies(row)
        prev_copy(row).wait()
        add_products(row, order, first, left, right, touched, total)

        @pl.when(open_row[row] > 0)
        def _():
            open_copy.start()

        @pl.when(open_row[row] == 0)
        def _():
            short[row] = total[row].astype(short.dtype)
            closed_copy.start()

        return carry

    def close_row(row, carry):
        open_copy, closed_copy = out_copies(row)

        @pl.when(open_row[row] > 0)
        def _():
            open_copy.wait()

        @pl.when(open_row[row] == 0)
        def _():
            closed_copy.wait()

        return carry

    lax.fori_loop(0, RB, one_row, 0)
    lax.fori_loop(0, RB, close_row, 0)
    leave.wait()


def last_kernel(parts_count, order, first, target, flags, touched, open_row, *refs):
    shifted, *parts = refs[: 1 + parts_count]
    (
        round_one, round_two, piece, back, *over, prev, _, out,
        left, right, total, short,
        sem_left, sem_right, sem_prev, sem_out,
    ) = refs[1 + parts_count :]
    size = left.shape[1]
    count = first[RB + 2]
    shift, lent = flags[1], flags[2]
    begin = AHEAD + PARTS[0] - shift

    def prev_copy(row):
        return pltpu.make_async_copy(strip_of(prev, row, size), total.at[row], sem_prev.at[row])

    def start_prev(row, carry):
        @pl.when(open_row[row] > 0)
        def _():
            prev_copy(row).start()

        return carry

    lax.fori_loop(0, RB, start_prev, 0)
    whole = start_left(shifted, parts, left, flags[0] > 0, sem_left)
    ahead = jnp.where(flags[3] > 0, AHEAD, 0)
    half = round_one.shape[0]
    low = ALWAYS
    sources = [
        (round_one, 0, 0, jnp.minimum(ahead, half)), (round_two, half, half, ahead),
        (piece, begin, begin, low - shift), (back, low, low, low + lent),
    ]
    low = low + lent
    for blocks in over:
        high = low + blocks.shape[0]
        sources.append((blocks, low, low, high))
        low = high
    start_right(sources, jnp.where(ahead > 0, 0, begin), count, target, right, sem_right)

    def out_copy(row):
        return pltpu.make_async_copy(short.at[row], strip_of(out, row, size), sem_out.at[row])

    whole.wait()
    finish_right(
        piece.at[0], right, sem_right,
        jnp.maximum(count - begin, 0) + jnp.minimum(count, ahead),
    )

    def one_row(row, carry):
        @pl.when(open_row[row] > 0)
        def _():
            prev_copy(row).wait()
            add_products(row, order, first, left, right, touched, total)
            short[row] = total[row].astype(short.dtype)
            out_copy(row).start()

        return carry

    def close_row(row, carry):
        @pl.when(open_row[row] > 0)
        def _():
            out_copy(row).wait()

        return carry

    lax.fori_loop(0, RB, one_row, 0)
    lax.fori_loop(0, RB, close_row, 0)


def step_call(kernel, scalars, operands, specs, out_shape, out_specs, scratch, slots, size):
    return pl.pallas_call(
        kernel,
        out_shape=out_shape,
        grid_spec=pltpu.PrefetchScalarGridSpec(
            num_scalar_prefetch=len(scalars),
            grid=(RB // GROUP,),
            in_specs=specs,
            out_specs=out_specs,
            scratch_shapes=[
                pltpu.VMEM((slots, size, size), jnp.bfloat16),
                pltpu.VMEM((KB, size, NJ * size), jnp.bfloat16),
                *scratch,
                pltpu.SemaphoreType.DMA,
                pltpu.SemaphoreType.DMA,
            ],
        ),
        compiler_params=pltpu.CompilerParams(
            dimension_semantics=("arbitrary",), vmem_limit_bytes=LIMIT
        ),
        cost_estimate=pl.CostEstimate(
            flops=2 * 24 * NJ * size * size * size,
            bytes_accessed=16 * 1024 * 1024,
            transcendentals=0,
        ),
    )(*scalars, *operands)


def table_kernel(where_ref, cols_ref, out, where, cols, tile, sems):
    copies = [
        pltpu.make_async_copy(where_ref, where, sems.at[0]),
        pltpu.make_async_copy(cols_ref, cols, sems.at[1]),
    ]
    for copy in copies:
        copy.start()
    rcap, across = cols.shape
    devices = where.shape[-1]
    tile[...] = jnp.zeros(tile.shape, tile.dtype)
    for copy in copies:
        copy.wait()
    for slot in range(rcap):
        tile[pl.ds(0, 1), pl.ds(slot * across, across)] = cols[pl.ds(slot, 1), :]
    for half in range(2):
        row, lane = divmod(half * devices, 128)
        tile[pl.ds(1 + row, 1), pl.ds(lane, devices)] = where[half]

    def fill(device, carry):
        out[device] = tile[...]
        return carry

    lax.fori_loop(0, out.shape[0], fill, 0)


def table_for_all(where, cols):
    devices = where.shape[-1]
    shape = (1 + -(-2 * devices // 128), 128)
    return pl.pallas_call(
        table_kernel,
        out_shape=jax.ShapeDtypeStruct((devices, *shape), jnp.int32),
        in_specs=[ANYWHERE, ANYWHERE],
        scratch_shapes=[
            pltpu.VMEM(where.shape, jnp.int32),
            pltpu.VMEM(cols.shape, jnp.int32),
            pltpu.VMEM(shape, jnp.int32),
            pltpu.SemaphoreType.DMA((2,)),
        ],
        compiler_params=pltpu.CompilerParams(vmem_limit_bytes=LIMIT),
    )(in_hbm(where), in_hbm(cols))


def needed(where_all, cols_all, rows_count, cols_count):
    grid = where_all.reshape(-1, 2, rows_count, cols_count)
    after = jnp.concatenate([grid[:, 0, :, 1:], grid[:, 1, :, :1]], axis=-1)
    columns = jnp.arange(KB, dtype=jnp.int32)
    hit = (after[..., None] >= 0) & (after[..., None] % KB == columns)
    wanted = jnp.any(hit, axis=0).astype(jnp.int32)
    counts = jnp.sum((cols_all >= 0).astype(jnp.int32), axis=1)
    counts = jnp.roll(counts.reshape(rows_count, cols_count, KB), -1, axis=0)
    return jnp.sum(wanted * counts, axis=-1)


def swapped(value):
    return lax.ppermute(value, "col", [(i, i ^ 1) for i in range(lax.axis_size("col"))])


def local(a_send, a_where, b_strips, b_cols):
    size = a_send.shape[-1]
    rows_count = lax.axis_size("row")
    cols_count = lax.axis_size("col")
    devices = rows_count * cols_count
    both = ("row", "col")
    row_index = lax.axis_index("row")
    col_index = lax.axis_index("col")
    rcap = b_strips.shape[3]
    last = cols_count - 1

    by_slot = jnp.swapaxes(b_cols, 2, 3).reshape(rcap, KB)
    tables = lax.all_to_all(
        table_for_all(a_where, by_slot), both, split_axis=0, concat_axis=0, tiled=True
    )
    after_col = (col_index + 1) % cols_count
    after_half = (col_index + 1) // cols_count
    row_before = (row_index + rows_count - 1) % rows_count
    row_after = (row_index + 1) % rows_count
    needs = needed(
        tables[:, 1:].reshape(devices, -1)[:, : 2 * devices],
        tables[:, 0].reshape(devices, rcap, KB), rows_count, cols_count,
    )
    room = ALWAYS - jnp.flip(needs.reshape(rows_count, -1, 2), -1).reshape(needs.shape)
    lent = jnp.maximum(jnp.minimum(jnp.minimum(needs - ALWAYS, room), LENT), 0)
    most = jnp.max(needs - lent)

    def lent_to(row, col):
        return lax.dynamic_slice(lent, (row, col), (1, 1))[0, 0]

    spot = jnp.stack([
        after_half,
        row_index * cols_count + col_index,
        row_index * cols_count + after_col,
        row_before * cols_count + after_col,
        row_after * cols_count + col_index,
        lent_to(row_before, col_index ^ 1),
        lent_to(row_before, col_index),
    ]).astype(jnp.int32)

    wrapped = a_send[1, 0].reshape(rows_count, cols_count, size, size)[:, 0]
    wrapped = wrapped.reshape(devices, size // cols_count, size)
    received = lax.all_to_all(
        jnp.concatenate([a_send[0, 0], wrapped], axis=1),
        both, split_axis=0, concat_axis=0, tiled=True,
    )

    def to_row_before(blocks):
        return lax.ppermute(
            blocks, "row", [(i, (i - 1) % rows_count) for i in range(rows_count)]
        )

    strips = b_strips.reshape(KB * rcap, size, size)
    half = AHEAD // 2
    spare = (LENT, *OVER)
    ahead, round_one, round_two, guests, *over = pack(
        pack_ahead, AHEAD + sum(spare),
        [(AHEAD, pltpu.VMEM), *((n, pltpu.HBM) for n in (half, half, *spare))],
        spot, tables, strips,
    )
    ahead = lax.ppermute(ahead, "row", [(i, i - 1) for i in range(1, rows_count)])
    begin, extra = ALWAYS, []
    for blocks in over:
        extra.append(lax.cond(most > begin, to_row_before, lambda same: same, blocks))
        begin += blocks.shape[0]
    early, late = pack(
        pack_main, sum(PARTS), [(n, pltpu.HBM) for n in PARTS],
        spot, tables, strips, swapped(guests),
        *(blocks[0, :16] for blocks in extra),
    )
    early, late = map(to_row_before, after([received[0, :16], ahead[0, :16]], [early, late]))

    shifted = lax.ppermute(
        received, "col", [(i, (i - 1) % cols_count) for i in range(cols_count)]
    )
    part = received[:, size:]
    parts = [lax.ppermute(part, "col", [(i, last)]) for i in range(1, last)] + [part]

    wide = NJ * size
    strip = pl.BlockSpec((GROUP * size, wide), lambda i, *_: (i, 0))
    begun, order, first, target = step_call(
        functools.partial(first_kernel, rcap),
        (spot,), (tables, received, in_hbm(strips)), [ANYWHERE, ANYWHERE, ANYWHERE],
        [
            pltpu.HBM((RB * size, wide), jnp.float32),
            jax.ShapeDtypeStruct((devices,), jnp.int32),
            jax.ShapeDtypeStruct((RB + 3,), jnp.int32),
            jax.ShapeDtypeStruct((KB * rcap,), jnp.int32),
        ],
        [strip, IN_SMEM, IN_SMEM, IN_SMEM],
        [
            pltpu.SMEM(tables.shape, jnp.int32),
            pltpu.SemaphoreType.DMA,
            pltpu.SMEM((devices,), jnp.int32),
            pltpu.SMEM((RB + 2,), jnp.int32),
            pltpu.SMEM((KB,), jnp.int32),
            pltpu.SMEM((KB,), jnp.int32),
        ],
        devices, size,
    )

    end_row = rows_count - 1
    round_one, round_two = after([order], [round_one, round_two])
    round_one = lax.ppermute(round_one, "row", [(0, end_row)])
    round_two = lax.ppermute(round_two, "row", [(0, end_row - 1)])
    round_two = lax.ppermute(round_two, "row", [(end_row - 1, end_row)])

    on_last = (col_index == last).astype(jnp.int32)
    on_round = (row_index == end_row).astype(jnp.int32)
    lent_here = [lent_to(row_index, col_index ^ 1), lent_to(row_index, col_index)]
    scalars = (order, first, target, jnp.stack([on_last, *lent_here, on_round]))
    lefts = (shifted, *parts)

    def finish_call(kernel, scalars, operands, out_shape, out_specs, scratch, marks, aliases):
        return pl.pallas_call(
            kernel,
            out_shape=out_shape,
            grid_spec=pltpu.PrefetchScalarGridSpec(
                num_scalar_prefetch=len(scalars),
                grid=(1,),
                in_specs=[ANYWHERE] * len(operands),
                out_specs=out_specs,
                scratch_shapes=[
                    *scratch,
                    pltpu.VMEM((devices, size, size), jnp.bfloat16),
                    pltpu.VMEM((KB, size, wide), jnp.bfloat16),
                    pltpu.VMEM((RB, size, wide), jnp.float32),
                    pltpu.VMEM((RB, size, wide), jnp.bfloat16),
                    *marks,
                    pltpu.SemaphoreType.DMA,
                    pltpu.SemaphoreType.DMA,
                    pltpu.SemaphoreType.DMA((RB,)),
                    pltpu.SemaphoreType.DMA((RB,)),
                ],
            ),
            input_output_aliases=aliases,
            compiler_params=pltpu.CompilerParams(vmem_limit_bytes=LIMIT),
            cost_estimate=pl.CostEstimate(
                flops=2 * 16 * NJ * size * size * size,
                bytes_accessed=12 * 1024 * 1024,
                transcendentals=0,
            ),
        )(*scalars, *operands)

    begun, rounded, guests, later, open_row = finish_call(
        functools.partial(middle_kernel, len(parts)), scalars,
        (*lefts, ahead, early, in_hbm(begun)),
        [
            pltpu.HBM((RB * size, wide), jnp.float32),
            pltpu.HBM((RB * size, wide), jnp.bfloat16),
            pltpu.HBM((LENT, size, size), jnp.bfloat16),
            jax.ShapeDtypeStruct((KB,), jnp.int32),
            jax.ShapeDtypeStruct((RB,), jnp.int32),
        ],
        [ANYWHERE, ANYWHERE, ANYWHERE, IN_SMEM, IN_SMEM],
        [
            pltpu.VMEM((LENT, size, size), jnp.bfloat16),
            pltpu.SemaphoreType.DMA,
            pltpu.SemaphoreType.DMA,
        ],
        [pltpu.SMEM((KB,), jnp.int32)], {},
    )
    back = swapped(guests)

    operands = (*lefts, round_one, round_two, late, back, *extra, in_hbm(begun), rounded)
    scalars = (*scalars, later, open_row)
    return finish_call(
        functools.partial(last_kernel, len(parts)), scalars, operands,
        jax.ShapeDtypeStruct((RB * size, wide), jnp.bfloat16),
        ANYWHERE, [], [], {len(scalars) + len(operands) - 1: 0},
    )


def solution(mesh):
    placed = (
        P(None, ("row", "col"), None, None, None),
        P(None, ("row", "col"), None),
        P("row", "col", None, None, None, None),
        P("row", "col", None, None),
    )
    return jax.shard_map(
        local, mesh=mesh, in_specs=placed, out_specs=P("row", "col"), check_vma=False
    )
```

```python
import functools

import jax
import jax.numpy as jnp
from jax import lax
from jax.experimental import pallas as pl
from jax.experimental.pallas import tpu as pltpu
from jax.sharding import PartitionSpec as P

RB = 16
KB = 16
NJ = 8
PARTS = (64, 24, 8, 8, 24)
ALWAYS = PARTS[0] + PARTS[1]
LENT = 16
GROUP = 4
IN_SMEM = pl.BlockSpec(memory_space=pltpu.SMEM)
ANYWHERE = pl.BlockSpec(memory_space=pl.ANY)
LIMIT = 24 * 1024 * 1024


def in_hbm(value):
    return pltpu.with_memory_space_constraint(value, pltpu.HBM)


def places_in(table, half, owner):
    at = half * table.shape[0] + owner
    return lambda source: table[source, 1 + at // 128, at % 128]


def columns_in(table, rcap, device):
    return lambda slot: table[device, 0, slot % rcap * KB + slot // rcap]


def mark_rows(place, slots, named):
    def reset(j, carry):
        named[j] = 0
        return carry

    def mark(s, carry):
        here = place(s)

        @pl.when(here >= 0)
        def _():
            named[here % KB] = 1

        return carry

    lax.fori_loop(0, KB, reset, 0)
    lax.fori_loop(0, slots, mark, 0)


def for_wanted(column, named, rcap, action):
    def visit(slot, number):
        wanted = (column(slot) >= 0) & (named[slot // rcap] > 0)

        @pl.when(wanted)
        def _():
            action(slot, number)

        return number + wanted.astype(jnp.int32)

    return lax.fori_loop(0, KB * rcap, visit, 0)


def pack_main(spot, tables, strips, guests, *refs):
    early, late, stage, table, sem_table, named, sem, sem_out = refs[-8:]
    shift = spot[5]
    stop = stage.shape[0] - shift

    def greet(number, carry):
        pltpu.make_async_copy(guests.at[number], stage.at[number], sem).start()
        return carry

    lax.fori_loop(0, shift, greet, 0)

    def fetch(slot, number):
        @pl.when(number < stop)
        def _():
            pltpu.make_async_copy(strips.at[slot], stage.at[number + shift], sem).start()

    count = find_wanted(spot, tables, strips, table, sem_table, named, fetch)
    finish_blocks(strips, stage, sem, jnp.minimum(count, stop) + shift)
    hand_over(stage, [early, late], sem_out)


def pack_spare(spot, tables, strips, guests, *refs):
    *over, stage, table, sem_table, named, sem, sem_out = refs
    lent = spot[6]

    def fetch(slot, number):
        beyond = number - ALWAYS

        @pl.when((beyond >= 0) & (beyond < LENT))
        def _():
            pltpu.make_async_copy(strips.at[slot], stage.at[beyond], sem).start()

        @pl.when(beyond >= lent)
        def _():
            at = LENT + beyond - lent
            pltpu.make_async_copy(strips.at[slot], stage.at[at], sem).start()

    count = find_wanted(spot, tables, strips, table, sem_table, named, fetch)
    beyond = jnp.maximum(count - ALWAYS, 0)
    copied = jnp.minimum(beyond, LENT) + jnp.maximum(beyond - lent, 0)
    finish_blocks(strips, stage, sem, copied)
    hand_over(stage, [guests, *over], sem_out)


def find_wanted(spot, tables, strips, table, sem_table, named, action):
    rcap = strips.shape[0] // KB
    table_copy = pltpu.make_async_copy(tables, table, sem_table)
    table_copy.start()
    table_copy.wait()
    mark_rows(places_in(table, spot[0], spot[3]), table.shape[0], named)
    return for_wanted(columns_in(table, rcap, spot[1]), named, rcap, action)


def finish_blocks(source, target, sem, count):
    def finish(number, carry):
        pltpu.make_async_copy(source.at[0], target.at[0], sem).wait()
        return carry

    lax.fori_loop(0, count, finish, 0)


def hand_over(stage, outs, sem_out):
    copies, low = [], 0
    for i, out in enumerate(outs):
        here = stage.at[pl.ds(low, out.shape[0])]
        copies.append(pltpu.make_async_copy(here, out, sem_out.at[i]))
        copies[-1].start()
        low += out.shape[0]
    for copy in copies:
        copy.wait()


def pack(kernel, counts, spot, tables, strips, *more):
    size = strips.shape[-1]
    return pl.pallas_call(
        kernel,
        out_shape=[pltpu.HBM((n, size, size), strips.dtype) for n in counts],
        grid_spec=pltpu.PrefetchScalarGridSpec(
            num_scalar_prefetch=1,
            grid=(1,),
            in_specs=[ANYWHERE] * (2 + len(more)),
            out_specs=[ANYWHERE] * len(counts),
            scratch_shapes=[
                pltpu.VMEM((sum(counts), size, size), strips.dtype),
                pltpu.SMEM(tables.shape, jnp.int32),
                pltpu.SemaphoreType.DMA,
                pltpu.SMEM((KB,), jnp.int32),
                pltpu.SemaphoreType.DMA,
                pltpu.SemaphoreType.DMA((len(counts),)),
            ],
        ),
        compiler_params=pltpu.CompilerParams(vmem_limit_bytes=LIMIT),
        cost_estimate=pl.CostEstimate(
            flops=0, bytes_accessed=4 * sum(counts) * size * size, transcendentals=0
        ),
    )(spot, tables, in_hbm(strips), *more)


def after(value, blocks):
    count = len(blocks)
    return pl.pallas_call(
        lambda *refs: None,
        out_shape=[pltpu.HBM(each.shape, each.dtype) for each in blocks],
        in_specs=[ANYWHERE] * (count + 1),
        out_specs=[ANYWHERE] * count,
        input_output_aliases={i: i for i in range(count)},
        compiler_params=pltpu.CompilerParams(vmem_limit_bytes=LIMIT),
    )(*blocks, value)


def by_block_row(place, slots, order, first):
    def reset(i, carry):
        first[i] = 0
        return carry

    def count(s, carry):
        here = place(s)

        @pl.when(here >= 0)
        def _():
            i = here // KB + 2
            first[i] = first[i] + 1

        return carry

    def scan(i, carry):
        first[i] = first[i] + first[i - 1]
        return carry

    def sort(s, carry):
        here = place(s)

        @pl.when(here >= 0)
        def _():
            i = here // KB + 1
            order[first[i]] = s * KB + here % KB
            first[i] = first[i] + 1

        return carry

    lax.fori_loop(0, RB + 2, reset, 0)
    lax.fori_loop(0, slots, count, 0)
    lax.fori_loop(1, RB + 2, scan, 0)
    lax.fori_loop(0, slots, sort, 0)


def clear(right, low):
    def one(j, carry):
        right[j] = jnp.zeros(right.shape[1:], right.dtype)
        return carry

    lax.fori_loop(low, KB, one, 0)


def add_product(total, left, right, pair):
    slot, column = pair // KB, pair % KB
    wide = right.shape[-1]
    step = 2 * left.shape[-1]
    for low in range(0, wide, step):
        here = pl.ds(low, step)
        total[:, here] += jnp.dot(
            left[slot], right[column, :, here], preferred_element_type=jnp.float32
        )


def add_rows(left, right, total, order, first):
    size = left.shape[1]

    def one_row(i, carry):
        row = pl.program_id(0) * GROUP + i
        here = pl.ds(pl.multiple_of(i * size, size), size)

        def add(entry, carry):
            add_product(total.at[here], left, right, order[entry])
            return carry

        return lax.fori_loop(first[row], first[row + 1], add, carry)

    lax.fori_loop(0, GROUP, one_row, 0)


def place_at(right, where):
    size = right.shape[1]
    start = pl.multiple_of((where % NJ) * size, size)
    return right.at[where // NJ, :, pl.ds(start, size)]


def finish_right(source, right, sem, count):
    def finish(number, carry):
        pltpu.make_async_copy(source, place_at(right, 0), sem).wait()
        return carry

    lax.fori_loop(0, count, finish, 0)


def first_kernel(
    rcap, spot, tables, received, strips,
    out, next_order, next_first, next_target,
    left, right, table, sem_table, order, first, named, other, sem_left, sem_right,
):
    slots, size, _ = left.shape

    @pl.when(pl.program_id(0) == 0)
    def _():
        left_copy = pltpu.make_async_copy(received.at[:, pl.ds(0, size)], left, sem_left)
        left_copy.start()
        table_copy = pltpu.make_async_copy(tables, table, sem_table)
        table_copy.start()
        clear(right, 0)
        table_copy.wait()
        place = places_in(table, 0, spot[1])
        column = columns_in(table, rcap, spot[1])
        mark_rows(place, slots, named)

        def fetch(slot, number):
            target = place_at(right, slot // rcap * NJ + column(slot))
            pltpu.make_async_copy(strips.at[slot], target, sem_right).start()

        count = for_wanted(column, named, rcap, fetch)
        by_block_row(place, slots, order, first)

        next_place = places_in(table, spot[0], spot[2])
        next_column = columns_in(table, rcap, spot[4])
        by_block_row(next_place, slots, next_order, next_first)
        mark_rows(next_place, slots, other)

        def note(slot, number):
            next_target[number] = slot // rcap * NJ + next_column(slot)

        next_first[RB + 2] = for_wanted(next_column, other, rcap, note)
        left_copy.wait()
        finish_right(strips.at[0], right, sem_right, count)

    out[...] = jnp.zeros(out.shape, out.dtype)
    add_rows(left, right, out, order, first)


def start_left(shifted, parts, left, on_last, sem):
    size = left.shape[1]
    step = shifted.shape[1] - size
    whole = pltpu.make_async_copy(shifted.at[:, pl.ds(0, size)], left, sem)

    @pl.when(on_last)
    def _():
        for q, part in enumerate([shifted.at[:, pl.ds(size, step)], *parts]):
            pltpu.make_async_copy(part, left.at[:, pl.ds(q * step, step)], sem).start()

    @pl.when(jnp.logical_not(on_last))
    def _():
        whole.start()

    return whole


def start_right(sources, begin, count, target, right, sem):
    clear(right, jnp.where(count > begin, target[begin] // NJ, KB))
    for blocks, low, start, stop in sources:

        def fetch(number, carry):
            pltpu.make_async_copy(
                blocks.at[number - low], place_at(right, target[number]), sem
            ).start()
            return carry

        lax.fori_loop(start, jnp.minimum(count, stop), fetch, 0)


def add_products(row, order, first, left, right, touched, total):
    def add(entry, carry):
        @pl.when(touched[order[entry] % KB] > 0)
        def _():
            add_product(total.at[row], left, right, order[entry])

        return carry

    lax.fori_loop(first[row], first[row + 1], add, 0)


def mark_targets(target, begin, end, marks):
    def reset(j, carry):
        marks[j] = 0
        return carry

    def mark(number, carry):
        marks[target[number] // NJ] = 1
        return carry

    lax.fori_loop(0, KB, reset, 0)
    lax.fori_loop(begin, end, mark, 0)


def mark_open(order, first, touched, open_row):
    def one(row, carry):
        def look(entry, found):
            return jnp.maximum(found, touched[order[entry] % KB])

        open_row[row] = lax.fori_loop(first[row], first[row + 1], look, jnp.int32(0))
        return carry

    lax.fori_loop(0, RB, one, 0)


def strip_of(ref, row, size):
    return ref.at[pl.ds(pl.multiple_of(row * size, size), size)]


def middle_kernel(parts_count, order, first, target, flags, *refs):
    shifted, *parts = refs[: 1 + parts_count]
    (
        piece, prev, out, rounded, guests, later, open_row,
        hall, sem_in, sem_home,
        left, right, total, short, touched,
        sem_left, sem_right, sem_prev, sem_out,
    ) = refs[1 + parts_count :]
    arrive = pltpu.make_async_copy(piece.at[pl.ds(0, LENT)], hall, sem_in)
    leave = pltpu.make_async_copy(hall, guests, sem_home)
    arrive.start()
    size = left.shape[1]
    count = first[RB + 2]
    shift = flags[1]
    end = piece.shape[0] - shift

    def prev_copy(row):
        return pltpu.make_async_copy(strip_of(prev, row, size), total.at[row], sem_prev.at[row])

    def start_prev(row, carry):
        prev_copy(row).start()
        return carry

    lax.fori_loop(0, RB, start_prev, 0)
    whole = start_left(shifted, parts, left, flags[0] > 0, sem_left)
    fetched = jnp.minimum(count, end)
    start_right([(piece, -shift, 0, end)], 0, fetched, target, right, sem_right)
    arrive.wait()
    leave.start()

    mark_targets(target, 0, fetched, touched)
    mark_targets(target, end, count, later)
    mark_open(order, first, later, open_row)
    whole.wait()
    finish_right(piece.at[0], right, sem_right, fetched)

    def out_copies(row):
        return (
            pltpu.make_async_copy(total.at[row], strip_of(out, row, size), sem_out.at[row]),
            pltpu.make_async_copy(short.at[row], strip_of(rounded, row, size), sem_out.at[row]),
        )

    def one_row(row, carry):
        open_copy, closed_copy = out_copies(row)
        prev_copy(row).wait()
        add_products(row, order, first, left, right, touched, total)

        @pl.when(open_row[row] > 0)
        def _():
            open_copy.start()

        @pl.when(open_row[row] == 0)
        def _():
            short[row] = total[row].astype(short.dtype)
            closed_copy.start()

        return carry

    def close_row(row, carry):
        open_copy, closed_copy = out_copies(row)

        @pl.when(open_row[row] > 0)
        def _():
            open_copy.wait()

        @pl.when(open_row[row] == 0)
        def _():
            closed_copy.wait()

        return carry

    lax.fori_loop(0, RB, one_row, 0)
    lax.fori_loop(0, RB, close_row, 0)
    leave.wait()


def last_kernel(parts_count, order, first, target, flags, touched, open_row, *refs):
    shifted, *parts = refs[: 1 + parts_count]
    (
        piece, back, *over, prev, _, out,
        left, right, total, short,
        sem_left, sem_right, sem_prev, sem_out,
    ) = refs[1 + parts_count :]
    size = left.shape[1]
    count = first[RB + 2]
    shift, lent = flags[1], flags[2]
    begin = PARTS[0] - shift

    def prev_copy(row):
        return pltpu.make_async_copy(strip_of(prev, row, size), total.at[row], sem_prev.at[row])

    def start_prev(row, carry):
        @pl.when(open_row[row] > 0)
        def _():
            prev_copy(row).start()

        return carry

    lax.fori_loop(0, RB, start_prev, 0)
    whole = start_left(shifted, parts, left, flags[0] > 0, sem_left)
    low = ALWAYS
    sources = [(piece, begin, begin, low - shift), (back, low, low, low + lent)]
    low = low + lent
    for blocks in over:
        high = low + blocks.shape[0]
        sources.append((blocks, low, low, high))
        low = high
    start_right(sources, begin, count, target, right, sem_right)

    def out_copy(row):
        return pltpu.make_async_copy(short.at[row], strip_of(out, row, size), sem_out.at[row])

    whole.wait()
    finish_right(piece.at[0], right, sem_right, count - begin)

    def one_row(row, carry):
        @pl.when(open_row[row] > 0)
        def _():
            prev_copy(row).wait()
            add_products(row, order, first, left, right, touched, total)
            short[row] = total[row].astype(short.dtype)
            out_copy(row).start()

        return carry

    def close_row(row, carry):
        @pl.when(open_row[row] > 0)
        def _():
            out_copy(row).wait()

        return carry

    lax.fori_loop(0, RB, one_row, 0)
    lax.fori_loop(0, RB, close_row, 0)


def step_call(kernel, scalars, operands, specs, out_shape, out_specs, scratch, slots, size):
    return pl.pallas_call(
        kernel,
        out_shape=out_shape,
        grid_spec=pltpu.PrefetchScalarGridSpec(
            num_scalar_prefetch=len(scalars),
            grid=(RB // GROUP,),
            in_specs=specs,
            out_specs=out_specs,
            scratch_shapes=[
                pltpu.VMEM((slots, size, size), jnp.bfloat16),
                pltpu.VMEM((KB, size, NJ * size), jnp.bfloat16),
                *scratch,
                pltpu.SemaphoreType.DMA,
                pltpu.SemaphoreType.DMA,
            ],
        ),
        compiler_params=pltpu.CompilerParams(
            dimension_semantics=("arbitrary",), vmem_limit_bytes=LIMIT
        ),
        cost_estimate=pl.CostEstimate(
            flops=2 * 24 * NJ * size * size * size,
            bytes_accessed=16 * 1024 * 1024,
            transcendentals=0,
        ),
    )(*scalars, *operands)


def table_kernel(where_ref, cols_ref, out, where, cols, tile, sems):
    copies = [
        pltpu.make_async_copy(where_ref, where, sems.at[0]),
        pltpu.make_async_copy(cols_ref, cols, sems.at[1]),
    ]
    for copy in copies:
        copy.start()
    rcap, across = cols.shape
    devices = where.shape[-1]
    tile[...] = jnp.zeros(tile.shape, tile.dtype)
    for copy in copies:
        copy.wait()
    for slot in range(rcap):
        tile[pl.ds(0, 1), pl.ds(slot * across, across)] = cols[pl.ds(slot, 1), :]
    for half in range(2):
        row, lane = divmod(half * devices, 128)
        tile[pl.ds(1 + row, 1), pl.ds(lane, devices)] = where[half]

    def fill(device, carry):
        out[device] = tile[...]
        return carry

    lax.fori_loop(0, out.shape[0], fill, 0)


def table_for_all(where, cols):
    devices = where.shape[-1]
    shape = (1 + -(-2 * devices // 128), 128)
    return pl.pallas_call(
        table_kernel,
        out_shape=jax.ShapeDtypeStruct((devices, *shape), jnp.int32),
        in_specs=[ANYWHERE, ANYWHERE],
        scratch_shapes=[
            pltpu.VMEM(where.shape, jnp.int32),
            pltpu.VMEM(cols.shape, jnp.int32),
            pltpu.VMEM(shape, jnp.int32),
            pltpu.SemaphoreType.DMA((2,)),
        ],
        compiler_params=pltpu.CompilerParams(vmem_limit_bytes=LIMIT),
    )(in_hbm(where), in_hbm(cols))


def needed(where_all, cols_all, rows_count, cols_count):
    grid = where_all.reshape(-1, 2, rows_count, cols_count)
    after = jnp.concatenate([grid[:, 0, :, 1:], grid[:, 1, :, :1]], axis=-1)
    columns = jnp.arange(KB, dtype=jnp.int32)
    hit = (after[..., None] >= 0) & (after[..., None] % KB == columns)
    wanted = jnp.any(hit, axis=0).astype(jnp.int32)
    counts = jnp.sum((cols_all >= 0).astype(jnp.int32), axis=1)
    counts = jnp.roll(counts.reshape(rows_count, cols_count, KB), -1, axis=0)
    return jnp.sum(wanted * counts, axis=-1)


def swapped(value):
    return lax.ppermute(value, "col", [(i, i ^ 1) for i in range(lax.axis_size("col"))])


def local(a_send, a_where, b_strips, b_cols):
    size = a_send.shape[-1]
    rows_count = lax.axis_size("row")
    cols_count = lax.axis_size("col")
    devices = rows_count * cols_count
    both = ("row", "col")
    row_index = lax.axis_index("row")
    col_index = lax.axis_index("col")
    rcap = b_strips.shape[3]
    last = cols_count - 1

    by_slot = jnp.swapaxes(b_cols, 2, 3).reshape(rcap, KB)
    tables = lax.all_to_all(
        table_for_all(a_where, by_slot), both, split_axis=0, concat_axis=0, tiled=True
    )
    after_col = (col_index + 1) % cols_count
    after_half = (col_index + 1) // cols_count
    row_before = (row_index + rows_count - 1) % rows_count
    row_after = (row_index + 1) % rows_count
    needs = needed(
        tables[:, 1:].reshape(devices, -1)[:, : 2 * devices],
        tables[:, 0].reshape(devices, rcap, KB), rows_count, cols_count,
    )
    room = ALWAYS - jnp.flip(needs.reshape(rows_count, -1, 2), -1).reshape(needs.shape)
    lent = jnp.maximum(jnp.minimum(jnp.minimum(needs - ALWAYS, room), LENT), 0)
    most = jnp.max(needs - lent)

    def lent_to(row, col):
        return lax.dynamic_slice(lent, (row, col), (1, 1))[0, 0]

    spot = jnp.stack([
        after_half,
        row_index * cols_count + col_index,
        row_index * cols_count + after_col,
        row_before * cols_count + after_col,
        row_after * cols_count + col_index,
        lent_to(row_before, col_index ^ 1),
        lent_to(row_before, col_index),
    ]).astype(jnp.int32)

    wrapped = a_send[1, 0].reshape(rows_count, cols_count, size, size)[:, 0]
    wrapped = wrapped.reshape(devices, size // cols_count, size)
    received = lax.all_to_all(
        jnp.concatenate([a_send[0, 0], wrapped], axis=1),
        both, split_axis=0, concat_axis=0, tiled=True,
    )

    def to_row_before(blocks):
        return lax.ppermute(
            blocks, "row", [(i, (i - 1) % rows_count) for i in range(rows_count)]
        )

    strips = b_strips.reshape(KB * rcap, size, size)
    guests, *over = pack(pack_spare, (LENT, *PARTS[2:]), spot, tables, strips)
    begin, extra = ALWAYS, []
    for blocks in over:
        extra.append(lax.cond(most > begin, to_row_before, lambda same: same, blocks))
        begin += blocks.shape[0]
    early, late = pack(
        pack_main, PARTS[:2], spot, tables, strips, swapped(guests),
        *(blocks[0, :16] for blocks in extra),
    )
    early, late = map(to_row_before, after(received, [early, late]))

    shifted = lax.ppermute(
        received, "col", [(i, (i - 1) % cols_count) for i in range(cols_count)]
    )
    part = received[:, size:]
    parts = [lax.ppermute(part, "col", [(i, last)]) for i in range(1, last)] + [part]

    wide = NJ * size
    strip = pl.BlockSpec((GROUP * size, wide), lambda i, *_: (i, 0))
    begun, order, first, target = step_call(
        functools.partial(first_kernel, rcap),
        (spot,), (tables, received, in_hbm(strips)), [ANYWHERE, ANYWHERE, ANYWHERE],
        [
            pltpu.HBM((RB * size, wide), jnp.float32),
            jax.ShapeDtypeStruct((devices,), jnp.int32),
            jax.ShapeDtypeStruct((RB + 3,), jnp.int32),
            jax.ShapeDtypeStruct((KB * rcap,), jnp.int32),
        ],
        [strip, IN_SMEM, IN_SMEM, IN_SMEM],
        [
            pltpu.SMEM(tables.shape, jnp.int32),
            pltpu.SemaphoreType.DMA,
            pltpu.SMEM((devices,), jnp.int32),
            pltpu.SMEM((RB + 2,), jnp.int32),
            pltpu.SMEM((KB,), jnp.int32),
            pltpu.SMEM((KB,), jnp.int32),
        ],
        devices, size,
    )

    on_last = (col_index == last).astype(jnp.int32)
    lent_here = [lent_to(row_index, col_index ^ 1), lent_to(row_index, col_index)]
    scalars = (order, first, target, jnp.stack([on_last, *lent_here]))
    lefts = (shifted, *parts)

    def finish_call(kernel, scalars, operands, out_shape, out_specs, scratch, marks, aliases):
        return pl.pallas_call(
            kernel,
            out_shape=out_shape,
            grid_spec=pltpu.PrefetchScalarGridSpec(
                num_scalar_prefetch=len(scalars),
                grid=(1,),
                in_specs=[ANYWHERE] * len(operands),
                out_specs=out_specs,
                scratch_shapes=[
                    *scratch,
                    pltpu.VMEM((devices, size, size), jnp.bfloat16),
                    pltpu.VMEM((KB, size, wide), jnp.bfloat16),
                    pltpu.VMEM((RB, size, wide), jnp.float32),
                    pltpu.VMEM((RB, size, wide), jnp.bfloat16),
                    *marks,
                    pltpu.SemaphoreType.DMA,
                    pltpu.SemaphoreType.DMA,
                    pltpu.SemaphoreType.DMA((RB,)),
                    pltpu.SemaphoreType.DMA((RB,)),
                ],
            ),
            input_output_aliases=aliases,
            compiler_params=pltpu.CompilerParams(vmem_limit_bytes=LIMIT),
            cost_estimate=pl.CostEstimate(
                flops=2 * 16 * NJ * size * size * size,
                bytes_accessed=12 * 1024 * 1024,
                transcendentals=0,
            ),
        )(*scalars, *operands)

    begun, rounded, guests, later, open_row = finish_call(
        functools.partial(middle_kernel, len(parts)), scalars,
        (*lefts, early, in_hbm(begun)),
        [
            pltpu.HBM((RB * size, wide), jnp.float32),
            pltpu.HBM((RB * size, wide), jnp.bfloat16),
            pltpu.HBM((LENT, size, size), jnp.bfloat16),
            jax.ShapeDtypeStruct((KB,), jnp.int32),
            jax.ShapeDtypeStruct((RB,), jnp.int32),
        ],
        [ANYWHERE, ANYWHERE, ANYWHERE, IN_SMEM, IN_SMEM],
        [
            pltpu.VMEM((LENT, size, size), jnp.bfloat16),
            pltpu.SemaphoreType.DMA,
            pltpu.SemaphoreType.DMA,
        ],
        [pltpu.SMEM((KB,), jnp.int32)], {},
    )
    back = swapped(guests)

    operands = (*lefts, late, back, *extra, in_hbm(begun), rounded)
    scalars = (*scalars, later, open_row)
    return finish_call(
        functools.partial(last_kernel, len(parts)), scalars, operands,
        jax.ShapeDtypeStruct((RB * size, wide), jnp.bfloat16),
        ANYWHERE, [], [], {len(scalars) + len(operands) - 1: 0},
    )


def solution(mesh):
    placed = (
        P(None, ("row", "col"), None, None, None),
        P(None, ("row", "col"), None),
        P("row", "col", None, None, None, None),
        P("row", "col", None, None),
    )
    return jax.shard_map(
        local, mesh=mesh, in_specs=placed, out_specs=P("row", "col"), check_vma=False
    )
```

```python
import functools

import jax
import jax.numpy as jnp
from jax import lax
from jax.experimental import pallas as pl
from jax.experimental.pallas import tpu as pltpu
from jax.sharding import PartitionSpec as P

RB = 16
KB = 16
NJ = 8
PARTS = (70, 22, 8, 8, 20)
ALWAYS = PARTS[0] + PARTS[1]
LENT = 16
GROUP = 4
IN_SMEM = pl.BlockSpec(memory_space=pltpu.SMEM)
ANYWHERE = pl.BlockSpec(memory_space=pl.ANY)
LIMIT = 24 * 1024 * 1024


def in_hbm(value):
    return pltpu.with_memory_space_constraint(value, pltpu.HBM)


def places_in(table, half, owner):
    at = half * table.shape[0] + owner
    return lambda source: table[source, 1 + at // 128, at % 128]


def columns_in(table, rcap, device):
    return lambda slot: table[device, 0, slot % rcap * KB + slot // rcap]


def mark_rows(place, slots, named):
    def reset(j, carry):
        named[j] = 0
        return carry

    def mark(s, carry):
        here = place(s)

        @pl.when(here >= 0)
        def _():
            named[here % KB] = 1

        return carry

    lax.fori_loop(0, KB, reset, 0)
    lax.fori_loop(0, slots, mark, 0)


def for_wanted(column, named, rcap, action):
    def visit(slot, number):
        wanted = (column(slot) >= 0) & (named[slot // rcap] > 0)

        @pl.when(wanted)
        def _():
            action(slot, number)

        return number + wanted.astype(jnp.int32)

    return lax.fori_loop(0, KB * rcap, visit, 0)


def pack_main(spot, tables, strips, guests, *refs):
    early, late, stage, table, sem_table, named, sem, sem_out = refs[-8:]
    shift = spot[5]
    stop = stage.shape[0] - shift

    def greet(number, carry):
        pltpu.make_async_copy(guests.at[number], stage.at[number], sem).start()
        return carry

    lax.fori_loop(0, shift, greet, 0)

    def fetch(slot, number):
        @pl.when(number < stop)
        def _():
            pltpu.make_async_copy(strips.at[slot], stage.at[number + shift], sem).start()

    count = find_wanted(spot, tables, strips, table, sem_table, named, fetch)
    finish_blocks(strips, stage, sem, jnp.minimum(count, stop) + shift)
    hand_over(stage, [early, late], sem_out)


def pack_spare(spot, tables, strips, guests, *refs):
    *over, stage, table, sem_table, named, sem, sem_out = refs
    lent = spot[6]

    def fetch(slot, number):
        beyond = number - ALWAYS

        @pl.when((beyond >= 0) & (beyond < LENT))
        def _():
            pltpu.make_async_copy(strips.at[slot], stage.at[beyond], sem).start()

        @pl.when(beyond >= lent)
        def _():
            at = LENT + beyond - lent
            pltpu.make_async_copy(strips.at[slot], stage.at[at], sem).start()

    count = find_wanted(spot, tables, strips, table, sem_table, named, fetch)
    beyond = jnp.maximum(count - ALWAYS, 0)
    copied = jnp.minimum(beyond, LENT) + jnp.maximum(beyond - lent, 0)
    finish_blocks(strips, stage, sem, copied)
    hand_over(stage, [guests, *over], sem_out)


def find_wanted(spot, tables, strips, table, sem_table, named, action):
    rcap = strips.shape[0] // KB
    table_copy = pltpu.make_async_copy(tables, table, sem_table)
    table_copy.start()
    table_copy.wait()
    mark_rows(places_in(table, spot[0], spot[3]), table.shape[0], named)
    return for_wanted(columns_in(table, rcap, spot[1]), named, rcap, action)


def finish_blocks(source, target, sem, count):
    def finish(number, carry):
        pltpu.make_async_copy(source.at[0], target.at[0], sem).wait()
        return carry

    lax.fori_loop(0, count, finish, 0)


def hand_over(stage, outs, sem_out):
    copies, low = [], 0
    for i, out in enumerate(outs):
        here = stage.at[pl.ds(low, out.shape[0])]
        copies.append(pltpu.make_async_copy(here, out, sem_out.at[i]))
        copies[-1].start()
        low += out.shape[0]
    for copy in copies:
        copy.wait()


def pack(kernel, counts, spot, tables, strips, *more):
    size = strips.shape[-1]
    return pl.pallas_call(
        kernel,
        out_shape=[pltpu.HBM((n, size, size), strips.dtype) for n in counts],
        grid_spec=pltpu.PrefetchScalarGridSpec(
            num_scalar_prefetch=1,
            grid=(1,),
            in_specs=[ANYWHERE] * (2 + len(more)),
            out_specs=[ANYWHERE] * len(counts),
            scratch_shapes=[
                pltpu.VMEM((sum(counts), size, size), strips.dtype),
                pltpu.SMEM(tables.shape, jnp.int32),
                pltpu.SemaphoreType.DMA,
                pltpu.SMEM((KB,), jnp.int32),
                pltpu.SemaphoreType.DMA,
                pltpu.SemaphoreType.DMA((len(counts),)),
            ],
        ),
        compiler_params=pltpu.CompilerParams(vmem_limit_bytes=LIMIT),
        cost_estimate=pl.CostEstimate(
            flops=0, bytes_accessed=4 * sum(counts) * size * size, transcendentals=0
        ),
    )(spot, tables, in_hbm(strips), *more)


def after(value, blocks):
    count = len(blocks)
    return pl.pallas_call(
        lambda *refs: None,
        out_shape=[pltpu.HBM(each.shape, each.dtype) for each in blocks],
        in_specs=[ANYWHERE] * (count + 1),
        out_specs=[ANYWHERE] * count,
        input_output_aliases={i: i for i in range(count)},
        compiler_params=pltpu.CompilerParams(vmem_limit_bytes=LIMIT),
    )(*blocks, value)


def by_block_row(place, slots, order, first):
    def reset(i, carry):
        first[i] = 0
        return carry

    def count(s, carry):
        here = place(s)

        @pl.when(here >= 0)
        def _():
            i = here // KB + 2
            first[i] = first[i] + 1

        return carry

    def scan(i, carry):
        first[i] = first[i] + first[i - 1]
        return carry

    def sort(s, carry):
        here = place(s)

        @pl.when(here >= 0)
        def _():
            i = here // KB + 1
            order[first[i]] = s * KB + here % KB
            first[i] = first[i] + 1

        return carry

    lax.fori_loop(0, RB + 2, reset, 0)
    lax.fori_loop(0, slots, count, 0)
    lax.fori_loop(1, RB + 2, scan, 0)
    lax.fori_loop(0, slots, sort, 0)


def clear(right, low):
    def one(j, carry):
        right[j] = jnp.zeros(right.shape[1:], right.dtype)
        return carry

    lax.fori_loop(low, KB, one, 0)


def add_product(total, left, right, pair):
    slot, column = pair // KB, pair % KB
    wide = right.shape[-1]
    step = 2 * left.shape[-1]
    for low in range(0, wide, step):
        here = pl.ds(low, step)
        total[:, here] += jnp.dot(
            left[slot], right[column, :, here], preferred_element_type=jnp.float32
        )


def add_rows(left, right, total, order, first):
    size = left.shape[1]

    def one_row(i, carry):
        row = pl.program_id(0) * GROUP + i
        here = pl.ds(pl.multiple_of(i * size, size), size)

        def add(entry, carry):
            add_product(total.at[here], left, right, order[entry])
            return carry

        return lax.fori_loop(first[row], first[row + 1], add, carry)

    lax.fori_loop(0, GROUP, one_row, 0)


def place_at(right, where):
    size = right.shape[1]
    start = pl.multiple_of((where % NJ) * size, size)
    return right.at[where // NJ, :, pl.ds(start, size)]


def finish_right(source, right, sem, count):
    def finish(number, carry):
        pltpu.make_async_copy(source, place_at(right, 0), sem).wait()
        return carry

    lax.fori_loop(0, count, finish, 0)


def first_kernel(
    rcap, spot, tables, received, strips,
    out, next_order, next_first, next_target,
    left, right, table, sem_table, order, first, named, other, sem_left, sem_right,
):
    slots, size, _ = left.shape

    @pl.when(pl.program_id(0) == 0)
    def _():
        left_copy = pltpu.make_async_copy(received.at[:, pl.ds(0, size)], left, sem_left)
        left_copy.start()
        table_copy = pltpu.make_async_copy(tables, table, sem_table)
        table_copy.start()
        clear(right, 0)
        table_copy.wait()
        place = places_in(table, 0, spot[1])
        column = columns_in(table, rcap, spot[1])
        mark_rows(place, slots, named)

        def fetch(slot, number):
            target = place_at(right, slot // rcap * NJ + column(slot))
            pltpu.make_async_copy(strips.at[slot], target, sem_right).start()

        count = for_wanted(column, named, rcap, fetch)
        by_block_row(place, slots, order, first)

        next_place = places_in(table, spot[0], spot[2])
        next_column = columns_in(table, rcap, spot[4])
        by_block_row(next_place, slots, next_order, next_first)
        mark_rows(next_place, slots, other)

        def note(slot, number):
            next_target[number] = slot // rcap * NJ + next_column(slot)

        next_first[RB + 2] = for_wanted(next_column, other, rcap, note)
        left_copy.wait()
        finish_right(strips.at[0], right, sem_right, count)

    out[...] = jnp.zeros(out.shape, out.dtype)
    add_rows(left, right, out, order, first)


def start_left(shifted, parts, left, on_last, sem):
    size = left.shape[1]
    step = shifted.shape[1] - size
    whole = pltpu.make_async_copy(shifted.at[:, pl.ds(0, size)], left, sem)

    @pl.when(on_last)
    def _():
        for q, part in enumerate([shifted.at[:, pl.ds(size, step)], *parts]):
            pltpu.make_async_copy(part, left.at[:, pl.ds(q * step, step)], sem).start()

    @pl.when(jnp.logical_not(on_last))
    def _():
        whole.start()

    return whole


def start_right(sources, begin, count, target, right, sem):
    clear(right, jnp.where(count > begin, target[begin] // NJ, KB))
    for blocks, low, start, stop in sources:

        def fetch(number, carry):
            pltpu.make_async_copy(
                blocks.at[number - low], place_at(right, target[number]), sem
            ).start()
            return carry

        lax.fori_loop(start, jnp.minimum(count, stop), fetch, 0)


def add_products(row, order, first, left, right, touched, total):
    def add(entry, carry):
        @pl.when(touched[order[entry] % KB] > 0)
        def _():
            add_product(total.at[row], left, right, order[entry])

        return carry

    lax.fori_loop(first[row], first[row + 1], add, 0)


def mark_targets(target, begin, end, marks):
    def reset(j, carry):
        marks[j] = 0
        return carry

    def mark(number, carry):
        marks[target[number] // NJ] = 1
        return carry

    lax.fori_loop(0, KB, reset, 0)
    lax.fori_loop(begin, end, mark, 0)


def mark_open(order, first, touched, open_row):
    def one(row, carry):
        def look(entry, found):
            return jnp.maximum(found, touched[order[entry] % KB])

        open_row[row] = lax.fori_loop(first[row], first[row + 1], look, jnp.int32(0))
        return carry

    lax.fori_loop(0, RB, one, 0)


def strip_of(ref, row, size):
    return ref.at[pl.ds(pl.multiple_of(row * size, size), size)]


def middle_kernel(parts_count, order, first, target, flags, *refs):
    shifted, *parts = refs[: 1 + parts_count]
    (
        piece, prev, out, rounded, guests, later, open_row,
        hall, sem_in, sem_home,
        left, right, total, short, touched,
        sem_left, sem_right, sem_prev, sem_out,
    ) = refs[1 + parts_count :]
    arrive = pltpu.make_async_copy(piece.at[pl.ds(0, LENT)], hall, sem_in)
    leave = pltpu.make_async_copy(hall, guests, sem_home)
    arrive.start()
    size = left.shape[1]
    count = first[RB + 2]
    shift = flags[1]
    end = piece.shape[0] - shift

    def prev_copy(row):
        return pltpu.make_async_copy(strip_of(prev, row, size), total.at[row], sem_prev.at[row])

    def start_prev(row, carry):
        prev_copy(row).start()
        return carry

    lax.fori_loop(0, RB, start_prev, 0)
    whole = start_left(shifted, parts, left, flags[0] > 0, sem_left)
    fetched = jnp.minimum(count, end)
    start_right([(piece, -shift, 0, end)], 0, fetched, target, right, sem_right)
    arrive.wait()
    leave.start()

    mark_targets(target, 0, fetched, touched)
    mark_targets(target, end, count, later)
    mark_open(order, first, later, open_row)
    whole.wait()
    finish_right(piece.at[0], right, sem_right, fetched)

    def out_copies(row):
        return (
            pltpu.make_async_copy(total.at[row], strip_of(out, row, size), sem_out.at[row]),
            pltpu.make_async_copy(short.at[row], strip_of(rounded, row, size), sem_out.at[row]),
        )

    def one_row(row, carry):
        open_copy, closed_copy = out_copies(row)
        prev_copy(row).wait()
        add_products(row, order, first, left, right, touched, total)

        @pl.when(open_row[row] > 0)
        def _():
            open_copy.start()

        @pl.when(open_row[row] == 0)
        def _():
            short[row] = total[row].astype(short.dtype)
            closed_copy.start()

        return carry

    def close_row(row, carry):
        open_copy, closed_copy = out_copies(row)

        @pl.when(open_row[row] > 0)
        def _():
            open_copy.wait()

        @pl.when(open_row[row] == 0)
        def _():
            closed_copy.wait()

        return carry

    lax.fori_loop(0, RB, one_row, 0)
    lax.fori_loop(0, RB, close_row, 0)
    leave.wait()


def last_kernel(parts_count, order, first, target, flags, touched, open_row, *refs):
    shifted, *parts = refs[: 1 + parts_count]
    (
        piece, back, *over, prev, _, out,
        left, right, total, short,
        sem_left, sem_right, sem_prev, sem_out,
    ) = refs[1 + parts_count :]
    size = left.shape[1]
    count = first[RB + 2]
    shift, lent = flags[1], flags[2]
    begin = PARTS[0] - shift

    def prev_copy(row):
        return pltpu.make_async_copy(strip_of(prev, row, size), total.at[row], sem_prev.at[row])

    def start_prev(row, carry):
        @pl.when(open_row[row] > 0)
        def _():
            prev_copy(row).start()

        return carry

    lax.fori_loop(0, RB, start_prev, 0)
    whole = start_left(shifted, parts, left, flags[0] > 0, sem_left)
    low = ALWAYS
    sources = [(piece, begin, begin, low - shift), (back, low, low, low + lent)]
    low = low + lent
    for blocks in over:
        high = low + blocks.shape[0]
        sources.append((blocks, low, low, high))
        low = high
    start_right(sources, begin, count, target, right, sem_right)

    def out_copy(row):
        return pltpu.make_async_copy(short.at[row], strip_of(out, row, size), sem_out.at[row])

    whole.wait()
    finish_right(piece.at[0], right, sem_right, count - begin)

    def one_row(row, carry):
        @pl.when(open_row[row] > 0)
        def _():
            prev_copy(row).wait()
            add_products(row, order, first, left, right, touched, total)
            short[row] = total[row].astype(short.dtype)
            out_copy(row).start()

        return carry

    def close_row(row, carry):
        @pl.when(open_row[row] > 0)
        def _():
            out_copy(row).wait()

        return carry

    lax.fori_loop(0, RB, one_row, 0)
    lax.fori_loop(0, RB, close_row, 0)


def step_call(kernel, scalars, operands, specs, out_shape, out_specs, scratch, slots, size):
    return pl.pallas_call(
        kernel,
        out_shape=out_shape,
        grid_spec=pltpu.PrefetchScalarGridSpec(
            num_scalar_prefetch=len(scalars),
            grid=(RB // GROUP,),
            in_specs=specs,
            out_specs=out_specs,
            scratch_shapes=[
                pltpu.VMEM((slots, size, size), jnp.bfloat16),
                pltpu.VMEM((KB, size, NJ * size), jnp.bfloat16),
                *scratch,
                pltpu.SemaphoreType.DMA,
                pltpu.SemaphoreType.DMA,
            ],
        ),
        compiler_params=pltpu.CompilerParams(
            dimension_semantics=("arbitrary",), vmem_limit_bytes=LIMIT
        ),
        cost_estimate=pl.CostEstimate(
            flops=2 * 24 * NJ * size * size * size,
            bytes_accessed=16 * 1024 * 1024,
            transcendentals=0,
        ),
    )(*scalars, *operands)


def table_kernel(where_ref, cols_ref, out, where, cols, tile, sems):
    copies = [
        pltpu.make_async_copy(where_ref, where, sems.at[0]),
        pltpu.make_async_copy(cols_ref, cols, sems.at[1]),
    ]
    for copy in copies:
        copy.start()
    rcap, across = cols.shape
    devices = where.shape[-1]
    tile[...] = jnp.zeros(tile.shape, tile.dtype)
    for copy in copies:
        copy.wait()
    for slot in range(rcap):
        tile[pl.ds(0, 1), pl.ds(slot * across, across)] = cols[pl.ds(slot, 1), :]
    for half in range(2):
        row, lane = divmod(half * devices, 128)
        tile[pl.ds(1 + row, 1), pl.ds(lane, devices)] = where[half]

    def fill(device, carry):
        out[device] = tile[...]
        return carry

    lax.fori_loop(0, out.shape[0], fill, 0)


def table_for_all(where, cols):
    devices = where.shape[-1]
    shape = (1 + -(-2 * devices // 128), 128)
    return pl.pallas_call(
        table_kernel,
        out_shape=jax.ShapeDtypeStruct((devices, *shape), jnp.int32),
        in_specs=[ANYWHERE, ANYWHERE],
        scratch_shapes=[
            pltpu.VMEM(where.shape, jnp.int32),
            pltpu.VMEM(cols.shape, jnp.int32),
            pltpu.VMEM(shape, jnp.int32),
            pltpu.SemaphoreType.DMA((2,)),
        ],
        compiler_params=pltpu.CompilerParams(vmem_limit_bytes=LIMIT),
    )(in_hbm(where), in_hbm(cols))


def needed(where_all, cols_all, rows_count, cols_count):
    grid = where_all.reshape(-1, 2, rows_count, cols_count)
    after = jnp.concatenate([grid[:, 0, :, 1:], grid[:, 1, :, :1]], axis=-1)
    columns = jnp.arange(KB, dtype=jnp.int32)
    hit = (after[..., None] >= 0) & (after[..., None] % KB == columns)
    wanted = jnp.any(hit, axis=0).astype(jnp.int32)
    counts = jnp.sum((cols_all >= 0).astype(jnp.int32), axis=1)
    counts = jnp.roll(counts.reshape(rows_count, cols_count, KB), -1, axis=0)
    return jnp.sum(wanted * counts, axis=-1)


def swapped(value):
    return lax.ppermute(value, "col", [(i, i ^ 1) for i in range(lax.axis_size("col"))])


def local(a_send, a_where, b_strips, b_cols):
    size = a_send.shape[-1]
    rows_count = lax.axis_size("row")
    cols_count = lax.axis_size("col")
    devices = rows_count * cols_count
    both = ("row", "col")
    row_index = lax.axis_index("row")
    col_index = lax.axis_index("col")
    rcap = b_strips.shape[3]
    last = cols_count - 1

    by_slot = jnp.swapaxes(b_cols, 2, 3).reshape(rcap, KB)
    tables = lax.all_to_all(
        table_for_all(a_where, by_slot), both, split_axis=0, concat_axis=0, tiled=True
    )
    after_col = (col_index + 1) % cols_count
    after_half = (col_index + 1) // cols_count
    row_before = (row_index + rows_count - 1) % rows_count
    row_after = (row_index + 1) % rows_count
    needs = needed(
        tables[:, 1:].reshape(devices, -1)[:, : 2 * devices],
        tables[:, 0].reshape(devices, rcap, KB), rows_count, cols_count,
    )
    room = ALWAYS - jnp.flip(needs.reshape(rows_count, -1, 2), -1).reshape(needs.shape)
    lent = jnp.maximum(jnp.minimum(jnp.minimum(needs - ALWAYS, room), LENT), 0)
    most = jnp.max(needs - lent)

    def lent_to(row, col):
        return lax.dynamic_slice(lent, (row, col), (1, 1))[0, 0]

    spot = jnp.stack([
        after_half,
        row_index * cols_count + col_index,
        row_index * cols_count + after_col,
        row_before * cols_count + after_col,
        row_after * cols_count + col_index,
        lent_to(row_before, col_index ^ 1),
        lent_to(row_before, col_index),
    ]).astype(jnp.int32)

    wrapped = a_send[1, 0].reshape(rows_count, cols_count, size, size)[:, 0]
    wrapped = wrapped.reshape(devices, size // cols_count, size)
    received = lax.all_to_all(
        jnp.concatenate([a_send[0, 0], wrapped], axis=1),
        both, split_axis=0, concat_axis=0, tiled=True,
    )

    def to_row_before(blocks):
        return lax.ppermute(
            blocks, "row", [(i, (i - 1) % rows_count) for i in range(rows_count)]
        )

    strips = b_strips.reshape(KB * rcap, size, size)
    guests, *over = pack(pack_spare, (LENT, *PARTS[2:]), spot, tables, strips)
    begin, extra = ALWAYS, []
    for blocks in over:
        extra.append(lax.cond(most > begin, to_row_before, lambda same: same, blocks))
        begin += blocks.shape[0]
    early, late = pack(
        pack_main, PARTS[:2], spot, tables, strips, swapped(guests),
        *(blocks[0, :16] for blocks in extra),
    )
    early, late = map(to_row_before, after(received, [early, late]))

    shifted = lax.ppermute(
        received, "col", [(i, (i - 1) % cols_count) for i in range(cols_count)]
    )
    part = received[:, size:]
    parts = [lax.ppermute(part, "col", [(i, last)]) for i in range(1, last)] + [part]

    wide = NJ * size
    strip = pl.BlockSpec((GROUP * size, wide), lambda i, *_: (i, 0))
    begun, order, first, target = step_call(
        functools.partial(first_kernel, rcap),
        (spot,), (tables, received, in_hbm(strips)), [ANYWHERE, ANYWHERE, ANYWHERE],
        [
            pltpu.HBM((RB * size, wide), jnp.float32),
            jax.ShapeDtypeStruct((devices,), jnp.int32),
            jax.ShapeDtypeStruct((RB + 3,), jnp.int32),
            jax.ShapeDtypeStruct((KB * rcap,), jnp.int32),
        ],
        [strip, IN_SMEM, IN_SMEM, IN_SMEM],
        [
            pltpu.SMEM(tables.shape, jnp.int32),
            pltpu.SemaphoreType.DMA,
            pltpu.SMEM((devices,), jnp.int32),
            pltpu.SMEM((RB + 2,), jnp.int32),
            pltpu.SMEM((KB,), jnp.int32),
            pltpu.SMEM((KB,), jnp.int32),
        ],
        devices, size,
    )

    on_last = (col_index == last).astype(jnp.int32)
    lent_here = [lent_to(row_index, col_index ^ 1), lent_to(row_index, col_index)]
    scalars = (order, first, target, jnp.stack([on_last, *lent_here]))
    lefts = (shifted, *parts)

    def finish_call(kernel, scalars, operands, out_shape, out_specs, scratch, marks, aliases):
        return pl.pallas_call(
            kernel,
            out_shape=out_shape,
            grid_spec=pltpu.PrefetchScalarGridSpec(
                num_scalar_prefetch=len(scalars),
                grid=(1,),
                in_specs=[ANYWHERE] * len(operands),
                out_specs=out_specs,
                scratch_shapes=[
                    *scratch,
                    pltpu.VMEM((devices, size, size), jnp.bfloat16),
                    pltpu.VMEM((KB, size, wide), jnp.bfloat16),
                    pltpu.VMEM((RB, size, wide), jnp.float32),
                    pltpu.VMEM((RB, size, wide), jnp.bfloat16),
                    *marks,
                    pltpu.SemaphoreType.DMA,
                    pltpu.SemaphoreType.DMA,
                    pltpu.SemaphoreType.DMA((RB,)),
                    pltpu.SemaphoreType.DMA((RB,)),
                ],
            ),
            input_output_aliases=aliases,
            compiler_params=pltpu.CompilerParams(vmem_limit_bytes=LIMIT),
            cost_estimate=pl.CostEstimate(
                flops=2 * 16 * NJ * size * size * size,
                bytes_accessed=12 * 1024 * 1024,
                transcendentals=0,
            ),
        )(*scalars, *operands)

    begun, rounded, guests, later, open_row = finish_call(
        functools.partial(middle_kernel, len(parts)), scalars,
        (*lefts, early, in_hbm(begun)),
        [
            pltpu.HBM((RB * size, wide), jnp.float32),
            pltpu.HBM((RB * size, wide), jnp.bfloat16),
            pltpu.HBM((LENT, size, size), jnp.bfloat16),
            jax.ShapeDtypeStruct((KB,), jnp.int32),
            jax.ShapeDtypeStruct((RB,), jnp.int32),
        ],
        [ANYWHERE, ANYWHERE, ANYWHERE, IN_SMEM, IN_SMEM],
        [
            pltpu.VMEM((LENT, size, size), jnp.bfloat16),
            pltpu.SemaphoreType.DMA,
            pltpu.SemaphoreType.DMA,
        ],
        [pltpu.SMEM((KB,), jnp.int32)], {},
    )
    back = swapped(guests)

    operands = (*lefts, late, back, *extra, in_hbm(begun), rounded)
    scalars = (*scalars, later, open_row)
    return finish_call(
        functools.partial(last_kernel, len(parts)), scalars, operands,
        jax.ShapeDtypeStruct((RB * size, wide), jnp.bfloat16),
        ANYWHERE, [], [], {len(scalars) + len(operands) - 1: 0},
    )


def solution(mesh):
    placed = (
        P(None, ("row", "col"), None, None, None),
        P(None, ("row", "col"), None),
        P("row", "col", None, None, None, None),
        P("row", "col", None, None),
    )
    return jax.shard_map(
        local, mesh=mesh, in_specs=placed, out_specs=P("row", "col"), check_vma=False
    )
```

```python
import functools

import jax
import jax.numpy as jnp
from jax import lax
from jax.experimental import pallas as pl
from jax.experimental.pallas import tpu as pltpu
from jax.sharding import PartitionSpec as P

RB = 16
KB = 16
NJ = 8
PARTS = (66, 26, 8, 8, 20)
ALWAYS = PARTS[0] + PARTS[1]
LENT = 16
GROUP = 4
IN_SMEM = pl.BlockSpec(memory_space=pltpu.SMEM)
ANYWHERE = pl.BlockSpec(memory_space=pl.ANY)
LIMIT = 24 * 1024 * 1024


def in_hbm(value):
    return pltpu.with_memory_space_constraint(value, pltpu.HBM)


def places_in(table, half, owner):
    at = half * table.shape[0] + owner
    return lambda source: table[source, 1 + at // 128, at % 128]


def columns_in(table, rcap, device):
    return lambda slot: table[device, 0, slot % rcap * KB + slot // rcap]


def mark_rows(place, slots, named):
    def reset(j, carry):
        named[j] = 0
        return carry

    def mark(s, carry):
        here = place(s)

        @pl.when(here >= 0)
        def _():
            named[here % KB] = 1

        return carry

    lax.fori_loop(0, KB, reset, 0)
    lax.fori_loop(0, slots, mark, 0)


def for_wanted(column, named, rcap, action):
    def visit(slot, number):
        wanted = (column(slot) >= 0) & (named[slot // rcap] > 0)

        @pl.when(wanted)
        def _():
            action(slot, number)

        return number + wanted.astype(jnp.int32)

    return lax.fori_loop(0, KB * rcap, visit, 0)


def pack_main(spot, tables, strips, guests, *refs):
    early, late, stage, table, sem_table, named, sem, sem_out = refs[-8:]
    shift = spot[5]
    stop = stage.shape[0] - shift

    def greet(number, carry):
        pltpu.make_async_copy(guests.at[number], stage.at[number], sem).start()
        return carry

    lax.fori_loop(0, shift, greet, 0)

    def fetch(slot, number):
        @pl.when(number < stop)
        def _():
            pltpu.make_async_copy(strips.at[slot], stage.at[number + shift], sem).start()

    count = find_wanted(spot, tables, strips, table, sem_table, named, fetch)
    finish_blocks(strips, stage, sem, jnp.minimum(count, stop) + shift)
    hand_over(stage, [early, late], sem_out)


def pack_spare(spot, tables, strips, guests, *refs):
    *over, stage, table, sem_table, named, sem, sem_out = refs
    lent = spot[6]

    def fetch(slot, number):
        beyond = number - ALWAYS

        @pl.when((beyond >= 0) & (beyond < LENT))
        def _():
            pltpu.make_async_copy(strips.at[slot], stage.at[beyond], sem).start()

        @pl.when(beyond >= lent)
        def _():
            at = LENT + beyond - lent
            pltpu.make_async_copy(strips.at[slot], stage.at[at], sem).start()

    count = find_wanted(spot, tables, strips, table, sem_table, named, fetch)
    beyond = jnp.maximum(count - ALWAYS, 0)
    copied = jnp.minimum(beyond, LENT) + jnp.maximum(beyond - lent, 0)
    finish_blocks(strips, stage, sem, copied)
    hand_over(stage, [guests, *over], sem_out)


def find_wanted(spot, tables, strips, table, sem_table, named, action):
    rcap = strips.shape[0] // KB
    table_copy = pltpu.make_async_copy(tables, table, sem_table)
    table_copy.start()
    table_copy.wait()
    mark_rows(places_in(table, spot[0], spot[3]), table.shape[0], named)
    return for_wanted(columns_in(table, rcap, spot[1]), named, rcap, action)


def finish_blocks(source, target, sem, count):
    def finish(number, carry):
        pltpu.make_async_copy(source.at[0], target.at[0], sem).wait()
        return carry

    lax.fori_loop(0, count, finish, 0)


def hand_over(stage, outs, sem_out):
    copies, low = [], 0
    for i, out in enumerate(outs):
        here = stage.at[pl.ds(low, out.shape[0])]
        copies.append(pltpu.make_async_copy(here, out, sem_out.at[i]))
        copies[-1].start()
        low += out.shape[0]
    for copy in copies:
        copy.wait()


def pack(kernel, counts, spot, tables, strips, *more):
    size = strips.shape[-1]
    return pl.pallas_call(
        kernel,
        out_shape=[pltpu.HBM((n, size, size), strips.dtype) for n in counts],
        grid_spec=pltpu.PrefetchScalarGridSpec(
            num_scalar_prefetch=1,
            grid=(1,),
            in_specs=[ANYWHERE] * (2 + len(more)),
            out_specs=[ANYWHERE] * len(counts),
            scratch_shapes=[
                pltpu.VMEM((sum(counts), size, size), strips.dtype),
                pltpu.SMEM(tables.shape, jnp.int32),
                pltpu.SemaphoreType.DMA,
                pltpu.SMEM((KB,), jnp.int32),
                pltpu.SemaphoreType.DMA,
                pltpu.SemaphoreType.DMA((len(counts),)),
            ],
        ),
        compiler_params=pltpu.CompilerParams(vmem_limit_bytes=LIMIT),
        cost_estimate=pl.CostEstimate(
            flops=0, bytes_accessed=4 * sum(counts) * size * size, transcendentals=0
        ),
    )(spot, tables, in_hbm(strips), *more)


def after(value, blocks):
    count = len(blocks)
    return pl.pallas_call(
        lambda *refs: None,
        out_shape=[pltpu.HBM(each.shape, each.dtype) for each in blocks],
        in_specs=[ANYWHERE] * (count + 1),
        out_specs=[ANYWHERE] * count,
        input_output_aliases={i: i for i in range(count)},
        compiler_params=pltpu.CompilerParams(vmem_limit_bytes=LIMIT),
    )(*blocks, value)


def by_block_row(place, slots, order, first):
    def reset(i, carry):
        first[i] = 0
        return carry

    def count(s, carry):
        here = place(s)

        @pl.when(here >= 0)
        def _():
            i = here // KB + 2
            first[i] = first[i] + 1

        return carry

    def scan(i, carry):
        first[i] = first[i] + first[i - 1]
        return carry

    def sort(s, carry):
        here = place(s)

        @pl.when(here >= 0)
        def _():
            i = here // KB + 1
            order[first[i]] = s * KB + here % KB
            first[i] = first[i] + 1

        return carry

    lax.fori_loop(0, RB + 2, reset, 0)
    lax.fori_loop(0, slots, count, 0)
    lax.fori_loop(1, RB + 2, scan, 0)
    lax.fori_loop(0, slots, sort, 0)


def clear(right, low):
    def one(j, carry):
        right[j] = jnp.zeros(right.shape[1:], right.dtype)
        return carry

    lax.fori_loop(low, KB, one, 0)


def add_product(total, left, right, pair):
    slot, column = pair // KB, pair % KB
    wide = right.shape[-1]
    step = 2 * left.shape[-1]
    for low in range(0, wide, step):
        here = pl.ds(low, step)
        total[:, here] += jnp.dot(
            left[slot], right[column, :, here], preferred_element_type=jnp.float32
        )


def add_rows(left, right, total, order, first):
    size = left.shape[1]

    def one_row(i, carry):
        row = pl.program_id(0) * GROUP + i
        here = pl.ds(pl.multiple_of(i * size, size), size)

        def add(entry, carry):
            add_product(total.at[here], left, right, order[entry])
            return carry

        return lax.fori_loop(first[row], first[row + 1], add, carry)

    lax.fori_loop(0, GROUP, one_row, 0)


def place_at(right, where):
    size = right.shape[1]
    start = pl.multiple_of((where % NJ) * size, size)
    return right.at[where // NJ, :, pl.ds(start, size)]


def finish_right(source, right, sem, count):
    def finish(number, carry):
        pltpu.make_async_copy(source, place_at(right, 0), sem).wait()
        return carry

    lax.fori_loop(0, count, finish, 0)


def first_kernel(
    rcap, spot, tables, received, strips,
    out, next_order, next_first, next_target,
    left, right, table, sem_table, order, first, named, other, sem_left, sem_right,
):
    slots, size, _ = left.shape

    @pl.when(pl.program_id(0) == 0)
    def _():
        left_copy = pltpu.make_async_copy(received, left, sem_left)
        left_copy.start()
        table_copy = pltpu.make_async_copy(tables, table, sem_table)
        table_copy.start()
        clear(right, 0)
        table_copy.wait()
        place = places_in(table, 0, spot[1])
        column = columns_in(table, rcap, spot[1])
        mark_rows(place, slots, named)

        def fetch(slot, number):
            target = place_at(right, slot // rcap * NJ + column(slot))
            pltpu.make_async_copy(strips.at[slot], target, sem_right).start()

        count = for_wanted(column, named, rcap, fetch)
        by_block_row(place, slots, order, first)

        next_place = places_in(table, spot[0], spot[2])
        next_column = columns_in(table, rcap, spot[4])
        by_block_row(next_place, slots, next_order, next_first)
        mark_rows(next_place, slots, other)

        def note(slot, number):
            next_target[number] = slot // rcap * NJ + next_column(slot)

        next_first[RB + 2] = for_wanted(next_column, other, rcap, note)
        left_copy.wait()
        finish_right(strips.at[0], right, sem_right, count)

    out[...] = jnp.zeros(out.shape, out.dtype)
    add_rows(left, right, out, order, first)


def start_left(shifted, parts, left, on_last, sem):
    step = left.shape[1] // len(parts)
    whole = pltpu.make_async_copy(shifted, left, sem)

    @pl.when(on_last)
    def _():
        for q, part in enumerate(parts):
            pltpu.make_async_copy(part, left.at[:, pl.ds(q * step, step)], sem).start()

    @pl.when(jnp.logical_not(on_last))
    def _():
        whole.start()

    return whole


def start_right(sources, begin, count, target, right, sem):
    clear(right, jnp.where(count > begin, target[begin] // NJ, KB))
    for blocks, low, start, stop in sources:

        def fetch(number, carry):
            pltpu.make_async_copy(
                blocks.at[number - low], place_at(right, target[number]), sem
            ).start()
            return carry

        lax.fori_loop(start, jnp.minimum(count, stop), fetch, 0)


def add_products(row, order, first, left, right, touched, total):
    def add(entry, carry):
        @pl.when(touched[order[entry] % KB] > 0)
        def _():
            add_product(total.at[row], left, right, order[entry])

        return carry

    lax.fori_loop(first[row], first[row + 1], add, 0)


def mark_targets(target, begin, end, marks):
    def reset(j, carry):
        marks[j] = 0
        return carry

    def mark(number, carry):
        marks[target[number] // NJ] = 1
        return carry

    lax.fori_loop(0, KB, reset, 0)
    lax.fori_loop(begin, end, mark, 0)


def mark_open(order, first, touched, open_row):
    def one(row, carry):
        def look(entry, found):
            return jnp.maximum(found, touched[order[entry] % KB])

        open_row[row] = lax.fori_loop(first[row], first[row + 1], look, jnp.int32(0))
        return carry

    lax.fori_loop(0, RB, one, 0)


def strip_of(ref, row, size):
    return ref.at[pl.ds(pl.multiple_of(row * size, size), size)]


def middle_kernel(parts_count, order, first, target, flags, *refs):
    shifted, *parts = refs[: 1 + parts_count]
    (
        piece, prev, out, rounded, guests, later, open_row,
        hall, sem_in, sem_home,
        left, right, total, short, touched,
        sem_left, sem_right, sem_prev, sem_out,
    ) = refs[1 + parts_count :]
    arrive = pltpu.make_async_copy(piece.at[pl.ds(0, LENT)], hall, sem_in)
    leave = pltpu.make_async_copy(hall, guests, sem_home)
    arrive.start()
    size = left.shape[1]
    count = first[RB + 2]
    shift = flags[1]
    end = piece.shape[0] - shift

    def prev_copy(row):
        return pltpu.make_async_copy(strip_of(prev, row, size), total.at[row], sem_prev.at[row])

    def start_prev(row, carry):
        prev_copy(row).start()
        return carry

    lax.fori_loop(0, RB, start_prev, 0)
    whole = start_left(shifted, parts, left, flags[0] > 0, sem_left)
    fetched = jnp.minimum(count, end)
    start_right([(piece, -shift, 0, end)], 0, fetched, target, right, sem_right)
    arrive.wait()
    leave.start()

    mark_targets(target, 0, fetched, touched)
    mark_targets(target, end, count, later)
    mark_open(order, first, later, open_row)
    whole.wait()
    finish_right(piece.at[0], right, sem_right, fetched)

    def out_copies(row):
        return (
            pltpu.make_async_copy(total.at[row], strip_of(out, row, size), sem_out.at[row]),
            pltpu.make_async_copy(short.at[row], strip_of(rounded, row, size), sem_out.at[row]),
        )

    def one_row(row, carry):
        open_copy, closed_copy = out_copies(row)
        prev_copy(row).wait()
        add_products(row, order, first, left, right, touched, total)

        @pl.when(open_row[row] > 0)
        def _():
            open_copy.start()

        @pl.when(open_row[row] == 0)
        def _():
            short[row] = total[row].astype(short.dtype)
            closed_copy.start()

        return carry

    def close_row(row, carry):
        open_copy, closed_copy = out_copies(row)

        @pl.when(open_row[row] > 0)
        def _():
            open_copy.wait()

        @pl.when(open_row[row] == 0)
        def _():
            closed_copy.wait()

        return carry

    lax.fori_loop(0, RB, one_row, 0)
    lax.fori_loop(0, RB, close_row, 0)
    leave.wait()


def last_kernel(parts_count, order, first, target, flags, touched, open_row, *refs):
    shifted, *parts = refs[: 1 + parts_count]
    (
        piece, back, *over, prev, _, out,
        left, right, total, short,
        sem_left, sem_right, sem_prev, sem_out,
    ) = refs[1 + parts_count :]
    size = left.shape[1]
    count = first[RB + 2]
    shift, lent = flags[1], flags[2]
    begin = PARTS[0] - shift

    def prev_copy(row):
        return pltpu.make_async_copy(strip_of(prev, row, size), total.at[row], sem_prev.at[row])

    def start_prev(row, carry):
        @pl.when(open_row[row] > 0)
        def _():
            prev_copy(row).start()

        return carry

    lax.fori_loop(0, RB, start_prev, 0)
    whole = start_left(shifted, parts, left, flags[0] > 0, sem_left)
    low = ALWAYS
    sources = [(piece, begin, begin, low - shift), (back, low, low, low + lent)]
    low = low + lent
    for blocks in over:
        high = low + blocks.shape[0]
        sources.append((blocks, low, low, high))
        low = high
    start_right(sources, begin, count, target, right, sem_right)

    def out_copy(row):
        return pltpu.make_async_copy(short.at[row], strip_of(out, row, size), sem_out.at[row])

    whole.wait()
    finish_right(piece.at[0], right, sem_right, count - begin)

    def one_row(row, carry):
        @pl.when(open_row[row] > 0)
        def _():
            prev_copy(row).wait()
            add_products(row, order, first, left, right, touched, total)
            short[row] = total[row].astype(short.dtype)
            out_copy(row).start()

        return carry

    def close_row(row, carry):
        @pl.when(open_row[row] > 0)
        def _():
            out_copy(row).wait()

        return carry

    lax.fori_loop(0, RB, one_row, 0)
    lax.fori_loop(0, RB, close_row, 0)


def step_call(kernel, scalars, operands, specs, out_shape, out_specs, scratch, slots, size):
    return pl.pallas_call(
        kernel,
        out_shape=out_shape,
        grid_spec=pltpu.PrefetchScalarGridSpec(
            num_scalar_prefetch=len(scalars),
            grid=(RB // GROUP,),
            in_specs=specs,
            out_specs=out_specs,
            scratch_shapes=[
                pltpu.VMEM((slots, size, size), jnp.bfloat16),
                pltpu.VMEM((KB, size, NJ * size), jnp.bfloat16),
                *scratch,
                pltpu.SemaphoreType.DMA,
                pltpu.SemaphoreType.DMA,
            ],
        ),
        compiler_params=pltpu.CompilerParams(
            dimension_semantics=("arbitrary",), vmem_limit_bytes=LIMIT
        ),
        cost_estimate=pl.CostEstimate(
            flops=2 * 24 * NJ * size * size * size,
            bytes_accessed=16 * 1024 * 1024,
            transcendentals=0,
        ),
    )(*scalars, *operands)


def first_news_kernel(where_ref, cols_ref, send, out, where, cols, blocks, tile, sems):
    copies = [
        pltpu.make_async_copy(where_ref, where, sems.at[0]),
        pltpu.make_async_copy(cols_ref, cols, sems.at[1]),
    ]
    devices, count = where.shape[-1], blocks.shape[0]
    shares = devices // count
    step = blocks.shape[1] // shares
    for row in range(count):
        copies.append(
            pltpu.make_async_copy(send.at[1, 0, row * shares], blocks.at[row], sems.at[2 + row])
        )
    for copy in copies:
        copy.start()
    rcap, across = cols.shape
    tile[...] = jnp.zeros(tile.shape, tile.dtype)
    for copy in copies:
        copy.wait()
    for slot in range(rcap):
        tile[pl.ds(0, 1), pl.ds(slot * across, across)] = cols[pl.ds(slot, 1), :]
    for half in range(2):
        row, lane = divmod(half * devices, 128)
        tile[pl.ds(1 + row, 1), pl.ds(lane, devices)] = where[half]
    table = tile[...].astype(jnp.float32).astype(out.dtype)

    def fill(device, carry):
        share = pl.multiple_of(device % shares * step, step)
        out[device, pl.ds(0, step), :] = blocks[device // shares, pl.ds(share, step), :]
        out[device, pl.ds(step, 16), :] = table
        return carry

    lax.fori_loop(0, devices, fill, 0)


def first_news(where, cols, send, rows_count):
    devices = where.shape[-1]
    size = send.shape[-1]
    step = size * rows_count // devices
    return pl.pallas_call(
        first_news_kernel,
        out_shape=jax.ShapeDtypeStruct((devices, step + 16, size), send.dtype),
        in_specs=[ANYWHERE] * 3,
        scratch_shapes=[
            pltpu.VMEM(where.shape, jnp.int32),
            pltpu.VMEM(cols.shape, jnp.int32),
            pltpu.VMEM((rows_count, size, size), send.dtype),
            pltpu.VMEM((16, size), jnp.int32),
            pltpu.SemaphoreType.DMA((2 + rows_count,)),
        ],
        compiler_params=pltpu.CompilerParams(vmem_limit_bytes=LIMIT),
    )(in_hbm(where), in_hbm(cols), in_hbm(send))


def needed(where_all, cols_all, rows_count, cols_count):
    grid = where_all.reshape(-1, 2, rows_count, cols_count)
    after = jnp.concatenate([grid[:, 0, :, 1:], grid[:, 1, :, :1]], axis=-1)
    columns = jnp.arange(KB, dtype=jnp.int32)
    hit = (after[..., None] >= 0) & (after[..., None] % KB == columns)
    wanted = jnp.any(hit, axis=0).astype(jnp.int32)
    counts = jnp.sum((cols_all >= 0).astype(jnp.int32), axis=1)
    counts = jnp.roll(counts.reshape(rows_count, cols_count, KB), -1, axis=0)
    return jnp.sum(wanted * counts, axis=-1)


def swapped(value):
    return lax.ppermute(value, "col", [(i, i ^ 1) for i in range(lax.axis_size("col"))])


def local(a_send, a_where, b_strips, b_cols):
    size = a_send.shape[-1]
    rows_count = lax.axis_size("row")
    cols_count = lax.axis_size("col")
    devices = rows_count * cols_count
    both = ("row", "col")
    row_index = lax.axis_index("row")
    col_index = lax.axis_index("col")
    rcap = b_strips.shape[3]
    last = cols_count - 1

    by_slot = jnp.swapaxes(b_cols, 2, 3).reshape(rcap, KB)
    news = lax.all_to_all(
        first_news(a_where, by_slot, a_send, rows_count),
        both, split_axis=0, concat_axis=0, tiled=True,
    )
    step = size // cols_count
    part = news[:, :step]
    tables = news[:, step : step + 1 + -(-2 * devices // 128)].astype(jnp.int32)
    after_col = (col_index + 1) % cols_count
    after_half = (col_index + 1) // cols_count
    row_before = (row_index + rows_count - 1) % rows_count
    row_after = (row_index + 1) % rows_count
    needs = needed(
        tables[:, 1:].reshape(devices, -1)[:, : 2 * devices],
        tables[:, 0].reshape(devices, rcap, KB), rows_count, cols_count,
    )
    room = ALWAYS - jnp.flip(needs.reshape(rows_count, -1, 2), -1).reshape(needs.shape)
    lent = jnp.maximum(jnp.minimum(jnp.minimum(needs - ALWAYS, room), LENT), 0)
    most = jnp.max(needs - lent)

    def lent_to(row, col):
        return lax.dynamic_slice(lent, (row, col), (1, 1))[0, 0]

    spot = jnp.stack([
        after_half,
        row_index * cols_count + col_index,
        row_index * cols_count + after_col,
        row_before * cols_count + after_col,
        row_after * cols_count + col_index,
        lent_to(row_before, col_index ^ 1),
        lent_to(row_before, col_index),
    ]).astype(jnp.int32)

    received = lax.all_to_all(a_send[0, 0], both, split_axis=0, concat_axis=0, tiled=True)

    def to_row_before(blocks):
        return lax.ppermute(
            blocks, "row", [(i, (i - 1) % rows_count) for i in range(rows_count)]
        )

    strips = b_strips.reshape(KB * rcap, size, size)
    guests, *over = pack(pack_spare, (LENT, *PARTS[2:]), spot, tables, strips)
    begin, extra = ALWAYS, []
    for blocks in over:
        extra.append(lax.cond(most > begin, to_row_before, lambda same: same, blocks))
        begin += blocks.shape[0]
    early, late = pack(
        pack_main, PARTS[:2], spot, tables, strips, swapped(guests),
        *(blocks[0, :16] for blocks in extra),
    )
    early, late = map(to_row_before, after(received, [early, late]))

    shifted = lax.ppermute(received, "col", [(i + 1, i) for i in range(last)])
    (part,) = after(guests, [part])
    parts = [lax.ppermute(part, "col", [(i, last)]) for i in range(last)] + [part]

    wide = NJ * size
    strip = pl.BlockSpec((GROUP * size, wide), lambda i, *_: (i, 0))
    begun, order, first, target = step_call(
        functools.partial(first_kernel, rcap),
        (spot,), (tables, received, in_hbm(strips)), [ANYWHERE, ANYWHERE, ANYWHERE],
        [
            pltpu.HBM((RB * size, wide), jnp.float32),
            jax.ShapeDtypeStruct((devices,), jnp.int32),
            jax.ShapeDtypeStruct((RB + 3,), jnp.int32),
            jax.ShapeDtypeStruct((KB * rcap,), jnp.int32),
        ],
        [strip, IN_SMEM, IN_SMEM, IN_SMEM],
        [
            pltpu.SMEM(tables.shape, jnp.int32),
            pltpu.SemaphoreType.DMA,
            pltpu.SMEM((devices,), jnp.int32),
            pltpu.SMEM((RB + 2,), jnp.int32),
            pltpu.SMEM((KB,), jnp.int32),
            pltpu.SMEM((KB,), jnp.int32),
        ],
        devices, size,
    )

    on_last = (col_index == last).astype(jnp.int32)
    lent_here = [lent_to(row_index, col_index ^ 1), lent_to(row_index, col_index)]
    scalars = (order, first, target, jnp.stack([on_last, *lent_here]))
    lefts = (shifted, *parts)

    def finish_call(kernel, scalars, operands, out_shape, out_specs, scratch, marks, aliases):
        return pl.pallas_call(
            kernel,
            out_shape=out_shape,
            grid_spec=pltpu.PrefetchScalarGridSpec(
                num_scalar_prefetch=len(scalars),
                grid=(1,),
                in_specs=[ANYWHERE] * len(operands),
                out_specs=out_specs,
                scratch_shapes=[
                    *scratch,
                    pltpu.VMEM((devices, size, size), jnp.bfloat16),
                    pltpu.VMEM((KB, size, wide), jnp.bfloat16),
                    pltpu.VMEM((RB, size, wide), jnp.float32),
                    pltpu.VMEM((RB, size, wide), jnp.bfloat16),
                    *marks,
                    pltpu.SemaphoreType.DMA,
                    pltpu.SemaphoreType.DMA,
                    pltpu.SemaphoreType.DMA((RB,)),
                    pltpu.SemaphoreType.DMA((RB,)),
                ],
            ),
            input_output_aliases=aliases,
            compiler_params=pltpu.CompilerParams(vmem_limit_bytes=LIMIT),
            cost_estimate=pl.CostEstimate(
                flops=2 * 16 * NJ * size * size * size,
                bytes_accessed=12 * 1024 * 1024,
                transcendentals=0,
            ),
        )(*scalars, *operands)

    begun, rounded, guests, later, open_row = finish_call(
        functools.partial(middle_kernel, len(parts)), scalars,
        (*lefts, early, in_hbm(begun)),
        [
            pltpu.HBM((RB * size, wide), jnp.float32),
            pltpu.HBM((RB * size, wide), jnp.bfloat16),
            pltpu.HBM((LENT, size, size), jnp.bfloat16),
            jax.ShapeDtypeStruct((KB,), jnp.int32),
            jax.ShapeDtypeStruct((RB,), jnp.int32),
        ],
        [ANYWHERE, ANYWHERE, ANYWHERE, IN_SMEM, IN_SMEM],
        [
            pltpu.VMEM((LENT, size, size), jnp.bfloat16),
            pltpu.SemaphoreType.DMA,
            pltpu.SemaphoreType.DMA,
        ],
        [pltpu.SMEM((KB,), jnp.int32)], {},
    )
    back = swapped(guests)

    operands = (*lefts, late, back, *extra, in_hbm(begun), rounded)
    scalars = (*scalars, later, open_row)
    return finish_call(
        functools.partial(last_kernel, len(parts)), scalars, operands,
        jax.ShapeDtypeStruct((RB * size, wide), jnp.bfloat16),
        ANYWHERE, [], [], {len(scalars) + len(operands) - 1: 0},
    )


def solution(mesh):
    placed = (
        P(None, ("row", "col"), None, None, None),
        P(None, ("row", "col"), None),
        P("row", "col", None, None, None, None),
        P("row", "col", None, None),
    )
    return jax.shard_map(
        local, mesh=mesh, in_specs=placed, out_specs=P("row", "col"), check_vma=False
    )
```

```python
import functools

import jax
import jax.numpy as jnp
from jax import lax
from jax.experimental import pallas as pl
from jax.experimental.pallas import tpu as pltpu
from jax.sharding import PartitionSpec as P

RB = 16
KB = 16
NJ = 8
PARTS = (66, 26, 8, 8, 20)
ALWAYS = PARTS[0] + PARTS[1]
LENT = 16
GROUP = 4
IN_SMEM = pl.BlockSpec(memory_space=pltpu.SMEM)
ANYWHERE = pl.BlockSpec(memory_space=pl.ANY)
LIMIT = 24 * 1024 * 1024


def in_hbm(value):
    return pltpu.with_memory_space_constraint(value, pltpu.HBM)


def places_in(table, half, owner):
    at = half * table.shape[0] + owner
    return lambda source: table[source, 1 + at // 128, at % 128]


def columns_in(table, rcap, device):
    return lambda slot: table[device, 0, slot % rcap * KB + slot // rcap]


def mark_rows(place, slots, named):
    def reset(j, carry):
        named[j] = 0
        return carry

    def mark(s, carry):
        here = place(s)

        @pl.when(here >= 0)
        def _():
            named[here % KB] = named[here % KB] + 1

        return carry

    lax.fori_loop(0, KB, reset, 0)
    lax.fori_loop(0, slots, mark, 0)


def for_wanted(column, named, rcap, action):
    def visit(slot, number):
        wanted = column(slot) >= 0

        @pl.when(wanted)
        def _():
            action(slot, number)

        return number + wanted.astype(jnp.int32)

    def visit_row(j, match, number):
        return lax.fori_loop(j * rcap, jnp.where(match, (j + 1) * rcap, j * rcap), visit, number)

    count = lax.fori_loop(0, KB, lambda j, n: visit_row(j, named[j] > 1, n), jnp.int32(0))
    return lax.fori_loop(0, KB, lambda j, n: visit_row(j, named[j] == 1, n), count)


def pack_main(spot, tables, strips, guests, *refs):
    early, late, stage, table, sem_table, named, sem, sem_out = refs[-8:]
    shift = spot[5]
    stop = stage.shape[0] - shift

    def greet(number, carry):
        pltpu.make_async_copy(guests.at[number], stage.at[number], sem).start()
        return carry

    lax.fori_loop(0, shift, greet, 0)

    def fetch(slot, number):
        @pl.when(number < stop)
        def _():
            pltpu.make_async_copy(strips.at[slot], stage.at[number + shift], sem).start()

    count = find_wanted(spot, tables, strips, table, sem_table, named, fetch)
    finish_blocks(strips, stage, sem, jnp.minimum(count, stop) + shift)
    hand_over(stage, [early, late], sem_out)


def pack_spare(spot, tables, strips, guests, *refs):
    *over, stage, table, sem_table, named, sem, sem_out = refs
    lent = spot[6]

    def fetch(slot, number):
        beyond = number - ALWAYS

        @pl.when((beyond >= 0) & (beyond < LENT))
        def _():
            pltpu.make_async_copy(strips.at[slot], stage.at[beyond], sem).start()

        @pl.when(beyond >= lent)
        def _():
            at = LENT + beyond - lent
            pltpu.make_async_copy(strips.at[slot], stage.at[at], sem).start()

    count = find_wanted(spot, tables, strips, table, sem_table, named, fetch)
    beyond = jnp.maximum(count - ALWAYS, 0)
    copied = jnp.minimum(beyond, LENT) + jnp.maximum(beyond - lent, 0)
    finish_blocks(strips, stage, sem, copied)
    hand_over(stage, [guests, *over], sem_out)


def find_wanted(spot, tables, strips, table, sem_table, named, action):
    rcap = strips.shape[0] // KB
    table_copy = pltpu.make_async_copy(tables, table, sem_table)
    table_copy.start()
    table_copy.wait()
    mark_rows(places_in(table, spot[0], spot[3]), table.shape[0], named)
    return for_wanted(columns_in(table, rcap, spot[1]), named, rcap, action)


def finish_blocks(source, target, sem, count):
    def finish(number, carry):
        pltpu.make_async_copy(source.at[0], target.at[0], sem).wait()
        return carry

    lax.fori_loop(0, count, finish, 0)


def hand_over(stage, outs, sem_out):
    copies, low = [], 0
    for i, out in enumerate(outs):
        here = stage.at[pl.ds(low, out.shape[0])]
        copies.append(pltpu.make_async_copy(here, out, sem_out.at[i]))
        copies[-1].start()
        low += out.shape[0]
    for copy in copies:
        copy.wait()


def pack(kernel, counts, spot, tables, strips, *more):
    size = strips.shape[-1]
    return pl.pallas_call(
        kernel,
        out_shape=[pltpu.HBM((n, size, size), strips.dtype) for n in counts],
        grid_spec=pltpu.PrefetchScalarGridSpec(
            num_scalar_prefetch=1,
            grid=(1,),
            in_specs=[ANYWHERE] * (2 + len(more)),
            out_specs=[ANYWHERE] * len(counts),
            scratch_shapes=[
                pltpu.VMEM((sum(counts), size, size), strips.dtype),
                pltpu.SMEM(tables.shape, jnp.int32),
                pltpu.SemaphoreType.DMA,
                pltpu.SMEM((KB,), jnp.int32),
                pltpu.SemaphoreType.DMA,
                pltpu.SemaphoreType.DMA((len(counts),)),
            ],
        ),
        compiler_params=pltpu.CompilerParams(vmem_limit_bytes=LIMIT),
        cost_estimate=pl.CostEstimate(
            flops=0, bytes_accessed=4 * sum(counts) * size * size, transcendentals=0
        ),
    )(spot, tables, in_hbm(strips), *more)


def after(value, blocks):
    count = len(blocks)
    return pl.pallas_call(
        lambda *refs: None,
        out_shape=[pltpu.HBM(each.shape, each.dtype) for each in blocks],
        in_specs=[ANYWHERE] * (count + 1),
        out_specs=[ANYWHERE] * count,
        input_output_aliases={i: i for i in range(count)},
        compiler_params=pltpu.CompilerParams(vmem_limit_bytes=LIMIT),
    )(*blocks, value)


def by_block_row(place, slots, order, first):
    def reset(i, carry):
        first[i] = 0
        return carry

    def count(s, carry):
        here = place(s)

        @pl.when(here >= 0)
        def _():
            i = here // KB + 2
            first[i] = first[i] + 1

        return carry

    def scan(i, carry):
        first[i] = first[i] + first[i - 1]
        return carry

    def sort(s, carry):
        here = place(s)

        @pl.when(here >= 0)
        def _():
            i = here // KB + 1
            order[first[i]] = s * KB + here % KB
            first[i] = first[i] + 1

        return carry

    lax.fori_loop(0, RB + 2, reset, 0)
    lax.fori_loop(0, slots, count, 0)
    lax.fori_loop(1, RB + 2, scan, 0)
    lax.fori_loop(0, slots, sort, 0)


def clear(right, wanted):
    def one(j, carry):
        @pl.when(wanted(j))
        def _():
            right[j] = jnp.zeros(right.shape[1:], right.dtype)

        return carry

    lax.fori_loop(0, KB, one, 0)


def add_product(total, left, right, pair):
    slot, column = pair // KB, pair % KB
    wide = right.shape[-1]
    step = 2 * left.shape[-1]
    for low in range(0, wide, step):
        here = pl.ds(low, step)
        total[:, here] += jnp.dot(
            left[slot], right[column, :, here], preferred_element_type=jnp.float32
        )


def add_rows(left, right, total, order, first):
    size = left.shape[1]

    def one_row(i, carry):
        row = pl.program_id(0) * GROUP + i
        here = pl.ds(pl.multiple_of(i * size, size), size)

        def add(entry, carry):
            add_product(total.at[here], left, right, order[entry])
            return carry

        return lax.fori_loop(first[row], first[row + 1], add, carry)

    lax.fori_loop(0, GROUP, one_row, 0)


def place_at(right, where):
    size = right.shape[1]
    start = pl.multiple_of((where % NJ) * size, size)
    return right.at[where // NJ, :, pl.ds(start, size)]


def finish_right(source, right, sem, count):
    def finish(number, carry):
        pltpu.make_async_copy(source, place_at(right, 0), sem).wait()
        return carry

    lax.fori_loop(0, count, finish, 0)


def first_kernel(
    rcap, spot, tables, received, strips,
    out, next_order, next_first, next_target,
    left, right, table, sem_table, order, first, named, other, sem_left, sem_right,
):
    slots, size, _ = left.shape

    @pl.when(pl.program_id(0) == 0)
    def _():
        left_copy = pltpu.make_async_copy(received, left, sem_left)
        left_copy.start()
        table_copy = pltpu.make_async_copy(tables, table, sem_table)
        table_copy.start()
        table_copy.wait()
        place = places_in(table, 0, spot[1])
        column = columns_in(table, rcap, spot[1])
        mark_rows(place, slots, named)
        clear(right, lambda j: named[j] > 0)

        def fetch(slot, number):
            target = place_at(right, slot // rcap * NJ + column(slot))
            pltpu.make_async_copy(strips.at[slot], target, sem_right).start()

        count = for_wanted(column, named, rcap, fetch)
        by_block_row(place, slots, order, first)

        next_place = places_in(table, spot[0], spot[2])
        next_column = columns_in(table, rcap, spot[4])
        by_block_row(next_place, slots, next_order, next_first)
        mark_rows(next_place, slots, other)

        def note(slot, number):
            next_target[number] = slot // rcap * NJ + next_column(slot)

        next_first[RB + 2] = for_wanted(next_column, other, rcap, note)
        left_copy.wait()
        finish_right(strips.at[0], right, sem_right, count)

    out[...] = jnp.zeros(out.shape, out.dtype)
    add_rows(left, right, out, order, first)


def start_left(shifted, parts, left, on_last, sem):
    step = left.shape[1] // len(parts)
    whole = pltpu.make_async_copy(shifted, left, sem)

    @pl.when(on_last)
    def _():
        for q, part in enumerate(parts):
            pltpu.make_async_copy(part, left.at[:, pl.ds(q * step, step)], sem).start()

    @pl.when(jnp.logical_not(on_last))
    def _():
        whole.start()

    return whole


def start_right(sources, count, target, right, sem):
    for blocks, low, start, stop in sources:

        def fetch(number, carry):
            pltpu.make_async_copy(
                blocks.at[number - low], place_at(right, target[number]), sem
            ).start()
            return carry

        lax.fori_loop(start, jnp.minimum(count, stop), fetch, 0)


def add_products(row, order, first, left, right, touched, total):
    def add(entry, carry):
        @pl.when(touched[order[entry] % KB] > 0)
        def _():
            add_product(total.at[row], left, right, order[entry])

        return carry

    lax.fori_loop(first[row], first[row + 1], add, 0)


def mark_targets(target, begin, end, marks):
    def reset(j, carry):
        marks[j] = 0
        return carry

    def mark(number, carry):
        marks[target[number] // NJ] = 1
        return carry

    lax.fori_loop(0, KB, reset, 0)
    lax.fori_loop(begin, end, mark, 0)


def mark_open(order, first, touched, open_row):
    def one(row, carry):
        def look(entry, found):
            return jnp.maximum(found, touched[order[entry] % KB])

        open_row[row] = lax.fori_loop(first[row], first[row + 1], look, jnp.int32(0))
        return carry

    lax.fori_loop(0, RB, one, 0)


def strip_of(ref, row, size):
    return ref.at[pl.ds(pl.multiple_of(row * size, size), size)]


def middle_kernel(parts_count, order, first, target, flags, *refs):
    shifted, *parts = refs[: 1 + parts_count]
    (
        piece, prev, out, rounded, guests, later, open_row,
        hall, sem_in, sem_home,
        left, right, total, short, touched,
        sem_left, sem_right, sem_prev, sem_out,
    ) = refs[1 + parts_count :]
    arrive = pltpu.make_async_copy(piece.at[pl.ds(0, LENT)], hall, sem_in)
    leave = pltpu.make_async_copy(hall, guests, sem_home)
    arrive.start()
    size = left.shape[1]
    count = first[RB + 2]
    shift = flags[1]
    end = piece.shape[0] - shift

    def prev_copy(row):
        return pltpu.make_async_copy(strip_of(prev, row, size), total.at[row], sem_prev.at[row])

    def start_prev(row, carry):
        prev_copy(row).start()
        return carry

    lax.fori_loop(0, RB, start_prev, 0)
    whole = start_left(shifted, parts, left, flags[0] > 0, sem_left)
    fetched = jnp.minimum(count, end)
    mark_targets(target, 0, fetched, touched)
    clear(right, lambda j: touched[j] > 0)
    start_right([(piece, -shift, 0, end)], fetched, target, right, sem_right)
    arrive.wait()
    leave.start()
    mark_targets(target, end, count, later)
    mark_open(order, first, later, open_row)
    whole.wait()
    finish_right(piece.at[0], right, sem_right, fetched)

    def out_copies(row):
        return (
            pltpu.make_async_copy(total.at[row], strip_of(out, row, size), sem_out.at[row]),
            pltpu.make_async_copy(short.at[row], strip_of(rounded, row, size), sem_out.at[row]),
        )

    def one_row(row, carry):
        open_copy, closed_copy = out_copies(row)
        prev_copy(row).wait()
        add_products(row, order, first, left, right, touched, total)

        @pl.when(open_row[row] > 0)
        def _():
            open_copy.start()

        @pl.when(open_row[row] == 0)
        def _():
            short[row] = total[row].astype(short.dtype)
            closed_copy.start()

        return carry

    def close_row(row, carry):
        open_copy, closed_copy = out_copies(row)

        @pl.when(open_row[row] > 0)
        def _():
            open_copy.wait()

        @pl.when(open_row[row] == 0)
        def _():
            closed_copy.wait()

        return carry

    lax.fori_loop(0, RB, one_row, 0)
    lax.fori_loop(0, RB, close_row, 0)
    leave.wait()


def last_kernel(parts_count, order, first, target, flags, touched, open_row, *refs):
    shifted, *parts = refs[: 1 + parts_count]
    (
        piece, back, *over, prev, _, out,
        left, right, total, short,
        sem_left, sem_right, sem_prev, sem_out,
    ) = refs[1 + parts_count :]
    size = left.shape[1]
    count = first[RB + 2]
    shift, lent = flags[1], flags[2]
    begin = PARTS[0] - shift

    def prev_copy(row):
        return pltpu.make_async_copy(strip_of(prev, row, size), total.at[row], sem_prev.at[row])

    def start_prev(row, carry):
        @pl.when(open_row[row] > 0)
        def _():
            prev_copy(row).start()

        return carry

    lax.fori_loop(0, RB, start_prev, 0)
    whole = start_left(shifted, parts, left, flags[0] > 0, sem_left)
    low = ALWAYS
    sources = [(piece, begin, begin, low - shift), (back, low, low, low + lent)]
    low = low + lent
    for blocks in over:
        high = low + blocks.shape[0]
        sources.append((blocks, low, low, high))
        low = high
    clear(right, lambda j: touched[j] > 0)
    start_right(sources, count, target, right, sem_right)

    def out_copy(row):
        return pltpu.make_async_copy(short.at[row], strip_of(out, row, size), sem_out.at[row])

    whole.wait()
    finish_right(piece.at[0], right, sem_right, count - begin)

    def one_row(row, carry):
        @pl.when(open_row[row] > 0)
        def _():
            prev_copy(row).wait()
            add_products(row, order, first, left, right, touched, total)
            short[row] = total[row].astype(short.dtype)
            out_copy(row).start()

        return carry

    def close_row(row, carry):
        @pl.when(open_row[row] > 0)
        def _():
            out_copy(row).wait()

        return carry

    lax.fori_loop(0, RB, one_row, 0)
    lax.fori_loop(0, RB, close_row, 0)


def step_call(kernel, scalars, operands, specs, out_shape, out_specs, scratch, slots, size):
    return pl.pallas_call(
        kernel,
        out_shape=out_shape,
        grid_spec=pltpu.PrefetchScalarGridSpec(
            num_scalar_prefetch=len(scalars),
            grid=(RB // GROUP,),
            in_specs=specs,
            out_specs=out_specs,
            scratch_shapes=[
                pltpu.VMEM((slots, size, size), jnp.bfloat16),
                pltpu.VMEM((KB, size, NJ * size), jnp.bfloat16),
                *scratch,
                pltpu.SemaphoreType.DMA,
                pltpu.SemaphoreType.DMA,
            ],
        ),
        compiler_params=pltpu.CompilerParams(
            dimension_semantics=("arbitrary",), vmem_limit_bytes=LIMIT
        ),
        cost_estimate=pl.CostEstimate(
            flops=2 * 24 * NJ * size * size * size,
            bytes_accessed=16 * 1024 * 1024,
            transcendentals=0,
        ),
    )(*scalars, *operands)


def first_news_kernel(where_ref, cols_ref, send, out, where, cols, blocks, tile, sems):
    copies = [
        pltpu.make_async_copy(where_ref, where, sems.at[0]),
        pltpu.make_async_copy(cols_ref, cols, sems.at[1]),
    ]
    devices, count = where.shape[-1], blocks.shape[0]
    shares = devices // count
    step = blocks.shape[1] // shares
    for row in range(count):
        copies.append(
            pltpu.make_async_copy(send.at[1, 0, row * shares], blocks.at[row], sems.at[2 + row])
        )
    for copy in copies:
        copy.start()
    rcap, across = cols.shape
    tile[...] = jnp.zeros(tile.shape, tile.dtype)
    for copy in copies:
        copy.wait()
    for slot in range(rcap):
        tile[pl.ds(0, 1), pl.ds(slot * across, across)] = cols[pl.ds(slot, 1), :]
    for half in range(2):
        row, lane = divmod(half * devices, 128)
        tile[pl.ds(1 + row, 1), pl.ds(lane, devices)] = where[half]
    table = tile[...].astype(jnp.float32).astype(out.dtype)

    def fill(device, carry):
        share = pl.multiple_of(device % shares * step, step)
        out[device, pl.ds(0, step), :] = blocks[device // shares, pl.ds(share, step), :]
        out[device, pl.ds(step, 16), :] = table
        return carry

    lax.fori_loop(0, devices, fill, 0)


def first_news(where, cols, send, rows_count):
    devices = where.shape[-1]
    size = send.shape[-1]
    step = size * rows_count // devices
    return pl.pallas_call(
        first_news_kernel,
        out_shape=jax.ShapeDtypeStruct((devices, step + 16, size), send.dtype),
        in_specs=[ANYWHERE] * 3,
        scratch_shapes=[
            pltpu.VMEM(where.shape, jnp.int32),
            pltpu.VMEM(cols.shape, jnp.int32),
            pltpu.VMEM((rows_count, size, size), send.dtype),
            pltpu.VMEM((16, size), jnp.int32),
            pltpu.SemaphoreType.DMA((2 + rows_count,)),
        ],
        compiler_params=pltpu.CompilerParams(vmem_limit_bytes=LIMIT),
    )(in_hbm(where), in_hbm(cols), in_hbm(send))


def needed(where_all, cols_all, rows_count, cols_count):
    grid = where_all.reshape(-1, 2, rows_count, cols_count)
    after = jnp.concatenate([grid[:, 0, :, 1:], grid[:, 1, :, :1]], axis=-1)
    columns = jnp.arange(KB, dtype=jnp.int32)
    hit = (after[..., None] >= 0) & (after[..., None] % KB == columns)
    wanted = jnp.any(hit, axis=0).astype(jnp.int32)
    counts = jnp.sum((cols_all >= 0).astype(jnp.int32), axis=1)
    counts = jnp.roll(counts.reshape(rows_count, cols_count, KB), -1, axis=0)
    return jnp.sum(wanted * counts, axis=-1)


def swapped(value):
    return lax.ppermute(value, "col", [(i, i ^ 1) for i in range(lax.axis_size("col"))])


def local(a_send, a_where, b_strips, b_cols):
    size = a_send.shape[-1]
    rows_count = lax.axis_size("row")
    cols_count = lax.axis_size("col")
    devices = rows_count * cols_count
    both = ("row", "col")
    row_index = lax.axis_index("row")
    col_index = lax.axis_index("col")
    rcap = b_strips.shape[3]
    last = cols_count - 1

    by_slot = jnp.swapaxes(b_cols, 2, 3).reshape(rcap, KB)
    news = lax.all_to_all(
        first_news(a_where, by_slot, a_send, rows_count),
        both, split_axis=0, concat_axis=0, tiled=True,
    )
    step = size // cols_count
    part = news[:, :step]
    tables = news[:, step : step + 1 + -(-2 * devices // 128)].astype(jnp.int32)
    after_col = (col_index + 1) % cols_count
    after_half = (col_index + 1) // cols_count
    row_before = (row_index + rows_count - 1) % rows_count
    row_after = (row_index + 1) % rows_count
    needs = needed(
        tables[:, 1:].reshape(devices, -1)[:, : 2 * devices],
        tables[:, 0].reshape(devices, rcap, KB), rows_count, cols_count,
    )
    room = ALWAYS - jnp.flip(needs.reshape(rows_count, -1, 2), -1).reshape(needs.shape)
    lent = jnp.maximum(jnp.minimum(jnp.minimum(needs - ALWAYS, room), LENT), 0)
    most = jnp.max(needs - lent)

    def lent_to(row, col):
        return lax.dynamic_slice(lent, (row, col), (1, 1))[0, 0]

    spot = jnp.stack([
        after_half,
        row_index * cols_count + col_index,
        row_index * cols_count + after_col,
        row_before * cols_count + after_col,
        row_after * cols_count + col_index,
        lent_to(row_before, col_index ^ 1),
        lent_to(row_before, col_index),
    ]).astype(jnp.int32)

    received = lax.all_to_all(a_send[0, 0], both, split_axis=0, concat_axis=0, tiled=True)

    def to_row_before(blocks):
        return lax.ppermute(
            blocks, "row", [(i, (i - 1) % rows_count) for i in range(rows_count)]
        )

    strips = b_strips.reshape(KB * rcap, size, size)
    guests, *over = pack(pack_spare, (LENT, *PARTS[2:]), spot, tables, strips)
    begin, extra = ALWAYS, []
    for blocks in over:
        extra.append(lax.cond(most > begin, to_row_before, lambda same: same, blocks))
        begin += blocks.shape[0]
    early, late = pack(
        pack_main, PARTS[:2], spot, tables, strips, swapped(guests),
        *(blocks[0, :16] for blocks in extra),
    )
    early, late = map(to_row_before, after(received, [early, late]))

    shifted = lax.ppermute(received, "col", [(i + 1, i) for i in range(last)])
    (part,) = after(guests, [part])
    parts = [lax.ppermute(part, "col", [(i, last)]) for i in range(last)] + [part]

    wide = NJ * size
    strip = pl.BlockSpec((GROUP * size, wide), lambda i, *_: (i, 0))
    begun, order, first, target = step_call(
        functools.partial(first_kernel, rcap),
        (spot,), (tables, received, in_hbm(strips)), [ANYWHERE, ANYWHERE, ANYWHERE],
        [
            pltpu.HBM((RB * size, wide), jnp.float32),
            jax.ShapeDtypeStruct((devices,), jnp.int32),
            jax.ShapeDtypeStruct((RB + 3,), jnp.int32),
            jax.ShapeDtypeStruct((KB * rcap,), jnp.int32),
        ],
        [strip, IN_SMEM, IN_SMEM, IN_SMEM],
        [
            pltpu.SMEM(tables.shape, jnp.int32),
            pltpu.SemaphoreType.DMA,
            pltpu.SMEM((devices,), jnp.int32),
            pltpu.SMEM((RB + 2,), jnp.int32),
            pltpu.SMEM((KB,), jnp.int32),
            pltpu.SMEM((KB,), jnp.int32),
        ],
        devices, size,
    )

    on_last = (col_index == last).astype(jnp.int32)
    lent_here = [lent_to(row_index, col_index ^ 1), lent_to(row_index, col_index)]
    scalars = (order, first, target, jnp.stack([on_last, *lent_here]))
    lefts = (shifted, *parts)

    def finish_call(kernel, scalars, operands, out_shape, out_specs, scratch, marks, aliases):
        return pl.pallas_call(
            kernel,
            out_shape=out_shape,
            grid_spec=pltpu.PrefetchScalarGridSpec(
                num_scalar_prefetch=len(scalars),
                grid=(1,),
                in_specs=[ANYWHERE] * len(operands),
                out_specs=out_specs,
                scratch_shapes=[
                    *scratch,
                    pltpu.VMEM((devices, size, size), jnp.bfloat16),
                    pltpu.VMEM((KB, size, wide), jnp.bfloat16),
                    pltpu.VMEM((RB, size, wide), jnp.float32),
                    pltpu.VMEM((RB, size, wide), jnp.bfloat16),
                    *marks,
                    pltpu.SemaphoreType.DMA,
                    pltpu.SemaphoreType.DMA,
                    pltpu.SemaphoreType.DMA((RB,)),
                    pltpu.SemaphoreType.DMA((RB,)),
                ],
            ),
            input_output_aliases=aliases,
            compiler_params=pltpu.CompilerParams(vmem_limit_bytes=LIMIT),
            cost_estimate=pl.CostEstimate(
                flops=2 * 16 * NJ * size * size * size,
                bytes_accessed=12 * 1024 * 1024,
                transcendentals=0,
            ),
        )(*scalars, *operands)

    begun, rounded, guests, later, open_row = finish_call(
        functools.partial(middle_kernel, len(parts)), scalars,
        (*lefts, early, in_hbm(begun)),
        [
            pltpu.HBM((RB * size, wide), jnp.float32),
            pltpu.HBM((RB * size, wide), jnp.bfloat16),
            pltpu.HBM((LENT, size, size), jnp.bfloat16),
            jax.ShapeDtypeStruct((KB,), jnp.int32),
            jax.ShapeDtypeStruct((RB,), jnp.int32),
        ],
        [ANYWHERE, ANYWHERE, ANYWHERE, IN_SMEM, IN_SMEM],
        [
            pltpu.VMEM((LENT, size, size), jnp.bfloat16),
            pltpu.SemaphoreType.DMA,
            pltpu.SemaphoreType.DMA,
        ],
        [pltpu.SMEM((KB,), jnp.int32)], {},
    )
    back = swapped(guests)

    operands = (*lefts, late, back, *extra, in_hbm(begun), rounded)
    scalars = (*scalars, later, open_row)
    return finish_call(
        functools.partial(last_kernel, len(parts)), scalars, operands,
        jax.ShapeDtypeStruct((RB * size, wide), jnp.bfloat16),
        ANYWHERE, [], [], {len(scalars) + len(operands) - 1: 0},
    )


def solution(mesh):
    placed = (
        P(None, ("row", "col"), None, None, None),
        P(None, ("row", "col"), None),
        P("row", "col", None, None, None, None),
        P("row", "col", None, None),
    )
    return jax.shard_map(
        local, mesh=mesh, in_specs=placed, out_specs=P("row", "col"), check_vma=False
    )
```

```python
import functools

import jax
import jax.numpy as jnp
from jax import lax
from jax.experimental import pallas as pl
from jax.experimental.pallas import tpu as pltpu
from jax.sharding import PartitionSpec as P

RB = 16
KB = 16
NJ = 8
PARTS = (66, 24, 8, 8, 22)
ALWAYS = PARTS[0] + PARTS[1]
LENT = 16
GROUP = 4
IN_SMEM = pl.BlockSpec(memory_space=pltpu.SMEM)
ANYWHERE = pl.BlockSpec(memory_space=pl.ANY)
LIMIT = 24 * 1024 * 1024


def in_hbm(value):
    return pltpu.with_memory_space_constraint(value, pltpu.HBM)


def places_in(table, half, owner):
    at = half * table.shape[0] + owner
    return lambda source: table[source, 1 + at // 128, at % 128]


def columns_in(table, rcap, device):
    return lambda slot: table[device, 0, slot % rcap * KB + slot // rcap]


def mark_rows(place, slots, named):
    def reset(j, carry):
        named[j] = 0
        return carry

    def mark(s, carry):
        here = place(s)

        @pl.when(here >= 0)
        def _():
            named[here % KB] = named[here % KB] + 1

        return carry

    lax.fori_loop(0, KB, reset, 0)
    lax.fori_loop(0, slots, mark, 0)


def for_wanted(column, named, rcap, action):
    def visit(slot, number):
        wanted = column(slot) >= 0

        @pl.when(wanted)
        def _():
            action(slot, number)

        return number + wanted.astype(jnp.int32)

    def visit_row(j, match, number):
        return lax.fori_loop(j * rcap, jnp.where(match, (j + 1) * rcap, j * rcap), visit, number)

    count = lax.fori_loop(0, KB, lambda j, n: visit_row(j, named[j] > 1, n), jnp.int32(0))
    return lax.fori_loop(0, KB, lambda j, n: visit_row(j, named[j] == 1, n), count)


def pack_main(spot, tables, strips, guests, *refs):
    early, late, stage, table, sem_table, named, sem, sem_out = refs[-8:]
    shift = spot[5]
    stop = stage.shape[0] - shift

    def greet(number, carry):
        pltpu.make_async_copy(guests.at[number], stage.at[number], sem).start()
        return carry

    lax.fori_loop(0, shift, greet, 0)

    def fetch(slot, number):
        @pl.when(number < stop)
        def _():
            pltpu.make_async_copy(strips.at[slot], stage.at[number + shift], sem).start()

    count = find_wanted(spot, tables, strips, table, sem_table, named, fetch)
    finish_blocks(strips, stage, sem, jnp.minimum(count, stop) + shift)
    hand_over(stage, [early, late], sem_out)


def pack_spare(spot, tables, strips, guests, *refs):
    *over, stage, table, sem_table, named, sem, sem_out = refs
    lent = spot[6]

    def fetch(slot, number):
        beyond = number - ALWAYS

        @pl.when((beyond >= 0) & (beyond < LENT))
        def _():
            pltpu.make_async_copy(strips.at[slot], stage.at[beyond], sem).start()

        @pl.when(beyond >= lent)
        def _():
            at = LENT + beyond - lent
            pltpu.make_async_copy(strips.at[slot], stage.at[at], sem).start()

    count = find_wanted(spot, tables, strips, table, sem_table, named, fetch)
    beyond = jnp.maximum(count - ALWAYS, 0)
    copied = jnp.minimum(beyond, LENT) + jnp.maximum(beyond - lent, 0)
    finish_blocks(strips, stage, sem, copied)
    hand_over(stage, [guests, *over], sem_out)


def find_wanted(spot, tables, strips, table, sem_table, named, action):
    rcap = strips.shape[0] // KB
    table_copy = pltpu.make_async_copy(tables, table, sem_table)
    table_copy.start()
    table_copy.wait()
    mark_rows(places_in(table, spot[0], spot[3]), table.shape[0], named)
    return for_wanted(columns_in(table, rcap, spot[1]), named, rcap, action)


def finish_blocks(source, target, sem, count):
    def finish(number, carry):
        pltpu.make_async_copy(source.at[0], target.at[0], sem).wait()
        return carry

    lax.fori_loop(0, count, finish, 0)


def hand_over(stage, outs, sem_out):
    copies, low = [], 0
    for i, out in enumerate(outs):
        here = stage.at[pl.ds(low, out.shape[0])]
        copies.append(pltpu.make_async_copy(here, out, sem_out.at[i]))
        copies[-1].start()
        low += out.shape[0]
    for copy in copies:
        copy.wait()


def pack(kernel, counts, spot, tables, strips, *more):
    size = strips.shape[-1]
    return pl.pallas_call(
        kernel,
        out_shape=[pltpu.HBM((n, size, size), strips.dtype) for n in counts],
        grid_spec=pltpu.PrefetchScalarGridSpec(
            num_scalar_prefetch=1,
            grid=(1,),
            in_specs=[ANYWHERE] * (2 + len(more)),
            out_specs=[ANYWHERE] * len(counts),
            scratch_shapes=[
                pltpu.VMEM((sum(counts), size, size), strips.dtype),
                pltpu.SMEM(tables.shape, jnp.int32),
                pltpu.SemaphoreType.DMA,
                pltpu.SMEM((KB,), jnp.int32),
                pltpu.SemaphoreType.DMA,
                pltpu.SemaphoreType.DMA((len(counts),)),
            ],
        ),
        compiler_params=pltpu.CompilerParams(vmem_limit_bytes=LIMIT),
        cost_estimate=pl.CostEstimate(
            flops=0, bytes_accessed=4 * sum(counts) * size * size, transcendentals=0
        ),
    )(spot, tables, in_hbm(strips), *more)


def after(values, blocks):
    count = len(blocks)
    return pl.pallas_call(
        lambda *refs: None,
        out_shape=[pltpu.HBM(each.shape, each.dtype) for each in blocks],
        in_specs=[ANYWHERE] * (count + len(values)),
        out_specs=[ANYWHERE] * count,
        input_output_aliases={i: i for i in range(count)},
        compiler_params=pltpu.CompilerParams(vmem_limit_bytes=LIMIT),
    )(*blocks, *values)


def by_block_row(place, slots, order, first):
    def reset(i, carry):
        first[i] = 0
        return carry

    def count(s, carry):
        here = place(s)

        @pl.when(here >= 0)
        def _():
            i = here // KB + 2
            first[i] = first[i] + 1

        return carry

    def scan(i, carry):
        first[i] = first[i] + first[i - 1]
        return carry

    def sort(s, carry):
        here = place(s)

        @pl.when(here >= 0)
        def _():
            i = here // KB + 1
            order[first[i]] = s * KB + here % KB
            first[i] = first[i] + 1

        return carry

    lax.fori_loop(0, RB + 2, reset, 0)
    lax.fori_loop(0, slots, count, 0)
    lax.fori_loop(1, RB + 2, scan, 0)
    lax.fori_loop(0, slots, sort, 0)


def clear(right, wanted):
    def one(j, carry):
        @pl.when(wanted(j))
        def _():
            right[j] = jnp.zeros(right.shape[1:], right.dtype)

        return carry

    lax.fori_loop(0, KB, one, 0)


def add_product(total, left, right, pair):
    slot, column = pair // KB, pair % KB
    wide = right.shape[-1]
    step = 2 * left.shape[-1]
    for low in range(0, wide, step):
        here = pl.ds(low, step)
        total[:, here] += jnp.dot(
            left[slot], right[column, :, here], preferred_element_type=jnp.float32
        )


def add_rows(left, right, total, order, first):
    size = left.shape[1]

    def one_row(i, carry):
        row = pl.program_id(0) * GROUP + i
        here = pl.ds(pl.multiple_of(i * size, size), size)

        def add(entry, carry):
            add_product(total.at[here], left, right, order[entry])
            return carry

        return lax.fori_loop(first[row], first[row + 1], add, carry)

    lax.fori_loop(0, GROUP, one_row, 0)


def place_at(right, where):
    size = right.shape[1]
    start = pl.multiple_of((where % NJ) * size, size)
    return right.at[where // NJ, :, pl.ds(start, size)]


def finish_right(source, right, sem, count):
    def finish(number, carry):
        pltpu.make_async_copy(source, place_at(right, 0), sem).wait()
        return carry

    lax.fori_loop(0, count, finish, 0)


def first_kernel(
    rcap, spot, tables, received, strips,
    out, next_order, next_first, next_target,
    left, right, table, sem_table, order, first, named, other, sem_left, sem_right,
):
    slots, size, _ = left.shape

    @pl.when(pl.program_id(0) == 0)
    def _():
        left_copy = pltpu.make_async_copy(received, left, sem_left)
        left_copy.start()
        table_copy = pltpu.make_async_copy(tables, table, sem_table)
        table_copy.start()
        table_copy.wait()
        place = places_in(table, 0, spot[1])
        column = columns_in(table, rcap, spot[1])
        mark_rows(place, slots, named)
        clear(right, lambda j: named[j] > 0)

        def fetch(slot, number):
            target = place_at(right, slot // rcap * NJ + column(slot))
            pltpu.make_async_copy(strips.at[slot], target, sem_right).start()

        count = for_wanted(column, named, rcap, fetch)
        by_block_row(place, slots, order, first)

        next_place = places_in(table, spot[0], spot[2])
        next_column = columns_in(table, rcap, spot[4])
        by_block_row(next_place, slots, next_order, next_first)
        mark_rows(next_place, slots, other)

        def note(slot, number):
            next_target[number] = slot // rcap * NJ + next_column(slot)

        next_first[RB + 2] = for_wanted(next_column, other, rcap, note)
        left_copy.wait()
        finish_right(strips.at[0], right, sem_right, count)

    out[...] = jnp.zeros(out.shape, out.dtype)
    add_rows(left, right, out, order, first)


def start_left(shifted, parts, left, on_last, sem):
    step = left.shape[1] // len(parts)
    whole = pltpu.make_async_copy(shifted, left, sem)

    @pl.when(on_last)
    def _():
        for q, part in enumerate(parts):
            pltpu.make_async_copy(part, left.at[:, pl.ds(q * step, step)], sem).start()

    @pl.when(jnp.logical_not(on_last))
    def _():
        whole.start()

    return whole


def start_right(sources, count, target, right, sem):
    for blocks, low, start, stop in sources:

        def fetch(number, carry):
            pltpu.make_async_copy(
                blocks.at[number - low], place_at(right, target[number]), sem
            ).start()
            return carry

        lax.fori_loop(start, jnp.minimum(count, stop), fetch, 0)


def add_products(row, order, first, left, right, touched, total):
    def add(entry, carry):
        @pl.when(touched[order[entry] % KB] > 0)
        def _():
            add_product(total.at[row], left, right, order[entry])

        return carry

    lax.fori_loop(first[row], first[row + 1], add, 0)


def mark_targets(target, begin, end, marks):
    def reset(j, carry):
        marks[j] = 0
        return carry

    def mark(number, carry):
        marks[target[number] // NJ] = 1
        return carry

    lax.fori_loop(0, KB, reset, 0)
    lax.fori_loop(begin, end, mark, 0)


def mark_open(order, first, touched, open_row):
    def one(row, carry):
        def look(entry, found):
            return jnp.maximum(found, touched[order[entry] % KB])

        open_row[row] = lax.fori_loop(first[row], first[row + 1], look, jnp.int32(0))
        return carry

    lax.fori_loop(0, RB, one, 0)


def strip_of(ref, row, size):
    return ref.at[pl.ds(pl.multiple_of(row * size, size), size)]


def middle_kernel(parts_count, order, first, target, flags, *refs):
    shifted, *parts = refs[: 1 + parts_count]
    (
        piece, prev, out, rounded, guests, later, open_row,
        hall, sem_in, sem_home,
        left, right, total, short, touched,
        sem_left, sem_right, sem_prev, sem_out,
    ) = refs[1 + parts_count :]
    arrive = pltpu.make_async_copy(piece.at[pl.ds(0, LENT)], hall, sem_in)
    leave = pltpu.make_async_copy(hall, guests, sem_home)
    arrive.start()
    size = left.shape[1]
    count = first[RB + 2]
    shift = flags[1]
    end = piece.shape[0] - shift

    def prev_copy(row):
        return pltpu.make_async_copy(strip_of(prev, row, size), total.at[row], sem_prev.at[row])

    def start_prev(row, carry):
        prev_copy(row).start()
        return carry

    lax.fori_loop(0, RB, start_prev, 0)
    whole = start_left(shifted, parts, left, flags[0] > 0, sem_left)
    fetched = jnp.minimum(count, end)
    mark_targets(target, 0, fetched, touched)
    clear(right, lambda j: touched[j] > 0)
    start_right([(piece, -shift, 0, end)], fetched, target, right, sem_right)
    arrive.wait()
    leave.start()
    mark_targets(target, end, count, later)
    mark_open(order, first, later, open_row)
    whole.wait()
    finish_right(piece.at[0], right, sem_right, fetched)

    def out_copies(row):
        return (
            pltpu.make_async_copy(total.at[row], strip_of(out, row, size), sem_out.at[row]),
            pltpu.make_async_copy(short.at[row], strip_of(rounded, row, size), sem_out.at[row]),
        )

    def one_row(row, carry):
        open_copy, closed_copy = out_copies(row)
        prev_copy(row).wait()
        add_products(row, order, first, left, right, touched, total)

        @pl.when(open_row[row] > 0)
        def _():
            open_copy.start()

        @pl.when(open_row[row] == 0)
        def _():
            short[row] = total[row].astype(short.dtype)
            closed_copy.start()

        return carry

    def close_row(row, carry):
        open_copy, closed_copy = out_copies(row)

        @pl.when(open_row[row] > 0)
        def _():
            open_copy.wait()

        @pl.when(open_row[row] == 0)
        def _():
            closed_copy.wait()

        return carry

    lax.fori_loop(0, RB, one_row, 0)
    lax.fori_loop(0, RB, close_row, 0)
    leave.wait()


def last_kernel(parts_count, order, first, target, flags, touched, open_row, *refs):
    shifted, *parts = refs[: 1 + parts_count]
    (
        piece, back, *over, prev, _, out,
        left, right, total, short,
        sem_left, sem_right, sem_prev, sem_out,
    ) = refs[1 + parts_count :]
    size = left.shape[1]
    count = first[RB + 2]
    shift, lent = flags[1], flags[2]
    begin = PARTS[0] - shift

    def prev_copy(row):
        return pltpu.make_async_copy(strip_of(prev, row, size), total.at[row], sem_prev.at[row])

    def start_prev(row, carry):
        @pl.when(open_row[row] > 0)
        def _():
            prev_copy(row).start()

        return carry

    lax.fori_loop(0, RB, start_prev, 0)
    whole = start_left(shifted, parts, left, flags[0] > 0, sem_left)
    low = ALWAYS
    sources = [(piece, begin, begin, low - shift), (back, low, low, low + lent)]
    low = low + lent
    for blocks in over:
        high = low + blocks.shape[0]
        sources.append((blocks, low, low, high))
        low = high
    clear(right, lambda j: touched[j] > 0)
    start_right(sources, count, target, right, sem_right)

    def out_copy(row):
        return pltpu.make_async_copy(short.at[row], strip_of(out, row, size), sem_out.at[row])

    whole.wait()
    finish_right(piece.at[0], right, sem_right, count - begin)

    def one_row(row, carry):
        @pl.when(open_row[row] > 0)
        def _():
            prev_copy(row).wait()
            add_products(row, order, first, left, right, touched, total)
            short[row] = total[row].astype(short.dtype)
            out_copy(row).start()

        return carry

    def close_row(row, carry):
        @pl.when(open_row[row] > 0)
        def _():
            out_copy(row).wait()

        return carry

    lax.fori_loop(0, RB, one_row, 0)
    lax.fori_loop(0, RB, close_row, 0)


def step_call(kernel, scalars, operands, specs, out_shape, out_specs, scratch, slots, size):
    return pl.pallas_call(
        kernel,
        out_shape=out_shape,
        grid_spec=pltpu.PrefetchScalarGridSpec(
            num_scalar_prefetch=len(scalars),
            grid=(RB // GROUP,),
            in_specs=specs,
            out_specs=out_specs,
            scratch_shapes=[
                pltpu.VMEM((slots, size, size), jnp.bfloat16),
                pltpu.VMEM((KB, size, NJ * size), jnp.bfloat16),
                *scratch,
                pltpu.SemaphoreType.DMA,
                pltpu.SemaphoreType.DMA,
            ],
        ),
        compiler_params=pltpu.CompilerParams(
            dimension_semantics=("arbitrary",), vmem_limit_bytes=LIMIT
        ),
        cost_estimate=pl.CostEstimate(
            flops=2 * 24 * NJ * size * size * size,
            bytes_accessed=16 * 1024 * 1024,
            transcendentals=0,
        ),
    )(*scalars, *operands)


def first_news_kernel(where_ref, cols_ref, send, out, where, cols, blocks, tile, sems):
    copies = [
        pltpu.make_async_copy(where_ref, where, sems.at[0]),
        pltpu.make_async_copy(cols_ref, cols, sems.at[1]),
    ]
    devices, count = where.shape[-1], blocks.shape[0]
    shares = devices // count
    step = blocks.shape[1] // shares
    for row in range(count):
        copies.append(
            pltpu.make_async_copy(send.at[1, 0, row * shares], blocks.at[row], sems.at[2 + row])
        )
    for copy in copies:
        copy.start()
    rcap, across = cols.shape
    tile[...] = jnp.zeros(tile.shape, tile.dtype)
    for copy in copies:
        copy.wait()
    for slot in range(rcap):
        tile[pl.ds(0, 1), pl.ds(slot * across, across)] = cols[pl.ds(slot, 1), :]
    for half in range(2):
        row, lane = divmod(half * devices, 128)
        tile[pl.ds(1 + row, 1), pl.ds(lane, devices)] = where[half]
    table = tile[...].astype(jnp.float32).astype(out.dtype)

    def fill(device, carry):
        share = pl.multiple_of(device % shares * step, step)
        out[device, pl.ds(0, step), :] = blocks[device // shares, pl.ds(share, step), :]
        out[device, pl.ds(step, 16), :] = table
        return carry

    lax.fori_loop(0, devices, fill, 0)


def first_news(where, cols, send, rows_count):
    devices = where.shape[-1]
    size = send.shape[-1]
    step = size * rows_count // devices
    return pl.pallas_call(
        first_news_kernel,
        out_shape=jax.ShapeDtypeStruct((devices, step + 16, size), send.dtype),
        in_specs=[ANYWHERE] * 3,
        scratch_shapes=[
            pltpu.VMEM(where.shape, jnp.int32),
            pltpu.VMEM(cols.shape, jnp.int32),
            pltpu.VMEM((rows_count, size, size), send.dtype),
            pltpu.VMEM((16, size), jnp.int32),
            pltpu.SemaphoreType.DMA((2 + rows_count,)),
        ],
        compiler_params=pltpu.CompilerParams(vmem_limit_bytes=LIMIT),
    )(in_hbm(where), in_hbm(cols), in_hbm(send))


def needed(where_all, cols_all, rows_count, cols_count):
    grid = where_all.reshape(-1, 2, rows_count, cols_count)
    after = jnp.concatenate([grid[:, 0, :, 1:], grid[:, 1, :, :1]], axis=-1)
    columns = jnp.arange(KB, dtype=jnp.int32)
    hit = (after[..., None] >= 0) & (after[..., None] % KB == columns)
    wanted = jnp.any(hit, axis=0).astype(jnp.int32)
    counts = jnp.sum((cols_all >= 0).astype(jnp.int32), axis=1)
    counts = jnp.roll(counts.reshape(rows_count, cols_count, KB), -1, axis=0)
    return jnp.sum(wanted * counts, axis=-1)


def swapped(value):
    return lax.ppermute(value, "col", [(i, i ^ 1) for i in range(lax.axis_size("col"))])


def local(a_send, a_where, b_strips, b_cols):
    size = a_send.shape[-1]
    rows_count = lax.axis_size("row")
    cols_count = lax.axis_size("col")
    devices = rows_count * cols_count
    both = ("row", "col")
    row_index = lax.axis_index("row")
    col_index = lax.axis_index("col")
    rcap = b_strips.shape[3]
    last = cols_count - 1

    by_slot = jnp.swapaxes(b_cols, 2, 3).reshape(rcap, KB)
    news = lax.all_to_all(
        first_news(a_where, by_slot, a_send, rows_count),
        both, split_axis=0, concat_axis=0, tiled=True,
    )
    step = size // cols_count
    part = news[:, :step]
    tables = news[:, step : step + 1 + -(-2 * devices // 128)].astype(jnp.int32)
    after_col = (col_index + 1) % cols_count
    after_half = (col_index + 1) // cols_count
    row_before = (row_index + rows_count - 1) % rows_count
    row_after = (row_index + 1) % rows_count
    needs = needed(
        tables[:, 1:].reshape(devices, -1)[:, : 2 * devices],
        tables[:, 0].reshape(devices, rcap, KB), rows_count, cols_count,
    )
    room = ALWAYS - jnp.flip(needs.reshape(rows_count, -1, 2), -1).reshape(needs.shape)
    lent = jnp.maximum(jnp.minimum(jnp.minimum(needs - ALWAYS, room), LENT), 0)
    most = jnp.max(needs - lent)

    def lent_to(row, col):
        return lax.dynamic_slice(lent, (row, col), (1, 1))[0, 0]

    spot = jnp.stack([
        after_half,
        row_index * cols_count + col_index,
        row_index * cols_count + after_col,
        row_before * cols_count + after_col,
        row_after * cols_count + col_index,
        lent_to(row_before, col_index ^ 1),
        lent_to(row_before, col_index),
    ]).astype(jnp.int32)

    received = lax.all_to_all(a_send[0, 0], both, split_axis=0, concat_axis=0, tiled=True)

    def to_row_before(blocks):
        return lax.ppermute(
            blocks, "row", [(i, (i - 1) % rows_count) for i in range(rows_count)]
        )

    strips = b_strips.reshape(KB * rcap, size, size)
    guests, *over = pack(pack_spare, (LENT, *PARTS[2:]), spot, tables, strips)
    early, late = pack(pack_main, PARTS[:2], spot, tables, strips, swapped(guests))
    begin, extra = ALWAYS, []
    for blocks in after([received, early], over):
        extra.append(lax.cond(most > begin, to_row_before, lambda same: same, blocks))
        begin += blocks.shape[0]
    early, late = map(to_row_before, after([received, *extra], [early, late]))

    shifted = lax.ppermute(received, "col", [(i + 1, i) for i in range(last)])
    (part,) = after([guests], [part])
    parts = [lax.ppermute(part, "col", [(i, last)]) for i in range(last)] + [part]

    wide = NJ * size
    strip = pl.BlockSpec((GROUP * size, wide), lambda i, *_: (i, 0))
    begun, order, first, target = step_call(
        functools.partial(first_kernel, rcap),
        (spot,), (tables, received, in_hbm(strips)), [ANYWHERE, ANYWHERE, ANYWHERE],
        [
            pltpu.HBM((RB * size, wide), jnp.float32),
            jax.ShapeDtypeStruct((devices,), jnp.int32),
            jax.ShapeDtypeStruct((RB + 3,), jnp.int32),
            jax.ShapeDtypeStruct((KB * rcap,), jnp.int32),
        ],
        [strip, IN_SMEM, IN_SMEM, IN_SMEM],
        [
            pltpu.SMEM(tables.shape, jnp.int32),
            pltpu.SemaphoreType.DMA,
            pltpu.SMEM((devices,), jnp.int32),
            pltpu.SMEM((RB + 2,), jnp.int32),
            pltpu.SMEM((KB,), jnp.int32),
            pltpu.SMEM((KB,), jnp.int32),
        ],
        devices, size,
    )

    on_last = (col_index == last).astype(jnp.int32)
    lent_here = [lent_to(row_index, col_index ^ 1), lent_to(row_index, col_index)]
    scalars = (order, first, target, jnp.stack([on_last, *lent_here]))
    lefts = (shifted, *parts)

    def finish_call(kernel, scalars, operands, out_shape, out_specs, scratch, marks, aliases):
        return pl.pallas_call(
            kernel,
            out_shape=out_shape,
            grid_spec=pltpu.PrefetchScalarGridSpec(
                num_scalar_prefetch=len(scalars),
                grid=(1,),
                in_specs=[ANYWHERE] * len(operands),
                out_specs=out_specs,
                scratch_shapes=[
                    *scratch,
                    pltpu.VMEM((devices, size, size), jnp.bfloat16),
                    pltpu.VMEM((KB, size, wide), jnp.bfloat16),
                    pltpu.VMEM((RB, size, wide), jnp.float32),
                    pltpu.VMEM((RB, size, wide), jnp.bfloat16),
                    *marks,
                    pltpu.SemaphoreType.DMA,
                    pltpu.SemaphoreType.DMA,
                    pltpu.SemaphoreType.DMA((RB,)),
                    pltpu.SemaphoreType.DMA((RB,)),
                ],
            ),
            input_output_aliases=aliases,
            compiler_params=pltpu.CompilerParams(vmem_limit_bytes=LIMIT),
            cost_estimate=pl.CostEstimate(
                flops=2 * 16 * NJ * size * size * size,
                bytes_accessed=12 * 1024 * 1024,
                transcendentals=0,
            ),
        )(*scalars, *operands)

    begun, rounded, guests, later, open_row = finish_call(
        functools.partial(middle_kernel, len(parts)), scalars,
        (*lefts, early, in_hbm(begun)),
        [
            pltpu.HBM((RB * size, wide), jnp.float32),
            pltpu.HBM((RB * size, wide), jnp.bfloat16),
            pltpu.HBM((LENT, size, size), jnp.bfloat16),
            jax.ShapeDtypeStruct((KB,), jnp.int32),
            jax.ShapeDtypeStruct((RB,), jnp.int32),
        ],
        [ANYWHERE, ANYWHERE, ANYWHERE, IN_SMEM, IN_SMEM],
        [
            pltpu.VMEM((LENT, size, size), jnp.bfloat16),
            pltpu.SemaphoreType.DMA,
            pltpu.SemaphoreType.DMA,
        ],
        [pltpu.SMEM((KB,), jnp.int32)], {},
    )
    back = swapped(guests)

    operands = (*lefts, late, back, *extra, in_hbm(begun), rounded)
    scalars = (*scalars, later, open_row)
    return finish_call(
        functools.partial(last_kernel, len(parts)), scalars, operands,
        jax.ShapeDtypeStruct((RB * size, wide), jnp.bfloat16),
        ANYWHERE, [], [], {len(scalars) + len(operands) - 1: 0},
    )


def solution(mesh):
    placed = (
        P(None, ("row", "col"), None, None, None),
        P(None, ("row", "col"), None),
        P("row", "col", None, None, None, None),
        P("row", "col", None, None),
    )
    return jax.shard_map(
        local, mesh=mesh, in_specs=placed, out_specs=P("row", "col"), check_vma=False
    )
```

```python
import functools

import jax
import jax.numpy as jnp
from jax import lax
from jax.experimental import pallas as pl
from jax.experimental.pallas import tpu as pltpu
from jax.sharding import PartitionSpec as P

RB = 16
KB = 16
NJ = 8
PARTS = (66, 24, 8, 8, 22)
ALWAYS = PARTS[0] + PARTS[1]
LENT = 16
GROUP = 4
IN_SMEM = pl.BlockSpec(memory_space=pltpu.SMEM)
ANYWHERE = pl.BlockSpec(memory_space=pl.ANY)
LIMIT = 24 * 1024 * 1024


def in_hbm(value):
    return pltpu.with_memory_space_constraint(value, pltpu.HBM)


def places_in(table, half, owner):
    at = half * table.shape[0] + owner
    return lambda source: table[source, 1 + at // 128, at % 128]


def columns_in(table, rcap, device):
    return lambda slot: table[device, 0, slot % rcap * KB + slot // rcap]


def mark_rows(place, slots, named):
    def reset(j, carry):
        named[j] = 0
        return carry

    def mark(s, carry):
        here = place(s)

        @pl.when(here >= 0)
        def _():
            named[here % KB] = named[here % KB] + 1

        return carry

    lax.fori_loop(0, KB, reset, 0)
    lax.fori_loop(0, slots, mark, 0)


def for_wanted(column, named, rcap, action):
    def visit(slot, number):
        wanted = column(slot) >= 0

        @pl.when(wanted)
        def _():
            action(slot, number)

        return number + wanted.astype(jnp.int32)

    def visit_row(j, match, number):
        return lax.fori_loop(j * rcap, jnp.where(match, (j + 1) * rcap, j * rcap), visit, number)

    count = lax.fori_loop(0, KB, lambda j, n: visit_row(j, named[j] > 1, n), jnp.int32(0))
    return lax.fori_loop(0, KB, lambda j, n: visit_row(j, named[j] == 1, n), count)


def pack_main(spot, tables, strips, guests, *refs):
    early, late, stage, table, sem_table, named, sem, sem_out = refs[-8:]
    shift = spot[5]
    stop = stage.shape[0] - shift

    def greet(number, carry):
        pltpu.make_async_copy(guests.at[number], stage.at[number], sem).start()
        return carry

    lax.fori_loop(0, shift, greet, 0)

    def fetch(slot, number):
        @pl.when(number < stop)
        def _():
            pltpu.make_async_copy(strips.at[slot], stage.at[number + shift], sem).start()

    count = find_wanted(spot, tables, strips, table, sem_table, named, fetch)
    finish_blocks(strips, stage, sem, jnp.minimum(count, stop) + shift)
    hand_over(stage, [early, late], sem_out)


def pack_spare(spot, tables, strips, guests, *refs):
    *over, stage, table, sem_table, named, sem, sem_out = refs
    lent = spot[6]

    def fetch(slot, number):
        beyond = number - ALWAYS

        @pl.when((beyond >= 0) & (beyond < LENT))
        def _():
            pltpu.make_async_copy(strips.at[slot], stage.at[beyond], sem).start()

        @pl.when(beyond >= lent)
        def _():
            at = LENT + beyond - lent
            pltpu.make_async_copy(strips.at[slot], stage.at[at], sem).start()

    count = find_wanted(spot, tables, strips, table, sem_table, named, fetch)
    beyond = jnp.maximum(count - ALWAYS, 0)
    copied = jnp.minimum(beyond, LENT) + jnp.maximum(beyond - lent, 0)
    finish_blocks(strips, stage, sem, copied)
    hand_over(stage, [guests, *over], sem_out)


def find_wanted(spot, tables, strips, table, sem_table, named, action):
    rcap = strips.shape[0] // KB
    table_copy = pltpu.make_async_copy(tables, table, sem_table)
    table_copy.start()
    table_copy.wait()
    mark_rows(places_in(table, spot[0], spot[3]), table.shape[0], named)
    return for_wanted(columns_in(table, rcap, spot[1]), named, rcap, action)


def finish_blocks(source, target, sem, count):
    def finish(number, carry):
        pltpu.make_async_copy(source.at[0], target.at[0], sem).wait()
        return carry

    lax.fori_loop(0, count, finish, 0)


def hand_over(stage, outs, sem_out):
    copies, low = [], 0
    for i, out in enumerate(outs):
        here = stage.at[pl.ds(low, out.shape[0])]
        copies.append(pltpu.make_async_copy(here, out, sem_out.at[i]))
        copies[-1].start()
        low += out.shape[0]
    for copy in copies:
        copy.wait()


def pack(kernel, counts, spot, tables, strips, *more):
    size = strips.shape[-1]
    return pl.pallas_call(
        kernel,
        out_shape=[pltpu.HBM((n, size, size), strips.dtype) for n in counts],
        grid_spec=pltpu.PrefetchScalarGridSpec(
            num_scalar_prefetch=1,
            grid=(1,),
            in_specs=[ANYWHERE] * (2 + len(more)),
            out_specs=[ANYWHERE] * len(counts),
            scratch_shapes=[
                pltpu.VMEM((sum(counts), size, size), strips.dtype),
                pltpu.SMEM(tables.shape, jnp.int32),
                pltpu.SemaphoreType.DMA,
                pltpu.SMEM((KB,), jnp.int32),
                pltpu.SemaphoreType.DMA,
                pltpu.SemaphoreType.DMA((len(counts),)),
            ],
        ),
        compiler_params=pltpu.CompilerParams(vmem_limit_bytes=LIMIT),
        cost_estimate=pl.CostEstimate(
            flops=0, bytes_accessed=4 * sum(counts) * size * size, transcendentals=0
        ),
    )(spot, tables, in_hbm(strips), *more)


def after(values, blocks):
    count = len(blocks)
    return pl.pallas_call(
        lambda *refs: None,
        out_shape=[pltpu.HBM(each.shape, each.dtype) for each in blocks],
        in_specs=[ANYWHERE] * (count + len(values)),
        out_specs=[ANYWHERE] * count,
        input_output_aliases={i: i for i in range(count)},
        compiler_params=pltpu.CompilerParams(vmem_limit_bytes=LIMIT),
    )(*blocks, *values)


def by_block_row(place, slots, order, first):
    def reset(i, carry):
        first[i] = 0
        return carry

    def count(s, carry):
        here = place(s)

        @pl.when(here >= 0)
        def _():
            i = here // KB + 2
            first[i] = first[i] + 1

        return carry

    def scan(i, carry):
        first[i] = first[i] + first[i - 1]
        return carry

    def sort(s, carry):
        here = place(s)

        @pl.when(here >= 0)
        def _():
            i = here // KB + 1
            order[first[i]] = s * KB + here % KB
            first[i] = first[i] + 1

        return carry

    lax.fori_loop(0, RB + 2, reset, 0)
    lax.fori_loop(0, slots, count, 0)
    lax.fori_loop(1, RB + 2, scan, 0)
    lax.fori_loop(0, slots, sort, 0)


def clear(right, wanted):
    def one(j, carry):
        @pl.when(wanted(j))
        def _():
            right[j] = jnp.zeros(right.shape[1:], right.dtype)

        return carry

    lax.fori_loop(0, KB, one, 0)


def add_product(total, left, right, pair):
    slot, column = pair // KB, pair % KB
    wide = right.shape[-1]
    step = 2 * left.shape[-1]
    for low in range(0, wide, step):
        here = pl.ds(low, step)
        total[:, here] += jnp.dot(
            left[slot], right[column, :, here], preferred_element_type=jnp.float32
        )


def add_rows(left, right, total, order, first):
    size = left.shape[1]

    def one_row(i, carry):
        row = pl.program_id(0) * GROUP + i
        here = pl.ds(pl.multiple_of(i * size, size), size)

        def add(entry, carry):
            add_product(total.at[here], left, right, order[entry])
            return carry

        return lax.fori_loop(first[row], first[row + 1], add, carry)

    lax.fori_loop(0, GROUP, one_row, 0)


def place_at(right, where):
    size = right.shape[1]
    start = pl.multiple_of((where % NJ) * size, size)
    return right.at[where // NJ, :, pl.ds(start, size)]


def finish_right(source, right, sem, count):
    def finish(number, carry):
        pltpu.make_async_copy(source, place_at(right, 0), sem).wait()
        return carry

    lax.fori_loop(0, count, finish, 0)


def first_kernel(
    rcap, spot, tables, received, strips,
    out, next_order, next_first, next_target,
    left, right, table, sem_table, order, first, named, other, sem_left, sem_right,
):
    slots, size, _ = left.shape

    @pl.when(pl.program_id(0) == 0)
    def _():
        left_copy = pltpu.make_async_copy(received, left, sem_left)
        left_copy.start()
        table_copy = pltpu.make_async_copy(tables, table, sem_table)
        table_copy.start()
        table_copy.wait()
        place = places_in(table, 0, spot[1])
        column = columns_in(table, rcap, spot[1])
        mark_rows(place, slots, named)
        clear(right, lambda j: named[j] > 0)

        def fetch(slot, number):
            target = place_at(right, slot // rcap * NJ + column(slot))
            pltpu.make_async_copy(strips.at[slot], target, sem_right).start()

        count = for_wanted(column, named, rcap, fetch)
        by_block_row(place, slots, order, first)

        next_place = places_in(table, spot[0], spot[2])
        next_column = columns_in(table, rcap, spot[4])
        by_block_row(next_place, slots, next_order, next_first)
        mark_rows(next_place, slots, other)

        def note(slot, number):
            next_target[number] = slot // rcap * NJ + next_column(slot)

        next_first[RB + 2] = for_wanted(next_column, other, rcap, note)
        left_copy.wait()
        finish_right(strips.at[0], right, sem_right, count)

    out[...] = jnp.zeros(out.shape, out.dtype)
    add_rows(left, right, out, order, first)


def start_left(shifted, parts, left, on_last, sem):
    step = left.shape[1] // len(parts)
    whole = pltpu.make_async_copy(shifted, left, sem)

    @pl.when(on_last)
    def _():
        for q, part in enumerate(parts):
            pltpu.make_async_copy(part, left.at[:, pl.ds(q * step, step)], sem).start()

    @pl.when(jnp.logical_not(on_last))
    def _():
        whole.start()

    return whole


def start_right(sources, count, target, right, sem):
    for blocks, low, start, stop in sources:

        def fetch(number, carry):
            pltpu.make_async_copy(
                blocks.at[number - low], place_at(right, target[number]), sem
            ).start()
            return carry

        lax.fori_loop(start, jnp.minimum(count, stop), fetch, 0)


def add_products(row, order, first, left, right, touched, total):
    def add(entry, carry):
        @pl.when(touched[order[entry] % KB] > 0)
        def _():
            add_product(total.at[row], left, right, order[entry])

        return carry

    lax.fori_loop(first[row], first[row + 1], add, 0)


def mark_targets(target, begin, end, marks):
    def reset(j, carry):
        marks[j] = 0
        return carry

    def mark(number, carry):
        marks[target[number] // NJ] = 1
        return carry

    lax.fori_loop(0, KB, reset, 0)
    lax.fori_loop(begin, end, mark, 0)


def mark_open(order, first, touched, open_row):
    def one(row, carry):
        def look(entry, found):
            return jnp.maximum(found, touched[order[entry] % KB])

        open_row[row] = lax.fori_loop(first[row], first[row + 1], look, jnp.int32(0))
        return carry

    lax.fori_loop(0, RB, one, 0)


def strip_of(ref, row, size):
    return ref.at[pl.ds(pl.multiple_of(row * size, size), size)]


def middle_kernel(parts_count, order, first, target, flags, *refs):
    shifted, *parts = refs[: 1 + parts_count]
    (
        piece, prev, out, rounded, guests, later, open_row,
        hall, sem_in, sem_home,
        left, right, total, short, touched,
        sem_left, sem_right, sem_prev, sem_out,
    ) = refs[1 + parts_count :]
    arrive = pltpu.make_async_copy(piece.at[pl.ds(0, LENT)], hall, sem_in)
    leave = pltpu.make_async_copy(hall, guests, sem_home)
    arrive.start()
    size = left.shape[1]
    count = first[RB + 2]
    shift = flags[1]
    end = piece.shape[0] - shift

    def prev_copy(row):
        return pltpu.make_async_copy(strip_of(prev, row, size), total.at[row], sem_prev.at[row])

    def start_prev(row, carry):
        prev_copy(row).start()
        return carry

    lax.fori_loop(0, RB, start_prev, 0)
    whole = start_left(shifted, parts, left, flags[0] > 0, sem_left)
    fetched = jnp.minimum(count, end)
    mark_targets(target, 0, fetched, touched)
    clear(right, lambda j: touched[j] > 0)
    start_right([(piece, -shift, 0, end)], fetched, target, right, sem_right)
    arrive.wait()
    leave.start()
    mark_targets(target, end, count, later)
    mark_open(order, first, later, open_row)
    whole.wait()
    finish_right(piece.at[0], right, sem_right, fetched)

    def out_copies(row):
        return (
            pltpu.make_async_copy(total.at[row], strip_of(out, row, size), sem_out.at[row]),
            pltpu.make_async_copy(short.at[row], strip_of(rounded, row, size), sem_out.at[row]),
        )

    def one_row(row, carry):
        open_copy, closed_copy = out_copies(row)
        prev_copy(row).wait()
        add_products(row, order, first, left, right, touched, total)

        @pl.when(open_row[row] > 0)
        def _():
            open_copy.start()

        @pl.when(open_row[row] == 0)
        def _():
            short[row] = total[row].astype(short.dtype)
            closed_copy.start()

        return carry

    def close_row(row, carry):
        open_copy, closed_copy = out_copies(row)

        @pl.when(open_row[row] > 0)
        def _():
            open_copy.wait()

        @pl.when(open_row[row] == 0)
        def _():
            closed_copy.wait()

        return carry

    lax.fori_loop(0, RB, one_row, 0)
    lax.fori_loop(0, RB, close_row, 0)
    leave.wait()


def last_kernel(parts_count, order, first, target, flags, touched, open_row, *refs):
    shifted, *parts = refs[: 1 + parts_count]
    (
        piece, back, *over, prev, _, out,
        left, right, total, short,
        sem_left, sem_right, sem_prev, sem_out,
    ) = refs[1 + parts_count :]
    size = left.shape[1]
    count = first[RB + 2]
    shift, lent = flags[1], flags[2]
    begin = PARTS[0] - shift

    def prev_copy(row):
        return pltpu.make_async_copy(strip_of(prev, row, size), total.at[row], sem_prev.at[row])

    def start_prev(row, carry):
        @pl.when(open_row[row] > 0)
        def _():
            prev_copy(row).start()

        return carry

    lax.fori_loop(0, RB, start_prev, 0)
    whole = start_left(shifted, parts, left, flags[0] > 0, sem_left)
    low = ALWAYS
    sources = [(piece, begin, begin, low - shift), (back, low, low, low + lent)]
    low = low + lent
    for blocks in over:
        high = low + blocks.shape[0]
        sources.append((blocks, low, low, high))
        low = high
    clear(right, lambda j: touched[j] > 0)
    start_right(sources, count, target, right, sem_right)

    def out_copy(row):
        return pltpu.make_async_copy(short.at[row], strip_of(out, row, size), sem_out.at[row])

    whole.wait()
    finish_right(piece.at[0], right, sem_right, count - begin)

    def one_row(row, carry):
        @pl.when(open_row[row] > 0)
        def _():
            prev_copy(row).wait()
            add_products(row, order, first, left, right, touched, total)
            short[row] = total[row].astype(short.dtype)
            out_copy(row).start()

        return carry

    def close_row(row, carry):
        @pl.when(open_row[row] > 0)
        def _():
            out_copy(row).wait()

        return carry

    lax.fori_loop(0, RB, one_row, 0)
    lax.fori_loop(0, RB, close_row, 0)


def step_call(kernel, scalars, operands, specs, out_shape, out_specs, scratch, slots, size):
    return pl.pallas_call(
        kernel,
        out_shape=out_shape,
        grid_spec=pltpu.PrefetchScalarGridSpec(
            num_scalar_prefetch=len(scalars),
            grid=(RB // GROUP,),
            in_specs=specs,
            out_specs=out_specs,
            scratch_shapes=[
                pltpu.VMEM((slots, size, size), jnp.bfloat16),
                pltpu.VMEM((KB, size, NJ * size), jnp.bfloat16),
                *scratch,
                pltpu.SemaphoreType.DMA,
                pltpu.SemaphoreType.DMA,
            ],
        ),
        compiler_params=pltpu.CompilerParams(
            dimension_semantics=("arbitrary",), vmem_limit_bytes=LIMIT
        ),
        cost_estimate=pl.CostEstimate(
            flops=2 * 24 * NJ * size * size * size,
            bytes_accessed=16 * 1024 * 1024,
            transcendentals=0,
        ),
    )(*scalars, *operands)


def first_news_kernel(where_ref, cols_ref, send, out, where, cols, blocks, tile, sems):
    copies = [
        pltpu.make_async_copy(where_ref, where, sems.at[0]),
        pltpu.make_async_copy(cols_ref, cols, sems.at[1]),
    ]
    devices, count = where.shape[-1], blocks.shape[0]
    shares = devices // count
    step = blocks.shape[1] // shares
    for row in range(count):
        copies.append(
            pltpu.make_async_copy(send.at[1, 0, row * shares], blocks.at[row], sems.at[2 + row])
        )
    for copy in copies:
        copy.start()
    rcap, across = cols.shape
    tile[...] = jnp.zeros(tile.shape, tile.dtype)
    for copy in copies:
        copy.wait()
    for slot in range(rcap):
        tile[pl.ds(0, 1), pl.ds(slot * across, across)] = cols[pl.ds(slot, 1), :]
    for half in range(2):
        row, lane = divmod(half * devices, 128)
        tile[pl.ds(1 + row, 1), pl.ds(lane, devices)] = where[half]
    table = tile[...].astype(jnp.float32).astype(out.dtype)

    def fill(device, carry):
        share = pl.multiple_of(device % shares * step, step)
        out[device, pl.ds(0, step), :] = blocks[device // shares, pl.ds(share, step), :]
        out[device, pl.ds(step, 16), :] = table
        return carry

    lax.fori_loop(0, devices, fill, 0)


def first_news(where, cols, send, rows_count):
    devices = where.shape[-1]
    size = send.shape[-1]
    step = size * rows_count // devices
    return pl.pallas_call(
        first_news_kernel,
        out_shape=jax.ShapeDtypeStruct((devices, step + 16, size), send.dtype),
        in_specs=[ANYWHERE] * 3,
        scratch_shapes=[
            pltpu.VMEM(where.shape, jnp.int32),
            pltpu.VMEM(cols.shape, jnp.int32),
            pltpu.VMEM((rows_count, size, size), send.dtype),
            pltpu.VMEM((16, size), jnp.int32),
            pltpu.SemaphoreType.DMA((2 + rows_count,)),
        ],
        compiler_params=pltpu.CompilerParams(vmem_limit_bytes=LIMIT),
    )(in_hbm(where), in_hbm(cols), in_hbm(send))


def needed(where_all, cols_all, rows_count, cols_count):
    grid = where_all.reshape(-1, 2, rows_count, cols_count)
    after = jnp.concatenate([grid[:, 0, :, 1:], grid[:, 1, :, :1]], axis=-1)
    columns = jnp.arange(KB, dtype=jnp.int32)
    hit = (after[..., None] >= 0) & (after[..., None] % KB == columns)
    wanted = jnp.any(hit, axis=0).astype(jnp.int32)
    counts = jnp.sum((cols_all >= 0).astype(jnp.int32), axis=1)
    counts = jnp.roll(counts.reshape(rows_count, cols_count, KB), -1, axis=0)
    return jnp.sum(wanted * counts, axis=-1)


def swapped(value):
    return lax.ppermute(value, "col", [(i, i ^ 1) for i in range(lax.axis_size("col"))])


def local(a_send, a_where, b_strips, b_cols):
    size = a_send.shape[-1]
    rows_count = lax.axis_size("row")
    cols_count = lax.axis_size("col")
    devices = rows_count * cols_count
    both = ("row", "col")
    row_index = lax.axis_index("row")
    col_index = lax.axis_index("col")
    rcap = b_strips.shape[3]
    last = cols_count - 1

    by_slot = jnp.swapaxes(b_cols, 2, 3).reshape(rcap, KB)
    news = lax.all_to_all(
        first_news(a_where, by_slot, a_send, rows_count),
        both, split_axis=0, concat_axis=0, tiled=True,
    )
    step = size // cols_count
    part = news[:, :step]
    tables = news[:, step : step + 1 + -(-2 * devices // 128)].astype(jnp.int32)
    after_col = (col_index + 1) % cols_count
    after_half = (col_index + 1) // cols_count
    row_before = (row_index + rows_count - 1) % rows_count
    row_after = (row_index + 1) % rows_count
    needs = needed(
        tables[:, 1:].reshape(devices, -1)[:, : 2 * devices],
        tables[:, 0].reshape(devices, rcap, KB), rows_count, cols_count,
    )
    room = ALWAYS - jnp.flip(needs.reshape(rows_count, -1, 2), -1).reshape(needs.shape)
    lent = jnp.maximum(jnp.minimum(jnp.minimum(needs - ALWAYS, room), LENT), 0)
    most = jnp.max(needs - lent)

    def lent_to(row, col):
        return lax.dynamic_slice(lent, (row, col), (1, 1))[0, 0]

    spot = jnp.stack([
        after_half,
        row_index * cols_count + col_index,
        row_index * cols_count + after_col,
        row_before * cols_count + after_col,
        row_after * cols_count + col_index,
        lent_to(row_before, col_index ^ 1),
        lent_to(row_before, col_index),
    ]).astype(jnp.int32)

    received = lax.all_to_all(a_send[0, 0], both, split_axis=0, concat_axis=0, tiled=True)

    def to_row_before(blocks):
        return lax.ppermute(
            blocks, "row", [(i, (i - 1) % rows_count) for i in range(rows_count)]
        )

    strips = b_strips.reshape(KB * rcap, size, size)
    guests, *over = pack(pack_spare, (LENT, *PARTS[2:]), spot, tables, strips)
    early, late = pack(pack_main, PARTS[:2], spot, tables, strips, swapped(guests))
    begin, extra = ALWAYS, []
    for blocks in (*after([received, early], over[:-1]), over[-1]):
        extra.append(lax.cond(most > begin, to_row_before, lambda same: same, blocks))
        begin += blocks.shape[0]
    early, late = map(to_row_before, after([received, *extra[:-1]], [early, late]))

    shifted = lax.ppermute(received, "col", [(i + 1, i) for i in range(last)])
    (part,) = after([guests], [part])
    parts = [lax.ppermute(part, "col", [(i, last)]) for i in range(last)] + [part]

    wide = NJ * size
    strip = pl.BlockSpec((GROUP * size, wide), lambda i, *_: (i, 0))
    begun, order, first, target = step_call(
        functools.partial(first_kernel, rcap),
        (spot,), (tables, received, in_hbm(strips)), [ANYWHERE, ANYWHERE, ANYWHERE],
        [
            pltpu.HBM((RB * size, wide), jnp.float32),
            jax.ShapeDtypeStruct((devices,), jnp.int32),
            jax.ShapeDtypeStruct((RB + 3,), jnp.int32),
            jax.ShapeDtypeStruct((KB * rcap,), jnp.int32),
        ],
        [strip, IN_SMEM, IN_SMEM, IN_SMEM],
        [
            pltpu.SMEM(tables.shape, jnp.int32),
            pltpu.SemaphoreType.DMA,
            pltpu.SMEM((devices,), jnp.int32),
            pltpu.SMEM((RB + 2,), jnp.int32),
            pltpu.SMEM((KB,), jnp.int32),
            pltpu.SMEM((KB,), jnp.int32),
        ],
        devices, size,
    )

    on_last = (col_index == last).astype(jnp.int32)
    lent_here = [lent_to(row_index, col_index ^ 1), lent_to(row_index, col_index)]
    scalars = (order, first, target, jnp.stack([on_last, *lent_here]))
    lefts = (shifted, *parts)

    def finish_call(kernel, scalars, operands, out_shape, out_specs, scratch, marks, aliases):
        return pl.pallas_call(
            kernel,
            out_shape=out_shape,
            grid_spec=pltpu.PrefetchScalarGridSpec(
                num_scalar_prefetch=len(scalars),
                grid=(1,),
                in_specs=[ANYWHERE] * len(operands),
                out_specs=out_specs,
                scratch_shapes=[
                    *scratch,
                    pltpu.VMEM((devices, size, size), jnp.bfloat16),
                    pltpu.VMEM((KB, size, wide), jnp.bfloat16),
                    pltpu.VMEM((RB, size, wide), jnp.float32),
                    pltpu.VMEM((RB, size, wide), jnp.bfloat16),
                    *marks,
                    pltpu.SemaphoreType.DMA,
                    pltpu.SemaphoreType.DMA,
                    pltpu.SemaphoreType.DMA((RB,)),
                    pltpu.SemaphoreType.DMA((RB,)),
                ],
            ),
            input_output_aliases=aliases,
            compiler_params=pltpu.CompilerParams(vmem_limit_bytes=LIMIT),
            cost_estimate=pl.CostEstimate(
                flops=2 * 16 * NJ * size * size * size,
                bytes_accessed=12 * 1024 * 1024,
                transcendentals=0,
            ),
        )(*scalars, *operands)

    begun, rounded, guests, later, open_row = finish_call(
        functools.partial(middle_kernel, len(parts)), scalars,
        (*lefts, early, in_hbm(begun)),
        [
            pltpu.HBM((RB * size, wide), jnp.float32),
            pltpu.HBM((RB * size, wide), jnp.bfloat16),
            pltpu.HBM((LENT, size, size), jnp.bfloat16),
            jax.ShapeDtypeStruct((KB,), jnp.int32),
            jax.ShapeDtypeStruct((RB,), jnp.int32),
        ],
        [ANYWHERE, ANYWHERE, ANYWHERE, IN_SMEM, IN_SMEM],
        [
            pltpu.VMEM((LENT, size, size), jnp.bfloat16),
            pltpu.SemaphoreType.DMA,
            pltpu.SemaphoreType.DMA,
        ],
        [pltpu.SMEM((KB,), jnp.int32)], {},
    )
    back = swapped(guests)

    operands = (*lefts, late, back, *extra, in_hbm(begun), rounded)
    scalars = (*scalars, later, open_row)
    return finish_call(
        functools.partial(last_kernel, len(parts)), scalars, operands,
        jax.ShapeDtypeStruct((RB * size, wide), jnp.bfloat16),
        ANYWHERE, [], [], {len(scalars) + len(operands) - 1: 0},
    )


def solution(mesh):
    placed = (
        P(None, ("row", "col"), None, None, None),
        P(None, ("row", "col"), None),
        P("row", "col", None, None, None, None),
        P("row", "col", None, None),
    )
    return jax.shard_map(
        local, mesh=mesh, in_specs=placed, out_specs=P("row", "col"), check_vma=False
    )
```

```python
import functools

import jax
import jax.numpy as jnp
from jax import lax
from jax.experimental import pallas as pl
from jax.experimental.pallas import tpu as pltpu
from jax.sharding import PartitionSpec as P

RB = 16
KB = 16
NJ = 8
PARTS = (70, 22, 8, 8, 20)
ALWAYS = PARTS[0] + PARTS[1]
LENT = 16
GROUP = 4
IN_SMEM = pl.BlockSpec(memory_space=pltpu.SMEM)
ANYWHERE = pl.BlockSpec(memory_space=pl.ANY)
LIMIT = 24 * 1024 * 1024


def in_hbm(value):
    return pltpu.with_memory_space_constraint(value, pltpu.HBM)


def places_in(table, half, owner):
    at = half * table.shape[0] + owner
    return lambda source: table[source, 1 + at // 128, at % 128]


def columns_in(table, rcap, device):
    return lambda slot: table[device, 0, slot % rcap * KB + slot // rcap]


def mark_rows(place, slots, named):
    def reset(j, carry):
        named[j] = 0
        return carry

    def mark(s, carry):
        here = place(s)

        @pl.when(here >= 0)
        def _():
            named[here % KB] = named[here % KB] + 1

        return carry

    lax.fori_loop(0, KB, reset, 0)
    lax.fori_loop(0, slots, mark, 0)


def for_wanted(column, named, rcap, action):
    def visit(slot, number):
        wanted = column(slot) >= 0

        @pl.when(wanted)
        def _():
            action(slot, number)

        return number + wanted.astype(jnp.int32)

    def visit_row(j, match, number):
        return lax.fori_loop(j * rcap, jnp.where(match, (j + 1) * rcap, j * rcap), visit, number)

    count = lax.fori_loop(0, KB, lambda j, n: visit_row(j, named[j] > 1, n), jnp.int32(0))
    return lax.fori_loop(0, KB, lambda j, n: visit_row(j, named[j] == 1, n), count)


def pack_main(spot, tables, strips, guests, *refs):
    early, late, stage, table, sem_table, named, sem, sem_out = refs[-8:]
    shift = spot[5]
    stop = stage.shape[0] - shift

    def greet(number, carry):
        pltpu.make_async_copy(guests.at[number], stage.at[number], sem).start()
        return carry

    lax.fori_loop(0, shift, greet, 0)

    def fetch(slot, number):
        @pl.when(number < stop)
        def _():
            pltpu.make_async_copy(strips.at[slot], stage.at[number + shift], sem).start()

    count = find_wanted(spot, tables, strips, table, sem_table, named, fetch)
    finish_blocks(strips, stage, sem, jnp.minimum(count, stop) + shift)
    hand_over(stage, [early, late], sem_out)


def pack_spare(spot, tables, strips, guests, *refs):
    *over, stage, table, sem_table, named, sem, sem_out = refs
    lent = spot[6]

    def fetch(slot, number):
        beyond = number - ALWAYS

        @pl.when((beyond >= 0) & (beyond < LENT))
        def _():
            pltpu.make_async_copy(strips.at[slot], stage.at[beyond], sem).start()

        @pl.when(beyond >= lent)
        def _():
            at = LENT + beyond - lent
            pltpu.make_async_copy(strips.at[slot], stage.at[at], sem).start()

    count = find_wanted(spot, tables, strips, table, sem_table, named, fetch)
    beyond = jnp.maximum(count - ALWAYS, 0)
    copied = jnp.minimum(beyond, LENT) + jnp.maximum(beyond - lent, 0)
    finish_blocks(strips, stage, sem, copied)
    hand_over(stage, [guests, *over], sem_out)


def find_wanted(spot, tables, strips, table, sem_table, named, action):
    rcap = strips.shape[0] // KB
    table_copy = pltpu.make_async_copy(tables, table, sem_table)
    table_copy.start()
    table_copy.wait()
    mark_rows(places_in(table, spot[0], spot[3]), table.shape[0], named)
    return for_wanted(columns_in(table, rcap, spot[1]), named, rcap, action)


def finish_blocks(source, target, sem, count):
    def finish(number, carry):
        pltpu.make_async_copy(source.at[0], target.at[0], sem).wait()
        return carry

    lax.fori_loop(0, count, finish, 0)


def hand_over(stage, outs, sem_out):
    copies, low = [], 0
    for i, out in enumerate(outs):
        here = stage.at[pl.ds(low, out.shape[0])]
        copies.append(pltpu.make_async_copy(here, out, sem_out.at[i]))
        copies[-1].start()
        low += out.shape[0]
    for copy in copies:
        copy.wait()


def pack(kernel, counts, spot, tables, strips, *more):
    size = strips.shape[-1]
    return pl.pallas_call(
        kernel,
        out_shape=[pltpu.HBM((n, size, size), strips.dtype) for n in counts],
        grid_spec=pltpu.PrefetchScalarGridSpec(
            num_scalar_prefetch=1,
            grid=(1,),
            in_specs=[ANYWHERE] * (2 + len(more)),
            out_specs=[ANYWHERE] * len(counts),
            scratch_shapes=[
                pltpu.VMEM((sum(counts), size, size), strips.dtype),
                pltpu.SMEM(tables.shape, jnp.int32),
                pltpu.SemaphoreType.DMA,
                pltpu.SMEM((KB,), jnp.int32),
                pltpu.SemaphoreType.DMA,
                pltpu.SemaphoreType.DMA((len(counts),)),
            ],
        ),
        compiler_params=pltpu.CompilerParams(vmem_limit_bytes=LIMIT),
        cost_estimate=pl.CostEstimate(
            flops=0, bytes_accessed=4 * sum(counts) * size * size, transcendentals=0
        ),
    )(spot, tables, in_hbm(strips), *more)


def after(value, blocks):
    count = len(blocks)
    return pl.pallas_call(
        lambda *refs: None,
        out_shape=[pltpu.HBM(each.shape, each.dtype) for each in blocks],
        in_specs=[ANYWHERE] * (count + 1),
        out_specs=[ANYWHERE] * count,
        input_output_aliases={i: i for i in range(count)},
        compiler_params=pltpu.CompilerParams(vmem_limit_bytes=LIMIT),
    )(*blocks, value)


def by_block_row(place, slots, order, first):
    def reset(i, carry):
        first[i] = 0
        return carry

    def count(s, carry):
        here = place(s)

        @pl.when(here >= 0)
        def _():
            i = here // KB + 2
            first[i] = first[i] + 1

        return carry

    def scan(i, carry):
        first[i] = first[i] + first[i - 1]
        return carry

    def sort(s, carry):
        here = place(s)

        @pl.when(here >= 0)
        def _():
            i = here // KB + 1
            order[first[i]] = s * KB + here % KB
            first[i] = first[i] + 1

        return carry

    lax.fori_loop(0, RB + 2, reset, 0)
    lax.fori_loop(0, slots, count, 0)
    lax.fori_loop(1, RB + 2, scan, 0)
    lax.fori_loop(0, slots, sort, 0)


def clear(right, wanted):
    def one(j, carry):
        @pl.when(wanted(j))
        def _():
            right[j] = jnp.zeros(right.shape[1:], right.dtype)

        return carry

    lax.fori_loop(0, KB, one, 0)


def add_product(total, left, right, pair):
    slot, column = pair // KB, pair % KB
    wide = right.shape[-1]
    step = 2 * left.shape[-1]
    for low in range(0, wide, step):
        here = pl.ds(low, step)
        total[:, here] += jnp.dot(
            left[slot], right[column, :, here], preferred_element_type=jnp.float32
        )


def add_rows(left, right, total, order, first):
    size = left.shape[1]

    def one_row(i, carry):
        row = pl.program_id(0) * GROUP + i
        here = pl.ds(pl.multiple_of(i * size, size), size)

        def add(entry, carry):
            add_product(total.at[here], left, right, order[entry])
            return carry

        return lax.fori_loop(first[row], first[row + 1], add, carry)

    lax.fori_loop(0, GROUP, one_row, 0)


def place_at(right, where):
    size = right.shape[1]
    start = pl.multiple_of((where % NJ) * size, size)
    return right.at[where // NJ, :, pl.ds(start, size)]


def finish_right(source, right, sem, count):
    def finish(number, carry):
        pltpu.make_async_copy(source, place_at(right, 0), sem).wait()
        return carry

    lax.fori_loop(0, count, finish, 0)


def first_kernel(
    rcap, spot, tables, received, strips,
    out, next_order, next_first, next_target,
    left, right, table, sem_table, order, first, named, other, sem_left, sem_right,
):
    slots, size, _ = left.shape

    @pl.when(pl.program_id(0) == 0)
    def _():
        left_copy = pltpu.make_async_copy(received, left, sem_left)
        left_copy.start()
        table_copy = pltpu.make_async_copy(tables, table, sem_table)
        table_copy.start()
        table_copy.wait()
        place = places_in(table, 0, spot[1])
        column = columns_in(table, rcap, spot[1])
        mark_rows(place, slots, named)
        clear(right, lambda j: named[j] > 0)

        def fetch(slot, number):
            target = place_at(right, slot // rcap * NJ + column(slot))
            pltpu.make_async_copy(strips.at[slot], target, sem_right).start()

        count = for_wanted(column, named, rcap, fetch)
        by_block_row(place, slots, order, first)

        next_place = places_in(table, spot[0], spot[2])
        next_column = columns_in(table, rcap, spot[4])
        by_block_row(next_place, slots, next_order, next_first)
        mark_rows(next_place, slots, other)

        def note(slot, number):
            next_target[number] = slot // rcap * NJ + next_column(slot)

        next_first[RB + 2] = for_wanted(next_column, other, rcap, note)
        left_copy.wait()
        finish_right(strips.at[0], right, sem_right, count)

    out[...] = jnp.zeros(out.shape, out.dtype)
    add_rows(left, right, out, order, first)


def start_left(shifted, parts, left, on_last, sem):
    step = left.shape[1] // len(parts)
    whole = pltpu.make_async_copy(shifted, left, sem)

    @pl.when(on_last)
    def _():
        for q, part in enumerate(parts):
            pltpu.make_async_copy(part, left.at[:, pl.ds(q * step, step)], sem).start()

    @pl.when(jnp.logical_not(on_last))
    def _():
        whole.start()

    return whole


def start_right(sources, count, target, right, sem):
    for blocks, low, start, stop in sources:

        def fetch(number, carry):
            pltpu.make_async_copy(
                blocks.at[number - low], place_at(right, target[number]), sem
            ).start()
            return carry

        lax.fori_loop(start, jnp.minimum(count, stop), fetch, 0)


def add_products(row, order, first, left, right, touched, total):
    def add(entry, carry):
        @pl.when(touched[order[entry] % KB] > 0)
        def _():
            add_product(total.at[row], left, right, order[entry])

        return carry

    lax.fori_loop(first[row], first[row + 1], add, 0)


def mark_targets(target, begin, end, marks):
    def reset(j, carry):
        marks[j] = 0
        return carry

    def mark(number, carry):
        marks[target[number] // NJ] = 1
        return carry

    lax.fori_loop(0, KB, reset, 0)
    lax.fori_loop(begin, end, mark, 0)


def mark_open(order, first, touched, open_row):
    def one(row, carry):
        def look(entry, found):
            return jnp.maximum(found, touched[order[entry] % KB])

        open_row[row] = lax.fori_loop(first[row], first[row + 1], look, jnp.int32(0))
        return carry

    lax.fori_loop(0, RB, one, 0)


def strip_of(ref, row, size):
    return ref.at[pl.ds(pl.multiple_of(row * size, size), size)]


def middle_kernel(parts_count, order, first, target, flags, *refs):
    shifted, *parts = refs[: 1 + parts_count]
    (
        piece, prev, out, rounded, guests, later, open_row,
        hall, sem_in, sem_home,
        left, right, total, short, touched,
        sem_left, sem_right, sem_prev, sem_out,
    ) = refs[1 + parts_count :]
    arrive = pltpu.make_async_copy(piece.at[pl.ds(0, LENT)], hall, sem_in)
    leave = pltpu.make_async_copy(hall, guests, sem_home)
    arrive.start()
    size = left.shape[1]
    count = first[RB + 2]
    shift = flags[1]
    end = piece.shape[0] - shift

    def prev_copy(row):
        return pltpu.make_async_copy(strip_of(prev, row, size), total.at[row], sem_prev.at[row])

    def start_prev(row, carry):
        prev_copy(row).start()
        return carry

    lax.fori_loop(0, RB, start_prev, 0)
    whole = start_left(shifted, parts, left, flags[0] > 0, sem_left)
    fetched = jnp.minimum(count, end)
    mark_targets(target, 0, fetched, touched)
    clear(right, lambda j: touched[j] > 0)
    start_right([(piece, -shift, 0, end)], fetched, target, right, sem_right)
    arrive.wait()
    leave.start()
    mark_targets(target, end, count, later)
    mark_open(order, first, later, open_row)
    whole.wait()
    finish_right(piece.at[0], right, sem_right, fetched)

    def out_copies(row):
        return (
            pltpu.make_async_copy(total.at[row], strip_of(out, row, size), sem_out.at[row]),
            pltpu.make_async_copy(short.at[row], strip_of(rounded, row, size), sem_out.at[row]),
        )

    def one_row(row, carry):
        open_copy, closed_copy = out_copies(row)
        prev_copy(row).wait()
        add_products(row, order, first, left, right, touched, total)

        @pl.when(open_row[row] > 0)
        def _():
            open_copy.start()

        @pl.when(open_row[row] == 0)
        def _():
            short[row] = total[row].astype(short.dtype)
            closed_copy.start()

        return carry

    def close_row(row, carry):
        open_copy, closed_copy = out_copies(row)

        @pl.when(open_row[row] > 0)
        def _():
            open_copy.wait()

        @pl.when(open_row[row] == 0)
        def _():
            closed_copy.wait()

        return carry

    lax.fori_loop(0, RB, one_row, 0)
    lax.fori_loop(0, RB, close_row, 0)
    leave.wait()


def last_kernel(parts_count, order, first, target, flags, touched, open_row, *refs):
    shifted, *parts = refs[: 1 + parts_count]
    (
        piece, back, *over, prev, _, out,
        left, right, total, short,
        sem_left, sem_right, sem_prev, sem_out,
    ) = refs[1 + parts_count :]
    size = left.shape[1]
    count = first[RB + 2]
    shift, lent = flags[1], flags[2]
    begin = PARTS[0] - shift

    def prev_copy(row):
        return pltpu.make_async_copy(strip_of(prev, row, size), total.at[row], sem_prev.at[row])

    def start_prev(row, carry):
        @pl.when(open_row[row] > 0)
        def _():
            prev_copy(row).start()

        return carry

    lax.fori_loop(0, RB, start_prev, 0)
    whole = start_left(shifted, parts, left, flags[0] > 0, sem_left)
    low = ALWAYS
    sources = [(piece, begin, begin, low - shift), (back, low, low, low + lent)]
    low = low + lent
    for blocks in over:
        high = low + blocks.shape[0]
        sources.append((blocks, low, low, high))
        low = high
    clear(right, lambda j: touched[j] > 0)
    start_right(sources, count, target, right, sem_right)

    def out_copy(row):
        return pltpu.make_async_copy(short.at[row], strip_of(out, row, size), sem_out.at[row])

    whole.wait()
    finish_right(piece.at[0], right, sem_right, count - begin)

    def one_row(row, carry):
        @pl.when(open_row[row] > 0)
        def _():
            prev_copy(row).wait()
            add_products(row, order, first, left, right, touched, total)
            short[row] = total[row].astype(short.dtype)
            out_copy(row).start()

        return carry

    def close_row(row, carry):
        @pl.when(open_row[row] > 0)
        def _():
            out_copy(row).wait()

        return carry

    lax.fori_loop(0, RB, one_row, 0)
    lax.fori_loop(0, RB, close_row, 0)


def step_call(kernel, scalars, operands, specs, out_shape, out_specs, scratch, slots, size):
    return pl.pallas_call(
        kernel,
        out_shape=out_shape,
        grid_spec=pltpu.PrefetchScalarGridSpec(
            num_scalar_prefetch=len(scalars),
            grid=(RB // GROUP,),
            in_specs=specs,
            out_specs=out_specs,
            scratch_shapes=[
                pltpu.VMEM((slots, size, size), jnp.bfloat16),
                pltpu.VMEM((KB, size, NJ * size), jnp.bfloat16),
                *scratch,
                pltpu.SemaphoreType.DMA,
                pltpu.SemaphoreType.DMA,
            ],
        ),
        compiler_params=pltpu.CompilerParams(
            dimension_semantics=("arbitrary",), vmem_limit_bytes=LIMIT
        ),
        cost_estimate=pl.CostEstimate(
            flops=2 * 24 * NJ * size * size * size,
            bytes_accessed=16 * 1024 * 1024,
            transcendentals=0,
        ),
    )(*scalars, *operands)


def first_news_kernel(where_ref, cols_ref, send, out, where, cols, blocks, tile, sems):
    copies = [
        pltpu.make_async_copy(where_ref, where, sems.at[0]),
        pltpu.make_async_copy(cols_ref, cols, sems.at[1]),
    ]
    devices, count = where.shape[-1], blocks.shape[0]
    shares = devices // count
    step = blocks.shape[1] // shares
    for row in range(count):
        copies.append(
            pltpu.make_async_copy(send.at[1, 0, row * shares], blocks.at[row], sems.at[2 + row])
        )
    for copy in copies:
        copy.start()
    rcap, across = cols.shape
    tile[...] = jnp.zeros(tile.shape, tile.dtype)
    for copy in copies:
        copy.wait()
    for slot in range(rcap):
        tile[pl.ds(0, 1), pl.ds(slot * across, across)] = cols[pl.ds(slot, 1), :]
    for half in range(2):
        row, lane = divmod(half * devices, 128)
        tile[pl.ds(1 + row, 1), pl.ds(lane, devices)] = where[half]
    table = tile[...].astype(jnp.float32).astype(out.dtype)

    def fill(device, carry):
        share = pl.multiple_of(device % shares * step, step)
        out[device, pl.ds(0, step), :] = blocks[device // shares, pl.ds(share, step), :]
        out[device, pl.ds(step, 16), :] = table
        return carry

    lax.fori_loop(0, devices, fill, 0)


def first_news(where, cols, send, rows_count):
    devices = where.shape[-1]
    size = send.shape[-1]
    step = size * rows_count // devices
    return pl.pallas_call(
        first_news_kernel,
        out_shape=jax.ShapeDtypeStruct((devices, step + 16, size), send.dtype),
        in_specs=[ANYWHERE] * 3,
        scratch_shapes=[
            pltpu.VMEM(where.shape, jnp.int32),
            pltpu.VMEM(cols.shape, jnp.int32),
            pltpu.VMEM((rows_count, size, size), send.dtype),
            pltpu.VMEM((16, size), jnp.int32),
            pltpu.SemaphoreType.DMA((2 + rows_count,)),
        ],
        compiler_params=pltpu.CompilerParams(vmem_limit_bytes=LIMIT),
    )(in_hbm(where), in_hbm(cols), in_hbm(send))


def needed(where_all, cols_all, rows_count, cols_count):
    grid = where_all.reshape(-1, 2, rows_count, cols_count)
    after = jnp.concatenate([grid[:, 0, :, 1:], grid[:, 1, :, :1]], axis=-1)
    columns = jnp.arange(KB, dtype=jnp.int32)
    hit = (after[..., None] >= 0) & (after[..., None] % KB == columns)
    wanted = jnp.any(hit, axis=0).astype(jnp.int32)
    counts = jnp.sum((cols_all >= 0).astype(jnp.int32), axis=1)
    counts = jnp.roll(counts.reshape(rows_count, cols_count, KB), -1, axis=0)
    return jnp.sum(wanted * counts, axis=-1)


def swapped(value):
    return lax.ppermute(value, "col", [(i, i ^ 1) for i in range(lax.axis_size("col"))])


def local(a_send, a_where, b_strips, b_cols):
    size = a_send.shape[-1]
    rows_count = lax.axis_size("row")
    cols_count = lax.axis_size("col")
    devices = rows_count * cols_count
    both = ("row", "col")
    row_index = lax.axis_index("row")
    col_index = lax.axis_index("col")
    rcap = b_strips.shape[3]
    last = cols_count - 1

    by_slot = jnp.swapaxes(b_cols, 2, 3).reshape(rcap, KB)
    news = lax.all_to_all(
        first_news(a_where, by_slot, a_send, rows_count),
        both, split_axis=0, concat_axis=0, tiled=True,
    )
    step = size // cols_count
    part = news[:, :step]
    tables = news[:, step : step + 1 + -(-2 * devices // 128)].astype(jnp.int32)
    after_col = (col_index + 1) % cols_count
    after_half = (col_index + 1) // cols_count
    row_before = (row_index + rows_count - 1) % rows_count
    row_after = (row_index + 1) % rows_count
    needs = needed(
        tables[:, 1:].reshape(devices, -1)[:, : 2 * devices],
        tables[:, 0].reshape(devices, rcap, KB), rows_count, cols_count,
    )
    room = ALWAYS - jnp.flip(needs.reshape(rows_count, -1, 2), -1).reshape(needs.shape)
    lent = jnp.maximum(jnp.minimum(jnp.minimum(needs - ALWAYS, room), LENT), 0)
    most = jnp.max(needs - lent)

    def lent_to(row, col):
        return lax.dynamic_slice(lent, (row, col), (1, 1))[0, 0]

    spot = jnp.stack([
        after_half,
        row_index * cols_count + col_index,
        row_index * cols_count + after_col,
        row_before * cols_count + after_col,
        row_after * cols_count + col_index,
        lent_to(row_before, col_index ^ 1),
        lent_to(row_before, col_index),
    ]).astype(jnp.int32)

    received = lax.all_to_all(a_send[0, 0], both, split_axis=0, concat_axis=0, tiled=True)

    def to_row_before(blocks):
        return lax.ppermute(
            blocks, "row", [(i, (i - 1) % rows_count) for i in range(rows_count)]
        )

    strips = b_strips.reshape(KB * rcap, size, size)
    guests, *over = pack(pack_spare, (LENT, *PARTS[2:]), spot, tables, strips)
    begin, extra = ALWAYS, []
    for blocks in over:
        extra.append(lax.cond(most > begin, to_row_before, lambda same: same, blocks))
        begin += blocks.shape[0]
    early, late = pack(
        pack_main, PARTS[:2], spot, tables, strips, swapped(guests),
        *(blocks[0, :16] for blocks in extra),
    )
    early, late = map(to_row_before, after(received, [early, late]))

    shifted = lax.ppermute(received, "col", [(i + 1, i) for i in range(last)])
    (part,) = after(guests, [part])
    parts = [lax.ppermute(part, "col", [(i, last)]) for i in range(last)] + [part]

    wide = NJ * size
    strip = pl.BlockSpec((GROUP * size, wide), lambda i, *_: (i, 0))
    begun, order, first, target = step_call(
        functools.partial(first_kernel, rcap),
        (spot,), (tables, received, in_hbm(strips)), [ANYWHERE, ANYWHERE, ANYWHERE],
        [
            pltpu.HBM((RB * size, wide), jnp.float32),
            jax.ShapeDtypeStruct((devices,), jnp.int32),
            jax.ShapeDtypeStruct((RB + 3,), jnp.int32),
            jax.ShapeDtypeStruct((KB * rcap,), jnp.int32),
        ],
        [strip, IN_SMEM, IN_SMEM, IN_SMEM],
        [
            pltpu.SMEM(tables.shape, jnp.int32),
            pltpu.SemaphoreType.DMA,
            pltpu.SMEM((devices,), jnp.int32),
            pltpu.SMEM((RB + 2,), jnp.int32),
            pltpu.SMEM((KB,), jnp.int32),
            pltpu.SMEM((KB,), jnp.int32),
        ],
        devices, size,
    )

    on_last = (col_index == last).astype(jnp.int32)
    lent_here = [lent_to(row_index, col_index ^ 1), lent_to(row_index, col_index)]
    scalars = (order, first, target, jnp.stack([on_last, *lent_here]))
    lefts = (shifted, *parts)

    def finish_call(kernel, scalars, operands, out_shape, out_specs, scratch, marks, aliases):
        return pl.pallas_call(
            kernel,
            out_shape=out_shape,
            grid_spec=pltpu.PrefetchScalarGridSpec(
                num_scalar_prefetch=len(scalars),
                grid=(1,),
                in_specs=[ANYWHERE] * len(operands),
                out_specs=out_specs,
                scratch_shapes=[
                    *scratch,
                    pltpu.VMEM((devices, size, size), jnp.bfloat16),
                    pltpu.VMEM((KB, size, wide), jnp.bfloat16),
                    pltpu.VMEM((RB, size, wide), jnp.float32),
                    pltpu.VMEM((RB, size, wide), jnp.bfloat16),
                    *marks,
                    pltpu.SemaphoreType.DMA,
                    pltpu.SemaphoreType.DMA,
                    pltpu.SemaphoreType.DMA((RB,)),
                    pltpu.SemaphoreType.DMA((RB,)),
                ],
            ),
            input_output_aliases=aliases,
            compiler_params=pltpu.CompilerParams(vmem_limit_bytes=LIMIT),
            cost_estimate=pl.CostEstimate(
                flops=2 * 16 * NJ * size * size * size,
                bytes_accessed=12 * 1024 * 1024,
                transcendentals=0,
            ),
        )(*scalars, *operands)

    begun, rounded, guests, later, open_row = finish_call(
        functools.partial(middle_kernel, len(parts)), scalars,
        (*lefts, early, in_hbm(begun)),
        [
            pltpu.HBM((RB * size, wide), jnp.float32),
            pltpu.HBM((RB * size, wide), jnp.bfloat16),
            pltpu.HBM((LENT, size, size), jnp.bfloat16),
            jax.ShapeDtypeStruct((KB,), jnp.int32),
            jax.ShapeDtypeStruct((RB,), jnp.int32),
        ],
        [ANYWHERE, ANYWHERE, ANYWHERE, IN_SMEM, IN_SMEM],
        [
            pltpu.VMEM((LENT, size, size), jnp.bfloat16),
            pltpu.SemaphoreType.DMA,
            pltpu.SemaphoreType.DMA,
        ],
        [pltpu.SMEM((KB,), jnp.int32)], {},
    )
    back = swapped(guests)

    operands = (*lefts, late, back, *extra, in_hbm(begun), rounded)
    scalars = (*scalars, later, open_row)
    return finish_call(
        functools.partial(last_kernel, len(parts)), scalars, operands,
        jax.ShapeDtypeStruct((RB * size, wide), jnp.bfloat16),
        ANYWHERE, [], [], {len(scalars) + len(operands) - 1: 0},
    )


def solution(mesh):
    placed = (
        P(None, ("row", "col"), None, None, None),
        P(None, ("row", "col"), None),
        P("row", "col", None, None, None, None),
        P("row", "col", None, None),
    )
    return jax.shard_map(
        local, mesh=mesh, in_specs=placed, out_specs=P("row", "col"), check_vma=False
    )
```

```python
import functools

import jax
import jax.numpy as jnp
from jax import lax
from jax.experimental import pallas as pl
from jax.experimental.pallas import tpu as pltpu
from jax.sharding import PartitionSpec as P

RB = 16
KB = 16
NJ = 8
PARTS = (64, 24, 8, 8, 24)
ALWAYS = PARTS[0] + PARTS[1]
LENT = 16
GROUP = 4
IN_SMEM = pl.BlockSpec(memory_space=pltpu.SMEM)
ANYWHERE = pl.BlockSpec(memory_space=pl.ANY)
LIMIT = 24 * 1024 * 1024


def in_hbm(value):
    return pltpu.with_memory_space_constraint(value, pltpu.HBM)


def places_in(table, half, owner):
    at = half * table.shape[0] + owner
    return lambda source: table[source, 1 + at // 128, at % 128]


def columns_in(table, rcap, device):
    return lambda slot: table[device, 0, slot % rcap * KB + slot // rcap]


def mark_rows(place, slots, named):
    def reset(j, carry):
        named[j] = 0
        return carry

    def mark(s, carry):
        here = place(s)

        @pl.when(here >= 0)
        def _():
            named[here % KB] = named[here % KB] + 1

        return carry

    lax.fori_loop(0, KB, reset, 0)
    lax.fori_loop(0, slots, mark, 0)


def for_wanted(column, named, rcap, action):
    def visit(slot, number):
        wanted = column(slot) >= 0

        @pl.when(wanted)
        def _():
            action(slot, number)

        return number + wanted.astype(jnp.int32)

    def visit_row(j, match, number):
        return lax.fori_loop(j * rcap, jnp.where(match, (j + 1) * rcap, j * rcap), visit, number)

    count = lax.fori_loop(0, KB, lambda j, n: visit_row(j, named[j] > 1, n), jnp.int32(0))
    return lax.fori_loop(0, KB, lambda j, n: visit_row(j, named[j] == 1, n), count)


def pack_main(spot, tables, strips, guests, *refs):
    early, late, stage, table, sem_table, named, sem, sem_out = refs[-8:]
    shift = spot[5]
    stop = stage.shape[0] - shift

    def greet(number, carry):
        pltpu.make_async_copy(guests.at[number], stage.at[number], sem).start()
        return carry

    lax.fori_loop(0, shift, greet, 0)

    def fetch(slot, number):
        @pl.when(number < stop)
        def _():
            pltpu.make_async_copy(strips.at[slot], stage.at[number + shift], sem).start()

    count = find_wanted(spot, tables, strips, table, sem_table, named, fetch)
    finish_blocks(strips, stage, sem, jnp.minimum(count, stop) + shift)
    hand_over(stage, [early, late], sem_out)


def pack_spare(spot, tables, strips, guests, *refs):
    *over, stage, table, sem_table, named, sem, sem_out = refs
    lent = spot[6]

    def fetch(slot, number):
        beyond = number - ALWAYS

        @pl.when((beyond >= 0) & (beyond < LENT))
        def _():
            pltpu.make_async_copy(strips.at[slot], stage.at[beyond], sem).start()

        @pl.when(beyond >= lent)
        def _():
            at = LENT + beyond - lent
            pltpu.make_async_copy(strips.at[slot], stage.at[at], sem).start()

    count = find_wanted(spot, tables, strips, table, sem_table, named, fetch)
    beyond = jnp.maximum(count - ALWAYS, 0)
    copied = jnp.minimum(beyond, LENT) + jnp.maximum(beyond - lent, 0)
    finish_blocks(strips, stage, sem, copied)
    hand_over(stage, [guests, *over], sem_out)


def find_wanted(spot, tables, strips, table, sem_table, named, action):
    rcap = strips.shape[0] // KB
    table_copy = pltpu.make_async_copy(tables, table, sem_table)
    table_copy.start()
    table_copy.wait()
    mark_rows(places_in(table, spot[0], spot[3]), table.shape[0], named)
    return for_wanted(columns_in(table, rcap, spot[1]), named, rcap, action)


def finish_blocks(source, target, sem, count):
    def finish(number, carry):
        pltpu.make_async_copy(source.at[0], target.at[0], sem).wait()
        return carry

    lax.fori_loop(0, count, finish, 0)


def hand_over(stage, outs, sem_out):
    copies, low = [], 0
    for i, out in enumerate(outs):
        here = stage.at[pl.ds(low, out.shape[0])]
        copies.append(pltpu.make_async_copy(here, out, sem_out.at[i]))
        copies[-1].start()
        low += out.shape[0]
    for copy in copies:
        copy.wait()


def pack(kernel, counts, spot, tables, strips, *more):
    size = strips.shape[-1]
    return pl.pallas_call(
        kernel,
        out_shape=[pltpu.HBM((n, size, size), strips.dtype) for n in counts],
        grid_spec=pltpu.PrefetchScalarGridSpec(
            num_scalar_prefetch=1,
            grid=(1,),
            in_specs=[ANYWHERE] * (2 + len(more)),
            out_specs=[ANYWHERE] * len(counts),
            scratch_shapes=[
                pltpu.VMEM((sum(counts), size, size), strips.dtype),
                pltpu.SMEM(tables.shape, jnp.int32),
                pltpu.SemaphoreType.DMA,
                pltpu.SMEM((KB,), jnp.int32),
                pltpu.SemaphoreType.DMA,
                pltpu.SemaphoreType.DMA((len(counts),)),
            ],
        ),
        compiler_params=pltpu.CompilerParams(vmem_limit_bytes=LIMIT),
        cost_estimate=pl.CostEstimate(
            flops=0, bytes_accessed=4 * sum(counts) * size * size, transcendentals=0
        ),
    )(spot, tables, in_hbm(strips), *more)


def after(value, blocks):
    count = len(blocks)
    return pl.pallas_call(
        lambda *refs: None,
        out_shape=[pltpu.HBM(each.shape, each.dtype) for each in blocks],
        in_specs=[ANYWHERE] * (count + 1),
        out_specs=[ANYWHERE] * count,
        input_output_aliases={i: i for i in range(count)},
    )(*blocks, value)


def by_block_row(place, slots, order, first):
    def reset(i, carry):
        first[i] = 0
        return carry

    def count(s, carry):
        here = place(s)

        @pl.when(here >= 0)
        def _():
            i = here // KB + 2
            first[i] = first[i] + 1

        return carry

    def scan(i, carry):
        first[i] = first[i] + first[i - 1]
        return carry

    def sort(s, carry):
        here = place(s)

        @pl.when(here >= 0)
        def _():
            i = here // KB + 1
            order[first[i]] = s * KB + here % KB
            first[i] = first[i] + 1

        return carry

    lax.fori_loop(0, RB + 2, reset, 0)
    lax.fori_loop(0, slots, count, 0)
    lax.fori_loop(1, RB + 2, scan, 0)
    lax.fori_loop(0, slots, sort, 0)


def clear(right, wanted):
    def one(j, carry):
        @pl.when(wanted(j))
        def _():
            right[j] = jnp.zeros(right.shape[1:], right.dtype)

        return carry

    lax.fori_loop(0, KB, one, 0)


def add_rows(left, right, total, order, first):
    size = left.shape[1]

    def one_row(i, carry):
        row = pl.program_id(0) * GROUP + i
        here = pl.ds(pl.multiple_of(i * size, size), size)

        def add(entry, carry):
            total[here, :] += jnp.dot(
                left[order[entry] // KB], right[order[entry] % KB],
                preferred_element_type=jnp.float32,
            )
            return carry

        return lax.fori_loop(first[row], first[row + 1], add, carry)

    lax.fori_loop(0, GROUP, one_row, 0)


def place_at(right, where):
    size = right.shape[1]
    start = pl.multiple_of((where % NJ) * size, size)
    return right.at[where // NJ, :, pl.ds(start, size)]


def finish_right(source, right, sem, count):
    def finish(number, carry):
        pltpu.make_async_copy(source, place_at(right, 0), sem).wait()
        return carry

    lax.fori_loop(0, count, finish, 0)


def first_kernel(
    rcap, spot, tables, received, strips,
    out, next_order, next_first, next_target,
    left, right, table, sem_table, order, first, named, other, sem_left, sem_right,
):
    slots, size, _ = left.shape

    @pl.when(pl.program_id(0) == 0)
    def _():
        left_copy = pltpu.make_async_copy(received.at[:, pl.ds(0, size)], left, sem_left)
        left_copy.start()
        table_copy = pltpu.make_async_copy(tables, table, sem_table)
        table_copy.start()
        table_copy.wait()
        place = places_in(table, 0, spot[1])
        column = columns_in(table, rcap, spot[1])
        mark_rows(place, slots, named)
        clear(right, lambda j: named[j] > 0)

        def fetch(slot, number):
            target = place_at(right, slot // rcap * NJ + column(slot))
            pltpu.make_async_copy(strips.at[slot], target, sem_right).start()

        count = for_wanted(column, named, rcap, fetch)
        by_block_row(place, slots, order, first)

        next_place = places_in(table, spot[0], spot[2])
        next_column = columns_in(table, rcap, spot[4])
        by_block_row(next_place, slots, next_order, next_first)
        mark_rows(next_place, slots, other)

        def note(slot, number):
            next_target[number] = slot // rcap * NJ + next_column(slot)

        next_first[RB + 2] = for_wanted(next_column, other, rcap, note)
        left_copy.wait()
        finish_right(strips.at[0], right, sem_right, count)

    out[...] = jnp.zeros(out.shape, out.dtype)
    add_rows(left, right, out, order, first)


def start_left(shifted, parts, left, on_last, sem):
    size = left.shape[1]
    step = shifted.shape[1] - size
    whole = pltpu.make_async_copy(shifted.at[:, pl.ds(0, size)], left, sem)

    @pl.when(on_last)
    def _():
        for q, part in enumerate([shifted.at[:, pl.ds(size, step)], *parts]):
            pltpu.make_async_copy(part, left.at[:, pl.ds(q * step, step)], sem).start()

    @pl.when(jnp.logical_not(on_last))
    def _():
        whole.start()

    return whole


def start_right(sources, count, target, right, sem):
    for blocks, low, start, stop in sources:

        def fetch(number, carry):
            pltpu.make_async_copy(
                blocks.at[number - low], place_at(right, target[number]), sem
            ).start()
            return carry

        lax.fori_loop(start, jnp.minimum(count, stop), fetch, 0)


def add_products(row, order, first, left, right, touched, total):
    def add(entry, carry):
        @pl.when(touched[order[entry] % KB] > 0)
        def _():
            total[row] += jnp.dot(
                left[order[entry] // KB], right[order[entry] % KB],
                preferred_element_type=jnp.float32,
            )

        return carry

    lax.fori_loop(first[row], first[row + 1], add, 0)


def mark_targets(target, begin, end, marks):
    def reset(j, carry):
        marks[j] = 0
        return carry

    def mark(number, carry):
        marks[target[number] // NJ] = 1
        return carry

    lax.fori_loop(0, KB, reset, 0)
    lax.fori_loop(begin, end, mark, 0)


def mark_open(order, first, touched, open_row):
    def one(row, carry):
        def look(entry, found):
            return jnp.maximum(found, touched[order[entry] % KB])

        open_row[row] = lax.fori_loop(first[row], first[row + 1], look, jnp.int32(0))
        return carry

    lax.fori_loop(0, RB, one, 0)


def strip_of(ref, row, size):
    return ref.at[pl.ds(pl.multiple_of(row * size, size), size)]


def middle_kernel(parts_count, order, first, target, flags, *refs):
    shifted, *parts = refs[: 1 + parts_count]
    (
        piece, prev, out, rounded, guests, later, open_row,
        hall, sem_in, sem_home,
        left, right, total, short, touched,
        sem_left, sem_right, sem_prev, sem_out,
    ) = refs[1 + parts_count :]
    arrive = pltpu.make_async_copy(piece.at[pl.ds(0, LENT)], hall, sem_in)
    leave = pltpu.make_async_copy(hall, guests, sem_home)
    arrive.start()
    size = left.shape[1]
    count = first[RB + 2]
    shift = flags[1]
    end = piece.shape[0] - shift

    def prev_copy(row):
        return pltpu.make_async_copy(strip_of(prev, row, size), total.at[row], sem_prev.at[row])

    def start_prev(row, carry):
        prev_copy(row).start()
        return carry

    lax.fori_loop(0, RB, start_prev, 0)
    whole = start_left(shifted, parts, left, flags[0] > 0, sem_left)
    fetched = jnp.minimum(count, end)
    mark_targets(target, 0, fetched, touched)
    clear(right, lambda j: touched[j] > 0)
    start_right([(piece, -shift, 0, end)], fetched, target, right, sem_right)
    arrive.wait()
    leave.start()
    mark_targets(target, end, count, later)
    mark_open(order, first, later, open_row)
    whole.wait()
    finish_right(piece.at[0], right, sem_right, fetched)

    def out_copies(row):
        return (
            pltpu.make_async_copy(total.at[row], strip_of(out, row, size), sem_out.at[row]),
            pltpu.make_async_copy(short.at[row], strip_of(rounded, row, size), sem_out.at[row]),
        )

    def one_row(row, carry):
        open_copy, closed_copy = out_copies(row)
        prev_copy(row).wait()
        add_products(row, order, first, left, right, touched, total)

        @pl.when(open_row[row] > 0)
        def _():
            open_copy.start()

        @pl.when(open_row[row] == 0)
        def _():
            short[row] = total[row].astype(short.dtype)
            closed_copy.start()

        return carry

    def close_row(row, carry):
        open_copy, closed_copy = out_copies(row)

        @pl.when(open_row[row] > 0)
        def _():
            open_copy.wait()

        @pl.when(open_row[row] == 0)
        def _():
            closed_copy.wait()

        return carry

    lax.fori_loop(0, RB, one_row, 0)
    lax.fori_loop(0, RB, close_row, 0)
    leave.wait()


def last_kernel(parts_count, order, first, target, flags, touched, open_row, *refs):
    shifted, *parts = refs[: 1 + parts_count]
    (
        piece, back, *over, prev, _, out,
        left, right, total, short,
        sem_left, sem_right, sem_prev, sem_out,
    ) = refs[1 + parts_count :]
    size = left.shape[1]
    count = first[RB + 2]
    shift, lent = flags[1], flags[2]
    begin = PARTS[0] - shift

    def prev_copy(row):
        return pltpu.make_async_copy(strip_of(prev, row, size), total.at[row], sem_prev.at[row])

    def start_prev(row, carry):
        @pl.when(open_row[row] > 0)
        def _():
            prev_copy(row).start()

        return carry

    lax.fori_loop(0, RB, start_prev, 0)
    whole = start_left(shifted, parts, left, flags[0] > 0, sem_left)
    low = ALWAYS
    sources = [(piece, begin, begin, low - shift), (back, low, low, low + lent)]
    low = low + lent
    for blocks in over:
        high = low + blocks.shape[0]
        sources.append((blocks, low, low, high))
        low = high
    clear(right, lambda j: touched[j] > 0)
    start_right(sources, count, target, right, sem_right)

    def out_copy(row):
        return pltpu.make_async_copy(short.at[row], strip_of(out, row, size), sem_out.at[row])

    whole.wait()
    finish_right(piece.at[0], right, sem_right, count - begin)

    def one_row(row, carry):
        @pl.when(open_row[row] > 0)
        def _():
            prev_copy(row).wait()
            add_products(row, order, first, left, right, touched, total)
            short[row] = total[row].astype(short.dtype)
            out_copy(row).start()

        return carry

    def close_row(row, carry):
        @pl.when(open_row[row] > 0)
        def _():
            out_copy(row).wait()

        return carry

    lax.fori_loop(0, RB, one_row, 0)
    lax.fori_loop(0, RB, close_row, 0)


def step_call(kernel, scalars, operands, specs, out_shape, out_specs, scratch, slots, size):
    return pl.pallas_call(
        kernel,
        out_shape=out_shape,
        grid_spec=pltpu.PrefetchScalarGridSpec(
            num_scalar_prefetch=len(scalars),
            grid=(RB // GROUP,),
            in_specs=specs,
            out_specs=out_specs,
            scratch_shapes=[
                pltpu.VMEM((slots, size, size), jnp.bfloat16),
                pltpu.VMEM((KB, size, NJ * size), jnp.bfloat16),
                *scratch,
                pltpu.SemaphoreType.DMA,
                pltpu.SemaphoreType.DMA,
            ],
        ),
        compiler_params=pltpu.CompilerParams(
            dimension_semantics=("arbitrary",), vmem_limit_bytes=LIMIT
        ),
        cost_estimate=pl.CostEstimate(
            flops=2 * 24 * NJ * size * size * size,
            bytes_accessed=16 * 1024 * 1024,
            transcendentals=0,
        ),
    )(*scalars, *operands)


def table_kernel(where_ref, cols_ref, out, where, cols, tile, sems):
    copies = [
        pltpu.make_async_copy(where_ref, where, sems.at[0]),
        pltpu.make_async_copy(cols_ref, cols, sems.at[1]),
    ]
    for copy in copies:
        copy.start()
    rcap, across = cols.shape
    devices = where.shape[-1]
    tile[...] = jnp.zeros(tile.shape, tile.dtype)
    for copy in copies:
        copy.wait()
    for slot in range(rcap):
        tile[pl.ds(0, 1), pl.ds(slot * across, across)] = cols[pl.ds(slot, 1), :]
    for half in range(2):
        row, lane = divmod(half * devices, 128)
        tile[pl.ds(1 + row, 1), pl.ds(lane, devices)] = where[half]

    def fill(device, carry):
        out[device] = tile[...]
        return carry

    lax.fori_loop(0, out.shape[0], fill, 0)


def table_for_all(where, cols):
    devices = where.shape[-1]
    shape = (1 + -(-2 * devices // 128), 128)
    return pl.pallas_call(
        table_kernel,
        out_shape=jax.ShapeDtypeStruct((devices, *shape), jnp.int32),
        in_specs=[ANYWHERE, ANYWHERE],
        scratch_shapes=[
            pltpu.VMEM(where.shape, jnp.int32),
            pltpu.VMEM(cols.shape, jnp.int32),
            pltpu.VMEM(shape, jnp.int32),
            pltpu.SemaphoreType.DMA((2,)),
        ],
        compiler_params=pltpu.CompilerParams(vmem_limit_bytes=LIMIT),
    )(in_hbm(where), in_hbm(cols))


def needed(where_all, cols_all, rows_count, cols_count):
    grid = where_all.reshape(-1, 2, rows_count, cols_count)
    after = jnp.concatenate([grid[:, 0, :, 1:], grid[:, 1, :, :1]], axis=-1)
    columns = jnp.arange(KB, dtype=jnp.int32)
    hit = (after[..., None] >= 0) & (after[..., None] % KB == columns)
    wanted = jnp.any(hit, axis=0).astype(jnp.int32)
    counts = jnp.sum((cols_all >= 0).astype(jnp.int32), axis=1)
    counts = jnp.roll(counts.reshape(rows_count, cols_count, KB), -1, axis=0)
    return jnp.sum(wanted * counts, axis=-1)


def swapped(value):
    return lax.ppermute(value, "col", [(i, i ^ 1) for i in range(lax.axis_size("col"))])


def local(a_send, a_where, b_strips, b_cols):
    size = a_send.shape[-1]
    rows_count = lax.axis_size("row")
    cols_count = lax.axis_size("col")
    devices = rows_count * cols_count
    both = ("row", "col")
    row_index = lax.axis_index("row")
    col_index = lax.axis_index("col")
    rcap = b_strips.shape[3]
    last = cols_count - 1

    by_slot = jnp.swapaxes(b_cols, 2, 3).reshape(rcap, KB)
    tables = lax.all_to_all(
        table_for_all(a_where, by_slot), both, split_axis=0, concat_axis=0, tiled=True
    )
    after_col = (col_index + 1) % cols_count
    after_half = (col_index + 1) // cols_count
    row_before = (row_index + rows_count - 1) % rows_count
    row_after = (row_index + 1) % rows_count
    needs = needed(
        tables[:, 1:].reshape(devices, -1)[:, : 2 * devices],
        tables[:, 0].reshape(devices, rcap, KB), rows_count, cols_count,
    )
    room = ALWAYS - jnp.flip(needs.reshape(rows_count, -1, 2), -1).reshape(needs.shape)
    lent = jnp.maximum(jnp.minimum(jnp.minimum(needs - ALWAYS, room), LENT), 0)
    most = jnp.max(needs - lent)

    def lent_to(row, col):
        return lax.dynamic_slice(lent, (row, col), (1, 1))[0, 0]

    spot = jnp.stack([
        after_half,
        row_index * cols_count + col_index,
        row_index * cols_count + after_col,
        row_before * cols_count + after_col,
        row_after * cols_count + col_index,
        lent_to(row_before, col_index ^ 1),
        lent_to(row_before, col_index),
    ]).astype(jnp.int32)

    wrapped = a_send[1, 0].reshape(rows_count, cols_count, size, size)[:, 0]
    wrapped = wrapped.reshape(devices, size // cols_count, size)
    received = lax.all_to_all(
        jnp.concatenate([a_send[0, 0], wrapped], axis=1),
        both, split_axis=0, concat_axis=0, tiled=True,
    )

    def to_row_before(blocks):
        return lax.ppermute(
            blocks, "row", [(i, (i - 1) % rows_count) for i in range(rows_count)]
        )

    strips = b_strips.reshape(KB * rcap, size, size)
    guests, *over = pack(pack_spare, (LENT, *PARTS[2:]), spot, tables, strips)
    begin, extra = ALWAYS, []
    for blocks in over:
        extra.append(lax.cond(most > begin, to_row_before, lambda same: same, blocks))
        begin += blocks.shape[0]
    early, late = pack(
        pack_main, PARTS[:2], spot, tables, strips, swapped(guests),
        *(blocks[0, :16] for blocks in extra),
    )
    early, late = map(to_row_before, after(received[0, :16], [early, late]))

    shifted = lax.ppermute(
        received, "col", [(i, (i - 1) % cols_count) for i in range(cols_count)]
    )
    part = received[:, size:]
    parts = [lax.ppermute(part, "col", [(i, last)]) for i in range(1, last)] + [part]

    wide = NJ * size
    strip = pl.BlockSpec((GROUP * size, wide), lambda i, *_: (i, 0))
    begun, order, first, target = step_call(
        functools.partial(first_kernel, rcap),
        (spot,), (tables, received, in_hbm(strips)), [ANYWHERE, ANYWHERE, ANYWHERE],
        [
            pltpu.HBM((RB * size, wide), jnp.float32),
            jax.ShapeDtypeStruct((devices,), jnp.int32),
            jax.ShapeDtypeStruct((RB + 3,), jnp.int32),
            jax.ShapeDtypeStruct((KB * rcap,), jnp.int32),
        ],
        [strip, IN_SMEM, IN_SMEM, IN_SMEM],
        [
            pltpu.SMEM(tables.shape, jnp.int32),
            pltpu.SemaphoreType.DMA,
            pltpu.SMEM((devices,), jnp.int32),
            pltpu.SMEM((RB + 2,), jnp.int32),
            pltpu.SMEM((KB,), jnp.int32),
            pltpu.SMEM((KB,), jnp.int32),
        ],
        devices, size,
    )

    on_last = (col_index == last).astype(jnp.int32)
    lent_here = [lent_to(row_index, col_index ^ 1), lent_to(row_index, col_index)]
    scalars = (order, first, target, jnp.stack([on_last, *lent_here]))
    lefts = (shifted, *parts)

    def finish_call(kernel, scalars, operands, out_shape, out_specs, scratch, marks, aliases):
        return pl.pallas_call(
            kernel,
            out_shape=out_shape,
            grid_spec=pltpu.PrefetchScalarGridSpec(
                num_scalar_prefetch=len(scalars),
                grid=(1,),
                in_specs=[ANYWHERE] * len(operands),
                out_specs=out_specs,
                scratch_shapes=[
                    *scratch,
                    pltpu.VMEM((devices, size, size), jnp.bfloat16),
                    pltpu.VMEM((KB, size, wide), jnp.bfloat16),
                    pltpu.VMEM((RB, size, wide), jnp.float32),
                    pltpu.VMEM((RB, size, wide), jnp.bfloat16),
                    *marks,
                    pltpu.SemaphoreType.DMA,
                    pltpu.SemaphoreType.DMA,
                    pltpu.SemaphoreType.DMA((RB,)),
                    pltpu.SemaphoreType.DMA((RB,)),
                ],
            ),
            input_output_aliases=aliases,
            compiler_params=pltpu.CompilerParams(vmem_limit_bytes=LIMIT),
            cost_estimate=pl.CostEstimate(
                flops=2 * 16 * NJ * size * size * size,
                bytes_accessed=12 * 1024 * 1024,
                transcendentals=0,
            ),
        )(*scalars, *operands)

    begun, rounded, guests, later, open_row = finish_call(
        functools.partial(middle_kernel, len(parts)), scalars,
        (*lefts, early, in_hbm(begun)),
        [
            pltpu.HBM((RB * size, wide), jnp.float32),
            pltpu.HBM((RB * size, wide), jnp.bfloat16),
            pltpu.HBM((LENT, size, size), jnp.bfloat16),
            jax.ShapeDtypeStruct((KB,), jnp.int32),
            jax.ShapeDtypeStruct((RB,), jnp.int32),
        ],
        [ANYWHERE, ANYWHERE, ANYWHERE, IN_SMEM, IN_SMEM],
        [
            pltpu.VMEM((LENT, size, size), jnp.bfloat16),
            pltpu.SemaphoreType.DMA,
            pltpu.SemaphoreType.DMA,
        ],
        [pltpu.SMEM((KB,), jnp.int32)], {},
    )
    back = swapped(guests)

    operands = (*lefts, late, back, *extra, in_hbm(begun), rounded)
    scalars = (*scalars, later, open_row)
    return finish_call(
        functools.partial(last_kernel, len(parts)), scalars, operands,
        jax.ShapeDtypeStruct((RB * size, wide), jnp.bfloat16),
        ANYWHERE, [], [], {len(scalars) + len(operands) - 1: 0},
    )


def solution(mesh):
    placed = (
        P(None, ("row", "col"), None, None, None),
        P(None, ("row", "col"), None),
        P("row", "col", None, None, None, None),
        P("row", "col", None, None),
    )
    return jax.shard_map(
        local, mesh=mesh, in_specs=placed, out_specs=P("row", "col"), check_vma=False
    )
```

```python
import functools

import jax
import jax.numpy as jnp
from jax import lax
from jax.experimental import pallas as pl
from jax.experimental.pallas import tpu as pltpu
from jax.sharding import PartitionSpec as P

RB = 16
KB = 16
NJ = 8
PARTS = (66, 22, 8, 8, 24)
ALWAYS = PARTS[0] + PARTS[1]
LENT = 16
GROUP = 4
IN_SMEM = pl.BlockSpec(memory_space=pltpu.SMEM)
ANYWHERE = pl.BlockSpec(memory_space=pl.ANY)
LIMIT = 24 * 1024 * 1024


def in_hbm(value):
    return pltpu.with_memory_space_constraint(value, pltpu.HBM)


def places_in(table, half, owner):
    at = half * table.shape[0] + owner
    return lambda source: table[source, 1 + at // 128, at % 128]


def columns_in(table, rcap, device):
    return lambda slot: table[device, 0, slot % rcap * KB + slot // rcap]


def mark_rows(place, slots, named):
    def reset(j, carry):
        named[j] = 0
        return carry

    def mark(s, carry):
        here = place(s)

        @pl.when(here >= 0)
        def _():
            named[here % KB] = named[here % KB] + 1

        return carry

    lax.fori_loop(0, KB, reset, 0)
    lax.fori_loop(0, slots, mark, 0)


def for_wanted(column, named, rcap, action):
    def visit(slot, number):
        wanted = column(slot) >= 0

        @pl.when(wanted)
        def _():
            action(slot, number)

        return number + wanted.astype(jnp.int32)

    def visit_row(j, match, number):
        return lax.fori_loop(j * rcap, jnp.where(match, (j + 1) * rcap, j * rcap), visit, number)

    count = lax.fori_loop(0, KB, lambda j, n: visit_row(j, named[j] > 1, n), jnp.int32(0))
    return lax.fori_loop(0, KB, lambda j, n: visit_row(j, named[j] == 1, n), count)


def pack_main(spot, tables, strips, guests, *refs):
    early, late, stage, table, sem_table, named, sem, sem_out = refs[-8:]
    shift = spot[5]
    stop = stage.shape[0] - shift

    def greet(number, carry):
        pltpu.make_async_copy(guests.at[number], stage.at[number], sem).start()
        return carry

    lax.fori_loop(0, shift, greet, 0)

    def fetch(slot, number):
        @pl.when(number < stop)
        def _():
            pltpu.make_async_copy(strips.at[slot], stage.at[number + shift], sem).start()

    count = find_wanted(spot, tables, strips, table, sem_table, named, fetch)
    finish_blocks(strips, stage, sem, jnp.minimum(count, stop) + shift)
    hand_over(stage, [early, late], sem_out)


def pack_spare(spot, tables, strips, guests, *refs):
    *over, stage, table, sem_table, named, sem, sem_out = refs
    lent = spot[6]

    def fetch(slot, number):
        beyond = number - ALWAYS

        @pl.when((beyond >= 0) & (beyond < LENT))
        def _():
            pltpu.make_async_copy(strips.at[slot], stage.at[beyond], sem).start()

        @pl.when(beyond >= lent)
        def _():
            at = LENT + beyond - lent
            pltpu.make_async_copy(strips.at[slot], stage.at[at], sem).start()

    count = find_wanted(spot, tables, strips, table, sem_table, named, fetch)
    beyond = jnp.maximum(count - ALWAYS, 0)
    copied = jnp.minimum(beyond, LENT) + jnp.maximum(beyond - lent, 0)
    finish_blocks(strips, stage, sem, copied)
    hand_over(stage, [guests, *over], sem_out)


def find_wanted(spot, tables, strips, table, sem_table, named, action):
    rcap = strips.shape[0] // KB
    table_copy = pltpu.make_async_copy(tables, table, sem_table)
    table_copy.start()
    table_copy.wait()
    mark_rows(places_in(table, spot[0], spot[3]), table.shape[0], named)
    return for_wanted(columns_in(table, rcap, spot[1]), named, rcap, action)


def finish_blocks(source, target, sem, count):
    def finish(number, carry):
        pltpu.make_async_copy(source.at[0], target.at[0], sem).wait()
        return carry

    lax.fori_loop(0, count, finish, 0)


def hand_over(stage, outs, sem_out):
    copies, low = [], 0
    for i, out in enumerate(outs):
        here = stage.at[pl.ds(low, out.shape[0])]
        copies.append(pltpu.make_async_copy(here, out, sem_out.at[i]))
        copies[-1].start()
        low += out.shape[0]
    for copy in copies:
        copy.wait()


def pack(kernel, counts, spot, tables, strips, *more):
    size = strips.shape[-1]
    return pl.pallas_call(
        kernel,
        out_shape=[pltpu.HBM((n, size, size), strips.dtype) for n in counts],
        grid_spec=pltpu.PrefetchScalarGridSpec(
            num_scalar_prefetch=1,
            grid=(1,),
            in_specs=[ANYWHERE] * (2 + len(more)),
            out_specs=[ANYWHERE] * len(counts),
            scratch_shapes=[
                pltpu.VMEM((sum(counts), size, size), strips.dtype),
                pltpu.SMEM(tables.shape, jnp.int32),
                pltpu.SemaphoreType.DMA,
                pltpu.SMEM((KB,), jnp.int32),
                pltpu.SemaphoreType.DMA,
                pltpu.SemaphoreType.DMA((len(counts),)),
            ],
        ),
        compiler_params=pltpu.CompilerParams(vmem_limit_bytes=LIMIT),
        cost_estimate=pl.CostEstimate(
            flops=0, bytes_accessed=4 * sum(counts) * size * size, transcendentals=0
        ),
    )(spot, tables, in_hbm(strips), *more)


def after(value, blocks):
    count = len(blocks)
    return pl.pallas_call(
        lambda *refs: None,
        out_shape=[pltpu.HBM(each.shape, each.dtype) for each in blocks],
        in_specs=[ANYWHERE] * (count + 1),
        out_specs=[ANYWHERE] * count,
        input_output_aliases={i: i for i in range(count)},
    )(*blocks, value)


def by_block_row(place, slots, order, first):
    def reset(i, carry):
        first[i] = 0
        return carry

    def count(s, carry):
        here = place(s)

        @pl.when(here >= 0)
        def _():
            i = here // KB + 2
            first[i] = first[i] + 1

        return carry

    def scan(i, carry):
        first[i] = first[i] + first[i - 1]
        return carry

    def sort(s, carry):
        here = place(s)

        @pl.when(here >= 0)
        def _():
            i = here // KB + 1
            order[first[i]] = s * KB + here % KB
            first[i] = first[i] + 1

        return carry

    lax.fori_loop(0, RB + 2, reset, 0)
    lax.fori_loop(0, slots, count, 0)
    lax.fori_loop(1, RB + 2, scan, 0)
    lax.fori_loop(0, slots, sort, 0)


def clear(right, wanted):
    def one(j, carry):
        @pl.when(wanted(j))
        def _():
            right[j] = jnp.zeros(right.shape[1:], right.dtype)

        return carry

    lax.fori_loop(0, KB, one, 0)


def add_rows(left, right, total, order, first):
    size = left.shape[1]

    def one_row(i, carry):
        row = pl.program_id(0) * GROUP + i
        here = pl.ds(pl.multiple_of(i * size, size), size)

        def add(entry, carry):
            total[here, :] += jnp.dot(
                left[order[entry] // KB], right[order[entry] % KB],
                preferred_element_type=jnp.float32,
            )
            return carry

        return lax.fori_loop(first[row], first[row + 1], add, carry)

    lax.fori_loop(0, GROUP, one_row, 0)


def place_at(right, where):
    size = right.shape[1]
    start = pl.multiple_of((where % NJ) * size, size)
    return right.at[where // NJ, :, pl.ds(start, size)]


def finish_right(source, right, sem, count):
    def finish(number, carry):
        pltpu.make_async_copy(source, place_at(right, 0), sem).wait()
        return carry

    lax.fori_loop(0, count, finish, 0)


def first_kernel(
    rcap, spot, tables, received, strips,
    out, next_order, next_first, next_target,
    left, right, table, sem_table, order, first, named, other, sem_left, sem_right,
):
    slots, size, _ = left.shape

    @pl.when(pl.program_id(0) == 0)
    def _():
        left_copy = pltpu.make_async_copy(received.at[:, pl.ds(0, size)], left, sem_left)
        left_copy.start()
        table_copy = pltpu.make_async_copy(tables, table, sem_table)
        table_copy.start()
        table_copy.wait()
        place = places_in(table, 0, spot[1])
        column = columns_in(table, rcap, spot[1])
        mark_rows(place, slots, named)
        clear(right, lambda j: named[j] > 0)

        def fetch(slot, number):
            target = place_at(right, slot // rcap * NJ + column(slot))
            pltpu.make_async_copy(strips.at[slot], target, sem_right).start()

        count = for_wanted(column, named, rcap, fetch)
        by_block_row(place, slots, order, first)

        next_place = places_in(table, spot[0], spot[2])
        next_column = columns_in(table, rcap, spot[4])
        by_block_row(next_place, slots, next_order, next_first)
        mark_rows(next_place, slots, other)

        def note(slot, number):
            next_target[number] = slot // rcap * NJ + next_column(slot)

        next_first[RB + 2] = for_wanted(next_column, other, rcap, note)
        left_copy.wait()
        finish_right(strips.at[0], right, sem_right, count)

    out[...] = jnp.zeros(out.shape, out.dtype)
    add_rows(left, right, out, order, first)


def start_left(shifted, parts, left, on_last, sem):
    size = left.shape[1]
    step = shifted.shape[1] - size
    whole = pltpu.make_async_copy(shifted.at[:, pl.ds(0, size)], left, sem)

    @pl.when(on_last)
    def _():
        for q, part in enumerate([shifted.at[:, pl.ds(size, step)], *parts]):
            pltpu.make_async_copy(part, left.at[:, pl.ds(q * step, step)], sem).start()

    @pl.when(jnp.logical_not(on_last))
    def _():
        whole.start()

    return whole


def start_right(sources, count, target, right, sem):
    for blocks, low, start, stop in sources:

        def fetch(number, carry):
            pltpu.make_async_copy(
                blocks.at[number - low], place_at(right, target[number]), sem
            ).start()
            return carry

        lax.fori_loop(start, jnp.minimum(count, stop), fetch, 0)


def add_products(row, order, first, left, right, touched, total):
    def add(entry, carry):
        @pl.when(touched[order[entry] % KB] > 0)
        def _():
            total[row] += jnp.dot(
                left[order[entry] // KB], right[order[entry] % KB],
                preferred_element_type=jnp.float32,
            )

        return carry

    lax.fori_loop(first[row], first[row + 1], add, 0)


def mark_targets(target, begin, end, marks):
    def reset(j, carry):
        marks[j] = 0
        return carry

    def mark(number, carry):
        marks[target[number] // NJ] = 1
        return carry

    lax.fori_loop(0, KB, reset, 0)
    lax.fori_loop(begin, end, mark, 0)


def mark_open(order, first, touched, open_row):
    def one(row, carry):
        def look(entry, found):
            return jnp.maximum(found, touched[order[entry] % KB])

        open_row[row] = lax.fori_loop(first[row], first[row + 1], look, jnp.int32(0))
        return carry

    lax.fori_loop(0, RB, one, 0)


def strip_of(ref, row, size):
    return ref.at[pl.ds(pl.multiple_of(row * size, size), size)]


def middle_kernel(parts_count, order, first, target, flags, *refs):
    shifted, *parts = refs[: 1 + parts_count]
    (
        piece, prev, out, rounded, guests, later, open_row,
        hall, sem_in, sem_home,
        left, right, total, short, touched,
        sem_left, sem_right, sem_prev, sem_out,
    ) = refs[1 + parts_count :]
    arrive = pltpu.make_async_copy(piece.at[pl.ds(0, LENT)], hall, sem_in)
    leave = pltpu.make_async_copy(hall, guests, sem_home)
    arrive.start()
    size = left.shape[1]
    count = first[RB + 2]
    shift = flags[1]
    end = piece.shape[0] - shift

    def prev_copy(row):
        return pltpu.make_async_copy(strip_of(prev, row, size), total.at[row], sem_prev.at[row])

    def start_prev(row, carry):
        prev_copy(row).start()
        return carry

    lax.fori_loop(0, RB, start_prev, 0)
    whole = start_left(shifted, parts, left, flags[0] > 0, sem_left)
    fetched = jnp.minimum(count, end)
    mark_targets(target, 0, fetched, touched)
    clear(right, lambda j: touched[j] > 0)
    start_right([(piece, -shift, 0, end)], fetched, target, right, sem_right)
    arrive.wait()
    leave.start()
    mark_targets(target, end, count, later)
    mark_open(order, first, later, open_row)
    whole.wait()
    finish_right(piece.at[0], right, sem_right, fetched)

    def out_copies(row):
        return (
            pltpu.make_async_copy(total.at[row], strip_of(out, row, size), sem_out.at[row]),
            pltpu.make_async_copy(short.at[row], strip_of(rounded, row, size), sem_out.at[row]),
        )

    def one_row(row, carry):
        open_copy, closed_copy = out_copies(row)
        prev_copy(row).wait()
        add_products(row, order, first, left, right, touched, total)

        @pl.when(open_row[row] > 0)
        def _():
            open_copy.start()

        @pl.when(open_row[row] == 0)
        def _():
            short[row] = total[row].astype(short.dtype)
            closed_copy.start()

        return carry

    def close_row(row, carry):
        open_copy, closed_copy = out_copies(row)

        @pl.when(open_row[row] > 0)
        def _():
            open_copy.wait()

        @pl.when(open_row[row] == 0)
        def _():
            closed_copy.wait()

        return carry

    lax.fori_loop(0, RB, one_row, 0)
    lax.fori_loop(0, RB, close_row, 0)
    leave.wait()


def last_kernel(parts_count, order, first, target, flags, touched, open_row, *refs):
    shifted, *parts = refs[: 1 + parts_count]
    (
        piece, back, *over, prev, _, out,
        left, right, total, short,
        sem_left, sem_right, sem_prev, sem_out,
    ) = refs[1 + parts_count :]
    size = left.shape[1]
    count = first[RB + 2]
    shift, lent = flags[1], flags[2]
    begin = PARTS[0] - shift

    def prev_copy(row):
        return pltpu.make_async_copy(strip_of(prev, row, size), total.at[row], sem_prev.at[row])

    def start_prev(row, carry):
        @pl.when(open_row[row] > 0)
        def _():
            prev_copy(row).start()

        return carry

    lax.fori_loop(0, RB, start_prev, 0)
    whole = start_left(shifted, parts, left, flags[0] > 0, sem_left)
    low = ALWAYS
    sources = [(piece, begin, begin, low - shift), (back, low, low, low + lent)]
    low = low + lent
    for blocks in over:
        high = low + blocks.shape[0]
        sources.append((blocks, low, low, high))
        low = high
    clear(right, lambda j: touched[j] > 0)
    start_right(sources, count, target, right, sem_right)

    def out_copy(row):
        return pltpu.make_async_copy(short.at[row], strip_of(out, row, size), sem_out.at[row])

    whole.wait()
    finish_right(piece.at[0], right, sem_right, count - begin)

    def one_row(row, carry):
        @pl.when(open_row[row] > 0)
        def _():
            prev_copy(row).wait()
            add_products(row, order, first, left, right, touched, total)
            short[row] = total[row].astype(short.dtype)
            out_copy(row).start()

        return carry

    def close_row(row, carry):
        @pl.when(open_row[row] > 0)
        def _():
            out_copy(row).wait()

        return carry

    lax.fori_loop(0, RB, one_row, 0)
    lax.fori_loop(0, RB, close_row, 0)


def step_call(kernel, scalars, operands, specs, out_shape, out_specs, scratch, slots, size):
    return pl.pallas_call(
        kernel,
        out_shape=out_shape,
        grid_spec=pltpu.PrefetchScalarGridSpec(
            num_scalar_prefetch=len(scalars),
            grid=(RB // GROUP,),
            in_specs=specs,
            out_specs=out_specs,
            scratch_shapes=[
                pltpu.VMEM((slots, size, size), jnp.bfloat16),
                pltpu.VMEM((KB, size, NJ * size), jnp.bfloat16),
                *scratch,
                pltpu.SemaphoreType.DMA,
                pltpu.SemaphoreType.DMA,
            ],
        ),
        compiler_params=pltpu.CompilerParams(
            dimension_semantics=("arbitrary",), vmem_limit_bytes=LIMIT
        ),
        cost_estimate=pl.CostEstimate(
            flops=2 * 24 * NJ * size * size * size,
            bytes_accessed=16 * 1024 * 1024,
            transcendentals=0,
        ),
    )(*scalars, *operands)


def table_kernel(where_ref, cols_ref, out, where, cols, tile, sems):
    copies = [
        pltpu.make_async_copy(where_ref, where, sems.at[0]),
        pltpu.make_async_copy(cols_ref, cols, sems.at[1]),
    ]
    for copy in copies:
        copy.start()
    rcap, across = cols.shape
    devices = where.shape[-1]
    tile[...] = jnp.zeros(tile.shape, tile.dtype)
    for copy in copies:
        copy.wait()
    for slot in range(rcap):
        tile[pl.ds(0, 1), pl.ds(slot * across, across)] = cols[pl.ds(slot, 1), :]
    for half in range(2):
        row, lane = divmod(half * devices, 128)
        tile[pl.ds(1 + row, 1), pl.ds(lane, devices)] = where[half]

    def fill(device, carry):
        out[device] = tile[...]
        return carry

    lax.fori_loop(0, out.shape[0], fill, 0)


def table_for_all(where, cols):
    devices = where.shape[-1]
    shape = (1 + -(-2 * devices // 128), 128)
    return pl.pallas_call(
        table_kernel,
        out_shape=jax.ShapeDtypeStruct((devices, *shape), jnp.int32),
        in_specs=[ANYWHERE, ANYWHERE],
        scratch_shapes=[
            pltpu.VMEM(where.shape, jnp.int32),
            pltpu.VMEM(cols.shape, jnp.int32),
            pltpu.VMEM(shape, jnp.int32),
            pltpu.SemaphoreType.DMA((2,)),
        ],
        compiler_params=pltpu.CompilerParams(vmem_limit_bytes=LIMIT),
    )(in_hbm(where), in_hbm(cols))


def needed(where_all, cols_all, rows_count, cols_count):
    grid = where_all.reshape(-1, 2, rows_count, cols_count)
    after = jnp.concatenate([grid[:, 0, :, 1:], grid[:, 1, :, :1]], axis=-1)
    columns = jnp.arange(KB, dtype=jnp.int32)
    hit = (after[..., None] >= 0) & (after[..., None] % KB == columns)
    wanted = jnp.any(hit, axis=0).astype(jnp.int32)
    counts = jnp.sum((cols_all >= 0).astype(jnp.int32), axis=1)
    counts = jnp.roll(counts.reshape(rows_count, cols_count, KB), -1, axis=0)
    return jnp.sum(wanted * counts, axis=-1)


def swapped(value):
    return lax.ppermute(value, "col", [(i, i ^ 1) for i in range(lax.axis_size("col"))])


def local(a_send, a_where, b_strips, b_cols):
    size = a_send.shape[-1]
    rows_count = lax.axis_size("row")
    cols_count = lax.axis_size("col")
    devices = rows_count * cols_count
    both = ("row", "col")
    row_index = lax.axis_index("row")
    col_index = lax.axis_index("col")
    rcap = b_strips.shape[3]
    last = cols_count - 1

    by_slot = jnp.swapaxes(b_cols, 2, 3).reshape(rcap, KB)
    tables = lax.all_to_all(
        table_for_all(a_where, by_slot), both, split_axis=0, concat_axis=0, tiled=True
    )
    after_col = (col_index + 1) % cols_count
    after_half = (col_index + 1) // cols_count
    row_before = (row_index + rows_count - 1) % rows_count
    row_after = (row_index + 1) % rows_count
    needs = needed(
        tables[:, 1:].reshape(devices, -1)[:, : 2 * devices],
        tables[:, 0].reshape(devices, rcap, KB), rows_count, cols_count,
    )
    room = ALWAYS - jnp.flip(needs.reshape(rows_count, -1, 2), -1).reshape(needs.shape)
    lent = jnp.maximum(jnp.minimum(jnp.minimum(needs - ALWAYS, room), LENT), 0)
    most = jnp.max(needs - lent)

    def lent_to(row, col):
        return lax.dynamic_slice(lent, (row, col), (1, 1))[0, 0]

    spot = jnp.stack([
        after_half,
        row_index * cols_count + col_index,
        row_index * cols_count + after_col,
        row_before * cols_count + after_col,
        row_after * cols_count + col_index,
        lent_to(row_before, col_index ^ 1),
        lent_to(row_before, col_index),
    ]).astype(jnp.int32)

    wrapped = a_send[1, 0].reshape(rows_count, cols_count, size, size)[:, 0]
    wrapped = wrapped.reshape(devices, size // cols_count, size)
    received = lax.all_to_all(
        jnp.concatenate([a_send[0, 0], wrapped], axis=1),
        both, split_axis=0, concat_axis=0, tiled=True,
    )

    def to_row_before(blocks):
        return lax.ppermute(
            blocks, "row", [(i, (i - 1) % rows_count) for i in range(rows_count)]
        )

    strips = b_strips.reshape(KB * rcap, size, size)
    guests, *over = pack(pack_spare, (LENT, *PARTS[2:]), spot, tables, strips)
    begin, extra = ALWAYS, []
    for blocks in over:
        extra.append(lax.cond(most > begin, to_row_before, lambda same: same, blocks))
        begin += blocks.shape[0]
    early, late = pack(
        pack_main, PARTS[:2], spot, tables, strips, swapped(guests),
        *(blocks[0, :16] for blocks in extra),
    )
    early, late = map(to_row_before, after(received[0, :16], [early, late]))

    shifted = lax.ppermute(
        received, "col", [(i, (i - 1) % cols_count) for i in range(cols_count)]
    )
    part = received[:, size:]
    parts = [lax.ppermute(part, "col", [(i, last)]) for i in range(1, last)] + [part]

    wide = NJ * size
    strip = pl.BlockSpec((GROUP * size, wide), lambda i, *_: (i, 0))
    begun, order, first, target = step_call(
        functools.partial(first_kernel, rcap),
        (spot,), (tables, received, in_hbm(strips)), [ANYWHERE, ANYWHERE, ANYWHERE],
        [
            pltpu.HBM((RB * size, wide), jnp.float32),
            jax.ShapeDtypeStruct((devices,), jnp.int32),
            jax.ShapeDtypeStruct((RB + 3,), jnp.int32),
            jax.ShapeDtypeStruct((KB * rcap,), jnp.int32),
        ],
        [strip, IN_SMEM, IN_SMEM, IN_SMEM],
        [
            pltpu.SMEM(tables.shape, jnp.int32),
            pltpu.SemaphoreType.DMA,
            pltpu.SMEM((devices,), jnp.int32),
            pltpu.SMEM((RB + 2,), jnp.int32),
            pltpu.SMEM((KB,), jnp.int32),
            pltpu.SMEM((KB,), jnp.int32),
        ],
        devices, size,
    )

    on_last = (col_index == last).astype(jnp.int32)
    lent_here = [lent_to(row_index, col_index ^ 1), lent_to(row_index, col_index)]
    scalars = (order, first, target, jnp.stack([on_last, *lent_here]))
    lefts = (shifted, *parts)

    def finish_call(kernel, scalars, operands, out_shape, out_specs, scratch, marks, aliases):
        return pl.pallas_call(
            kernel,
            out_shape=out_shape,
            grid_spec=pltpu.PrefetchScalarGridSpec(
                num_scalar_prefetch=len(scalars),
                grid=(1,),
                in_specs=[ANYWHERE] * len(operands),
                out_specs=out_specs,
                scratch_shapes=[
                    *scratch,
                    pltpu.VMEM((devices, size, size), jnp.bfloat16),
                    pltpu.VMEM((KB, size, wide), jnp.bfloat16),
                    pltpu.VMEM((RB, size, wide), jnp.float32),
                    pltpu.VMEM((RB, size, wide), jnp.bfloat16),
                    *marks,
                    pltpu.SemaphoreType.DMA,
                    pltpu.SemaphoreType.DMA,
                    pltpu.SemaphoreType.DMA((RB,)),
                    pltpu.SemaphoreType.DMA((RB,)),
                ],
            ),
            input_output_aliases=aliases,
            compiler_params=pltpu.CompilerParams(vmem_limit_bytes=LIMIT),
            cost_estimate=pl.CostEstimate(
                flops=2 * 16 * NJ * size * size * size,
                bytes_accessed=12 * 1024 * 1024,
                transcendentals=0,
            ),
        )(*scalars, *operands)

    begun, rounded, guests, later, open_row = finish_call(
        functools.partial(middle_kernel, len(parts)), scalars,
        (*lefts, early, in_hbm(begun)),
        [
            pltpu.HBM((RB * size, wide), jnp.float32),
            pltpu.HBM((RB * size, wide), jnp.bfloat16),
            pltpu.HBM((LENT, size, size), jnp.bfloat16),
            jax.ShapeDtypeStruct((KB,), jnp.int32),
            jax.ShapeDtypeStruct((RB,), jnp.int32),
        ],
        [ANYWHERE, ANYWHERE, ANYWHERE, IN_SMEM, IN_SMEM],
        [
            pltpu.VMEM((LENT, size, size), jnp.bfloat16),
            pltpu.SemaphoreType.DMA,
            pltpu.SemaphoreType.DMA,
        ],
        [pltpu.SMEM((KB,), jnp.int32)], {},
    )
    back = swapped(guests)

    operands = (*lefts, late, back, *extra, in_hbm(begun), rounded)
    scalars = (*scalars, later, open_row)
    return finish_call(
        functools.partial(last_kernel, len(parts)), scalars, operands,
        jax.ShapeDtypeStruct((RB * size, wide), jnp.bfloat16),
        ANYWHERE, [], [], {len(scalars) + len(operands) - 1: 0},
    )


def solution(mesh):
    placed = (
        P(None, ("row", "col"), None, None, None),
        P(None, ("row", "col"), None),
        P("row", "col", None, None, None, None),
        P("row", "col", None, None),
    )
    return jax.shard_map(
        local, mesh=mesh, in_specs=placed, out_specs=P("row", "col"), check_vma=False
    )
```
